32 devices in a mesh: role: 2 (over core), dp: 16 (over z, y, x).
Axes of the slice: x: 2, y: 2, z: 4, core: 2. Of those that a mesh axis runs over, the one named last changes fastest.
Arguments:
- frames: bfloat16 [32, 384, 512], P('dp'), may hold values from -6 to 6
- step_lengths: int32 [32], P('dp'), may hold values from 48 to 192, as said below
- characters: int32 [16, 2, 72], P('dp', 'role'), may hold values from 0 to 29
- char_lengths: int32 [16, 2], P('dp', 'role'), may hold values from 18 to 72, as said below
- listen_input: bfloat16 [2, 1024, 1024], P('role'), may hold values from -0.1875 to 0.1875
- listen_hidden: bfloat16 [2, 256, 1024], P('role'), may hold values from -0.375 to 0.375
- listen_bias: bfloat16 [2, 1024], P('role'), may hold values from -3 to 7
- lower_input: bfloat16 [768, 2048], replicated, may hold values from -0.21875 to 0.21875
- lower_hidden: bfloat16 [512, 2048], replicated, may hold values from -0.25 to 0.25
- lower_bias: bfloat16 [2048], replicated, may hold values from -3 to 7
- upper_input: bfloat16 [512, 2048], replicated, may hold values from -0.25 to 0.25
- upper_hidden: bfloat16 [512, 2048], replicated, may hold values from -0.25 to 0.25
- upper_bias: bfloat16 [2048], replicated, may hold values from -3 to 7
- key_proj: bfloat16 [512, 512], replicated, may hold values from -0.5 to 0.5
- query_proj: bfloat16 [512, 512], replicated, may hold values from -0.5 to 0.5
- score_vector: bfloat16 [512], replicated, may hold values from -1 to 1
- output_proj: bfloat16 [1024, 30], replicated, may hold values from -1.5 to 1.5
- output_bias: bfloat16 [30], replicated, may hold values from -4 to 4
- char_table: bfloat16 [30, 256], replicated, may hold values from -5 to 5
Outputs:
- loss: float32 [16, 2], P('dp', 'role')
- frames_grad: float32 [32, 384, 512], P('dp', 'role')
- grad_listen_input: float32 [2, 1024, 1024], P('role')
- grad_listen_hidden: float32 [2, 256, 1024], P('role')
- grad_listen_bias: float32 [2, 1024], P('role')
- grad_lower_input: float32 [768, 2048], replicated
- grad_lower_hidden: float32 [512, 2048], replicated
- grad_lower_bias: float32 [2048], replicated
- grad_upper_input: float32 [512, 2048], replicated
- grad_upper_hidden: float32 [512, 2048], replicated
- grad_upper_bias: float32 [2048], replicated
- grad_key_proj: float32 [512, 512], replicated
- grad_query_proj: float32 [512, 512], replicated
- grad_score_vector: float32 [512], replicated
- grad_output_proj: float32 [1024, 30], replicated
- grad_output_bias: float32 [30], replicated
- grad_char_table: float32 [30, 256], replicated
The draws below stay inside these ranges and needn't reach their ends.
Inputs may be any that keep to these rules, and one draw needn't show every extreme that they name: `step_lengths`: every draw has an utterance of 192 frame pairs. `char_lengths`: every draw has a transcript of 72 characters.
All inputs are finite; a program needn't handle non-finite values.
Results may differ from the reference program's by a relative error of at most 0.008.
Values may be sent and summed in bfloat16 or wider, within the bound.
A program may use at most 192 MiB of HBM per device.

```python
import math
import jax
import jax.numpy as jnp
import numpy as np
from jax import lax

FEAT = 512
HID = 256
SP = 512
ATT = 512
EMB = 256
VOCAB = 30
TL = 192
CHARS = 72
UTT_DEV = 2
UTTS = 32
N_DP = 16


def draw_step_lengths(key, part):
    key = jax.random.fold_in(key, 11)
    first, second = jax.random.split(key)
    values = jax.random.randint(first, (UTTS,), TL // 4, TL + 1)
    place = jax.random.randint(second, (), 0, UTTS)
    return jnp.where(jnp.arange(UTTS) == place, TL, values).astype(jnp.int32)


def draw_char_lengths(key, part):
    key = jax.random.fold_in(key, 23)
    first, second = jax.random.split(key)
    values = jax.random.randint(first, (UTTS,), CHARS // 4, CHARS + 1)
    place = jax.random.randint(second, (), 0, UTTS)
    values = jnp.where(jnp.arange(UTTS) == place, CHARS, values).astype(jnp.int32)
    return values.reshape(UTTS // UTT_DEV, UTT_DEV)


def gate_biases(key, lead, units, slow_share, base_values):
    flag_key, forget_key, input_key = jax.random.split(key, 3)
    slow = jax.random.bernoulli(flag_key, slow_share, lead + (units,))
    forget_slow = jax.random.uniform(forget_key, lead + (units,), jnp.float32, 5.0, 7.0)
    input_slow = jax.random.uniform(input_key, lead + (units,), jnp.float32, -3.0, -2.0)
    input_part = jnp.where(slow, input_slow, base_values[..., :units])
    forget_part = jnp.where(slow, forget_slow, base_values[..., units:2 * units])
    return jnp.concatenate([input_part, forget_part, base_values[..., 2 * units:]], -1)


def base_normal(key, shape):
    return jnp.clip(0.5 * jax.random.normal(key, shape, jnp.float32), -3.0, 3.0)


def draw_listen_bias(key, part):
    key = jax.random.fold_in(key, 37)
    first, second = jax.random.split(key)
    values = gate_biases(second, (2,), HID, 0.5, base_normal(first, (2, 4 * HID)))
    return values.astype(jnp.bfloat16)


def draw_lower_bias(key, part):
    key = jax.random.fold_in(key, 41)
    first, second = jax.random.split(key)
    values = gate_biases(second, (), SP, 0.5, base_normal(first, (4 * SP,)))
    return values.astype(jnp.bfloat16)


def draw_upper_bias(key, part):
    key = jax.random.fold_in(key, 43)
    first, second = jax.random.split(key)
    values = gate_biases(second, (), SP, 0.5, base_normal(first, (4 * SP,)))
    return values.astype(jnp.bfloat16)


def with_ends(values, stream_key, low, top_value):
    spot = [jax.random.randint(jax.random.fold_in(stream_key, axis), (), 0, length) for axis, length in enumerate(values.shape)]
    widest = values.shape.index(max(values.shape))
    beside = spot[:widest] + [(spot[widest] + 1) % values.shape[widest]] + spot[widest + 1:]
    return values.at[tuple(spot)].set(low).at[tuple(beside)].set(top_value)


def block_levels(stream_key, dims, cuts, least, largest):
    gain = 1.0
    for axis_at, shards_of in cuts:
        draws = jax.random.uniform(jax.random.fold_in(jax.random.fold_in(stream_key, 6), axis_at), (shards_of,), jnp.float32, least / len(cuts), largest / len(cuts))
        gain = gain * jnp.repeat(jnp.exp(draws), dims[axis_at] // shards_of).reshape((-1,) + (1,) * (len(dims) - 1 - axis_at))
    return gain


def cumulative_ranks(number_of, lean):
    loads = [(1 << 20) // math.isqrt(standing ** lean) + 1 for standing in range(1, number_of + 1)]
    scale = 1 + sum(loads) // (1 << 30)
    return np.cumsum(np.array([max(1, weight // scale) for weight in loads]))


def skewed_ids(own_key, dims, number_of, lean):
    grid = cumulative_ranks(number_of, lean)
    ticket = jax.random.randint(jax.random.fold_in(own_key, 1), dims, 0, int(grid[number_of - 1]))
    grade = jnp.searchsorted(jnp.asarray(grid, jnp.int32), ticket, side="right")
    return jax.random.permutation(jax.random.fold_in(own_key, 2), number_of)[grade].astype(jnp.int32)


def noise(stream_key, shape, scale, bound, cuts=(), held_as=jnp.bfloat16):
    result = scale * jax.random.normal(stream_key, shape, jnp.float32)
    if cuts:
        result = result * block_levels(stream_key, shape, cuts, -0.22, 0.18)
    return jnp.clip(result, -bound, bound).astype(held_as)


def setup_inputs(seed: int = 0) -> dict:
    key_list = jax.random.split(jax.random.key(seed), 20)
    return {
        "frames": noise(key_list[0], (UTTS, 2 * TL, FEAT), 1.0, 6.0, ((0, 16),)),
        "step_lengths": draw_step_lengths(jax.random.fold_in(key_list[19], 71), 0),
        "characters": with_ends(skewed_ids(key_list[2], (N_DP, UTT_DEV, CHARS), VOCAB, 2), jax.random.fold_in(key_list[2], 3), 0, VOCAB - 1).astype(jnp.int32),
        "char_lengths": draw_char_lengths(jax.random.fold_in(key_list[19], 71), 0),
        "listen_input": noise(key_list[4], (2, 2 * FEAT, 4 * HID), (2 * FEAT) ** -0.5, 0.1875, ((0, 2),)),
        "listen_hidden": noise(key_list[5], (2, HID, 4 * HID), HID ** -0.5, 0.375, ((0, 2),)),
        "listen_bias": draw_listen_bias(jax.random.fold_in(key_list[19], 71), 0),
        "lower_input": noise(key_list[7], (EMB + 2 * HID, 4 * SP), (EMB + 2 * HID) ** -0.5, 0.21875),
        "lower_hidden": noise(key_list[8], (SP, 4 * SP), SP ** -0.5, 0.25),
        "lower_bias": draw_lower_bias(jax.random.fold_in(key_list[19], 71), 0),
        "upper_input": noise(key_list[10], (SP, 4 * SP), SP ** -0.5, 0.25),
        "upper_hidden": noise(key_list[11], (SP, 4 * SP), SP ** -0.5, 0.25),
        "upper_bias": draw_upper_bias(jax.random.fold_in(key_list[19], 71), 0),
        "key_proj": noise(key_list[13], (2 * HID, ATT), (2 * HID // 4) ** -0.5, 0.5),
        "query_proj": noise(key_list[14], (SP, ATT), (SP // 4) ** -0.5, 0.5),
        "score_vector": noise(key_list[15], (ATT,), 0.15, 1.0),
        "output_proj": noise(key_list[16], (SP + 2 * HID, VOCAB), 0.25, 1.5),
        "output_bias": noise(key_list[17], (VOCAB,), 1.0, 4.0),
        "char_table": noise(key_list[18], (VOCAB, EMB), 1.0, 5.0),
    }


@jax.custom_vjp
def low(v):
    return lax.optimization_barrier(v.astype(jnp.bfloat16)).astype(jnp.float32)

@jax.custom_vjp
def low_back(v):
    return v

def low_keep(v):
    return (low(v), None)

def low_pass(kept, grad):
    return (grad,)

def back_keep(v):
    return (v, None)

def back_low(kept, grad):
    return (low(grad),)
low.defvjp(low_keep, low_pass)
low_back.defvjp(back_keep, back_low)

def matmul(left, right):
    return jnp.dot(left, right, precision=lax.Precision.HIGHEST)

def lstm_cell(preact, cell_prev):
    quarter = preact.shape[-1] // 4
    in_gate = jax.nn.sigmoid(preact[..., :quarter])
    forget = jax.nn.sigmoid(preact[..., quarter:2 * quarter])
    candid = jnp.tanh(preact[..., 2 * quarter:3 * quarter])
    out_gate = jax.nn.sigmoid(preact[..., 3 * quarter:])
    cell_new = forget * cell_prev + in_gate * candid
    return (out_gate * jnp.tanh(cell_new), cell_new)

def listen_dir(frame_pairs, frame_mask, weight_in, weight_rec, bias_vec):
    batch_rows, time_len, in_width = frame_pairs.shape
    projected = matmul(frame_pairs.reshape(batch_rows * time_len, in_width), weight_in)
    projected = projected.reshape(batch_rows, time_len, -1) + bias_vec
    units = weight_rec.shape[0]

    def listen_step(carried, inputs):
        hidden, cell_state = carried
        proj_t, mask_t = inputs
        preact = low_back(proj_t + matmul(low(hidden), weight_rec))
        hidden_new, cell_new = lstm_cell(preact, cell_state)
        mask_col = mask_t[:, None]
        hidden_next = mask_col * hidden_new + (1.0 - mask_col) * hidden
        cell_next = mask_col * cell_new + (1.0 - mask_col) * cell_state
        return ((hidden_next, cell_next), mask_col * low(hidden_next))
    zeros_state = jnp.zeros((batch_rows, units), jnp.float32)
    _, emitted = lax.scan(jax.checkpoint(listen_step), (zeros_state, zeros_state), (jnp.swapaxes(projected, 0, 1), frame_mask.T))
    return jnp.swapaxes(emitted, 0, 1)

def speller(key_feats, step_lengths, characters, char_lengths, lower_input, lower_hidden, lower_bias, upper_input, upper_hidden, upper_bias, key_proj, query_proj, score_vector, output_proj, output_bias, char_table):
    batch_rows, time_len, _ = key_feats.shape
    text_steps = characters.shape[1]
    vocab_size = char_table.shape[0]
    units = lower_hidden.shape[0]
    keys_proj = low_back(jnp.einsum('btd,da->bta', key_feats, key_proj, precision=lax.Precision.HIGHEST))
    frame_ok = jnp.arange(time_len)[None, :] < step_lengths[:, None]
    previous = jnp.concatenate([jnp.zeros((batch_rows, 1), jnp.int32), characters[:, :-1]], 1)
    prev_onehot = (previous.T[..., None] == jnp.arange(vocab_size)[None, None, :]).astype(jnp.float32)
    embedded = jnp.einsum('cbv,ve->cbe', prev_onehot, char_table, precision=lax.Precision.HIGHEST)
    target_onehot = (characters.T[..., None] == jnp.arange(vocab_size)[None, None, :]).astype(jnp.float32)

    def spell_step(carried, inputs):
        hidden_one, cell_one, hidden_two, cell_two, context = carried
        emb_t, target_t = inputs
        joined = jnp.concatenate([emb_t, context], -1)
        preact_one = low_back(matmul(joined, lower_input) + matmul(low(hidden_one), lower_hidden) + lower_bias)
        hidden_one_new, cell_one_new = lstm_cell(preact_one, cell_one)
        lower_out = low(hidden_one_new)
        preact_two = low_back(matmul(lower_out, upper_input) + matmul(low(hidden_two), upper_hidden) + upper_bias)
        hidden_two_new, cell_two_new = lstm_cell(preact_two, cell_two)
        upper_out = low(hidden_two_new)
        query_vec = low_back(matmul(upper_out, query_proj))
        energy = jnp.tanh(keys_proj + query_vec[:, None, :])
        scores = jnp.einsum('bta,a->bt', energy, score_vector, precision=lax.Precision.HIGHEST)
        scores = jnp.where(frame_ok, scores, -1000000000.0)
        weights = low(jax.nn.softmax(scores, axis=-1))
        context_new = low(low_back(jnp.einsum('bt,btd->bd', weights, key_feats, precision=lax.Precision.HIGHEST)))
        logits = low_back(matmul(jnp.concatenate([upper_out, context_new], -1), output_proj) + output_bias)
        cross = jax.nn.logsumexp(logits, axis=-1) - lax.optimization_barrier(jnp.sum(logits * target_t, -1))
        return ((hidden_one_new, cell_one_new, hidden_two_new, cell_two_new, context_new), cross)
    zeros_state = jnp.zeros((batch_rows, units), jnp.float32)
    zeros_ctx = jnp.zeros((batch_rows, key_feats.shape[-1]), jnp.float32)
    _, crosses = lax.scan(jax.checkpoint(spell_step), (zeros_state, zeros_state, zeros_state, zeros_state, zeros_ctx), (embedded, target_onehot))
    text_mask = (jnp.arange(text_steps)[:, None] < char_lengths[None, :]).astype(jnp.float32)
    return lax.optimization_barrier(jnp.sum(crosses * text_mask, 0)) / char_lengths.astype(jnp.float32)

def reference(frames, step_lengths, characters, char_lengths, listen_input, listen_hidden, listen_bias, lower_input, lower_hidden, lower_bias, upper_input, upper_hidden, upper_bias, key_proj, query_proj, score_vector, output_proj, output_bias, char_table):
    chars_flat = characters.reshape(UTTS, CHARS)
    lengths_flat = char_lengths.reshape(UTTS)
    frame_mask = (jnp.arange(TL)[None, :] < step_lengths[:, None]).astype(jnp.float32)

    def forward(frames_f, lin, lhid, lbias, w_one, h_one, b_one, w_two, h_two, b_two, kproj, qproj, svec, oproj, obias, table):
        frame_pairs = frames_f.reshape(UTTS, TL, 2 * FEAT)
        ahead = listen_dir(frame_pairs, frame_mask, lin[0], lhid[0], lbias[0])
        behind = jnp.flip(listen_dir(jnp.flip(frame_pairs, 1), jnp.flip(frame_mask, 1), lin[1], lhid[1], lbias[1]), 1)
        key_feats = low_back(jnp.concatenate([ahead, behind], -1))
        return speller(key_feats, step_lengths, chars_flat, lengths_flat, w_one, h_one, b_one, w_two, h_two, b_two, kproj, qproj, svec, oproj, obias, table)
    floats = [frames, listen_input, listen_hidden, listen_bias, lower_input, lower_hidden, lower_bias, upper_input, upper_hidden, upper_bias, key_proj, query_proj, score_vector, output_proj, output_bias, char_table]
    floats = [item.astype(jnp.float32) for item in floats]
    losses, pullback = jax.vjp(forward, *floats)
    grads = pullback(jnp.ones_like(losses))
    return (losses.reshape(N_DP, UTT_DEV), grads[0], grads[1], grads[2], grads[3], grads[4], grads[5], grads[6], grads[7], grads[8], grads[9], grads[10], grads[11], grads[12], grads[13], grads[14], grads[15])
```

```python
import functools

import jax
import jax.numpy as jnp
from jax import lax
from jax.experimental import pallas as pl
from jax.experimental.pallas import tpu as pltpu
from jax.sharding import PartitionSpec as P

F32 = jnp.float32
BF16 = jnp.bfloat16
VMEM_BYTES = 60 * 1024 * 1024
SAFE_SCORE = 80.0


def mm(left, right):
    return jnp.dot(left, right, preferred_element_type=F32)


def mm_nt(left, right):
    return lax.dot_general(left, right, (((1,), (1,)), ((), ())), preferred_element_type=F32)


def mm_tn(left, right):
    return lax.dot_general(left, right, (((0,), (0,)), ((), ())), preferred_element_type=F32)


def sigmoid(x):
    return 0.5 * jnp.tanh(0.5 * x) + 0.5


def cell_forward(preact, cell_prev):
    n = preact.shape[-1] // 4
    in_gate = sigmoid(preact[:, :n])
    forget = sigmoid(preact[:, n : 2 * n])
    candid = jnp.tanh(preact[:, 2 * n : 3 * n])
    out_gate = sigmoid(preact[:, 3 * n :])
    cell_new = forget * cell_prev + in_gate * candid
    tanh_cell = jnp.tanh(cell_new)
    hidden = out_gate * tanh_cell
    factors = (
        candid * in_gate * (1.0 - in_gate),
        cell_prev * forget * (1.0 - forget),
        in_gate * (1.0 - candid * candid),
        tanh_cell * out_gate * (1.0 - out_gate),
        out_gate * (1.0 - tanh_cell * tanh_cell),
        forget,
    )
    return cell_new, hidden, factors


def cell_backward(factors, grad_hidden, grad_cell):
    n = factors.shape[-1] // 6
    part = lambda k: factors[:, k * n : (k + 1) * n]
    total = grad_cell + grad_hidden * part(4)
    grad_preact = jnp.concatenate(
        [total * part(0), total * part(1), total * part(2), grad_hidden * part(3)], -1
    )
    return grad_preact, total * part(5)


def listen_forward_kernel(
    lengths, frames, w_in, w_rec, bias, pairs_out, factors_out, hprev_out, mine_out, other_out,
    proj, emit,
):
    role = lax.axis_index("role")
    utts, time_len, width4 = proj.shape
    units = width4 // 4
    feat = frames.shape[-1]
    rows = lax.broadcasted_iota(jnp.int32, (time_len, 2 * time_len), 0)
    cols = lax.broadcasted_iota(jnp.int32, (time_len, 2 * time_len), 1)
    for half in range(2):
        pick = jnp.where(cols == 2 * rows + half, 1.0, 0.0).astype(BF16)
        for u in range(utts):
            pairs_out[u, :, half * feat : (half + 1) * feat] = mm(pick, frames[u]).astype(BF16)
    bias_row = bias[...].astype(F32)
    for u in range(utts):
        proj[u] = mm(pairs_out[u], w_in[...]) + bias_row
    first = lax.broadcasted_iota(jnp.int32, (8, 1), 0) == 0
    row_lengths = jnp.where(first, lengths[0], lengths[1])

    def step(s, carry):
        hidden, cell = carry
        t = jnp.where(role == 1, time_len - 1 - s, s)
        at = pl.ds(t, 1)
        pre_in = jnp.where(first, proj[0, at, :], proj[1, at, :])
        low = hidden.astype(BF16)
        cell_new, hidden_new, factors = cell_forward(pre_in + mm(low, w_rec[...]), cell)
        live = t < row_lengths
        hidden_next = jnp.where(live, hidden_new, hidden)
        cell_next = jnp.where(live, cell_new, cell)
        emitted = jnp.where(live, hidden_new, 0.0)
        for u in range(2):
            for k in range(6):
                factors_out[u, at, k * units : (k + 1) * units] = factors[k][u : u + 1]
            hprev_out[u, at, :] = hidden[u : u + 1]
            emit[u, at, :] = emitted[u : u + 1]
        return hidden_next, cell_next

    zero = jnp.zeros((8, units), F32)
    lax.fori_loop(0, time_len, step, (zero, zero))
    mine_out[...] = emit[role].astype(BF16)
    other_out[...] = emit[1 - role].astype(BF16)


def listen_forward(lengths, frames, w_in, w_rec, bias):
    utts, frame_len, feat = frames.shape
    time_len = frame_len // 2
    units = w_rec.shape[0]
    vmem = pl.BlockSpec(memory_space=pltpu.VMEM)
    shape = jax.ShapeDtypeStruct
    return pl.pallas_call(
        listen_forward_kernel,
        out_shape=(
            shape((utts, time_len, 2 * feat), BF16),
            shape((utts, time_len, 6 * units), F32),
            shape((utts, time_len, units), F32),
            shape((time_len, units), BF16),
            shape((time_len, units), BF16),
        ),
        in_specs=[pl.BlockSpec(memory_space=pltpu.SMEM)] + [vmem] * 4,
        out_specs=(vmem,) * 5,
        scratch_shapes=[
            pltpu.VMEM((utts, time_len, 4 * units), F32),
            pltpu.VMEM((utts, time_len, units), F32),
        ],
        compiler_params=pltpu.CompilerParams(vmem_limit_bytes=VMEM_BYTES),
    )(lengths, frames, w_in, w_rec, bias)


def listen_backward_kernel(
    lengths, pairs, factors, hprev, grad_mine, grad_other, w_in, w_rec,
    grad_in, grad_rec, grad_bias, grad_pairs, grad_pre, grad_out,
):
    role = lax.axis_index("role")
    utts, time_len, width4 = grad_pre.shape
    units = width4 // 4
    grad_out[role] = grad_mine[...].astype(F32)
    grad_out[1 - role] = grad_other[...].astype(F32)
    first = lax.broadcasted_iota(jnp.int32, (8, 1), 0) == 0
    row_lengths = jnp.where(first, lengths[0], lengths[1])

    def step(s, carry):
        grad_hidden, grad_cell = carry
        t = jnp.where(role == 1, s, time_len - 1 - s)
        at = pl.ds(t, 1)
        live = t < row_lengths
        fact = jnp.where(first, factors[0, at, :], factors[1, at, :])
        arrived = jnp.where(first, grad_out[0, at, :], grad_out[1, at, :])
        fact = jnp.where(live, fact, 0.0)
        total = grad_hidden + jnp.where(live, arrived, 0.0)
        pre, cell_back = cell_backward(fact, total, grad_cell)
        pre_low = pre.astype(BF16)
        for u in range(2):
            grad_pre[u, at, :] = pre[u : u + 1]
        back = mm_nt(pre_low, w_rec[...])
        return jnp.where(live, back, total), jnp.where(live, cell_back, grad_cell)

    zero = jnp.zeros((8, units), F32)
    lax.fori_loop(0, time_len, step, (zero, zero))
    in_sum = None
    for u in range(utts):
        low = grad_pre[u].astype(BF16)
        grad_pairs[u] = mm_nt(low, w_in[...])
        bias_part = jnp.sum(low.astype(F32), 0, keepdims=True)
        if u == 0:
            grad_in[...] = mm_tn(pairs[u], low)
            grad_rec[...] = mm_tn(hprev[u].astype(BF16), low)
            grad_bias[...] = bias_part
        else:
            grad_in[...] += mm_tn(pairs[u], low)
            grad_rec[...] += mm_tn(hprev[u].astype(BF16), low)
            grad_bias[...] += bias_part


def listen_backward(lengths, pairs, factors, hprev, grad_mine, grad_other, w_in, w_rec):
    utts, time_len, width = pairs.shape
    units = w_rec.shape[0]
    vmem = pl.BlockSpec(memory_space=pltpu.VMEM)
    shape = jax.ShapeDtypeStruct
    return pl.pallas_call(
        listen_backward_kernel,
        out_shape=(
            shape((width, 4 * units), F32),
            shape((units, 4 * units), F32),
            shape((1, 4 * units), F32),
            shape((utts, time_len, width), F32),
        ),
        in_specs=[pl.BlockSpec(memory_space=pltpu.SMEM)] + [vmem] * 7,
        out_specs=(vmem,) * 4,
        scratch_shapes=[
            pltpu.VMEM((utts, time_len, 4 * units), F32),
            pltpu.VMEM((utts, time_len, units), F32),
        ],
        compiler_params=pltpu.CompilerParams(vmem_limit_bytes=VMEM_BYTES),
    )(lengths, pairs, factors, hprev, grad_mine, grad_other, w_in, w_rec)


def shift_down(rows):
    rolled = pltpu.roll(rows, 1, 0)
    at = lax.broadcasted_iota(jnp.int32, rows.shape, 0)
    return jnp.where(at == 0, 0.0, rolled)


def shift_up(rows):
    count = rows.shape[0]
    rolled = pltpu.roll(rows, count - 1, 0)
    at = lax.broadcasted_iota(jnp.int32, rows.shape, 0)
    return jnp.where(at == count - 1, 0.0, rolled)


def speller_kernel(
    lengths, text_lens,
    mine, other, prev_onehot, target_onehot,
    w_lin, w_lhid, b_low, w_uin, w_uhid, b_up, w_key, w_query, vec, w_out, b_out, table,
    loss, grad_mine, grad_other,
    g_lin, g_lhid, g_lbias, g_uin, g_uhid, g_ubias, g_key, g_query, g_vec, g_out, g_obias, g_table,
    key, keys_proj, key_low, key_low_t, emb_proj,
    fact1, fact2, s1_rows, s2_rows, q_rows, w_rows, feat_rows, dw_rows,
    dp1_rows, dp2_rows, dq_rows, m_scr, keys_acc, vec_acc,
):
    role = lax.axis_index("role")
    time_len, units = mine.shape
    steps = emb_proj.shape[0]
    cells = w_lhid.shape[0]
    embed = table.shape[1]
    pad_time = key.shape[0]
    length = lengths[role]
    text_len = text_lens[0, 0]

    key[time_len:, :] = jnp.zeros((pad_time - time_len, 2 * units), BF16)
    key[:time_len, :units] = jnp.where(role == 0, mine[...], other[...])
    key[:time_len, units:] = jnp.where(role == 0, other[...], mine[...])
    keys_proj[...] = mm(key[:time_len, :], w_key[...])
    key_low_f32 = mm(key[...], w_lin[embed:, :])
    key_low[...] = key_low_f32.astype(BF16)
    key_low_t[...] = jnp.transpose(key_low_f32).astype(BF16)
    emb = mm(prev_onehot[...], table[...]).astype(BF16)
    emb_proj[...] = mm(emb, w_lin[:embed, :]) + b_low[...].astype(F32)
    bias_up = b_up[...].astype(F32)
    vec_row = vec[...].astype(F32)
    lane = lax.broadcasted_iota(jnp.int32, (1, pad_time), 1)
    frame_ok = lane < length
    ones = jnp.ones((1, 256), BF16)
    tail = jnp.zeros((pad_time - time_len, 256), BF16)

    def forward_step(shift_by_max, i, carry):
        cell1, cell2, hid1, hid2, expw, rinv = carry
        at = pl.ds(i, 1)
        pre1 = emb_proj[at, :] + hid1 + mm(expw, key_low[...]) * rinv
        cell1, s1, factors = cell_forward(pre1, cell1)
        for k in range(6):
            fact1[at, k * cells : (k + 1) * cells] = factors[k]
        s1_rows[at, :] = s1
        s1_low = s1.astype(BF16)
        pre2 = hid2 + bias_up + mm(s1_low, w_uin[...])
        hid1 = mm(s1_low, w_lhid[...])
        cell2, s2, factors = cell_forward(pre2, cell2)
        for k in range(6):
            fact2[at, k * cells : (k + 1) * cells] = factors[k]
        s2_rows[at, :] = s2
        s2_low = s2.astype(BF16)
        query = mm(s2_low, w_query[...])
        hid2 = mm(s2_low, w_uhid[...])
        q_rows[at, :] = query
        part = None
        for j in range(query.shape[1] // 128):
            cut = slice(j * 128, (j + 1) * 128)
            term = jnp.tanh(keys_proj[:, cut] + query[:, cut]) * vec_row[:, cut]
            part = term if part is None else part + term
        high = part.astype(BF16)
        low = (part - high.astype(F32)).astype(BF16)
        split = jnp.concatenate([jnp.concatenate([high, low], 1), tail], 0)
        scores = mm_nt(ones, split)
        if shift_by_max:
            scores = jnp.where(frame_ok, scores, -1000000000.0)
            scores = scores - jnp.max(scores, -1, keepdims=True)
        expf = jnp.where(frame_ok, jnp.exp(scores), 0.0)
        rinv = 1.0 / jnp.sum(expf, -1, keepdims=True)
        w_rows[at, :] = expf * rinv
        return cell1, cell2, hid1, hid2, expf.astype(BF16), rinv

    zero = jnp.zeros((1, cells), F32)
    wide = jnp.zeros((1, 4 * cells), F32)
    start = (zero, zero, wide, wide, jnp.zeros((1, pad_time), BF16), jnp.ones((1, 1), F32))
    bound = jnp.sum(jnp.abs(vec_row))

    @pl.when(bound <= SAFE_SCORE)
    def _():
        lax.fori_loop(0, steps, functools.partial(forward_step, False), start)

    @pl.when(bound > SAFE_SCORE)
    def _():
        lax.fori_loop(0, steps, functools.partial(forward_step, True), start)

    w_low = w_rows[...].astype(BF16)
    ctx = mm(w_low, key[...]).astype(BF16)
    s2_low = s2_rows[...].astype(BF16)
    logits = mm(s2_low, w_out[:cells, :]) + mm(ctx, w_out[cells:, :]) + b_out[...].astype(F32)
    top = jnp.max(logits, -1, keepdims=True)
    log_total = top + jnp.log(jnp.sum(jnp.exp(logits - top), -1, keepdims=True))
    target = target_onehot[...]
    cross = log_total - jnp.sum(logits * target, -1, keepdims=True)
    text = text_len.astype(F32)
    alive = lax.broadcasted_iota(jnp.int32, (steps, 1), 0) < text_len
    loss[...] = jnp.sum(jnp.where(alive, cross, 0.0), 0, keepdims=True) / text
    scale = jnp.where(alive, 1.0 / text, 0.0)
    logit_grad = (scale * (jnp.exp(logits - log_total) - target)).astype(BF16)
    feat_rows[...] = mm_nt(logit_grad, w_out[...])
    dw_rows[...] = mm_nt(feat_rows[:, cells:].astype(BF16), key[...])
    keys_acc[...] = jnp.zeros_like(keys_acc)
    vec_acc[...] = jnp.zeros_like(vec_acc)
    m_scr[time_len:, :] = jnp.zeros((pad_time - time_len, m_scr.shape[1]), BF16)

    def backward_step(s, carry):
        dp1, back1, back2, dcell1, dcell2 = carry
        i = steps - 1 - s
        at = pl.ds(i, 1)
        query = q_rows[at, :]
        weights = w_rows[at, :]
        dweights = dw_rows[at, :] + mm(dp1, key_low_t[...])
        dscore = weights * (dweights - jnp.sum(weights * dweights, -1, keepdims=True))
        dcol = jnp.transpose(jnp.broadcast_to(dscore, (8, pad_time)))[:time_len, :1]
        for j in range(query.shape[1] // 128):
            cut = slice(j * 128, (j + 1) * 128)
            energy = jnp.tanh(keys_proj[:, cut] + query[:, cut])
            slope = 1.0 - energy * energy
            m_scr[:time_len, cut] = slope.astype(BF16)
            keys_acc[:, cut] += dcol * slope
            vec_acc[:, cut] += jnp.sum((dcol * energy).reshape(time_len // 8, 8, 128), 0)
        dquery = (mm(dscore.astype(BF16), m_scr[...]) * vec_row).astype(BF16)
        dq_rows[at, :] = dquery.astype(F32)
        ds2 = back2 + feat_rows[at, :cells] + mm_nt(dquery, w_query[...])
        pre2, dcell2 = cell_backward(fact2[at, :], ds2, dcell2)
        dp2_rows[at, :] = pre2
        dp2 = pre2.astype(BF16)
        ds1 = back1 + mm_nt(dp2, w_uin[...])
        back2 = mm_nt(dp2, w_uhid[...])
        pre1, dcell1 = cell_backward(fact1[at, :], ds1, dcell1)
        dp1_rows[at, :] = pre1
        dp1 = pre1.astype(BF16)
        back1 = mm_nt(dp1, w_lhid[...])
        return dp1, back1, back2, dcell1, dcell2

    lax.fori_loop(0, steps, backward_step, (wide.astype(BF16), zero, zero, zero, zero))

    dp1 = dp1_rows[...].astype(BF16)
    dp2 = dp2_rows[...].astype(BF16)
    dq = dq_rows[...].astype(BF16)
    s1 = s1_rows[...].astype(BF16)
    next_dp1 = shift_up(dp1.astype(F32)).astype(BF16)
    ctx_grad = (feat_rows[:, cells:] + mm_nt(next_dp1, w_lin[embed:, :])).astype(BF16)
    keys_grad = (keys_acc[...] * vec_row).astype(BF16)
    key_grad = mm_nt(keys_grad, w_key[...]) + mm_tn(w_low, ctx_grad)[:time_len, :]
    key_grad = key_grad.astype(BF16)
    grad_mine[...] = jnp.where(role == 0, key_grad[:, :units], key_grad[:, units:])
    grad_other[...] = jnp.where(role == 0, key_grad[:, units:], key_grad[:, :units])
    g_lin[:embed, :] = mm_tn(emb, dp1)
    g_lin[embed:, :] = mm_tn(shift_down(ctx.astype(F32)).astype(BF16), dp1)
    g_lhid[...] = mm_tn(shift_down(s1.astype(F32)).astype(BF16), dp1)
    g_lbias[...] = jnp.sum(dp1.astype(F32), 0, keepdims=True)
    g_uin[...] = mm_tn(s1, dp2)
    g_uhid[...] = mm_tn(shift_down(s2_low.astype(F32)).astype(BF16), dp2)
    g_ubias[...] = jnp.sum(dp2.astype(F32), 0, keepdims=True)
    g_key[...] = mm_tn(key[:time_len, :], keys_grad)
    g_query[...] = mm_tn(s2_low, dq)
    g_vec[...] = jnp.sum(vec_acc[...], 0, keepdims=True)
    g_out[:cells, :] = mm_tn(s2_low, logit_grad)
    g_out[cells:, :] = mm_tn(ctx, logit_grad)
    g_obias[...] = jnp.sum(logit_grad.astype(F32), 0, keepdims=True)
    emb_grad = mm_nt(dp1, w_lin[:embed, :])
    hot = prev_onehot[...]
    total = None
    for _ in range(3):
        low = emb_grad.astype(BF16)
        emb_grad = emb_grad - low.astype(F32)
        total = mm_tn(hot, low) if total is None else total + mm_tn(hot, low)
    g_table[...] = total


def speller(
    lengths, text_lens, mine, other, prev_onehot, target_onehot,
    w_lin, w_lhid, b_low, w_uin, w_uhid, b_up, w_key, w_query, vec, w_out, b_out, table,
):
    time_len, units = mine.shape
    steps, vocab = prev_onehot.shape
    cells = w_lhid.shape[0]
    att = w_key.shape[1]
    embed = table.shape[1]
    pad_time = -(-time_len // 256) * 256
    vmem = pl.BlockSpec(memory_space=pltpu.VMEM)
    smem = pl.BlockSpec(memory_space=pltpu.SMEM)
    shape = jax.ShapeDtypeStruct
    outs = (
        shape((1, 1), F32),
        shape((time_len, units), BF16),
        shape((time_len, units), BF16),
        shape(w_lin.shape, F32),
        shape(w_lhid.shape, F32),
        shape(b_low.shape, F32),
        shape(w_uin.shape, F32),
        shape(w_uhid.shape, F32),
        shape(b_up.shape, F32),
        shape(w_key.shape, F32),
        shape(w_query.shape, F32),
        shape(vec.shape, F32),
        shape(w_out.shape, F32),
        shape(b_out.shape, F32),
        shape(table.shape, F32),
    )
    return pl.pallas_call(
        speller_kernel,
        out_shape=outs,
        in_specs=[smem] * 2 + [vmem] * 16,
        out_specs=(vmem,) * len(outs),
        scratch_shapes=[
            pltpu.VMEM((pad_time, 2 * units), BF16),
            pltpu.VMEM((time_len, att), F32),
            pltpu.VMEM((pad_time, 4 * cells), BF16),
            pltpu.VMEM((4 * cells, pad_time), BF16),
            pltpu.VMEM((steps, 4 * cells), F32),
            pltpu.VMEM((steps, 6 * cells), F32),
            pltpu.VMEM((steps, 6 * cells), F32),
            pltpu.VMEM((steps, cells), F32),
            pltpu.VMEM((steps, cells), F32),
            pltpu.VMEM((steps, att), F32),
            pltpu.VMEM((steps, pad_time), F32),
            pltpu.VMEM((steps, w_out.shape[0]), F32),
            pltpu.VMEM((steps, pad_time), F32),
            pltpu.VMEM((steps, 4 * cells), F32),
            pltpu.VMEM((steps, 4 * cells), F32),
            pltpu.VMEM((steps, att), F32),
            pltpu.VMEM((pad_time, att), BF16),
            pltpu.VMEM((time_len, att), F32),
            pltpu.VMEM((8, att), F32),
        ],
        compiler_params=pltpu.CompilerParams(vmem_limit_bytes=VMEM_BYTES),
    )(
        lengths, text_lens, mine, other, prev_onehot, target_onehot,
        w_lin, w_lhid, b_low, w_uin, w_uhid, b_up, w_key, w_query, vec, w_out, b_out, table,
    )


def shards(
    frames,
    step_lengths,
    characters,
    char_lengths,
    listen_input,
    listen_hidden,
    listen_bias,
    lower_input,
    lower_hidden,
    lower_bias,
    upper_input,
    upper_hidden,
    upper_bias,
    key_proj,
    query_proj,
    score_vector,
    output_proj,
    output_bias,
    char_table,
):
    utts, frame_len, feat = frames.shape
    time_len = frame_len // 2
    swap = [(0, 1), (1, 0)]
    w_in, w_rec = listen_input[0], listen_hidden[0]
    pairs, factors, hprev, mine, other = listen_forward(
        step_lengths, frames, w_in, w_rec, listen_bias
    )
    other = lax.ppermute(other, "role", swap)
    chars = characters[0, 0]
    vocab = char_table.shape[0]
    previous = jnp.concatenate([jnp.zeros((1,), jnp.int32), chars[:-1]])
    ids = jnp.arange(vocab)[None, :]
    prev_onehot = (previous[:, None] == ids).astype(BF16)
    target_onehot = (chars[:, None] == ids).astype(F32)
    loss, grad_mine, grad_other, *grads = speller(
        step_lengths, char_lengths, mine, other, prev_onehot, target_onehot,
        lower_input, lower_hidden, lower_bias[None], upper_input, upper_hidden, upper_bias[None],
        key_proj, query_proj, score_vector[None], output_proj, output_bias[None], char_table,
    )
    grad_other = lax.ppermute(grad_other, "role", swap)
    grad_in, grad_rec, grad_bias, grad_pairs = listen_backward(
        step_lengths, pairs, factors, hprev, grad_mine, grad_other, w_in, w_rec
    )
    frame_grad = lax.psum_scatter(
        grad_pairs.reshape(utts, frame_len, feat), "role", scatter_dimension=1, tiled=True
    )
    summed = lax.psum(tuple(grads), ("role", "dp"))
    sum_in, sum_rec, sum_bias = lax.psum((grad_in, grad_rec, grad_bias), "dp")
    flat = {2: lower_bias, 5: upper_bias, 8: score_vector, 10: output_bias}
    summed = [item.reshape(flat[k].shape) if k in flat else item for k, item in enumerate(summed)]
    return (loss, frame_grad, sum_in[None], sum_rec[None], sum_bias, *summed)


def solution(mesh):
    whole = P()
    return jax.shard_map(
        shards,
        mesh=mesh,
        in_specs=(
            P("dp", None, None),
            P("dp"),
            P("dp", "role", None),
            P("dp", "role"),
            P("role", None, None),
            P("role", None, None),
            P("role", None),
        )
        + (whole,) * 12,
        out_specs=(
            P("dp", "role"),
            P("dp", "role", None),
            P("role", None, None),
            P("role", None, None),
            P("role", None),
        )
        + (whole,) * 12,
        check_vma=False,
    )
```

```python
import functools

import jax
import jax.numpy as jnp
from jax import lax
from jax.experimental import pallas as pl
from jax.experimental.pallas import tpu as pltpu
from jax.sharding import PartitionSpec as P

F32 = jnp.float32
BF16 = jnp.bfloat16
VMEM_BYTES = 60 * 1024 * 1024
SAFE_SCORE = 80.0


def mm(left, right):
    return jnp.dot(left, right, preferred_element_type=F32)


def mm_nt(left, right):
    return lax.dot_general(left, right, (((1,), (1,)), ((), ())), preferred_element_type=F32)


def mm_tn(left, right):
    return lax.dot_general(left, right, (((0,), (0,)), ((), ())), preferred_element_type=F32)


def sigmoid(x):
    return 0.5 * jnp.tanh(0.5 * x) + 0.5


def cell_forward(preact, cell_prev):
    n = preact.shape[-1] // 4
    in_gate = sigmoid(preact[:, :n])
    forget = sigmoid(preact[:, n : 2 * n])
    candid = jnp.tanh(preact[:, 2 * n : 3 * n])
    out_gate = sigmoid(preact[:, 3 * n :])
    cell_new = forget * cell_prev + in_gate * candid
    tanh_cell = jnp.tanh(cell_new)
    hidden = out_gate * tanh_cell
    factors = (
        candid * in_gate * (1.0 - in_gate),
        cell_prev * forget * (1.0 - forget),
        in_gate * (1.0 - candid * candid),
        tanh_cell * out_gate * (1.0 - out_gate),
        out_gate * (1.0 - tanh_cell * tanh_cell),
        forget,
    )
    return cell_new, hidden, factors


def cell_backward(factors, grad_hidden, grad_cell):
    n = factors.shape[-1] // 6
    part = lambda k: factors[:, k * n : (k + 1) * n]
    total = grad_cell + grad_hidden * part(4)
    grad_preact = jnp.concatenate(
        [total * part(0), total * part(1), total * part(2), grad_hidden * part(3)], -1
    )
    return grad_preact, total * part(5)


def listen_forward_kernel(
    lengths, pairs, w_in, w_rec, bias, rows_out, factors_out, mine_out, other_out,
    proj, emit, hprev,
):
    role = lax.axis_index("role")
    utts, time_len, width4 = proj.shape
    units = width4 // 4
    bias_row = bias[...].astype(F32)
    for u in range(utts):
        proj[u] = mm(pairs[u], w_in[...]) + bias_row
    first = lax.broadcasted_iota(jnp.int32, (8, 1), 0) == 0
    row_lengths = jnp.where(first, lengths[0], lengths[1])

    def step(s, carry):
        hidden, cell = carry
        t = jnp.where(role == 1, time_len - 1 - s, s)
        at = pl.ds(t, 1)
        pre_in = jnp.where(first, proj[0, at, :], proj[1, at, :])
        low = hidden.astype(BF16)
        cell_new, hidden_new, factors = cell_forward(pre_in + mm(low, w_rec[...]), cell)
        live = t < row_lengths
        hidden_next = jnp.where(live, hidden_new, hidden)
        cell_next = jnp.where(live, cell_new, cell)
        emitted = jnp.where(live, hidden_new, 0.0)
        for u in range(2):
            for k in range(6):
                factors_out[u, at, k * units : (k + 1) * units] = factors[k][u : u + 1]
            hprev[u, at, :] = hidden[u : u + 1]
            emit[u, at, :] = emitted[u : u + 1]
        return hidden_next, cell_next

    zero = jnp.zeros((8, units), F32)
    lax.fori_loop(0, time_len, step, (zero, zero))
    mine_out[...] = emit[role].astype(BF16)
    other_out[...] = emit[1 - role].astype(BF16)
    for u in range(utts):
        own = slice(u * time_len, (u + 1) * time_len)
        rows_out[own, :units] = hprev[u].astype(BF16)
    rows_out[:, units:] = jnp.ones((utts * time_len, rows_out.shape[1] - units), BF16)


def listen_forward(lengths, pairs, w_in, w_rec, bias):
    utts, time_len, _ = pairs.shape
    units = w_rec.shape[0]
    vmem = pl.BlockSpec(memory_space=pltpu.VMEM)
    shape = jax.ShapeDtypeStruct
    return pl.pallas_call(
        listen_forward_kernel,
        out_shape=(
            shape((utts * time_len, units + 64), BF16),
            shape((utts, time_len, 6 * units), F32),
            shape((time_len, units), BF16),
            shape((time_len, units), BF16),
        ),
        in_specs=[pl.BlockSpec(memory_space=pltpu.SMEM)] + [vmem] * 4,
        out_specs=(vmem,) * 4,
        scratch_shapes=[
            pltpu.VMEM((utts, time_len, 4 * units), F32),
            pltpu.VMEM((utts, time_len, units), F32),
            pltpu.VMEM((utts, time_len, units), F32),
        ],
        compiler_params=pltpu.CompilerParams(vmem_limit_bytes=VMEM_BYTES),
    )(lengths, pairs, w_in, w_rec, bias)


def speller_forward_kernel(
    lengths, text_lens,
    mine, other, prev_onehot, target_onehot,
    w_lin, w_lhid, b_low, w_uin, w_uhid, b_up, w_key, w_query, vec, w_out, b_out, table,
    loss, acts, key, keys_proj, key_low_t, fact1, fact2, q_rows, w_rows, feat_rows, dw_rows,
    logit_grad_out,
    key_low, emb_proj, s1_rows, s2_rows,
):
    role = lax.axis_index("role")
    time_len, units = mine.shape
    steps = emb_proj.shape[0]
    cells = w_lhid.shape[0]
    embed = table.shape[1]
    pad_time = key.shape[0]
    length = lengths[role]
    text_len = text_lens[0, 0]

    key[time_len:, :] = jnp.zeros((pad_time - time_len, 2 * units), BF16)
    key[:time_len, :units] = jnp.where(role == 0, mine[...], other[...])
    key[:time_len, units:] = jnp.where(role == 0, other[...], mine[...])
    keys_proj[...] = mm(key[:time_len, :], w_key[...])
    key_low_f32 = mm(key[...], w_lin[embed:, :])
    key_low[...] = key_low_f32.astype(BF16)
    key_low_t[...] = jnp.transpose(key_low_f32).astype(BF16)
    emb = mm(prev_onehot[...], table[...]).astype(BF16)
    emb_proj[...] = mm(emb, w_lin[:embed, :]) + b_low[...].astype(F32)
    bias_up = b_up[...].astype(F32)
    vec_row = vec[...].astype(F32)
    lane = lax.broadcasted_iota(jnp.int32, (1, pad_time), 1)
    frame_ok = lane < length
    ones = jnp.ones((1, 256), BF16)
    tail = jnp.zeros((pad_time - time_len, 256), BF16)

    def forward_step(shift_by_max, i, carry):
        cell1, cell2, hid1, hid2, expw, rinv = carry
        at = pl.ds(i, 1)
        pre1 = emb_proj[at, :] + hid1 + mm(expw, key_low[...]) * rinv
        cell1, s1, factors = cell_forward(pre1, cell1)
        for k in range(6):
            fact1[at, k * cells : (k + 1) * cells] = factors[k]
        s1_rows[at, :] = s1
        s1_low = s1.astype(BF16)
        pre2 = hid2 + bias_up + mm(s1_low, w_uin[...])
        hid1 = mm(s1_low, w_lhid[...])
        cell2, s2, factors = cell_forward(pre2, cell2)
        for k in range(6):
            fact2[at, k * cells : (k + 1) * cells] = factors[k]
        s2_rows[at, :] = s2
        s2_low = s2.astype(BF16)
        query = mm(s2_low, w_query[...])
        hid2 = mm(s2_low, w_uhid[...])
        q_rows[at, :] = query
        part = None
        for j in range(query.shape[1] // 128):
            cut = slice(j * 128, (j + 1) * 128)
            term = jnp.tanh(keys_proj[:, cut] + query[:, cut]) * vec_row[:, cut]
            part = term if part is None else part + term
        high = part.astype(BF16)
        low = (part - high.astype(F32)).astype(BF16)
        split = jnp.concatenate([jnp.concatenate([high, low], 1), tail], 0)
        scores = mm_nt(ones, split)
        if shift_by_max:
            scores = jnp.where(frame_ok, scores, -1000000000.0)
            scores = scores - jnp.max(scores, -1, keepdims=True)
        expf = jnp.where(frame_ok, jnp.exp(scores), 0.0)
        rinv = 1.0 / jnp.sum(expf, -1, keepdims=True)
        w_rows[at, :] = expf * rinv
        return cell1, cell2, hid1, hid2, expf.astype(BF16), rinv

    zero = jnp.zeros((1, cells), F32)
    wide = jnp.zeros((1, 4 * cells), F32)
    start = (zero, zero, wide, wide, jnp.zeros((1, pad_time), BF16), jnp.ones((1, 1), F32))
    bound = jnp.sum(jnp.abs(vec_row))

    @pl.when(bound <= SAFE_SCORE)
    def _():
        lax.fori_loop(0, steps, functools.partial(forward_step, False), start)

    @pl.when(bound > SAFE_SCORE)
    def _():
        lax.fori_loop(0, steps, functools.partial(forward_step, True), start)

    w_low = w_rows[...].astype(BF16)
    ctx = mm(w_low, key[...]).astype(BF16)
    s2_low = s2_rows[...].astype(BF16)
    logits = mm(s2_low, w_out[:cells, :]) + mm(ctx, w_out[cells:, :]) + b_out[...].astype(F32)
    top = jnp.max(logits, -1, keepdims=True)
    log_total = top + jnp.log(jnp.sum(jnp.exp(logits - top), -1, keepdims=True))
    target = target_onehot[...]
    cross = log_total - jnp.sum(logits * target, -1, keepdims=True)
    text = text_len.astype(F32)
    alive = lax.broadcasted_iota(jnp.int32, (steps, 1), 0) < text_len
    loss[...] = jnp.sum(jnp.where(alive, cross, 0.0), 0, keepdims=True) / text
    scale = jnp.where(alive, 1.0 / text, 0.0)
    logit_grad = (scale * (jnp.exp(logits - log_total) - target)).astype(BF16)
    logit_grad_out[...] = logit_grad
    feat_rows[...] = mm_nt(logit_grad, w_out[...])
    dw_rows[...] = mm_nt(feat_rows[:, cells:].astype(BF16), key[...])
    acts[steps:, :] = jnp.zeros((acts.shape[0] - steps, acts.shape[1]), BF16)
    acts[:steps, :embed] = emb
    acts[:steps, embed : embed + 2 * units] = ctx
    acts[:steps, embed + 2 * units : embed + 2 * units + cells] = s1_rows[...].astype(BF16)
    acts[:steps, embed + 2 * units + cells :] = s2_low


def speller_forward(
    lengths, text_lens, mine, other, prev_onehot, target_onehot,
    w_lin, w_lhid, b_low, w_uin, w_uhid, b_up, w_key, w_query, vec, w_out, b_out, table,
):
    time_len, units = mine.shape
    steps, vocab = prev_onehot.shape
    cells = w_lhid.shape[0]
    att = w_key.shape[1]
    embed = table.shape[1]
    pad_time = -(-time_len // 256) * 256
    pad_steps = -(-steps // 16) * 16
    vmem = pl.BlockSpec(memory_space=pltpu.VMEM)
    smem = pl.BlockSpec(memory_space=pltpu.SMEM)
    shape = jax.ShapeDtypeStruct
    outs = (
        shape((1, 1), F32),
        shape((pad_steps, embed + 2 * units + 2 * cells), BF16),
        shape((pad_time, 2 * units), BF16),
        shape((time_len, att), F32),
        shape((4 * cells, pad_time), BF16),
        shape((steps, 6 * cells), F32),
        shape((steps, 6 * cells), F32),
        shape((steps, att), F32),
        shape((steps, pad_time), F32),
        shape((steps, w_out.shape[0]), F32),
        shape((steps, pad_time), F32),
        shape((steps, vocab), BF16),
    )
    return pl.pallas_call(
        speller_forward_kernel,
        out_shape=outs,
        in_specs=[smem] * 2 + [vmem] * 16,
        out_specs=(vmem,) * len(outs),
        scratch_shapes=[
            pltpu.VMEM((pad_time, 4 * cells), BF16),
            pltpu.VMEM((steps, 4 * cells), F32),
            pltpu.VMEM((steps, cells), F32),
            pltpu.VMEM((steps, cells), F32),
        ],
        compiler_params=pltpu.CompilerParams(vmem_limit_bytes=VMEM_BYTES),
    )(
        lengths, text_lens, mine, other, prev_onehot, target_onehot,
        w_lin, w_lhid, b_low, w_uin, w_uhid, b_up, w_key, w_query, vec, w_out, b_out, table,
    )


SMALL = 32


def shift_up(rows):
    count = rows.shape[0]
    rolled = pltpu.roll(rows, count - 1, 0)
    at = lax.broadcasted_iota(jnp.int32, rows.shape, 0)
    return jnp.where(at == count - 1, 0.0, rolled)


def speller_backward_kernel(
    w_lin, w_lhid, w_uin, w_uhid, w_key, w_query, vec, prev_onehot,
    acts, key, keys_proj, key_low_t, fact1, fact2, q_rows, w_rows, feat_rows, dw_rows, logit_grad,
    grad_mine, grad_other, dp1_out, dp2_out, pack,
    dp1_rows, dp2_rows, dq_rows, m_scr, keys_acc, vec_acc, small,
):
    role = lax.axis_index("role")
    time_len, att = keys_proj.shape
    steps, vocab = logit_grad.shape
    pad_time = key.shape[0]
    units = key.shape[1] // 2
    cells = w_lhid.shape[0]
    embed = acts.shape[1] - 2 * units - 2 * cells
    vec_row = vec[...].astype(F32)
    zero = jnp.zeros((1, cells), F32)
    wide = jnp.zeros((1, 4 * cells), BF16)
    keys_acc[...] = jnp.zeros_like(keys_acc)
    vec_acc[...] = jnp.zeros_like(vec_acc)
    m_scr[time_len:, :] = jnp.zeros((pad_time - time_len, m_scr.shape[1]), BF16)

    def backward_step(s, carry):
        dp1, back1, back2, dcell1, dcell2 = carry
        i = steps - 1 - s
        at = pl.ds(i, 1)
        query = q_rows[at, :]
        weights = w_rows[at, :]
        dweights = dw_rows[at, :] + mm(dp1, key_low_t[...])
        dscore = weights * (dweights - jnp.sum(weights * dweights, -1, keepdims=True))
        dcol = jnp.transpose(jnp.broadcast_to(dscore, (8, pad_time)))[:time_len, :1]
        for j in range(query.shape[1] // 128):
            cut = slice(j * 128, (j + 1) * 128)
            energy = jnp.tanh(keys_proj[:, cut] + query[:, cut])
            slope = 1.0 - energy * energy
            m_scr[:time_len, cut] = slope.astype(BF16)
            keys_acc[:, cut] += dcol * slope
            vec_acc[:, cut] += jnp.sum((dcol * energy).reshape(time_len // 8, 8, 128), 0)
        dquery = (mm(dscore.astype(BF16), m_scr[...]) * vec_row).astype(BF16)
        dq_rows[at, :] = dquery.astype(F32)
        ds2 = back2 + feat_rows[at, :cells] + mm_nt(dquery, w_query[...])
        pre2, dcell2 = cell_backward(fact2[at, :], ds2, dcell2)
        dp2_rows[at, :] = pre2
        dp2 = pre2.astype(BF16)
        ds1 = back1 + mm_nt(dp2, w_uin[...])
        back2 = mm_nt(dp2, w_uhid[...])
        pre1, dcell1 = cell_backward(fact1[at, :], ds1, dcell1)
        dp1_rows[at, :] = pre1
        dp1 = pre1.astype(BF16)
        back1 = mm_nt(dp1, w_lhid[...])
        return dp1, back1, back2, dcell1, dcell2

    lax.fori_loop(0, steps, backward_step, (wide, zero, zero, zero, zero))

    dp1 = dp1_rows[...].astype(BF16)
    dp2 = dp2_rows[...].astype(BF16)
    dq = dq_rows[...].astype(BF16)
    extra = jnp.zeros((dp1_out.shape[0] - steps, 4 * cells), BF16)
    dp1_out[steps:, :] = extra
    dp2_out[steps:, :] = extra
    dp1_out[:steps, :] = dp1
    dp2_out[:steps, :] = dp2
    next_dp1 = shift_up(dp1.astype(F32)).astype(BF16)
    ctx_grad = (feat_rows[:, cells:] + mm_nt(next_dp1, w_lin[embed:, :])).astype(BF16)
    keys_grad = (keys_acc[...] * vec_row).astype(BF16)
    w_low = w_rows[...].astype(BF16)
    key_grad = mm_nt(keys_grad, w_key[...]) + mm_tn(w_low, ctx_grad)[:time_len, :]
    key_grad = key_grad.astype(BF16)
    grad_mine[...] = jnp.where(role == 0, key_grad[:, :units], key_grad[:, units:])
    grad_other[...] = jnp.where(role == 0, key_grad[:, units:], key_grad[:, :units])
    ctx = acts[:steps, embed : embed + 2 * units]
    s2 = acts[:steps, embed + 2 * units + cells :]
    wide = pack.shape[1]
    deep = 2 * units * att // wide
    g_key = mm_tn(key[:time_len, :], keys_grad)
    g_query = mm_tn(s2, dq)
    for k in range(wide // att):
        cut = slice(k * att, (k + 1) * att)
        pack[:deep, cut] = g_key[k * deep : (k + 1) * deep].astype(BF16)
        pack[deep : 2 * deep, cut] = g_query[k * deep : (k + 1) * deep].astype(BF16)
    emb_grad = mm_nt(dp1, w_lin[:embed, :])
    hot = prev_onehot[...]
    total = None
    for _ in range(3):
        low = emb_grad.astype(BF16)
        emb_grad = emb_grad - low.astype(F32)
        total = mm_tn(hot, low) if total is None else total + mm_tn(hot, low)
    small[...] = jnp.zeros_like(small)
    small[:vocab, :cells] = mm_tn(logit_grad[...], s2)
    small[:vocab, cells : cells + 2 * units] = mm_tn(logit_grad[...], ctx)
    base = cells + 2 * units
    small[:vocab, base : base + embed] = total
    base += embed
    small[0:1, base : base + att] = jnp.sum(vec_acc[...], 0, keepdims=True)
    small[1:2, base : base + vocab] = jnp.sum(logit_grad[...].astype(F32), 0, keepdims=True)
    low_bias = jnp.sum(dp1.astype(F32), 0, keepdims=True)
    up_bias = jnp.sum(dp2.astype(F32), 0, keepdims=True)
    for k in range(4):
        small[2 + k : 3 + k, base : base + cells] = low_bias[:, k * cells : (k + 1) * cells]
        small[6 + k : 7 + k, base : base + cells] = up_bias[:, k * cells : (k + 1) * cells]
    high = small[...].astype(BF16)
    rows = small.shape[0]
    pack[2 * deep : 2 * deep + rows, :] = high
    pack[2 * deep + rows :, :] = (small[...] - high.astype(F32)).astype(BF16)


def speller_backward(
    w_lin, w_lhid, w_uin, w_uhid, w_key, w_query, vec, prev_onehot,
    acts, key, keys_proj, key_low_t, fact1, fact2, q_rows, w_rows, feat_rows, dw_rows, logit_grad,
):
    time_len, att = keys_proj.shape
    steps, vocab = logit_grad.shape
    pad_time = key.shape[0]
    units = key.shape[1] // 2
    cells = w_lhid.shape[0]
    pad_steps = acts.shape[0]
    vmem = pl.BlockSpec(memory_space=pltpu.VMEM)
    shape = jax.ShapeDtypeStruct
    outs = (
        shape((time_len, units), BF16),
        shape((time_len, units), BF16),
        shape((pad_steps, 4 * cells), BF16),
        shape((pad_steps, 4 * cells), BF16),
        shape(((2 * units + cells) * att // (4 * cells) + 2 * SMALL, 4 * cells), BF16),
    )
    return pl.pallas_call(
        speller_backward_kernel,
        out_shape=outs,
        in_specs=[vmem] * 19,
        out_specs=(vmem,) * len(outs),
        scratch_shapes=[
            pltpu.VMEM((steps, 4 * cells), F32),
            pltpu.VMEM((steps, 4 * cells), F32),
            pltpu.VMEM((steps, att), F32),
            pltpu.VMEM((pad_time, att), BF16),
            pltpu.VMEM((time_len, att), F32),
            pltpu.VMEM((8, att), F32),
            pltpu.VMEM((SMALL, 4 * cells), F32),
        ],
        compiler_params=pltpu.CompilerParams(vmem_limit_bytes=VMEM_BYTES),
    )(
        w_lin, w_lhid, w_uin, w_uhid, w_key, w_query, vec, prev_onehot,
        acts, key, keys_proj, key_low_t, fact1, fact2, q_rows, w_rows, feat_rows, dw_rows, logit_grad,
    )


def unpack(pack, units, cells, att, vocab, embed):
    wide = pack.shape[1]
    deep = 2 * units * att // wide
    unfold = lambda part: part.reshape(deep, wide // att, att).swapaxes(0, 1).reshape(-1, att)
    g_key = unfold(pack[:deep].astype(F32))
    g_query = unfold(pack[deep : 2 * deep].astype(F32))
    small = pack[2 * deep : 2 * deep + SMALL].astype(F32) + pack[2 * deep + SMALL :].astype(F32)
    base = cells + 2 * units
    g_out = small[:vocab, :base].T
    g_table = small[:vocab, base : base + embed]
    base += embed
    low_bias = small[2:6, base : base + cells].reshape(-1)
    up_bias = small[6:10, base : base + cells].reshape(-1)
    g_vec = small[0, base : base + att]
    g_obias = small[1, base : base + vocab]
    return low_bias, up_bias, g_key, g_query, g_vec, g_out, g_obias, g_table


def backward_steps(role, lengths, factors, grad_out, w_rec, grad_pre, first_step, count, carry):
    time_len = factors.shape[1]
    first = lax.broadcasted_iota(jnp.int32, (8, 1), 0) == 0
    row_lengths = jnp.where(first, lengths[0], lengths[1])

    def step(s, carry):
        grad_hidden, grad_cell = carry
        t = jnp.where(role == 1, s, time_len - 1 - s)
        at = pl.ds(t, 1)
        live = t < row_lengths
        fact = jnp.where(first, factors[0, at, :], factors[1, at, :])
        arrived = jnp.where(first, grad_out[0, at, :], grad_out[1, at, :])
        fact = jnp.where(live, fact, 0.0)
        total = grad_hidden + jnp.where(live, arrived, 0.0)
        pre, cell_back = cell_backward(fact, total, grad_cell)
        for u in range(2):
            grad_pre[u, at, :] = pre[u : u + 1]
        back = mm_nt(pre.astype(BF16), w_rec[...])
        return jnp.where(live, back, total), jnp.where(live, cell_back, grad_cell)

    return lax.fori_loop(first_step, first_step + count, step, carry)


def listen_backward_kernel(
    lengths, factors, grad_mine, grad_other, w_rec, pre_out, grad_pre, grad_out
):
    role = lax.axis_index("role")
    grad_out[role] = grad_mine[...].astype(F32)
    grad_out[1 - role] = grad_other[...].astype(F32)
    zero = jnp.zeros((8, w_rec.shape[0]), F32)
    backward_steps(
        role, lengths, factors, grad_out, w_rec, grad_pre, 0, factors.shape[1], (zero, zero)
    )
    pre_out[...] = grad_pre[...].astype(BF16)


def listen_backward(lengths, factors, grad_mine, grad_other, w_rec):
    utts, time_len, _ = factors.shape
    units = w_rec.shape[0]
    vmem = pl.BlockSpec(memory_space=pltpu.VMEM)
    return pl.pallas_call(
        listen_backward_kernel,
        out_shape=jax.ShapeDtypeStruct((utts, time_len, 4 * units), BF16),
        in_specs=[pl.BlockSpec(memory_space=pltpu.SMEM)] + [vmem] * 4,
        out_specs=vmem,
        scratch_shapes=[
            pltpu.VMEM((utts, time_len, 4 * units), F32),
            pltpu.VMEM((utts, time_len, units), F32),
        ],
        compiler_params=pltpu.CompilerParams(vmem_limit_bytes=VMEM_BYTES),
    )(lengths, factors, grad_mine, grad_other, w_rec)


SEGMENT = 32
STREAMS = ((0, 3), (3, 5), (5, 6))


def remote(src, dst, send, recv, device):
    return pltpu.make_async_remote_copy(
        src_ref=src, dst_ref=dst, send_sem=send, recv_sem=recv,
        device_id=device, device_id_type=pl.DeviceIdType.MESH,
    )


def start(copies):
    for copy in copies:
        copy.start()


def wait(copies):
    for copy in copies:
        copy.wait()


class Gather:
    def __init__(self, dims, me, view, chunks, sems):
        self.dims, self.view, self.chunks = dims, view, chunks
        self.role, self.z, self.y, self.x = me
        self.send, self.recv = sems

    def device(self, z, y, x):
        _, ny, nx = self.dims
        return (self.role, (z * ny + y) * nx + x)

    def copies(self, k, which, spans, others, base):
        out = []
        for device in others:
            for span in spans:
                ref = self.view(which, k, *span)
                out.append(
                    remote(ref, ref, self.send.at[k, base], self.recv.at[k, base], device)
                )
                base += 1
        return out

    def along_x(self):
        nx = self.dims[2]
        return [self.device(self.z, self.y, (self.x + j) % nx) for j in range(1, nx)]

    def along_y(self):
        ny = self.dims[1]
        return [self.device(self.z, (self.y + j) % ny, self.x) for j in range(1, ny)]

    def first(self, k):
        nz, ny, nx = self.dims
        slot = (self.y * nx + self.x) * nz + self.z
        others = [self.device((self.z + j) % nz, self.y, self.x) for j in range(1, nz)]
        return self.copies(k, None, [(slot, 1)], others, 0)

    def second(self, k):
        nz, ny, nx = self.dims
        column = ((self.y * nx + self.x) * nz, nz)
        base = nz - 1
        to_x = self.copies(k, 0, [column], self.along_x(), base)
        return to_x + self.copies(k, 1, [column], self.along_y(), base + nx - 1)

    def third(self, k):
        nz, ny, nx = self.dims
        base = nz - 1 + nx - 1 + ny - 1
        to_y = self.copies(k, 0, [(self.y * nx * nz, nx * nz)], self.along_y(), base)
        spans = [((b * nx + self.x) * nz, nz) for b in range(ny)]
        return to_y + self.copies(k, 1, spans, self.along_x(), base + ny - 1)

    @staticmethod
    def semaphores(dims, chunks):
        nz, ny, nx = dims
        count = nz - 1 + 2 * (nx - 1) + 2 * (ny - 1) + (nx - 1) * (ny - 1)
        return pltpu.SemaphoreType.DMA((len(chunks), count))


SP_CHUNKS = ((0, 352), (352, 352), (704, 320), (1024, 320))
LI_CHUNKS = ((0, 352), (352, 320))


def exchange_kernel(
    dims,
    lengths, factors, grad_mine, grad_other, w_in, w_rec, dp1, dp2, pack, acts_all, pairs_all, rows_all,
    frames_out, li_out, sp_out,
    grad_pre, grad_out, acts_buf, pairs_buf, rows_buf, dp_pair, got, got_t, prod, column,
    li_send, li_got, li_rows, li_acc, li_all, fr_send, fr_got, weave,
    pk_pair, pk_x, pk_xsum, pk_y, pk_ysum, pk_z,
    local_sem, chip_send, chip_recv, aa_send, aa_recv, li_aa_send, li_aa_recv,
    sp_send, sp_recv, li_ag_send, li_ag_recv, pk_send, pk_recv,
):
    nz, ny, nx = dims
    chips = nz * ny * nx
    role = lax.axis_index("role")
    dp = lax.axis_index("dp")
    z, y, x = dp // (ny * nx), (dp // nx) % ny, dp % nx
    utts, time_len, width = grad_pre.shape
    units = w_rec.shape[0]
    cells = dp1.shape[1] // 4
    half_time = time_len // 2
    pads = dp1.shape[0]
    twin = (1 - role, dp)

    def slot_of(chip):
        return (((chip // nx) % ny) * nx + chip % nx) * nz + chip // (ny * nx)

    slot = slot_of(dp)
    lanes = pl.ds(pl.multiple_of(slot * 128, 128), 128)

    barrier = pltpu.get_barrier_semaphore()
    mesh = pl.DeviceIdType.MESH

    def greet(k, _):
        pl.semaphore_signal(barrier, inc=1, device_id=(role, (dp + k) % chips), device_id_type=mesh)
        return 0

    pl.semaphore_signal(barrier, inc=1, device_id=twin, device_id_type=mesh)
    lax.fori_loop(1, chips, greet, 0)
    load_acts = pltpu.make_async_copy(
        acts_all.at[:, pl.ds(pl.multiple_of(role * cells, 128), acts_buf.shape[1])],
        acts_buf, local_sem.at[0],
    )
    load_acts.start()
    load_rows = pltpu.make_async_copy(rows_all, rows_buf, local_sem.at[1])
    load_rows.start()
    load_pairs = pltpu.make_async_copy(pairs_all, pairs_buf, local_sem.at[4])
    load_pairs.start()
    dp_pair[role] = jnp.where(role == 0, dp1[...], dp2[...])
    dp_pair[2] = jnp.where(role == 0, dp2[...], dp1[...])
    grad_out[role] = grad_mine[...].astype(F32)
    grad_out[1 - role] = grad_other[...].astype(F32)
    pl.semaphore_wait(barrier, chips)

    to_twin = remote(dp_pair.at[2], dp_pair.at[role], chip_send.at[0], chip_recv.at[0], twin)
    to_twin.start()
    pack_twin = remote(pack, pk_pair, pk_send.at[0], pk_recv.at[0], twin)

    @pl.when(role == 0)
    def _():
        pack_twin.start()

    to_twin.wait()

    def block(k):
        chip = (dp + k) % chips
        cut = pl.ds(pl.multiple_of(slot_of(chip) * 128, 128), 128)
        return remote(
            dp_pair.at[pl.ds(0, 2), :, cut], got.at[dp],
            aa_send.at[k - 1], aa_recv.at[k - 1], (role, chip),
        )

    lax.fori_loop(1, chips, lambda k, _: (block(k).start(), 0)[1], 0)
    own_block = pltpu.make_async_copy(
        dp_pair.at[pl.ds(0, 2), :, lanes], got.at[dp], local_sem.at[2]
    )
    own_block.start()

    plain = pack.shape[0] - 2 * SMALL

    def rounded(total):
        value = total[plain : plain + SMALL] + total[plain + SMALL :]
        high = value.astype(BF16)
        low = (value - high.astype(F32)).astype(BF16)
        return jnp.concatenate([total[:plain].astype(BF16), high, low], 0)

    chip_at = lambda a, b, c: (role, (a * ny + b) * nx + c)
    x_other, y_other = (x + 1) % nx, (y + 1) % ny
    column_wide = nz * 128

    def pack_x(b):
        first = pl.multiple_of((b * nx + x_other) * column_wide, 128)
        return remote(
            pk_pair.at[:, pl.ds(first, column_wide)], pk_x.at[b],
            pk_send.at[1 + b], pk_recv.at[1 + b], chip_at(z, y, x_other),
        )

    pack_y = remote(
        pk_xsum.at[y_other], pk_y, pk_send.at[1 + ny], pk_recv.at[1 + ny], chip_at(z, y_other, x)
    )

    def pack_z(j):
        to = (z + j) % nz
        return remote(
            pk_ysum.at[:, pl.ds(pl.multiple_of(to * 128, 128), 128)], pk_z.at[z],
            pk_send.at[1 + ny + j], pk_recv.at[1 + ny + j], chip_at(to, y, x),
        )

    @pl.when(role == 0)
    def _():
        pack_twin.wait_send()

    @pl.when(role == 1)
    def _():
        pack_twin.wait_recv()

        def add(b, _):
            cut = pl.ds(pl.multiple_of(b * 128, 128), 128)
            total = pk_pair[:, cut].astype(F32) + pack[:, cut].astype(F32)
            pk_pair[:, cut] = rounded(total)
            return 0

        lax.fori_loop(0, pack.shape[1] // 128, add, 0)
        for b in range(ny):
            pack_x(b).start()

    def pack_after_x():
        for b in range(ny):
            pack_x(b).wait()
            first = pl.multiple_of((b * nx + x) * column_wide, 128)

            def add(c, _):
                here = pl.ds(pl.multiple_of(first + c * 128, 128), 128)
                cut = pl.ds(pl.multiple_of(c * 128, 128), 128)
                total = pk_pair[:, here].astype(F32) + pk_x[b, :, cut].astype(F32)
                pk_xsum[b, :, cut] = rounded(total)
                return 0

            lax.fori_loop(0, nz, add, 0)
        pack_y.start()

    def pack_after_y():
        pack_y.wait()

        def add(c, _):
            cut = pl.ds(pl.multiple_of(c * 128, 128), 128)
            total = pk_xsum[y, :, cut].astype(F32) + pk_y[:, cut].astype(F32)
            pk_ysum[:, cut] = rounded(total)
            return 0

        lax.fori_loop(0, nz, add, 0)
        for j in range(1, nz):
            pack_z(j).start()

    def pack_after_z():
        for j in range(1, nz):
            pack_z(j).wait()
        pk_z[z] = pk_ysum[:, pl.ds(pl.multiple_of(z * 128, 128), 128)]
        total = pk_z[0].astype(F32)
        for j in range(1, nz):
            total = total + pk_z[j].astype(F32)
        column[column.shape[0] - total.shape[0] :, :] = rounded(total)

    def view_sp(which, k, first, count):
        rows = SP_CHUNKS[k]
        if which is not None:
            rows = (rows[0] + which * rows[1] // 2, rows[1] // 2)
        cut = pl.ds(pl.multiple_of(first * 128, 128), count * 128)
        return sp_out.at[role, pl.ds(*rows), cut]

    def view_li(which, k, first, count):
        rows = LI_CHUNKS[k]
        if which is not None:
            rows = (rows[0] + which * rows[1] // 2, rows[1] // 2)
        return li_all.at[pl.ds(first, count), pl.ds(*rows)]

    me = (role, z, y, x)
    sp = Gather(dims, me, view_sp, SP_CHUNKS, (sp_send, sp_recv))
    li = Gather(dims, me, view_li, LI_CHUNKS, (li_ag_send, li_ag_recv))

    def sp_last(k):
        ref = sp_out.at[role, pl.ds(*SP_CHUNKS[k])]
        return [remote(ref, ref, chip_send.at[2 + k], chip_recv.at[2 + k], twin)]

    def rows_of(j):
        return jnp.where(role == 1, SEGMENT * j, time_len - SEGMENT * (j + 1))

    def pack_columns(first_segment, last_segment):
        lane = lax.broadcasted_iota(jnp.int32, (SEGMENT, 128), 1)
        for j in range(first_segment, last_segment):
            rows = pl.ds(pl.multiple_of(rows_of(j), SEGMENT), SEGMENT)
            for b in range(width // 128):
                one = grad_pre[0, rows, b * 128 : (b + 1) * 128]
                two = grad_pre[1, rows, b * 128 : (b + 1) * 128]
                even = jnp.where(lane < 64, one, pltpu.roll(two, 64, 1))
                odd = jnp.where(lane < 64, pltpu.roll(one, 64, 1), two)
                li_send[2 * b, rows, :] = even.astype(BF16)
                li_send[2 * b + 1, rows, :] = odd.astype(BF16)

    def stream(n):
        first_segment, last_segment = STREAMS[n]
        count = SEGMENT * (last_segment - first_segment)
        begin = jnp.where(role == 1, SEGMENT * first_segment, time_len - SEGMENT * last_segment)
        rows = pl.ds(pl.multiple_of(begin, SEGMENT), count)

        def one(k):
            chip = (dp + k) % chips
            return remote(
                li_send.at[slot_of(chip), rows], li_got.at[dp, rows],
                li_aa_send.at[n, k - 1], li_aa_recv.at[n, k - 1], (role, chip),
            )

        return one

    def start_stream(n):
        pack_columns(*STREAMS[n])
        one = stream(n)
        lax.fori_loop(1, chips, lambda k, _: (one(k).start(), 0)[1], 0)

    def wait_stream(n):
        one = stream(n)
        lax.fori_loop(1, chips, lambda k, _: (one(k).wait(), 0)[1], 0)

    zero = jnp.zeros((8, units), F32)
    carry = (zero, zero)

    def run(j, carry):
        return backward_steps(
            role, lengths, factors, grad_out, w_rec, grad_pre, SEGMENT * j, SEGMENT, carry
        )

    carry = run(0, carry)
    pl.when(role == 1)(pack_after_x)
    carry = run(1, carry)
    pl.when(role == 1)(pack_after_y)

    lax.fori_loop(1, chips, lambda k, _: (block(k).wait(), 0)[1], 0)
    own_block.wait()
    load_acts.wait()
    both = got[...].reshape(chips * 2 * pads, 128).astype(F32)
    rolled = pltpu.roll(both, chips * 2 * pads - 1, 0)
    got_t[0] = jnp.transpose(both).astype(BF16)
    got_t[1] = jnp.transpose(rolled).astype(BF16)
    groups = acts_buf.shape[1] // 256
    span = groups * 256
    for g in range(groups):
        cut = slice(g * 256, (g + 1) * 256)
        if g == 0:
            left = got_t[0]
        elif g < groups - cells // 256:
            left = got_t[1 - role]
        else:
            left = got_t[1]
        to = (g + groups - 1) % groups * 256
        prod[:, to : to + 256] = mm(left, acts_buf[:, cut])
    column[:span, :] = jnp.transpose(prod[...]).astype(BF16)
    column[span:, :] = jnp.zeros((column.shape[0] - span, 128), BF16)

    def place(first, count):
        copy = pltpu.make_async_copy(
            column.at[pl.ds(first, count)], sp_out.at[role, pl.ds(first, count), lanes],
            local_sem.at[3],
        )
        copy.start()
        copy.wait()

    tail_first, tail_count = SP_CHUNKS[-1]
    place(0, tail_first)
    for k in range(len(SP_CHUNKS) - 1):
        start(sp.first(k))

    carry = run(2, carry)
    pl.when(role == 1)(pack_after_z)
    place(tail_first, tail_count)
    start(sp.first(len(SP_CHUNKS) - 1))
    start_stream(0)
    far = jnp.where(role == 0, half_time, 0)
    near = half_time - far
    for u in range(utts):
        rows = pl.ds(pl.multiple_of(far, half_time), half_time)
        fr_send[u] = mm_nt(grad_pre[u, rows, :].astype(BF16), w_in[...]).astype(BF16)
    frames_copy = remote(fr_send, fr_got, chip_send.at[1], chip_recv.at[1], twin)
    frames_copy.start()
    wait(sp.first(0))
    start(sp.second(0))
    carry = run(3, carry)
    wait(sp.first(1))
    start(sp.second(1))
    wait(sp.second(0))
    start(sp.third(0))
    carry = run(4, carry)
    start_stream(1)
    wait(sp.first(2))
    start(sp.second(2))
    wait(sp.second(1))
    start(sp.third(1))
    carry = run(5, carry)
    start_stream(2)
    wait(sp.first(3))
    start(sp.second(3))
    wait(sp.second(2))
    start(sp.third(2))

    frames_copy.wait()
    feat = frames_out.shape[2]
    for u in range(utts):
        rows = pl.ds(pl.multiple_of(near, half_time), half_time)
        total = mm_nt(grad_pre[u, rows, :].astype(BF16), w_in[...]) + fr_got[u].astype(F32)
        for j in range(feat // 128):
            for half in range(2):
                cut = slice(half * feat + j * 128, half * feat + (j + 1) * 128)
                weave[pl.ds(half, half_time, stride=2), :] = total[:, cut]
            frames_out[u, :, j * 128 : (j + 1) * 128] = weave[...]

    li_got[dp] = li_send[slot]
    load_rows.wait()
    load_pairs.wait()
    for n in range(len(STREAMS)):
        wait_stream(n)

    def spread(c, _):
        value = li_got[c].astype(F32)
        base = pl.multiple_of(c * 2 * time_len, 16)
        li_rows[pl.ds(base, time_len), :] = value.astype(BF16)
        base = pl.multiple_of(c * 2 * time_len + time_len, 16)
        li_rows[pl.ds(base, time_len), :] = pltpu.roll(value, 64, 1).astype(BF16)
        return 0

    lax.fori_loop(0, chips, spread, 0)
    li_acc[...] = jnp.zeros_like(li_acc)
    deep = 4 * time_len
    features = pairs_buf.shape[1]

    def accumulate(c, _):
        rows = pl.ds(pl.multiple_of(c * deep, 256), deep)
        left = jnp.transpose(li_rows[rows, :])
        li_acc[:, :features] += mm(left, pairs_buf[rows, :])
        li_acc[:, features:] += mm(left, rows_buf[rows, :])
        return 0

    lax.fori_loop(0, chips * 2 * time_len // deep, accumulate, 0)
    flipped = jnp.transpose(li_acc[...])
    tall = flipped.shape[0] // 2
    lane = lax.broadcasted_iota(jnp.int32, (tall, 128), 1)
    packed = jnp.where(lane < 64, flipped[:tall], pltpu.roll(flipped[tall:], 64, 1))
    li_all[slot] = packed.astype(BF16)

    for k in range(len(LI_CHUNKS)):
        start(li.first(k))
    wait(sp.second(3))
    start(sp.third(3))
    wait(li.first(0))
    start(li.second(0))
    wait(sp.third(0))
    start(sp_last(0))
    wait(sp.third(1))
    start(sp_last(1))
    wait(li.first(1))
    start(li.second(1))
    wait(li.second(0))
    start(li.third(0))
    wait(sp.third(2))
    start(sp_last(2))
    wait(li.second(1))
    start(li.third(1))
    wait(sp.third(3))
    start(sp_last(3))
    wait(li.third(0))
    wait(li.third(1))

    def assemble(b, _):
        cut = pl.ds(pl.multiple_of(b * 128, 128), 128)
        even = li_all[2 * b].astype(F32)
        odd = li_all[2 * b + 1].astype(F32)
        li_out[:tall, cut] = jnp.where(lane < 64, even, pltpu.roll(odd, 64, 1)).astype(BF16)
        li_out[tall:, cut] = jnp.where(lane < 64, pltpu.roll(even, 64, 1), odd).astype(BF16)
        return 0

    lax.fori_loop(0, width // 128, assemble, 0)
    for k in range(len(SP_CHUNKS)):
        wait(sp_last(k))


def exchange(
    dims, lengths, factors, grad_mine, grad_other, w_in, w_rec, dp1, dp2, pack, acts_all, pairs_all, rows_all
):
    utts, time_len, _ = factors.shape
    units = w_rec.shape[0]
    width = 4 * units
    pads, wide = dp1.shape
    cells = wide // 4
    chips = dims[0] * dims[1] * dims[2]
    span = acts_all.shape[1] - cells
    deep = sum(rows for _, rows in SP_CHUNKS)
    nz, ny, _ = dims
    packed = pack.shape[0]
    total = pairs_all.shape[1] + rows_all.shape[1]
    feat = w_in.shape[0] // 2
    half_time = time_len // 2
    vmem = pl.BlockSpec(memory_space=pltpu.VMEM)
    anywhere = pl.BlockSpec(memory_space=pl.ANY)
    shape = jax.ShapeDtypeStruct
    dma = pltpu.SemaphoreType.DMA
    sp_sems = Gather.semaphores(dims, SP_CHUNKS)
    li_sems = Gather.semaphores(dims, LI_CHUNKS)
    return pl.pallas_call(
        functools.partial(exchange_kernel, dims),
        out_shape=(
            shape((utts, time_len, feat), F32),
            shape((total, width), BF16),
            shape((2, deep, wide), BF16),
        ),
        in_specs=[pl.BlockSpec(memory_space=pltpu.SMEM)] + [vmem] * 8 + [anywhere] * 3,
        out_specs=(vmem, vmem, anywhere),
        scratch_shapes=[
            pltpu.VMEM((utts, time_len, width), F32),
            pltpu.VMEM((utts, time_len, units), F32),
            pltpu.VMEM((acts_all.shape[0], span), BF16),
            pltpu.VMEM(pairs_all.shape, BF16),
            pltpu.VMEM(rows_all.shape, BF16),
            pltpu.VMEM((3, pads, wide), BF16),
            pltpu.VMEM((chips, 2, pads, 128), BF16),
            pltpu.VMEM((2, 128, chips * 2 * pads), BF16),
            pltpu.VMEM((128, span), F32),
            pltpu.VMEM((deep, 128), BF16),
            pltpu.VMEM((chips, time_len, 128), BF16),
            pltpu.VMEM((chips, time_len, 128), BF16),
            pltpu.VMEM((chips * 2 * time_len, 128), BF16),
            pltpu.VMEM((128, total), F32),
            pltpu.VMEM((chips, total // 2, 128), BF16),
            pltpu.VMEM((utts, half_time, 2 * feat), BF16),
            pltpu.VMEM((utts, half_time, 2 * feat), BF16),
            pltpu.VMEM((time_len, 128), F32),
            pltpu.VMEM((packed, wide), BF16),
            pltpu.VMEM((ny, packed, nz * 128), BF16),
            pltpu.VMEM((ny, packed, nz * 128), BF16),
            pltpu.VMEM((packed, nz * 128), BF16),
            pltpu.VMEM((packed, nz * 128), BF16),
            pltpu.VMEM((nz, packed, 128), BF16),
            dma((5,)),
            dma((2 + len(SP_CHUNKS),)),
            dma((2 + len(SP_CHUNKS),)),
            dma((chips - 1,)),
            dma((chips - 1,)),
            dma((len(STREAMS), chips - 1)),
            dma((len(STREAMS), chips - 1)),
            sp_sems,
            sp_sems,
            li_sems,
            li_sems,
            dma((1 + ny + nz,)),
            dma((1 + ny + nz,)),
        ],
        compiler_params=pltpu.CompilerParams(
            vmem_limit_bytes=VMEM_BYTES, collective_id=0, has_side_effects=True
        ),
        cost_estimate=pl.CostEstimate(
            flops=100_000_000_000, bytes_accessed=100_000_000, transcendentals=0
        ),
    )(
        lengths, factors, grad_mine, grad_other, w_in, w_rec, dp1, dp2, pack,
        acts_all, pairs_all, rows_all,
    )


def shards(
    frames,
    step_lengths,
    characters,
    char_lengths,
    listen_input,
    listen_hidden,
    listen_bias,
    lower_input,
    lower_hidden,
    lower_bias,
    upper_input,
    upper_hidden,
    upper_bias,
    key_proj,
    query_proj,
    score_vector,
    output_proj,
    output_bias,
    char_table,
):
    chips = lax.axis_size("dp")
    utts, frame_len, feat = frames.shape
    time_len = frame_len // 2
    swap = [(0, 1), (1, 0)]
    w_in, w_rec = listen_input[0], listen_hidden[0]
    units = w_rec.shape[0]
    cells = lower_hidden.shape[0]
    vocab, embed = char_table.shape
    pairs = frames.reshape(utts, time_len, 2 * feat)
    rows, factors, mine, other = listen_forward(step_lengths, pairs, w_in, w_rec, listen_bias)
    other = lax.ppermute(other, "role", swap)
    chars = characters[0, 0]
    previous = jnp.concatenate([jnp.zeros((1,), jnp.int32), chars[:-1]])
    ids = jnp.arange(vocab)[None, :]
    prev_onehot = (previous[:, None] == ids).astype(BF16)
    target_onehot = (chars[:, None] == ids).astype(F32)
    vec = score_vector[None]
    loss, acts, key, *kept = speller_forward(
        step_lengths, char_lengths, mine, other, prev_onehot, target_onehot,
        lower_input, lower_hidden, lower_bias[None], upper_input, upper_hidden, upper_bias[None],
        key_proj, query_proj, vec, output_proj, output_bias[None], char_table,
    )
    grad_mine, grad_other, dp1, dp2, pack = speller_backward(
        lower_input, lower_hidden, upper_input, upper_hidden, key_proj, query_proj, vec,
        prev_onehot, acts, key, *kept,
    )
    grad_other = lax.ppermute(grad_other, "role", swap)
    fits = (
        chips % 4 == 0
        and 4 * cells == 128 * chips
        and 4 * units == 64 * chips
        and embed == 256
        and cells == 2 * units
        and time_len == SEGMENT * STREAMS[-1][1]
        and cells + 2 * units == SP_CHUNKS[-1][0]
        and pack.shape[0] == SP_CHUNKS[-1][1]
        and 2 * feat + units + 64 == 2 * sum(rows for _, rows in LI_CHUNKS)
    )
    if fits:
        own_pairs = lax.dynamic_index_in_dim(pairs, lax.axis_index("role"), 0, keepdims=False)
        pairs_all = lax.all_gather(own_pairs, ("dp", "role"), tiled=True)
        rows_all = lax.all_gather(rows, "dp", tiled=True)
        acts_all = lax.all_gather(acts, ("dp", "role"), tiled=True)
        frame_grad, li, sp = exchange(
            (chips // 4, 2, 2), step_lengths, factors, grad_mine, grad_other, w_in, w_rec,
            dp1, dp2, pack, acts_all, pairs_all, rows_all,
        )
        width = 2 * feat
        sum_in, sum_rec = li[:width].astype(F32), li[width : width + units].astype(F32)
        sum_bias = li[width + units : width + units + 1].astype(F32)
        low, high = 2 * units, 2 * units + cells
        lower = (
            jnp.concatenate([sp[0, high : high + embed], sp[0, :low]], 0).astype(F32),
            sp[0, low:high].astype(F32),
        )
        upper = (sp[1, :cells].astype(F32), sp[1, cells:high].astype(F32))
        pack = sp[1, high:]
    else:
        pack = lax.psum(pack.astype(F32), ("role", "dp"))
        pre = listen_backward(step_lengths, factors, grad_mine, grad_other, w_rec)
        flat = pre.reshape(utts * time_len, 4 * units)
        sums = mm(jnp.concatenate([pairs.reshape(flat.shape[0], 2 * feat), rows], 1).T, flat)
        sums = lax.psum(sums, "dp")
        width = 2 * feat
        sum_in, sum_rec = sums[:width], sums[width : width + units]
        sum_bias = sums[width + units : width + units + 1]
        grad_pairs = mm(flat, w_in.T).reshape(utts, frame_len, feat)
        frame_grad = lax.psum_scatter(grad_pairs, "role", scatter_dimension=1, tiled=True)
        cuts = [embed, embed + 2 * units, embed + 2 * units + cells]
        emb, ctx, s1, s2 = jnp.split(acts, cuts, axis=1)
        local = (
            jnp.concatenate([mm(emb.T, dp1), mm(ctx[:-1].T, dp1[1:])], 0),
            mm(s1[:-1].T, dp1[1:]),
            mm(s1.T, dp2),
            mm(s2[:-1].T, dp2[1:]),
        )
        local = lax.psum(local, ("role", "dp"))
        lower, upper = local[:2], local[2:]
    low_bias, up_bias, g_key, g_query, g_vec, g_out, g_obias, g_table = unpack(
        pack, units, cells, key_proj.shape[1], vocab, embed
    )
    return (
        loss, frame_grad, sum_in[None], sum_rec[None], sum_bias,
        *lower, low_bias, *upper, up_bias,
        g_key, g_query, g_vec, g_out, g_obias, g_table,
    )


def solution(mesh):
    whole = P()
    return jax.shard_map(
        shards,
        mesh=mesh,
        in_specs=(
            P("dp", None, None),
            P("dp"),
            P("dp", "role", None),
            P("dp", "role"),
            P("role", None, None),
            P("role", None, None),
            P("role", None),
        )
        + (whole,) * 12,
        out_specs=(
            P("dp", "role"),
            P("dp", "role", None),
            P("role", None, None),
            P("role", None, None),
            P("role", None),
        )
        + (whole,) * 12,
        check_vma=False,
    )
```

```python
import functools

import jax
import jax.numpy as jnp
from jax import lax
from jax.experimental import pallas as pl
from jax.experimental.pallas import tpu as pltpu
from jax.sharding import PartitionSpec as P

F32 = jnp.float32
BF16 = jnp.bfloat16
VMEM_BYTES = 60 * 1024 * 1024


def mm(left, right):
    return jnp.dot(left, right, preferred_element_type=F32)


def mm_nt(left, right):
    return lax.dot_general(left, right, (((1,), (1,)), ((), ())), preferred_element_type=F32)


def mm_tn(left, right):
    return lax.dot_general(left, right, (((0,), (0,)), ((), ())), preferred_element_type=F32)


def sigmoid(x):
    return 0.5 * jnp.tanh(0.5 * x) + 0.5


def cell_forward(preact, cell_prev):
    n = preact.shape[-1] // 4
    in_gate = sigmoid(preact[:, :n])
    forget = sigmoid(preact[:, n : 2 * n])
    candid = jnp.tanh(preact[:, 2 * n : 3 * n])
    out_gate = sigmoid(preact[:, 3 * n :])
    cell_new = forget * cell_prev + in_gate * candid
    tanh_cell = jnp.tanh(cell_new)
    hidden = out_gate * tanh_cell
    factors = (
        candid * in_gate * (1.0 - in_gate),
        cell_prev * forget * (1.0 - forget),
        in_gate * (1.0 - candid * candid),
        tanh_cell * out_gate * (1.0 - out_gate),
        out_gate * (1.0 - tanh_cell * tanh_cell),
        forget,
    )
    return cell_new, hidden, factors


def cell_backward(factors, grad_hidden, grad_cell):
    n = factors.shape[-1] // 6
    part = lambda k: factors[:, k * n : (k + 1) * n]
    total = grad_cell + grad_hidden * part(4)
    grad_preact = jnp.concatenate(
        [total * part(0), total * part(1), total * part(2), grad_hidden * part(3)], -1
    )
    return grad_preact, total * part(5)


def remote(src, dst, send, recv, device):
    return pltpu.make_async_remote_copy(
        src_ref=src, dst_ref=dst, send_sem=send, recv_sem=recv,
        device_id=device, device_id_type=pl.DeviceIdType.MESH,
    )


def start(copies):
    for copy in copies:
        copy.start()


def wait(copies):
    for copy in copies:
        copy.wait()


def listen_forward_kernel(
    dims, lengths, pairs, w_in, w_rec, bias, rows_out, factors_out, mine_out, other_out, *rest
):
    role = lax.axis_index("role")
    twin = (1 - role, lax.axis_index("dp"))
    if dims is not None:
        proj, emit, hprev, to_other, cross = rest
        barrier = pltpu.get_barrier_semaphore()
        pl.semaphore_signal(
            barrier, inc=1, device_id=twin, device_id_type=pl.DeviceIdType.MESH
        )
        pl.semaphore_wait(barrier, 1)
    else:
        proj, emit, hprev = rest
    utts, time_len, width4 = proj.shape
    units = width4 // 4
    bias_row = bias[...].astype(F32)
    for u in range(utts):
        proj[u] = mm(pairs[u], w_in[...]) + bias_row
    first = lax.broadcasted_iota(jnp.int32, (8, 1), 0) == 0
    row_lengths = jnp.where(first, lengths[0], lengths[1])

    def step(s, carry):
        hidden, cell = carry
        t = jnp.where(role == 1, time_len - 1 - s, s)
        at = pl.ds(t, 1)
        pre_in = jnp.where(first, proj[0, at, :], proj[1, at, :])
        low = hidden.astype(BF16)
        cell_new, hidden_new, factors = cell_forward(pre_in + mm(low, w_rec[...]), cell)
        live = t < row_lengths
        hidden_next = jnp.where(live, hidden_new, hidden)
        cell_next = jnp.where(live, cell_new, cell)
        emitted = jnp.where(live, hidden_new, 0.0)
        for u in range(2):
            for k in range(6):
                factors_out[u, at, k * units : (k + 1) * units] = factors[k][u : u + 1]
            hprev[u, at, :] = hidden[u : u + 1]
            emit[u, at, :] = emitted[u : u + 1]
        return hidden_next, cell_next

    zero = jnp.zeros((8, units), F32)
    lax.fori_loop(0, time_len, step, (zero, zero))
    mine_out[...] = emit[role].astype(BF16)
    if dims is None:
        other_out[...] = emit[1 - role].astype(BF16)
    else:
        to_other[...] = emit[1 - role].astype(BF16)
        crossing = remote(to_other, other_out, cross.at[0], cross.at[1], twin)
        crossing.start()
    for u in range(utts):
        own = slice(u * time_len, (u + 1) * time_len)
        rows_out[own, :] = hprev[u].astype(BF16)
    if dims is not None:
        crossing.wait()


def listen_forward(dims, lengths, pairs, w_in, w_rec, bias):
    utts, time_len, width = pairs.shape
    units = w_rec.shape[0]
    vmem = pl.BlockSpec(memory_space=pltpu.VMEM)
    shape = jax.ShapeDtypeStruct
    outs = [
        shape((utts * time_len, units), BF16),
        shape((utts, time_len, 6 * units), F32),
        shape((time_len, units), BF16),
        shape((time_len, units), BF16),
    ]
    out_specs = [vmem] * 4
    scratch = [
        pltpu.VMEM((utts, time_len, 4 * units), F32),
        pltpu.VMEM((utts, time_len, units), F32),
        pltpu.VMEM((utts, time_len, units), F32),
    ]
    params = dict(vmem_limit_bytes=VMEM_BYTES)
    if dims is not None:
        scratch += [pltpu.VMEM((time_len, units), BF16), pltpu.SemaphoreType.DMA((2,))]
        params.update(collective_id=1, has_side_effects=True)
    return pl.pallas_call(
        functools.partial(listen_forward_kernel, dims),
        out_shape=outs,
        in_specs=[pl.BlockSpec(memory_space=pltpu.SMEM)] + [vmem] * 4,
        out_specs=out_specs,
        scratch_shapes=scratch,
        compiler_params=pltpu.CompilerParams(**params),
    )(lengths, pairs, w_in, w_rec, bias)


class Gather:
    def __init__(self, dims, me, view, chunks, sems):
        self.dims, self.view, self.chunks = dims, view, chunks
        self.role, self.z, self.y, self.x = me
        self.send, self.recv = sems

    def device(self, z, y, x):
        _, ny, nx = self.dims
        return (self.role, (z * ny + y) * nx + x)

    def copies(self, k, which, spans, others, base):
        out = []
        for device in others:
            for span in spans:
                ref = self.view(which, k, *span)
                out.append(
                    remote(ref, ref, self.send.at[k, base], self.recv.at[k, base], device)
                )
                base += 1
        return out

    def along_x(self):
        nx = self.dims[2]
        return [self.device(self.z, self.y, (self.x + j) % nx) for j in range(1, nx)]

    def along_y(self):
        ny = self.dims[1]
        return [self.device(self.z, (self.y + j) % ny, self.x) for j in range(1, ny)]

    def first(self, k):
        nz, ny, nx = self.dims
        slot = (self.y * nx + self.x) * nz + self.z
        others = [self.device((self.z + j) % nz, self.y, self.x) for j in range(1, nz)]
        return self.copies(k, None, [(slot, 1)], others, 0)

    def second(self, k):
        nz, ny, nx = self.dims
        column = ((self.y * nx + self.x) * nz, nz)
        base = nz - 1
        to_x = self.copies(k, 0, [column], self.along_x(), base)
        return to_x + self.copies(k, 1, [column], self.along_y(), base + nx - 1)

    def third(self, k):
        nz, ny, nx = self.dims
        base = nz - 1 + nx - 1 + ny - 1
        to_y = self.copies(k, 0, [(self.y * nx * nz, nx * nz)], self.along_y(), base)
        spans = [((b * nx + self.x) * nz, nz) for b in range(ny)]
        return to_y + self.copies(k, 1, spans, self.along_x(), base + ny - 1)

    @staticmethod
    def semaphores(dims, chunks):
        nz, ny, nx = dims
        count = nz - 1 + 2 * (nx - 1) + 2 * (ny - 1) + (nx - 1) * (ny - 1)
        return pltpu.SemaphoreType.DMA((len(chunks), count))


ROW_CHUNKS = tuple((96 * k, 96) for k in range(4))
FRAME_CHUNKS = tuple((32 * k, 32) for k in range(6))
FRAME_EVENTS = {
    2: ([(0, 0)], [(1, 0)]),
    6: ([(1, 0), (0, 1)], [(2, 0), (1, 1)]),
    10: ([(0, 2)], [(1, 2)]),
    12: ([(2, 0)], []),
    14: ([(1, 1), (0, 3)], [(2, 1), (1, 3)]),
    16: ([(1, 2)], [(2, 2)]),
    18: ([(0, 4)], [(1, 4)]),
    20: ([(2, 1)], []),
    22: ([(1, 3)], [(2, 3)]),
    24: ([(0, 5)], [(1, 5)]),
    26: ([(2, 2)], []),
    28: ([(1, 4), (0, 6)], [(2, 4), (1, 6)]),
    32: ([(2, 3)], []),
    34: ([(1, 5), (0, 7)], [(2, 5), (1, 7)]),
    38: ([(0, 8)], [(1, 8)]),
    40: ([(2, 4)], [(3, 4)]),
    42: ([(1, 6), (0, 9)], [(2, 6), (1, 9)]),
    46: ([(2, 5)], [(3, 5)]),
    48: ([(1, 7)], [(2, 7)]),
    52: ([(1, 8)], [(2, 8)]),
    56: ([(2, 6)], [(3, 6)]),
    58: ([(1, 9)], [(2, 9)]),
    64: ([(2, 7)], [(3, 7)]),
    68: ([(2, 8)], [(3, 8)]),
    72: ([(2, 9)], [(3, 9)]),
}


class Gathers:
    def __init__(self, dims, role, dp, states, frames, sems):
        nz, ny, nx = dims
        me = (role, dp // (ny * nx), (dp // nx) % ny, dp % nx)
        self.twin = (1 - role, dp)
        self.role, self.frames = role, frames
        row_send, row_recv, frame_send, frame_recv, self.last_send, self.last_recv = sems

        def cut(chunk, which):
            first, count = chunk
            if which is not None:
                first, count = first + which * count // 2, count // 2
            return pl.ds(first, count)

        def view_states(which, k, first, count):
            return states.at[pl.ds(first, count), cut(ROW_CHUNKS[k], which)]

        def view_frames(which, k, first, count):
            return frames.at[role, pl.ds(first, count), cut(FRAME_CHUNKS[k], which)]

        self.one = Gather(dims, me, view_states, ROW_CHUNKS, (row_send, row_recv))
        self.two = Gather(dims, me, view_frames, FRAME_CHUNKS, (frame_send, frame_recv))
        self.slot = (me[2] * nx + me[3]) * nz + me[1]
        one = self.one
        to_z = [one.device((one.z + j) % nz, one.y, one.x) for j in range(1, nz)]
        self.partners = to_z + one.along_x() + one.along_y() + [self.twin]

    def phase(self, n, c):
        if n == 3:
            k = c - len(ROW_CHUNKS)
            ref = self.frames.at[self.role, :, pl.ds(*FRAME_CHUNKS[k])]
            return [remote(ref, ref, self.last_send.at[k], self.last_recv.at[k], self.twin)]
        gather, k = (self.one, c) if c < len(ROW_CHUNKS) else (self.two, c - len(ROW_CHUNKS))
        return (gather.first, gather.second, gather.third)[n](k)

    def begin(self):
        for c in range(len(ROW_CHUNKS) + len(FRAME_CHUNKS)):
            start(self.phase(0, c))

    def event(self, ended, begun):
        for n, c in ended:
            wait(self.phase(n, c))
        for n, c in begun:
            start(self.phase(n, c))

    def look(self, step):
        def some():
            for at, (ended, begun) in FRAME_EVENTS.items():
                pl.when(step == at)(functools.partial(self.event, ended, begun))

        pl.when(step % 2 == 0)(some)

    def finish(self, steps):
        for at, (ended, begun) in FRAME_EVENTS.items():
            if at >= steps:
                self.event(ended, begun)
        for k in range(len(FRAME_CHUNKS)):
            wait(self.phase(3, len(ROW_CHUNKS) + k))


def speller_forward_kernel(
    dims, lengths, text_lens, pairs, states,
    mine, other, prev_onehot, target_onehot,
    w_lin, w_lhid, b_low, w_uin, w_uhid, b_up, w_key, w_query, vec, w_out, b_out, table,
    loss, acts, key, keys_proj, key_low, fact1, fact2, q_rows, w_cols, feat_rows, dw_cols,
    logit_grad_out, *rest
):
    role = lax.axis_index("role")
    gather = None
    if dims is not None:
        pairs_all, states_all, *rest = rest
        rest, (stage, own_sem), sems = rest[:-8], rest[-8:-6], rest[-6:]
        gather = Gathers(dims, role, lax.axis_index("dp"), states_all, pairs_all, sems)
        barrier = pltpu.get_barrier_semaphore()
        for device in gather.partners:
            pl.semaphore_signal(
                barrier, inc=1, device_id=device, device_id_type=pl.DeviceIdType.MESH
            )
        load = pltpu.make_async_copy(pairs.at[role], stage, own_sem.at[0])
        load.start()
        place = [
            pltpu.make_async_copy(stage, pairs_all.at[role, gather.slot], own_sem.at[1]),
            pltpu.make_async_copy(states, states_all.at[gather.slot], own_sem.at[2]),
        ]
        place[1].start()
        load.wait()
        place[0].start()
        wait(place)
        pl.semaphore_wait(barrier, len(gather.partners))
        gather.begin()
    emb_proj, s1_rows, s2_rows = rest
    time_len, units = mine.shape
    steps = emb_proj.shape[0]
    cells = w_lhid.shape[0]
    embed = table.shape[1]
    length = lengths[role]
    text_len = text_lens[0, 0]

    key[:, :units] = jnp.where(role == 0, mine[...], other[...])
    key[:, units:] = jnp.where(role == 0, other[...], mine[...])
    keys_proj[...] = mm(key[...], w_key[...])
    key_low[...] = mm(key[...], w_lin[embed:, :])
    emb = mm(prev_onehot[...], table[...]).astype(BF16)
    emb_proj[...] = mm(emb, w_lin[:embed, :]) + b_low[...].astype(F32)
    bias_up = b_up[...].astype(F32)
    vec_row = vec[...].astype(F32)
    frame_ok = lax.broadcasted_iota(jnp.int32, (time_len, 1), 0) < length
    lane = lax.broadcasted_iota(jnp.int32, w_cols.shape, 1)
    w_cols[...] = jnp.zeros_like(w_cols)

    def forward_step(i, carry):
        cell1, cell2, hid1, hid2, ctx_low = carry
        if gather is not None:
            gather.look(i)
        at = pl.ds(i, 1)
        pre1 = emb_proj[at, :] + hid1 + ctx_low
        cell1, s1, factors = cell_forward(pre1, cell1)
        for k in range(6):
            fact1[at, k * cells : (k + 1) * cells] = factors[k]
        s1_rows[at, :] = s1
        s1_low = s1.astype(BF16)
        pre2 = hid2 + bias_up + mm(s1_low, w_uin[...])
        hid1 = mm(s1_low, w_lhid[...])
        cell2, s2, factors = cell_forward(pre2, cell2)
        for k in range(6):
            fact2[at, k * cells : (k + 1) * cells] = factors[k]
        s2_rows[at, :] = s2
        s2_low = s2.astype(BF16)
        query = mm(s2_low, w_query[...])
        hid2 = mm(s2_low, w_uhid[...])
        q_rows[at, :] = query
        part = None
        for j in range(query.shape[1] // 128):
            cut = slice(j * 128, (j + 1) * 128)
            term = jnp.tanh(keys_proj[:, cut] + query[:, cut]) * vec_row[:, cut]
            part = term if part is None else part + term
        scores = jnp.sum(part, -1, keepdims=True)
        scores = jnp.where(frame_ok, scores, -1000000000.0)
        scores = scores - jnp.max(scores, 0, keepdims=True)
        expf = jnp.where(frame_ok, jnp.exp(scores), 0.0)
        rinv = 1.0 / jnp.sum(expf, 0, keepdims=True)
        w_cols[...] = jnp.where(lane == i, expf * rinv, w_cols[...])
        ctx_low = jnp.concatenate(
            [
                jnp.sum(expf * key_low[:, j * 128 : (j + 1) * 128], 0, keepdims=True)
                for j in range(key_low.shape[1] // 128)
            ],
            1,
        )
        return cell1, cell2, hid1, hid2, ctx_low * rinv

    zero = jnp.zeros((1, cells), F32)
    wide = jnp.zeros((1, 4 * cells), F32)
    lax.fori_loop(0, steps, forward_step, (zero, zero, wide, wide, wide))

    w_low = jnp.transpose(w_cols[...])[:steps].astype(BF16)
    ctx = mm(w_low, key[...]).astype(BF16)
    s2_low = s2_rows[...].astype(BF16)
    logits = mm_nt(s2_low, w_out[:, :cells]) + mm_nt(ctx, w_out[:, cells:]) + b_out[...].astype(F32)
    top = jnp.max(logits, -1, keepdims=True)
    log_total = top + jnp.log(jnp.sum(jnp.exp(logits - top), -1, keepdims=True))
    target = target_onehot[...]
    cross = log_total - jnp.sum(logits * target, -1, keepdims=True)
    text = text_len.astype(F32)
    alive = lax.broadcasted_iota(jnp.int32, (steps, 1), 0) < text_len
    loss[...] = jnp.sum(jnp.where(alive, cross, 0.0), 0, keepdims=True) / text
    scale = jnp.where(alive, 1.0 / text, 0.0)
    logit_grad = (scale * (jnp.exp(logits - log_total) - target)).astype(BF16)
    logit_grad_out[...] = logit_grad
    feat_rows[...] = mm(logit_grad, w_out[...])
    dw_cols[...] = jnp.zeros_like(dw_cols)
    dw_cols[:, :steps] = mm_nt(key[...], feat_rows[:, cells:].astype(BF16))
    acts[steps:, :] = jnp.zeros((acts.shape[0] - steps, acts.shape[1]), BF16)
    acts[:steps, :embed] = emb
    acts[:steps, embed : embed + 2 * units] = ctx
    acts[:steps, embed + 2 * units : embed + 2 * units + cells] = s1_rows[...].astype(BF16)
    acts[:steps, embed + 2 * units + cells :] = s2_low
    if gather is not None:
        gather.finish(steps)


def speller_forward(
    dims, lengths, text_lens, pairs, states, mine, other, prev_onehot, target_onehot,
    w_lin, w_lhid, b_low, w_uin, w_uhid, b_up, w_key, w_query, vec, w_out, b_out, table,
):
    time_len, units = mine.shape
    steps, vocab = prev_onehot.shape
    cells = w_lhid.shape[0]
    att = w_key.shape[1]
    embed = table.shape[1]
    pad_steps = -(-steps // 16) * 16
    vmem = pl.BlockSpec(memory_space=pltpu.VMEM)
    smem = pl.BlockSpec(memory_space=pltpu.SMEM)
    shape = jax.ShapeDtypeStruct
    outs = [
        shape((1, 1), F32),
        shape((pad_steps, embed + 2 * units + 2 * cells), BF16),
        shape((time_len, 2 * units), BF16),
        shape((time_len, att), F32),
        shape((time_len, 4 * cells), F32),
        shape((steps, 6 * cells), F32),
        shape((steps, 6 * cells), F32),
        shape((steps, att), F32),
        shape((time_len, -(-steps // 128) * 128), F32),
        shape((steps, w_out.shape[1]), F32),
        shape((time_len, -(-steps // 128) * 128), F32),
        shape((steps, vocab), BF16),
    ]
    out_specs = [vmem] * len(outs)
    scratch = [
        pltpu.VMEM((steps, 4 * cells), F32),
        pltpu.VMEM((steps, cells), F32),
        pltpu.VMEM((steps, cells), F32),
    ]
    params = dict(vmem_limit_bytes=VMEM_BYTES)
    if dims is not None:
        chips = dims[0] * dims[1] * dims[2]
        dma = pltpu.SemaphoreType.DMA
        outs += [shape((2, chips, *pairs.shape[1:]), BF16), shape((chips, *states.shape), BF16)]
        out_specs += [pl.BlockSpec(memory_space=pl.ANY)] * 2
        scratch += [pltpu.VMEM(pairs.shape[1:], BF16), dma((3,))]
        scratch += [Gather.semaphores(dims, ROW_CHUNKS)] * 2
        scratch += [Gather.semaphores(dims, FRAME_CHUNKS)] * 2
        scratch += [dma((len(FRAME_CHUNKS),))] * 2
        params.update(collective_id=2, has_side_effects=True)
    return pl.pallas_call(
        functools.partial(speller_forward_kernel, dims),
        out_shape=outs,
        in_specs=[smem] * 2 + [pl.BlockSpec(memory_space=pl.ANY)] + [vmem] * 17,
        out_specs=out_specs,
        scratch_shapes=scratch,
        compiler_params=pltpu.CompilerParams(**params),
    )(
        lengths, text_lens, pairs, states, mine, other, prev_onehot, target_onehot,
        w_lin, w_lhid, b_low, w_uin, w_uhid, b_up, w_key, w_query, vec, w_out, b_out, table,
    )


SMALL = 32


def shift_up(rows):
    count = rows.shape[0]
    rolled = pltpu.roll(rows, count - 1, 0)
    at = lax.broadcasted_iota(jnp.int32, rows.shape, 0)
    return jnp.where(at == count - 1, 0.0, rolled)


def speller_backward_kernel(
    w_lin, w_lhid, w_uin, w_uhid, w_key, w_query, vec, prev_onehot,
    acts, key, keys_proj, key_low, fact1, fact2, q_rows, w_cols, feat_rows, dw_cols, logit_grad,
    grad_mine, grad_other, dp1_out, dp2_out, pack,
    dp1_rows, dp2_rows, dq_rows, keys_acc, vec_acc, small, t_lhid, t_uin, t_uhid, t_query,
):
    role = lax.axis_index("role")
    time_len, att = keys_proj.shape
    steps, vocab = logit_grad.shape
    units = key.shape[1] // 2
    cells = w_lhid.shape[0]
    embed = acts.shape[1] - 2 * units - 2 * cells
    vec_row = vec[...].astype(F32)
    zero = jnp.zeros((1, cells), F32)
    wide = jnp.zeros((1, 4 * cells), BF16)
    keys_acc[...] = jnp.zeros_like(keys_acc)
    vec_acc[...] = jnp.zeros_like(vec_acc)
    t_lhid[...] = w_lhid[...].T
    t_uin[...] = w_uin[...].T
    t_uhid[...] = w_uhid[...].T
    t_query[...] = w_query[...].T
    lane = lax.broadcasted_iota(jnp.int32, w_cols.shape, 1)

    def backward_step(s, carry):
        dp1, dp2, dcell1, dcell2 = carry
        i = steps - 1 - s
        at = pl.ds(i, 1)
        query = q_rows[at, :]
        dp1_row = dp1.astype(F32)
        here = lane == i
        part = jnp.where(here, dw_cols[...], 0.0)
        for j in range(key_low.shape[1] // 128):
            cut = slice(j * 128, (j + 1) * 128)
            part = part + dp1_row[:, cut] * key_low[:, cut]
        dweights = jnp.sum(part, -1, keepdims=True)
        weights = jnp.sum(jnp.where(here, w_cols[...], 0.0), -1, keepdims=True)
        back2 = mm(dp2, t_uhid[...])
        back1 = mm(dp1, t_lhid[...])
        shared = weights * dweights
        dscore = shared - weights * jnp.sum(shared, 0, keepdims=True)
        sums = []
        for j in range(query.shape[1] // 128):
            cut = slice(j * 128, (j + 1) * 128)
            energy = jnp.tanh(keys_proj[:, cut] + query[:, cut])
            moved = dscore * (1.0 - energy * energy)
            keys_acc[:, cut] += moved
            sums.append(jnp.sum(moved, 0, keepdims=True))
            vec_acc[:, cut] += jnp.sum((dscore * energy).reshape(time_len // 8, 8, 128), 0)
        dquery = (jnp.concatenate(sums, 1) * vec_row).astype(BF16)
        dq_rows[at, :] = dquery.astype(F32)
        ds2 = back2 + feat_rows[at, :cells] + mm(dquery, t_query[...])
        pre2, dcell2 = cell_backward(fact2[at, :], ds2, dcell2)
        dp2_rows[at, :] = pre2
        dp2 = pre2.astype(BF16)
        ds1 = back1 + mm(dp2, t_uin[...])
        pre1, dcell1 = cell_backward(fact1[at, :], ds1, dcell1)
        dp1_rows[at, :] = pre1
        return pre1.astype(BF16), dp2, dcell1, dcell2

    lax.fori_loop(0, steps, backward_step, (wide, wide, zero, zero))

    dp1 = dp1_rows[...].astype(BF16)
    dp2 = dp2_rows[...].astype(BF16)
    dq = dq_rows[...].astype(BF16)
    extra = jnp.zeros((dp1_out.shape[0] - steps, 4 * cells), BF16)
    dp1_out[steps:, :] = extra
    dp2_out[steps:, :] = extra
    dp1_out[:steps, :] = dp1
    dp2_out[:steps, :] = dp2
    next_dp1 = shift_up(dp1.astype(F32)).astype(BF16)
    ctx_grad = (feat_rows[:, cells:] + mm_nt(next_dp1, w_lin[embed:, :])).astype(BF16)
    keys_grad = (keys_acc[...] * vec_row).astype(BF16)
    w_low = w_cols[...].astype(BF16)[:, :steps]
    key_grad = mm_nt(keys_grad, w_key[...]) + mm(w_low, ctx_grad)
    key_grad = key_grad.astype(BF16)
    grad_mine[...] = jnp.where(role == 0, key_grad[:, :units], key_grad[:, units:])
    grad_other[...] = jnp.where(role == 0, key_grad[:, units:], key_grad[:, :units])
    ctx = acts[:steps, embed : embed + 2 * units]
    s2 = acts[:steps, embed + 2 * units + cells :]
    wide = pack.shape[1]
    deep = 2 * units * att // wide
    g_key = mm_tn(key[...], keys_grad)
    g_query = mm_tn(s2, dq)
    for k in range(wide // att):
        cut = slice(k * att, (k + 1) * att)
        first = 2 * SMALL
        pack[first : first + deep, cut] = g_key[k * deep : (k + 1) * deep].astype(BF16)
        first += deep
        pack[first : first + deep, cut] = g_query[k * deep : (k + 1) * deep].astype(BF16)
    emb_grad = mm_nt(dp1, w_lin[:embed, :])
    hot = prev_onehot[...]
    total = None
    for _ in range(3):
        low = emb_grad.astype(BF16)
        emb_grad = emb_grad - low.astype(F32)
        total = mm_tn(hot, low) if total is None else total + mm_tn(hot, low)
    small[...] = jnp.zeros_like(small)
    small[:vocab, :cells] = mm_tn(logit_grad[...], s2)
    small[:vocab, cells : cells + 2 * units] = mm_tn(logit_grad[...], ctx)
    base = cells + 2 * units
    small[:vocab, base : base + embed] = total
    base += embed
    small[0:1, base : base + att] = jnp.sum(vec_acc[...], 0, keepdims=True)
    small[1:2, base : base + vocab] = jnp.sum(logit_grad[...].astype(F32), 0, keepdims=True)
    low_bias = jnp.sum(dp1.astype(F32), 0, keepdims=True)
    up_bias = jnp.sum(dp2.astype(F32), 0, keepdims=True)
    for k in range(4):
        small[2 + k : 3 + k, base : base + cells] = low_bias[:, k * cells : (k + 1) * cells]
        small[6 + k : 7 + k, base : base + cells] = up_bias[:, k * cells : (k + 1) * cells]
    high = small[...].astype(BF16)
    pack[:SMALL, :] = high
    pack[SMALL : 2 * SMALL, :] = (small[...] - high.astype(F32)).astype(BF16)


def speller_backward(
    w_lin, w_lhid, w_uin, w_uhid, w_key, w_query, vec, prev_onehot,
    acts, key, keys_proj, key_low, fact1, fact2, q_rows, w_cols, feat_rows, dw_cols, logit_grad,
):
    time_len, att = keys_proj.shape
    steps, vocab = logit_grad.shape
    units = key.shape[1] // 2
    cells = w_lhid.shape[0]
    pad_steps = acts.shape[0]
    vmem = pl.BlockSpec(memory_space=pltpu.VMEM)
    shape = jax.ShapeDtypeStruct
    outs = [
        shape((time_len, units), BF16),
        shape((time_len, units), BF16),
        shape((pad_steps, 4 * cells), BF16),
        shape((pad_steps, 4 * cells), BF16),
        shape(((2 * units + cells) * att // (4 * cells) + 2 * SMALL, 4 * cells), BF16),
    ]
    out_specs = [vmem] * 5
    scratch = [
        pltpu.VMEM((steps, 4 * cells), F32),
        pltpu.VMEM((steps, 4 * cells), F32),
        pltpu.VMEM((steps, att), F32),
        pltpu.VMEM((time_len, att), F32),
        pltpu.VMEM((8, att), F32),
        pltpu.VMEM((SMALL, 4 * cells), F32),
        pltpu.VMEM((4 * cells, cells), BF16),
        pltpu.VMEM((4 * cells, cells), BF16),
        pltpu.VMEM((4 * cells, cells), BF16),
        pltpu.VMEM((att, cells), BF16),
    ]
    return pl.pallas_call(
        speller_backward_kernel,
        out_shape=outs,
        in_specs=[vmem] * 19,
        out_specs=out_specs,
        scratch_shapes=scratch,
        compiler_params=pltpu.CompilerParams(vmem_limit_bytes=VMEM_BYTES),
    )(
        w_lin, w_lhid, w_uin, w_uhid, w_key, w_query, vec, prev_onehot,
        acts, key, keys_proj, key_low, fact1, fact2, q_rows, w_cols, feat_rows, dw_cols, logit_grad,
    )


def unfold(folded, width):
    deep = folded.shape[0]
    return folded.reshape(deep, -1, width).swapaxes(0, 1).reshape(-1, width)


def unpack(small, units, cells, att, vocab, embed):
    small = small[:SMALL].astype(F32) + small[SMALL:].astype(F32)
    base = cells + 2 * units
    g_out = small[:vocab, :base].T
    g_table = small[:vocab, base : base + embed]
    base += embed
    low_bias = small[2:6, base : base + cells].reshape(-1)
    up_bias = small[6:10, base : base + cells].reshape(-1)
    g_vec = small[0, base : base + att]
    g_obias = small[1, base : base + vocab]
    return low_bias, up_bias, g_vec, g_out, g_obias, g_table


def backward_steps(role, lengths, factors, grad_out, w_rec, grad_pre, first_step, count, carry):
    time_len = factors.shape[1]
    first = lax.broadcasted_iota(jnp.int32, (8, 1), 0) == 0
    row_lengths = jnp.where(first, lengths[0], lengths[1])

    def step(s, carry):
        grad_hidden, grad_cell = carry
        t = jnp.where(role == 1, s, time_len - 1 - s)
        at = pl.ds(t, 1)
        live = t < row_lengths
        fact = jnp.where(first, factors[0, at, :], factors[1, at, :])
        arrived = jnp.where(first, grad_out[0, at, :], grad_out[1, at, :])
        fact = jnp.where(live, fact, 0.0)
        total = grad_hidden + jnp.where(live, arrived, 0.0)
        pre, cell_back = cell_backward(fact, total, grad_cell)
        for u in range(2):
            grad_pre[u, at, :] = pre[u : u + 1]
        back = mm_nt(pre.astype(BF16), w_rec[...])
        return jnp.where(live, back, total), jnp.where(live, cell_back, grad_cell)

    return lax.fori_loop(first_step, first_step + count, step, carry)


def listen_backward_kernel(
    lengths, factors, grad_mine, grad_other, w_rec, pre_out, grad_pre, grad_out
):
    role = lax.axis_index("role")
    grad_out[role] = grad_mine[...].astype(F32)
    grad_out[1 - role] = grad_other[...].astype(F32)
    zero = jnp.zeros((8, w_rec.shape[0]), F32)
    backward_steps(
        role, lengths, factors, grad_out, w_rec, grad_pre, 0, factors.shape[1], (zero, zero)
    )
    pre_out[...] = grad_pre[...].astype(BF16)


def listen_backward(lengths, factors, grad_mine, grad_other, w_rec):
    utts, time_len, _ = factors.shape
    units = w_rec.shape[0]
    vmem = pl.BlockSpec(memory_space=pltpu.VMEM)
    return pl.pallas_call(
        listen_backward_kernel,
        out_shape=jax.ShapeDtypeStruct((utts, time_len, 4 * units), BF16),
        in_specs=[pl.BlockSpec(memory_space=pltpu.SMEM)] + [vmem] * 4,
        out_specs=vmem,
        scratch_shapes=[
            pltpu.VMEM((utts, time_len, 4 * units), F32),
            pltpu.VMEM((utts, time_len, units), F32),
        ],
        compiler_params=pltpu.CompilerParams(vmem_limit_bytes=VMEM_BYTES),
    )(lengths, factors, grad_mine, grad_other, w_rec)


SEGMENT = 32
STREAMS = ((0, 3), (3, 5), (5, 6))


SP_CHUNKS = ((320, 352), (672, 352), (1024, 320), (0, 320))
LI_CHUNKS = ((0, 352), (352, 320))


def exchange_kernel(
    dims,
    lengths, factors, grad_mine, grad_other, w_in, w_rec, dp1, dp2, pack, acts_all, pairs_all, rows_all,
    frames_out, li_out, sp_out, kq_out,
    grad_pre, grad_out, acts_buf, pairs_buf, rows_buf, dp_pair, got, got_t, prod, column,
    li_send, li_got, li_rows, li_acc, li_all, fr_send, fr_got, weave,
    pk_pair, pk_x, pk_xsum, pk_y, pk_ysum, pk_z,
    local_sem, chip_send, chip_recv, aa_send, aa_recv, li_aa_send, li_aa_recv,
    sp_send, sp_recv, li_ag_send, li_ag_recv, pk_send, pk_recv, far_grad,
):
    nz, ny, nx = dims
    chips = nz * ny * nx
    role = lax.axis_index("role")
    dp = lax.axis_index("dp")
    z, y, x = dp // (ny * nx), (dp // nx) % ny, dp % nx
    utts, time_len, width = grad_pre.shape
    units = w_rec.shape[0]
    cells = dp1.shape[1] // 4
    half_time = time_len // 2
    pads = dp1.shape[0]
    twin = (1 - role, dp)

    def slot_of(chip):
        return (((chip // nx) % ny) * nx + chip % nx) * nz + chip // (ny * nx)

    slot = slot_of(dp)
    lanes = pl.ds(pl.multiple_of(slot * 128, 128), 128)

    barrier = pltpu.get_barrier_semaphore()
    mesh = pl.DeviceIdType.MESH

    def greet(k, _):
        pl.semaphore_signal(barrier, inc=1, device_id=(role, (dp + k) % chips), device_id_type=mesh)
        return 0

    pl.semaphore_signal(barrier, inc=1, device_id=twin, device_id_type=mesh)
    lax.fori_loop(1, chips, greet, 0)
    load_acts = pltpu.make_async_copy(
        acts_all.at[:, pl.ds(pl.multiple_of(role * cells, 128), acts_buf.shape[1])],
        acts_buf, local_sem.at[0],
    )
    load_acts.start()
    load_rows = [
        pltpu.make_async_copy(
            rows_all.at[c, pl.ds(u * time_len, time_len)],
            rows_buf.at[pl.ds((u * chips + c) * time_len, time_len), pl.ds(0, units)],
            local_sem.at[5 + c * utts + u],
        )
        for c in range(chips)
        for u in range(utts)
    ]
    rows_buf[:, units:] = jnp.ones((rows_buf.shape[0], rows_buf.shape[1] - units), BF16)
    start(load_rows)
    load_pairs = pltpu.make_async_copy(pairs_all, pairs_buf, local_sem.at[4])
    load_pairs.start()
    dp_pair[role] = jnp.where(role == 0, dp1[...], dp2[...])
    dp_pair[2] = jnp.where(role == 0, dp2[...], dp1[...])
    grad_out[role] = grad_mine[...].astype(F32)
    pl.semaphore_wait(barrier, chips)
    last = chip_send.shape[0] - 1
    crossing = remote(grad_other, far_grad, chip_send.at[last], chip_recv.at[last], twin)
    crossing.start()

    to_twin = remote(dp_pair.at[2], dp_pair.at[role], chip_send.at[0], chip_recv.at[0], twin)
    to_twin.start()
    pack_twin = remote(pack, pk_pair, pk_send.at[0], pk_recv.at[0], twin)

    @pl.when(role == 0)
    def _():
        pack_twin.start()

    to_twin.wait()

    def block(k):
        chip = (dp + k) % chips
        cut = pl.ds(pl.multiple_of(slot_of(chip) * 128, 128), 128)
        return remote(
            dp_pair.at[pl.ds(0, 2), :, cut], got.at[dp],
            aa_send.at[k - 1], aa_recv.at[k - 1], (role, chip),
        )

    lax.fori_loop(1, chips, lambda k, _: (block(k).start(), 0)[1], 0)
    own_block = pltpu.make_async_copy(
        dp_pair.at[pl.ds(0, 2), :, lanes], got.at[dp], local_sem.at[2]
    )
    own_block.start()

    def rounded(total):
        value = total[:SMALL] + total[SMALL : 2 * SMALL]
        high = value.astype(BF16)
        low = (value - high.astype(F32)).astype(BF16)
        return jnp.concatenate([high, low, total[2 * SMALL :].astype(BF16)], 0)

    chip_at = lambda a, b, c: (role, (a * ny + b) * nx + c)
    x_other, y_other = (x + 1) % nx, (y + 1) % ny
    column_wide = nz * 128

    def pack_x(b):
        first = pl.multiple_of((b * nx + x_other) * column_wide, 128)
        return remote(
            pk_pair.at[:, pl.ds(first, column_wide)], pk_x.at[b],
            pk_send.at[1 + b], pk_recv.at[1 + b], chip_at(z, y, x_other),
        )

    pack_y = remote(
        pk_xsum.at[y_other], pk_y, pk_send.at[1 + ny], pk_recv.at[1 + ny], chip_at(z, y_other, x)
    )

    def pack_z(j):
        to = (z + j) % nz
        return remote(
            pk_ysum.at[:, pl.ds(pl.multiple_of(to * 128, 128), 128)], pk_z.at[z],
            pk_send.at[1 + ny + j], pk_recv.at[1 + ny + j], chip_at(to, y, x),
        )

    @pl.when(role == 0)
    def _():
        pack_twin.wait_send()

    @pl.when(role == 1)
    def _():
        pack_twin.wait_recv()

        def add(b, _):
            cut = pl.ds(pl.multiple_of(b * 128, 128), 128)
            total = pk_pair[:, cut].astype(F32) + pack[:, cut].astype(F32)
            pk_pair[:, cut] = rounded(total)
            return 0

        lax.fori_loop(0, pack.shape[1] // 128, add, 0)
        for b in range(ny):
            pack_x(b).start()

    def pack_after_x():
        for b in range(ny):
            pack_x(b).wait()
            first = pl.multiple_of((b * nx + x) * column_wide, 128)

            def add(c, _):
                here = pl.ds(pl.multiple_of(first + c * 128, 128), 128)
                cut = pl.ds(pl.multiple_of(c * 128, 128), 128)
                total = pk_pair[:, here].astype(F32) + pk_x[b, :, cut].astype(F32)
                pk_xsum[b, :, cut] = rounded(total)
                return 0

            lax.fori_loop(0, nz, add, 0)
        pack_y.start()

    def pack_after_y():
        pack_y.wait()

        def add(c, _):
            cut = pl.ds(pl.multiple_of(c * 128, 128), 128)
            total = pk_xsum[y, :, cut].astype(F32) + pk_y[:, cut].astype(F32)
            pk_ysum[:, cut] = rounded(total)
            return 0

        lax.fori_loop(0, nz, add, 0)
        for j in range(1, nz):
            pack_z(j).start()

    def pack_after_z():
        for j in range(1, nz):
            pack_z(j).wait()
        pk_z[z] = pk_ysum[:, pl.ds(pl.multiple_of(z * 128, 128), 128)]
        total = pk_z[0].astype(F32)
        for j in range(1, nz):
            total = total + pk_z[j].astype(F32)
        column[: total.shape[0], :] = rounded(total)

    def view_sp(which, k, first, count):
        rows = SP_CHUNKS[k]
        if which is not None:
            rows = (rows[0] + which * rows[1] // 2, rows[1] // 2)
        cut = pl.ds(pl.multiple_of(first * 128, 128), count * 128)
        return sp_out.at[role, pl.ds(*rows), cut]

    def view_li(which, k, first, count):
        rows = LI_CHUNKS[k]
        if which is not None:
            rows = (rows[0] + which * rows[1] // 2, rows[1] // 2)
        return li_all.at[pl.ds(first, count), pl.ds(*rows)]

    me = (role, z, y, x)
    sp = Gather(dims, me, view_sp, SP_CHUNKS, (sp_send, sp_recv))
    li = Gather(dims, me, view_li, LI_CHUNKS, (li_ag_send, li_ag_recv))

    def sp_last(k):
        ref = sp_out.at[role, pl.ds(*SP_CHUNKS[k])]
        return [remote(ref, ref, chip_send.at[2 + k], chip_recv.at[2 + k], twin)]

    def rows_of(j):
        return jnp.where(role == 1, SEGMENT * j, time_len - SEGMENT * (j + 1))

    def pack_columns(first_segment, last_segment):
        lane = lax.broadcasted_iota(jnp.int32, (SEGMENT, 128), 1)
        for j in range(first_segment, last_segment):
            rows = pl.ds(pl.multiple_of(rows_of(j), SEGMENT), SEGMENT)
            for b in range(width // 128):
                one = grad_pre[0, rows, b * 128 : (b + 1) * 128]
                two = grad_pre[1, rows, b * 128 : (b + 1) * 128]
                even = jnp.where(lane < 64, one, pltpu.roll(two, 64, 1))
                odd = jnp.where(lane < 64, pltpu.roll(one, 64, 1), two)
                li_send[2 * b, rows, :] = even.astype(BF16)
                li_send[2 * b + 1, rows, :] = odd.astype(BF16)

    def stream(n):
        first_segment, last_segment = STREAMS[n]
        count = SEGMENT * (last_segment - first_segment)
        begin = jnp.where(role == 1, SEGMENT * first_segment, time_len - SEGMENT * last_segment)
        rows = pl.ds(pl.multiple_of(begin, SEGMENT), count)

        def one(k):
            chip = (dp + k) % chips
            return remote(
                li_send.at[slot_of(chip), rows], li_got.at[dp, rows],
                li_aa_send.at[n, k - 1], li_aa_recv.at[n, k - 1], (role, chip),
            )

        return one

    def start_stream(n):
        pack_columns(*STREAMS[n])
        one = stream(n)
        lax.fori_loop(1, chips, lambda k, _: (one(k).start(), 0)[1], 0)

    def wait_stream(n):
        one = stream(n)
        lax.fori_loop(1, chips, lambda k, _: (one(k).wait(), 0)[1], 0)

    crossing.wait()
    grad_out[1 - role] = far_grad[...].astype(F32)
    zero = jnp.zeros((8, units), F32)
    carry = (zero, zero)

    def run(j, carry):
        return backward_steps(
            role, lengths, factors, grad_out, w_rec, grad_pre, SEGMENT * j, SEGMENT, carry
        )

    carry = run(0, carry)
    pl.when(role == 1)(pack_after_x)
    carry = run(1, carry)
    pl.when(role == 1)(pack_after_y)

    lax.fori_loop(1, chips, lambda k, _: (block(k).wait(), 0)[1], 0)
    own_block.wait()
    load_acts.wait()
    both = got[...].reshape(chips * 2 * pads, 128).astype(F32)
    rolled = pltpu.roll(both, chips * 2 * pads - 1, 0)
    got_t[0] = jnp.transpose(both).astype(BF16)
    got_t[1] = jnp.transpose(rolled).astype(BF16)
    groups = acts_buf.shape[1] // 256
    for g in range(groups):
        cut = slice(g * 256, (g + 1) * 256)
        if g == 0:
            left = got_t[0]
        elif g < groups - cells // 256:
            left = got_t[1 - role]
        else:
            left = got_t[1]
        prod[:, cut] = mm(left, acts_buf[:, cut])
    column[2 * SMALL :, :] = jnp.transpose(prod[...]).astype(BF16)
    column[: 2 * SMALL, :] = jnp.zeros((2 * SMALL, 128), BF16)

    def place(first, count):
        copy = pltpu.make_async_copy(
            column.at[pl.ds(first, count)], sp_out.at[role, pl.ds(first, count), lanes],
            local_sem.at[3],
        )
        copy.start()
        copy.wait()

    head = SP_CHUNKS[-1][1]
    place(head, column.shape[0] - head)
    for k in range(len(SP_CHUNKS) - 1):
        start(sp.first(k))

    carry = run(2, carry)
    pl.when(role == 1)(pack_after_z)
    place(0, head)
    start(sp.first(len(SP_CHUNKS) - 1))
    start_stream(0)
    far = jnp.where(role == 0, half_time, 0)
    near = half_time - far
    for u in range(utts):
        rows = pl.ds(pl.multiple_of(far, half_time), half_time)
        fr_send[u] = mm_nt(grad_pre[u, rows, :].astype(BF16), w_in[...]).astype(BF16)
    frames_copy = remote(fr_send, fr_got, chip_send.at[1], chip_recv.at[1], twin)
    frames_copy.start()
    wait(sp.first(0))
    start(sp.second(0))
    carry = run(3, carry)
    wait(sp.first(1))
    start(sp.second(1))
    wait(sp.second(0))
    start(sp.third(0))
    carry = run(4, carry)
    start_stream(1)
    wait(sp.first(2))
    start(sp.second(2))
    wait(sp.second(1))
    start(sp.third(1))
    carry = run(5, carry)
    start_stream(2)
    wait(sp.first(3))
    start(sp.second(3))
    wait(sp.second(2))
    start(sp.third(2))

    frames_copy.wait()
    feat = frames_out.shape[2]
    for u in range(utts):
        rows = pl.ds(pl.multiple_of(near, half_time), half_time)
        total = mm_nt(grad_pre[u, rows, :].astype(BF16), w_in[...]) + fr_got[u].astype(F32)
        for j in range(feat // 128):
            for half in range(2):
                cut = slice(half * feat + j * 128, half * feat + (j + 1) * 128)
                weave[pl.ds(half, half_time, stride=2), :] = total[:, cut]
            frames_out[u, :, j * 128 : (j + 1) * 128] = weave[...]

    li_got[dp] = li_send[slot]
    wait(load_rows)
    load_pairs.wait()
    for n in range(len(STREAMS)):
        wait_stream(n)

    def spread(c, _):
        value = li_got[c].astype(F32)
        for u, part in enumerate((value, pltpu.roll(value, 64, 1))):
            base = pl.multiple_of((u * chips + slot_of(c)) * time_len, 16)
            li_rows[pl.ds(base, time_len), :] = part.astype(BF16)
        return 0

    lax.fori_loop(0, chips, spread, 0)
    li_acc[...] = jnp.zeros_like(li_acc)
    deep = 4 * time_len
    features = pairs_buf.shape[1]

    def accumulate(c, _):
        rows = pl.ds(pl.multiple_of(c * deep, 256), deep)
        left = jnp.transpose(li_rows[rows, :])
        li_acc[:, :features] += mm(left, pairs_buf[rows, :])
        li_acc[:, features:] += mm(left, rows_buf[rows, :])
        return 0

    lax.fori_loop(0, chips * 2 * time_len // deep, accumulate, 0)
    flipped = jnp.transpose(li_acc[...])
    tall = flipped.shape[0] // 2
    lane = lax.broadcasted_iota(jnp.int32, (tall, 128), 1)
    packed = jnp.where(lane < 64, flipped[:tall], pltpu.roll(flipped[tall:], 64, 1))
    li_all[slot] = packed.astype(BF16)

    for k in range(len(LI_CHUNKS)):
        start(li.first(k))
    wait(sp.second(3))
    start(sp.third(3))
    wait(li.first(0))
    start(li.second(0))
    wait(sp.third(0))
    start(sp_last(0))
    wait(sp.third(1))
    start(sp_last(1))
    wait(li.first(1))
    start(li.second(1))
    wait(li.second(0))
    start(li.third(0))
    wait(sp.third(2))
    start(sp_last(2))
    wait(li.second(1))
    start(li.third(1))
    wait(sp.third(3))
    start(sp_last(3))
    wait(li.third(0))
    wait(li.third(1))

    def assemble(b, _):
        cut = pl.ds(pl.multiple_of(b * 128, 128), 128)
        even = li_all[2 * b].astype(F32)
        odd = li_all[2 * b + 1].astype(F32)
        li_out[:tall, cut] = jnp.where(lane < 64, even, pltpu.roll(odd, 64, 1)).astype(BF16)
        li_out[tall:, cut] = jnp.where(lane < 64, pltpu.roll(even, 64, 1), odd).astype(BF16)
        return 0

    lax.fori_loop(0, width // 128, assemble, 0)
    for k in range(len(SP_CHUNKS)):
        wait(sp_last(k))
    att = kq_out.shape[2]
    folds = sp_out.shape[2] // att
    deep = att // folds
    unfold = [
        pltpu.make_async_copy(
            sp_out.at[1, pl.ds(2 * SMALL + which * deep, deep), pl.ds(k * att, att)],
            kq_out.at[which, pl.ds(k * deep, deep)],
            local_sem.at[5 + which * folds + k],
        )
        for which in range(2)
        for k in range(folds)
    ]
    start(unfold)
    wait(unfold)


def exchange(
    dims, lengths, factors, grad_mine, grad_other, w_in, w_rec, dp1, dp2, pack, acts_all, pairs_all, rows_all
):
    utts, time_len, _ = factors.shape
    units = w_rec.shape[0]
    width = 4 * units
    pads, wide = dp1.shape
    cells = wide // 4
    chips = dims[0] * dims[1] * dims[2]
    span = acts_all.shape[1] - cells
    deep = sum(rows for _, rows in SP_CHUNKS)
    nz, ny, _ = dims
    packed = pack.shape[0]
    total = pairs_all.shape[1] + units + 64
    feat = w_in.shape[0] // 2
    half_time = time_len // 2
    vmem = pl.BlockSpec(memory_space=pltpu.VMEM)
    anywhere = pl.BlockSpec(memory_space=pl.ANY)
    shape = jax.ShapeDtypeStruct
    dma = pltpu.SemaphoreType.DMA
    sp_sems = Gather.semaphores(dims, SP_CHUNKS)
    li_sems = Gather.semaphores(dims, LI_CHUNKS)
    return pl.pallas_call(
        functools.partial(exchange_kernel, dims),
        out_shape=(
            shape((utts, time_len, feat), F32),
            shape((total, width), BF16),
            shape((2, deep, wide), BF16),
            shape((2, cells, cells), BF16),
        ),
        in_specs=[pl.BlockSpec(memory_space=pltpu.SMEM)] + [vmem] * 8 + [anywhere] * 3,
        out_specs=(vmem, vmem, anywhere, vmem),
        scratch_shapes=[
            pltpu.VMEM((utts, time_len, width), F32),
            pltpu.VMEM((utts, time_len, units), F32),
            pltpu.VMEM((acts_all.shape[0], span), BF16),
            pltpu.VMEM(pairs_all.shape, BF16),
            pltpu.VMEM((chips * utts * time_len, units + 64), BF16),
            pltpu.VMEM((3, pads, wide), BF16),
            pltpu.VMEM((chips, 2, pads, 128), BF16),
            pltpu.VMEM((2, 128, chips * 2 * pads), BF16),
            pltpu.VMEM((128, span), F32),
            pltpu.VMEM((deep, 128), BF16),
            pltpu.VMEM((chips, time_len, 128), BF16),
            pltpu.VMEM((chips, time_len, 128), BF16),
            pltpu.VMEM((chips * 2 * time_len, 128), BF16),
            pltpu.VMEM((128, total), F32),
            pltpu.VMEM((chips, total // 2, 128), BF16),
            pltpu.VMEM((utts, half_time, 2 * feat), BF16),
            pltpu.VMEM((utts, half_time, 2 * feat), BF16),
            pltpu.VMEM((time_len, 128), F32),
            pltpu.VMEM((packed, wide), BF16),
            pltpu.VMEM((ny, packed, nz * 128), BF16),
            pltpu.VMEM((ny, packed, nz * 128), BF16),
            pltpu.VMEM((packed, nz * 128), BF16),
            pltpu.VMEM((packed, nz * 128), BF16),
            pltpu.VMEM((nz, packed, 128), BF16),
            dma((5 + chips * utts,)),
            dma((3 + len(SP_CHUNKS),)),
            dma((3 + len(SP_CHUNKS),)),
            dma((chips - 1,)),
            dma((chips - 1,)),
            dma((len(STREAMS), chips - 1)),
            dma((len(STREAMS), chips - 1)),
            sp_sems,
            sp_sems,
            li_sems,
            li_sems,
            dma((1 + ny + nz,)),
            dma((1 + ny + nz,)),
            pltpu.VMEM(grad_other.shape, BF16),
        ],
        compiler_params=pltpu.CompilerParams(
            vmem_limit_bytes=VMEM_BYTES, collective_id=0, has_side_effects=True
        ),
    )(
        lengths, factors, grad_mine, grad_other, w_in, w_rec, dp1, dp2, pack,
        acts_all, pairs_all, rows_all,
    )


def shards(
    frames,
    step_lengths,
    characters,
    char_lengths,
    listen_input,
    listen_hidden,
    listen_bias,
    lower_input,
    lower_hidden,
    lower_bias,
    upper_input,
    upper_hidden,
    upper_bias,
    key_proj,
    query_proj,
    score_vector,
    output_proj,
    output_bias,
    char_table,
):
    chips = lax.axis_size("dp")
    utts, frame_len, feat = frames.shape
    time_len = frame_len // 2
    swap = [(0, 1), (1, 0)]
    w_in, w_rec = listen_input[0], listen_hidden[0]
    units = w_rec.shape[0]
    cells = lower_hidden.shape[0]
    vocab, embed = char_table.shape
    pairs = frames.reshape(utts, time_len, 2 * feat)
    fits = (
        chips % 4 == 0
        and 4 * cells == 128 * chips
        and 4 * units == 64 * chips
        and embed == 256
        and cells == 2 * units
        and time_len == SEGMENT * STREAMS[-1][1]
        and embed + 2 * units + cells + 2 * SMALL == sum(rows for _, rows in SP_CHUNKS)
        and embed + 2 * SMALL == SP_CHUNKS[-1][1]
        and time_len == sum(count for _, count in FRAME_CHUNKS)
        and utts * time_len == sum(count for _, count in ROW_CHUNKS)
        and 2 * feat + units + 64 == 2 * sum(rows for _, rows in LI_CHUNKS)
    )
    dims = (chips // 4, 2, 2) if fits else None
    rows, factors, mine, other = listen_forward(
        dims, step_lengths, pairs, w_in, w_rec, listen_bias
    )
    if not fits:
        other = lax.ppermute(other, "role", swap)
    chars = characters[0, 0]
    previous = jnp.concatenate([jnp.zeros((1,), jnp.int32), chars[:-1]])
    ids = jnp.arange(vocab)[None, :]
    prev_onehot = (previous[:, None] == ids).astype(BF16)
    target_onehot = (chars[:, None] == ids).astype(F32)
    vec = score_vector[None]
    loss, acts, key, *kept = speller_forward(
        dims, step_lengths, char_lengths, pairs, rows, mine, other, prev_onehot, target_onehot,
        lower_input, lower_hidden, lower_bias[None], upper_input, upper_hidden, upper_bias[None],
        key_proj, query_proj, vec, output_proj.T, output_bias[None], char_table,
    )
    if fits:
        *kept, pairs_all, rows_all = kept
    grad_mine, grad_other, dp1, dp2, pack = speller_backward(
        lower_input, lower_hidden, upper_input, upper_hidden, key_proj, query_proj, vec,
        prev_onehot, acts, key, *kept,
    )
    if fits:
        pairs_all = pairs_all.reshape(chips * utts * time_len, 2 * feat)
        acts_all = lax.all_gather(acts, ("dp", "role"), tiled=True)
        frame_grad, li, sp, kq = exchange(
            dims, step_lengths, factors, grad_mine, grad_other, w_in, w_rec,
            dp1, dp2, pack, acts_all, pairs_all, rows_all,
        )
        width = 2 * feat
        sum_in, sum_rec = li[:width].astype(F32), li[width : width + units].astype(F32)
        sum_bias = li[width + units : width + units + 1].astype(F32)
        first = 2 * SMALL
        low, high = first + embed, first + embed + 2 * units
        lower = (sp[0, first:high].astype(F32), sp[0, high:].astype(F32))
        upper = (sp[1, low : low + cells].astype(F32), sp[1, low + cells :].astype(F32))
        small = sp[1, :first]
        g_key, g_query = kq[0].astype(F32), kq[1].astype(F32)
    else:
        grad_other = lax.ppermute(grad_other, "role", swap)
        pack = lax.psum(pack.astype(F32), ("role", "dp"))
        small = pack[: 2 * SMALL]
        g_key, g_query = (
            unfold(part, cells) for part in jnp.split(pack[2 * SMALL :], 2, axis=0)
        )
        pre = listen_backward(step_lengths, factors, grad_mine, grad_other, w_rec)
        flat = pre.reshape(utts * time_len, 4 * units)
        sums = mm(jnp.concatenate([pairs.reshape(flat.shape[0], 2 * feat), rows], 1).T, flat)
        sums = lax.psum(sums, "dp")
        width = 2 * feat
        sum_in, sum_rec = sums[:width], sums[width : width + units]
        sum_bias = lax.psum(jnp.sum(flat.astype(F32), 0, keepdims=True), "dp")
        grad_pairs = mm(flat, w_in.T).reshape(utts, frame_len, feat)
        frame_grad = lax.psum_scatter(grad_pairs, "role", scatter_dimension=1, tiled=True)
        cuts = [embed, embed + 2 * units, embed + 2 * units + cells]
        emb, ctx, s1, s2 = jnp.split(acts, cuts, axis=1)
        local = (
            jnp.concatenate([mm(emb.T, dp1), mm(ctx[:-1].T, dp1[1:])], 0),
            mm(s1[:-1].T, dp1[1:]),
            mm(s1.T, dp2),
            mm(s2[:-1].T, dp2[1:]),
        )
        local = lax.psum(local, ("role", "dp"))
        lower, upper = local[:2], local[2:]
    low_bias, up_bias, g_vec, g_out, g_obias, g_table = unpack(
        small, units, cells, key_proj.shape[1], vocab, embed
    )
    return (
        loss, frame_grad, sum_in[None], sum_rec[None], sum_bias,
        *lower, low_bias, *upper, up_bias,
        g_key, g_query, g_vec, g_out, g_obias, g_table,
    )


def solution(mesh):
    whole = P()
    return jax.shard_map(
        shards,
        mesh=mesh,
        in_specs=(
            P("dp", None, None),
            P("dp"),
            P("dp", "role", None),
            P("dp", "role"),
            P("role", None, None),
            P("role", None, None),
            P("role", None),
        )
        + (whole,) * 12,
        out_specs=(
            P("dp", "role"),
            P("dp", "role", None),
            P("role", None, None),
            P("role", None, None),
            P("role", None),
        )
        + (whole,) * 12,
        check_vma=False,
    )
```

```python
import functools

import jax
import jax.numpy as jnp
from jax import lax
from jax.experimental import pallas as pl
from jax.experimental.pallas import tpu as pltpu
from jax.sharding import PartitionSpec as P

F32 = jnp.float32
BF16 = jnp.bfloat16
VMEM_BYTES = 60 * 1024 * 1024


def mm(left, right):
    return jnp.dot(left, right, preferred_element_type=F32)


def mm_nt(left, right):
    return lax.dot_general(left, right, (((1,), (1,)), ((), ())), preferred_element_type=F32)


def mm_tn(left, right):
    return lax.dot_general(left, right, (((0,), (0,)), ((), ())), preferred_element_type=F32)


def sigmoid(x):
    return 0.5 * jnp.tanh(0.5 * x) + 0.5


def cell_forward(preact, cell_prev):
    n = preact.shape[-1] // 4
    in_gate = sigmoid(preact[:, :n])
    forget = sigmoid(preact[:, n : 2 * n])
    candid = jnp.tanh(preact[:, 2 * n : 3 * n])
    out_gate = sigmoid(preact[:, 3 * n :])
    cell_new = forget * cell_prev + in_gate * candid
    tanh_cell = jnp.tanh(cell_new)
    hidden = out_gate * tanh_cell
    factors = (
        candid * in_gate * (1.0 - in_gate),
        cell_prev * forget * (1.0 - forget),
        in_gate * (1.0 - candid * candid),
        tanh_cell * out_gate * (1.0 - out_gate),
        out_gate * (1.0 - tanh_cell * tanh_cell),
        forget,
    )
    return cell_new, hidden, factors


def cell_backward(factors, grad_hidden, grad_cell):
    n = factors.shape[-1] // 6
    part = lambda k: factors[:, k * n : (k + 1) * n]
    total = grad_cell + grad_hidden * part(4)
    grad_preact = jnp.concatenate(
        [total * part(0), total * part(1), total * part(2), grad_hidden * part(3)], -1
    )
    return grad_preact, total * part(5)


def remote(src, dst, send, recv, device):
    return pltpu.make_async_remote_copy(
        src_ref=src, dst_ref=dst, send_sem=send, recv_sem=recv,
        device_id=device, device_id_type=pl.DeviceIdType.MESH,
    )


def start(copies):
    for copy in copies:
        copy.start()


def wait(copies):
    for copy in copies:
        copy.wait()


class Gather:
    def __init__(self, dims, me, view, chunks, sems):
        self.dims, self.view, self.chunks = dims, view, chunks
        self.role, self.z, self.y, self.x = me
        self.send, self.recv = sems

    def device(self, z, y, x):
        _, ny, nx = self.dims
        return (self.role, (z * ny + y) * nx + x)

    def copies(self, k, which, spans, others, base):
        out = []
        for device in others:
            for span in spans:
                ref = self.view(which, k, *span)
                out.append(
                    remote(ref, ref, self.send.at[k, base], self.recv.at[k, base], device)
                )
                base += 1
        return out

    def along_x(self):
        nx = self.dims[2]
        return [self.device(self.z, self.y, (self.x + j) % nx) for j in range(1, nx)]

    def along_y(self):
        ny = self.dims[1]
        return [self.device(self.z, (self.y + j) % ny, self.x) for j in range(1, ny)]

    def first(self, k):
        nz, ny, nx = self.dims
        slot = (self.y * nx + self.x) * nz + self.z
        others = [self.device((self.z + j) % nz, self.y, self.x) for j in range(1, nz)]
        return self.copies(k, None, [(slot, 1)], others, 0)

    def second(self, k):
        nz, ny, nx = self.dims
        column = ((self.y * nx + self.x) * nz, nz)
        base = nz - 1
        to_x = self.copies(k, 0, [column], self.along_x(), base)
        return to_x + self.copies(k, 1, [column], self.along_y(), base + nx - 1)

    def third(self, k):
        nz, ny, nx = self.dims
        base = nz - 1 + nx - 1 + ny - 1
        to_y = self.copies(k, 0, [(self.y * nx * nz, nx * nz)], self.along_y(), base)
        spans = [((b * nx + self.x) * nz, nz) for b in range(ny)]
        return to_y + self.copies(k, 1, spans, self.along_x(), base + ny - 1)

    @staticmethod
    def semaphores(dims, chunks):
        nz, ny, nx = dims
        count = nz - 1 + 2 * (nx - 1) + 2 * (ny - 1) + (nx - 1) * (ny - 1)
        return pltpu.SemaphoreType.DMA((len(chunks), count))


PART = 64
LISTEN_GROUPS = 6
LISTEN_CHUNKS = ((0, 0, 32), (0, 32, 32))
LISTEN_EVENTS = (
    ((), ((0, 0), (0, 1))),
    (((0, 0),), ((1, 0),)),
    (((1, 0), (0, 1)), ((2, 0), (1, 1))),
    (((2, 0),), ((3, 0),)),
    (((1, 1),), ((2, 1),)),
    (((2, 1),), ((3, 1),)),
    ((), ()),
)
SPELL_GROUPS = 18
SPELL_CHUNKS = ((0, 0, PART), (1, 0, PART))
SPELL_EVENTS = (
    ((), ((0, 0), (0, 1))),
    ((), ()),
    (((0, 0),), ((1, 0), (0, 2))),
    (((0, 1),), ((1, 1), (0, 3))),
    (((1, 0),), ((2, 0),)),
    (((1, 1), (0, 2)), ((2, 1), (1, 2), (0, 4))),
    (((2, 0),), ()),
    (((0, 3), (2, 1)), ((1, 3),)),
    (((1, 2),), ((2, 2),)),
    (((1, 3),), ((2, 3),)),
    (((0, 4),), ((1, 4),)),
    (((2, 2),), ()),
    ((), ()),
    (((2, 3),), ((3, 3),)),
    (((1, 4),), ((2, 4),)),
    ((), ()),
    ((), ()),
    (((2, 4),), ((3, 4),)),
    ((), ()),
)


class Gathers:
    def __init__(self, dims, role, dp, events, frames, chunks, states, sems):
        nz, ny, nx = dims
        me = (role, dp // (ny * nx), (dp // nx) % ny, dp % nx)
        self.twin = (1 - role, dp)
        self.role, self.frames, self.chunks, self.events = role, frames, chunks, events
        send, recv, self.last_send, self.last_recv = sems[:4]
        self.slot = (me[2] * nx + me[3]) * nz + me[1]

        def half(first, count, which):
            if which is not None:
                first, count = first + which * count // 2, count // 2
            return pl.ds(first, count)

        def view_frames(which, k, first, count):
            part, *rows = chunks[k]
            return frames.at[part, role, pl.ds(first, count), half(*rows, which)]

        self.two = Gather(dims, me, view_frames, chunks, (send, recv))
        self.lead = 0
        if states is not None:
            self.lead = states.shape[0]

            def view_states(which, k, first, count):
                rows = half(0, states.shape[3], which)
                return states.at[k, :, pl.ds(first, count), rows]

            self.one = Gather(dims, me, view_states, range(self.lead), sems[4:])
        g = self.two
        to_z = [g.device((g.z + j) % nz, g.y, g.x) for j in range(1, nz)]
        self.partners = to_z + g.along_x() + g.along_y() + [self.twin]

    def greet(self):
        barrier = pltpu.get_barrier_semaphore()
        for device in self.partners:
            pl.semaphore_signal(
                barrier, inc=1, device_id=device, device_id_type=pl.DeviceIdType.MESH
            )

    def phase(self, n, c):
        if n == 3:
            k = c - self.lead
            part, *rows = self.chunks[k]
            ref = self.frames.at[part, self.role, :, pl.ds(*rows)]
            return [remote(ref, ref, self.last_send.at[k], self.last_recv.at[k], self.twin)]
        gather, k = (self.one, c) if c < self.lead else (self.two, c - self.lead)
        return (gather.first, gather.second, gather.third)[n](k)

    def begin(self):
        pl.semaphore_wait(pltpu.get_barrier_semaphore(), len(self.partners))

    def look(self, group):
        ended, begun = self.events[group]
        for n, c in ended:
            wait(self.phase(n, c))
        for n, c in begun:
            start(self.phase(n, c))

    def finish(self):
        for k in range(len(self.chunks)):
            wait(self.phase(3, self.lead + k))

    @staticmethod
    def scratch(dims, chunks, states):
        dma = pltpu.SemaphoreType.DMA
        sems = [Gather.semaphores(dims, chunks)] * 2 + [dma((len(chunks),))] * 2
        if states:
            sems += [Gather.semaphores(dims, range(states))] * 2
        return sems


def listen_forward_kernel(
    dims, lengths, frames, w_in, w_rec, bias,
    pairs, rows_out, factors_out, mine_out, other_out, *rest
):
    role = lax.axis_index("role")
    if dims is not None:
        pairs_all, proj, emit, hprev, to_other, cross, *sems = rest
        gather = Gathers(
            dims, role, lax.axis_index("dp"), LISTEN_EVENTS, pairs_all, LISTEN_CHUNKS, None, sems
        )
        gather.greet()
    else:
        proj, emit, hprev = rest
    utts, time_len, width4 = proj.shape
    units = width4 // 4
    feat = frames.shape[-1]
    rows = lax.broadcasted_iota(jnp.int32, (time_len, 2 * time_len), 0)
    cols = lax.broadcasted_iota(jnp.int32, (time_len, 2 * time_len), 1)
    for half in range(2):
        pick = jnp.where(cols == 2 * rows + half, 1.0, 0.0).astype(BF16)
        for u in range(utts):
            pairs[u, :, half * feat : (half + 1) * feat] = mm(pick, frames[u]).astype(BF16)
    if dims is not None:
        place = pltpu.make_async_copy(
            pairs.at[role, pl.ds(0, PART)], pairs_all.at[0, role, gather.slot], cross.at[2]
        )
        place.start()
    bias_row = bias[...].astype(F32)
    for u in range(utts):
        proj[u] = mm(pairs[u], w_in[...]) + bias_row
    if dims is not None:
        place.wait()
        gather.begin()
    first = lax.broadcasted_iota(jnp.int32, (8, 1), 0) == 0
    row_lengths = jnp.where(first, lengths[0], lengths[1])

    def step(s, carry):
        hidden, cell = carry
        t = jnp.where(role == 1, time_len - 1 - s, s)
        at = pl.ds(t, 1)
        pre_in = jnp.where(first, proj[0, at, :], proj[1, at, :])
        low = hidden.astype(BF16)
        cell_new, hidden_new, factors = cell_forward(pre_in + mm(low, w_rec[...]), cell)
        live = t < row_lengths
        hidden_next = jnp.where(live, hidden_new, hidden)
        cell_next = jnp.where(live, cell_new, cell)
        emitted = jnp.where(live, hidden_new, 0.0)
        for u in range(2):
            for k in range(6):
                factors_out[u, at, k * units : (k + 1) * units] = factors[k][u : u + 1]
            hprev[u, at, :] = hidden[u : u + 1]
            emit[u, at, :] = emitted[u : u + 1]
        return hidden_next, cell_next

    zero = jnp.zeros((8, units), F32)
    carry = (zero, zero)
    if dims is None:
        lax.fori_loop(0, time_len, step, carry)
    else:
        count = time_len // LISTEN_GROUPS
        for group in range(LISTEN_GROUPS):
            gather.look(group)
            carry = lax.fori_loop(group * count, (group + 1) * count, step, carry)
    mine_out[...] = emit[role].astype(BF16)
    if dims is None:
        other_out[...] = emit[1 - role].astype(BF16)
    else:
        to_other[...] = emit[1 - role].astype(BF16)
        crossing = remote(to_other, other_out, cross.at[0], cross.at[1], gather.twin)
        crossing.start()
        gather.look(LISTEN_GROUPS)
    for u in range(utts):
        own = slice(u * time_len, (u + 1) * time_len)
        rows_out[own, :] = hprev[u].astype(BF16)
    if dims is not None:
        crossing.wait()
        gather.finish()


def listen_forward(dims, lengths, frames, w_in, w_rec, bias):
    utts, time_len, width = frames.shape[0], frames.shape[1] // 2, 2 * frames.shape[2]
    units = w_rec.shape[0]
    vmem = pl.BlockSpec(memory_space=pltpu.VMEM)
    shape = jax.ShapeDtypeStruct
    outs = [
        shape((utts, time_len, width), BF16),
        shape((utts * time_len, units), BF16),
        shape((utts, time_len, 6 * units), F32),
        shape((time_len, units), BF16),
        shape((time_len, units), BF16),
    ]
    out_specs = [vmem] * 5
    scratch = [
        pltpu.VMEM((utts, time_len, 4 * units), F32),
        pltpu.VMEM((utts, time_len, units), F32),
        pltpu.VMEM((utts, time_len, units), F32),
    ]
    params = dict(vmem_limit_bytes=VMEM_BYTES)
    if dims is not None:
        chips = dims[0] * dims[1] * dims[2]
        outs.append(shape((1, 2, chips, PART, width), BF16))
        out_specs.append(pl.BlockSpec(memory_space=pl.ANY))
        scratch += [pltpu.VMEM((time_len, units), BF16), pltpu.SemaphoreType.DMA((3,))]
        scratch += Gathers.scratch(dims, LISTEN_CHUNKS, 0)
        params.update(collective_id=1, has_side_effects=True)
    return pl.pallas_call(
        functools.partial(listen_forward_kernel, dims),
        out_shape=outs,
        in_specs=[pl.BlockSpec(memory_space=pltpu.SMEM)] + [vmem] * 4,
        out_specs=out_specs,
        scratch_shapes=scratch,
        compiler_params=pltpu.CompilerParams(**params),
    )(lengths, frames, w_in, w_rec, bias)


def speller_forward_kernel(
    dims, lengths, text_lens, chars, pairs, states,
    mine, other,
    w_lin, w_lhid, b_low, w_uin, w_uhid, b_up, w_key, w_query, vec, w_out, b_out, table,
    loss, prev_onehot, acts, key, keys_proj, key_low, fact1, fact2, q_rows, w_cols, feat_rows, dw_cols,
    logit_grad_out, *rest
):
    role = lax.axis_index("role")
    gather = None
    if dims is not None:
        pairs_all, states_all, emb_proj, s1_rows, s2_rows, hot, stage, own_sem, *sems = rest
        gather = Gathers(
            dims, role, lax.axis_index("dp"), SPELL_EVENTS, pairs_all, SPELL_CHUNKS, states_all, sems
        )
        gather.greet()
        load = pltpu.make_async_copy(
            pairs.at[role, pl.ds(PART, stage.shape[0])], stage, own_sem.at[0]
        )
        load.start()
        parts, utts = states_all.shape[:2]
        place = [
            pltpu.make_async_copy(
                states.at[pl.ds((u * parts + part) * PART, PART)],
                states_all.at[part, u, gather.slot],
                own_sem.at[1 + u * parts + part],
            )
            for u in range(utts)
            for part in range(parts)
        ]
        start(place)
        staged = [
            pltpu.make_async_copy(
                stage.at[pl.ds(part * PART, PART)],
                pairs_all.at[part, role, gather.slot],
                own_sem.at[1 + len(place) + part],
            )
            for part in range(pairs_all.shape[0])
        ]
    else:
        emb_proj, s1_rows, s2_rows, hot = rest
    time_len, units = mine.shape
    steps = emb_proj.shape[0]
    cells = w_lhid.shape[0]
    embed = table.shape[1]
    length = lengths[role]
    text_len = text_lens[0, 0]

    key[:, :units] = jnp.where(role == 0, mine[...], other[...])
    key[:, units:] = jnp.where(role == 0, other[...], mine[...])
    keys_proj[...] = mm(key[...], w_key[...])
    if gather is not None:
        load.wait()
        start(staged)
    key_low[...] = mm(key[...], w_lin[embed:, :])
    ids = lax.broadcasted_iota(jnp.int32, (1, hot.shape[2]), 1)

    def mark(i, previous):
        here = chars[0, 0, i]
        hot[0, pl.ds(i, 1), :] = jnp.where(ids == previous, 1.0, 0.0)
        hot[1, pl.ds(i, 1), :] = jnp.where(ids == here, 1.0, 0.0)
        return here

    lax.fori_loop(0, steps, mark, 0)
    prev_onehot[...] = hot[0].astype(BF16)
    emb = mm(prev_onehot[...], table[...]).astype(BF16)
    emb_proj[...] = mm(emb, w_lin[:embed, :]) + b_low[...].astype(F32)[None]
    bias_up = b_up[...].astype(F32)[None]
    vec_row = vec[...].astype(F32)[None]
    frame_ok = lax.broadcasted_iota(jnp.int32, (time_len, 1), 0) < length
    lane = lax.broadcasted_iota(jnp.int32, w_cols.shape, 1)
    w_cols[...] = jnp.zeros_like(w_cols)
    if gather is not None:
        wait(place)
        wait(staged)
        gather.begin()

    def forward_step(i, carry):
        cell1, cell2, hid1, hid2, ctx_low = carry
        at = pl.ds(i, 1)
        pre1 = emb_proj[at, :] + hid1 + ctx_low
        cell1, s1, factors = cell_forward(pre1, cell1)
        for k in range(6):
            fact1[at, k * cells : (k + 1) * cells] = factors[k]
        s1_rows[at, :] = s1
        s1_low = s1.astype(BF16)
        pre2 = hid2 + bias_up + mm(s1_low, w_uin[...])
        hid1 = mm(s1_low, w_lhid[...])
        cell2, s2, factors = cell_forward(pre2, cell2)
        for k in range(6):
            fact2[at, k * cells : (k + 1) * cells] = factors[k]
        s2_rows[at, :] = s2
        s2_low = s2.astype(BF16)
        query = mm(s2_low, w_query[...])
        hid2 = mm(s2_low, w_uhid[...])
        q_rows[at, :] = query
        part = None
        for j in range(query.shape[1] // 128):
            cut = slice(j * 128, (j + 1) * 128)
            term = jnp.tanh(keys_proj[:, cut] + query[:, cut]) * vec_row[:, cut]
            part = term if part is None else part + term
        scores = jnp.sum(part, -1, keepdims=True)
        scores = jnp.where(frame_ok, scores, -1000000000.0)
        scores = scores - jnp.max(scores, 0, keepdims=True)
        expf = jnp.where(frame_ok, jnp.exp(scores), 0.0)
        rinv = 1.0 / jnp.sum(expf, 0, keepdims=True)
        w_cols[...] = jnp.where(lane == i, expf * rinv, w_cols[...])
        ctx_low = jnp.concatenate(
            [
                jnp.sum(expf * key_low[:, j * 128 : (j + 1) * 128], 0, keepdims=True)
                for j in range(key_low.shape[1] // 128)
            ],
            1,
        )
        return cell1, cell2, hid1, hid2, ctx_low * rinv

    zero = jnp.zeros((1, cells), F32)
    wide = jnp.zeros((1, 4 * cells), F32)
    carry = (zero, zero, wide, wide, wide)
    if gather is None:
        lax.fori_loop(0, steps, forward_step, carry)
    else:
        count = steps // SPELL_GROUPS
        for group in range(SPELL_GROUPS):
            gather.look(group)
            carry = lax.fori_loop(group * count, (group + 1) * count, forward_step, carry)
        gather.look(SPELL_GROUPS)

    w_low = jnp.transpose(w_cols[...])[:steps].astype(BF16)
    ctx = mm(w_low, key[...]).astype(BF16)
    s2_low = s2_rows[...].astype(BF16)
    logits = mm_nt(s2_low, w_out[:, :cells]) + mm_nt(ctx, w_out[:, cells:]) + b_out[...].astype(F32)[None]
    top = jnp.max(logits, -1, keepdims=True)
    log_total = top + jnp.log(jnp.sum(jnp.exp(logits - top), -1, keepdims=True))
    target = hot[1]
    cross = log_total - jnp.sum(logits * target, -1, keepdims=True)
    text = text_len.astype(F32)
    alive = lax.broadcasted_iota(jnp.int32, (steps, 1), 0) < text_len
    loss[...] = jnp.sum(jnp.where(alive, cross, 0.0), 0, keepdims=True) / text
    scale = jnp.where(alive, 1.0 / text, 0.0)
    logit_grad = (scale * (jnp.exp(logits - log_total) - target)).astype(BF16)
    logit_grad_out[...] = logit_grad
    feat_rows[...] = mm(logit_grad, w_out[...])
    dw_cols[...] = jnp.zeros_like(dw_cols)
    dw_cols[:, :steps] = mm_nt(key[...], feat_rows[:, cells:].astype(BF16))
    acts[steps:, :] = jnp.zeros((acts.shape[0] - steps, acts.shape[1]), BF16)
    acts[:steps, :embed] = emb
    acts[:steps, embed : embed + 2 * units] = ctx
    acts[:steps, embed + 2 * units : embed + 2 * units + cells] = s1_rows[...].astype(BF16)
    acts[:steps, embed + 2 * units + cells :] = s2_low
    if gather is not None:
        gather.finish()


def speller_forward(
    dims, lengths, text_lens, chars, pairs, states, mine, other,
    w_lin, w_lhid, b_low, w_uin, w_uhid, b_up, w_key, w_query, vec, w_out, b_out, table,
):
    time_len, units = mine.shape
    steps, vocab = chars.shape[2], table.shape[0]
    cells = w_lhid.shape[0]
    att = w_key.shape[1]
    embed = table.shape[1]
    pad_steps = -(-steps // 16) * 16
    vmem = pl.BlockSpec(memory_space=pltpu.VMEM)
    smem = pl.BlockSpec(memory_space=pltpu.SMEM)
    shape = jax.ShapeDtypeStruct
    outs = [
        shape((1, 1), F32),
        shape((steps, vocab), BF16),
        shape((pad_steps, embed + 2 * units + 2 * cells), BF16),
        shape((time_len, 2 * units), BF16),
        shape((time_len, att), F32),
        shape((time_len, 4 * cells), F32),
        shape((steps, 6 * cells), F32),
        shape((steps, 6 * cells), F32),
        shape((steps, att), F32),
        shape((time_len, -(-steps // 128) * 128), F32),
        shape((steps, w_out.shape[1]), F32),
        shape((time_len, -(-steps // 128) * 128), F32),
        shape((steps, vocab), BF16),
    ]
    out_specs = [vmem] * len(outs)
    scratch = [
        pltpu.VMEM((steps, 4 * cells), F32),
        pltpu.VMEM((steps, cells), F32),
        pltpu.VMEM((steps, cells), F32),
        pltpu.VMEM((2, steps, vocab), F32),
    ]
    params = dict(vmem_limit_bytes=VMEM_BYTES)
    if dims is not None:
        chips = dims[0] * dims[1] * dims[2]
        dma = pltpu.SemaphoreType.DMA
        utts, _, width = pairs.shape
        parts = time_len // PART
        high = parts - 1
        outs.append(shape((high, utts, chips, PART, width), BF16))
        outs.append(shape((parts, utts, chips, PART, units), BF16))
        out_specs += [pl.BlockSpec(memory_space=pl.ANY)] * 2
        scratch += [pltpu.VMEM((high * PART, width), BF16), dma((1 + high + utts * parts,))]
        scratch += Gathers.scratch(dims, SPELL_CHUNKS, parts)
        params.update(collective_id=2, has_side_effects=True)
    return pl.pallas_call(
        functools.partial(speller_forward_kernel, dims),
        out_shape=outs,
        in_specs=[smem] * 3 + [pl.BlockSpec(memory_space=pl.ANY)] + [vmem] * 15,
        out_specs=out_specs,
        scratch_shapes=scratch,
        compiler_params=pltpu.CompilerParams(**params),
    )(
        lengths, text_lens, chars, pairs, states, mine, other,
        w_lin, w_lhid, b_low, w_uin, w_uhid, b_up, w_key, w_query, vec, w_out, b_out, table,
    )


SMALL = 32


def shift_up(rows):
    count = rows.shape[0]
    rolled = pltpu.roll(rows, count - 1, 0)
    at = lax.broadcasted_iota(jnp.int32, rows.shape, 0)
    return jnp.where(at == count - 1, 0.0, rolled)


def speller_backward_kernel(
    w_lin, w_lhid, w_uin, w_uhid, w_key, w_query, vec, prev_onehot,
    acts, key, keys_proj, key_low, fact1, fact2, q_rows, w_cols, feat_rows, dw_cols, logit_grad,
    grad_mine, grad_other, dp1_out, dp2_out, pack,
    dp1_rows, dp2_rows, dq_rows, keys_acc, vec_acc, small, t_lhid, t_uin, t_uhid, t_query,
):
    role = lax.axis_index("role")
    time_len, att = keys_proj.shape
    steps, vocab = logit_grad.shape
    units = key.shape[1] // 2
    cells = w_lhid.shape[0]
    embed = acts.shape[1] - 2 * units - 2 * cells
    vec_row = vec[...].astype(F32)[None]
    zero = jnp.zeros((1, cells), F32)
    wide = jnp.zeros((1, 4 * cells), BF16)
    keys_acc[...] = jnp.zeros_like(keys_acc)
    vec_acc[...] = jnp.zeros_like(vec_acc)
    t_lhid[...] = w_lhid[...].T
    t_uin[...] = w_uin[...].T
    t_uhid[...] = w_uhid[...].T
    t_query[...] = w_query[...].T
    lane = lax.broadcasted_iota(jnp.int32, w_cols.shape, 1)

    def backward_step(s, carry):
        dp1, dp2, dcell1, dcell2 = carry
        i = steps - 1 - s
        at = pl.ds(i, 1)
        query = q_rows[at, :]
        dp1_row = dp1.astype(F32)
        here = lane == i
        part = jnp.where(here, dw_cols[...], 0.0)
        for j in range(key_low.shape[1] // 128):
            cut = slice(j * 128, (j + 1) * 128)
            part = part + dp1_row[:, cut] * key_low[:, cut]
        dweights = jnp.sum(part, -1, keepdims=True)
        weights = jnp.sum(jnp.where(here, w_cols[...], 0.0), -1, keepdims=True)
        back2 = mm(dp2, t_uhid[...])
        back1 = mm(dp1, t_lhid[...])
        shared = weights * dweights
        dscore = shared - weights * jnp.sum(shared, 0, keepdims=True)
        sums = []
        for j in range(query.shape[1] // 128):
            cut = slice(j * 128, (j + 1) * 128)
            energy = jnp.tanh(keys_proj[:, cut] + query[:, cut])
            moved = dscore * (1.0 - energy * energy)
            keys_acc[:, cut] += moved
            sums.append(jnp.sum(moved, 0, keepdims=True))
            vec_acc[:, cut] += jnp.sum((dscore * energy).reshape(time_len // 8, 8, 128), 0)
        dquery = (jnp.concatenate(sums, 1) * vec_row).astype(BF16)
        dq_rows[at, :] = dquery.astype(F32)
        ds2 = back2 + feat_rows[at, :cells] + mm(dquery, t_query[...])
        pre2, dcell2 = cell_backward(fact2[at, :], ds2, dcell2)
        dp2_rows[at, :] = pre2
        dp2 = pre2.astype(BF16)
        ds1 = back1 + mm(dp2, t_uin[...])
        pre1, dcell1 = cell_backward(fact1[at, :], ds1, dcell1)
        dp1_rows[at, :] = pre1
        return pre1.astype(BF16), dp2, dcell1, dcell2

    lax.fori_loop(0, steps, backward_step, (wide, wide, zero, zero))

    dp1 = dp1_rows[...].astype(BF16)
    dp2 = dp2_rows[...].astype(BF16)
    dq = dq_rows[...].astype(BF16)
    extra = jnp.zeros((dp1_out.shape[0] - steps, 4 * cells), BF16)
    dp1_out[steps:, :] = extra
    dp2_out[steps:, :] = extra
    dp1_out[:steps, :] = dp1
    dp2_out[:steps, :] = dp2
    next_dp1 = shift_up(dp1.astype(F32)).astype(BF16)
    ctx_grad = (feat_rows[:, cells:] + mm_nt(next_dp1, w_lin[embed:, :])).astype(BF16)
    keys_grad = (keys_acc[...] * vec_row).astype(BF16)
    w_low = w_cols[...].astype(BF16)[:, :steps]
    key_grad = mm_nt(keys_grad, w_key[...]) + mm(w_low, ctx_grad)
    key_grad = key_grad.astype(BF16)
    grad_mine[...] = jnp.where(role == 0, key_grad[:, :units], key_grad[:, units:])
    grad_other[...] = jnp.where(role == 0, key_grad[:, units:], key_grad[:, :units])
    ctx = acts[:steps, embed : embed + 2 * units]
    s2 = acts[:steps, embed + 2 * units + cells :]
    wide = pack.shape[1]
    deep = 2 * units * att // wide
    g_key = mm_tn(key[...], keys_grad)
    g_query = mm_tn(s2, dq)
    for k in range(wide // att):
        cut = slice(k * att, (k + 1) * att)
        first = 2 * SMALL
        pack[first : first + deep, cut] = g_key[k * deep : (k + 1) * deep].astype(BF16)
        first += deep
        pack[first : first + deep, cut] = g_query[k * deep : (k + 1) * deep].astype(BF16)
    emb_grad = mm_nt(dp1, w_lin[:embed, :])
    hot = prev_onehot[...]
    total = None
    for _ in range(3):
        low = emb_grad.astype(BF16)
        emb_grad = emb_grad - low.astype(F32)
        total = mm_tn(hot, low) if total is None else total + mm_tn(hot, low)
    small[...] = jnp.zeros_like(small)
    small[:vocab, :cells] = mm_tn(logit_grad[...], s2)
    small[:vocab, cells : cells + 2 * units] = mm_tn(logit_grad[...], ctx)
    base = cells + 2 * units
    small[:vocab, base : base + embed] = total
    base += embed
    small[0:1, base : base + att] = jnp.sum(vec_acc[...], 0, keepdims=True)
    small[1:2, base : base + vocab] = jnp.sum(logit_grad[...].astype(F32), 0, keepdims=True)
    low_bias = jnp.sum(dp1.astype(F32), 0, keepdims=True)
    up_bias = jnp.sum(dp2.astype(F32), 0, keepdims=True)
    for k in range(4):
        small[2 + k : 3 + k, base : base + cells] = low_bias[:, k * cells : (k + 1) * cells]
        small[6 + k : 7 + k, base : base + cells] = up_bias[:, k * cells : (k + 1) * cells]
    high = small[...].astype(BF16)
    pack[:SMALL, :] = high
    pack[SMALL : 2 * SMALL, :] = (small[...] - high.astype(F32)).astype(BF16)


def speller_backward(
    w_lin, w_lhid, w_uin, w_uhid, w_key, w_query, vec, prev_onehot,
    acts, key, keys_proj, key_low, fact1, fact2, q_rows, w_cols, feat_rows, dw_cols, logit_grad,
):
    time_len, att = keys_proj.shape
    steps, vocab = logit_grad.shape
    units = key.shape[1] // 2
    cells = w_lhid.shape[0]
    pad_steps = acts.shape[0]
    vmem = pl.BlockSpec(memory_space=pltpu.VMEM)
    shape = jax.ShapeDtypeStruct
    outs = [
        shape((time_len, units), BF16),
        shape((time_len, units), BF16),
        shape((pad_steps, 4 * cells), BF16),
        shape((pad_steps, 4 * cells), BF16),
        shape(((2 * units + cells) * att // (4 * cells) + 2 * SMALL, 4 * cells), BF16),
    ]
    out_specs = [vmem] * 5
    scratch = [
        pltpu.VMEM((steps, 4 * cells), F32),
        pltpu.VMEM((steps, 4 * cells), F32),
        pltpu.VMEM((steps, att), F32),
        pltpu.VMEM((time_len, att), F32),
        pltpu.VMEM((8, att), F32),
        pltpu.VMEM((SMALL, 4 * cells), F32),
        pltpu.VMEM((4 * cells, cells), BF16),
        pltpu.VMEM((4 * cells, cells), BF16),
        pltpu.VMEM((4 * cells, cells), BF16),
        pltpu.VMEM((att, cells), BF16),
    ]
    return pl.pallas_call(
        speller_backward_kernel,
        out_shape=outs,
        in_specs=[vmem] * 19,
        out_specs=out_specs,
        scratch_shapes=scratch,
        compiler_params=pltpu.CompilerParams(vmem_limit_bytes=VMEM_BYTES),
    )(
        w_lin, w_lhid, w_uin, w_uhid, w_key, w_query, vec, prev_onehot,
        acts, key, keys_proj, key_low, fact1, fact2, q_rows, w_cols, feat_rows, dw_cols, logit_grad,
    )


def unfold(folded, width):
    deep = folded.shape[0]
    return folded.reshape(deep, -1, width).swapaxes(0, 1).reshape(-1, width)


def unpack(small, units, cells, att, vocab, embed):
    small = small[:SMALL].astype(F32) + small[SMALL:].astype(F32)
    base = cells + 2 * units
    g_out = small[:vocab, :base].T
    g_table = small[:vocab, base : base + embed]
    base += embed
    low_bias = small[2:6, base : base + cells].reshape(-1)
    up_bias = small[6:10, base : base + cells].reshape(-1)
    g_vec = small[0, base : base + att]
    g_obias = small[1, base : base + vocab]
    return low_bias, up_bias, g_vec, g_out, g_obias, g_table


def backward_steps(role, lengths, factors, grad_out, w_rec, grad_pre, first_step, count, carry):
    time_len = factors.shape[1]
    first = lax.broadcasted_iota(jnp.int32, (8, 1), 0) == 0
    row_lengths = jnp.where(first, lengths[0], lengths[1])

    def step(s, carry):
        grad_hidden, grad_cell = carry
        t = jnp.where(role == 1, s, time_len - 1 - s)
        at = pl.ds(t, 1)
        live = t < row_lengths
        fact = jnp.where(first, factors[0, at, :], factors[1, at, :])
        arrived = jnp.where(first, grad_out[0, at, :], grad_out[1, at, :])
        fact = jnp.where(live, fact, 0.0)
        total = grad_hidden + jnp.where(live, arrived, 0.0)
        pre, cell_back = cell_backward(fact, total, grad_cell)
        for u in range(2):
            grad_pre[u, at, :] = pre[u : u + 1]
        back = mm_nt(pre.astype(BF16), w_rec[...])
        return jnp.where(live, back, total), jnp.where(live, cell_back, grad_cell)

    return lax.fori_loop(first_step, first_step + count, step, carry)


def listen_backward_kernel(
    lengths, factors, grad_mine, grad_other, w_rec, pre_out, grad_pre, grad_out
):
    role = lax.axis_index("role")
    grad_out[role] = grad_mine[...].astype(F32)
    grad_out[1 - role] = grad_other[...].astype(F32)
    zero = jnp.zeros((8, w_rec.shape[0]), F32)
    backward_steps(
        role, lengths, factors, grad_out, w_rec, grad_pre, 0, factors.shape[1], (zero, zero)
    )
    pre_out[...] = grad_pre[...].astype(BF16)


def listen_backward(lengths, factors, grad_mine, grad_other, w_rec):
    utts, time_len, _ = factors.shape
    units = w_rec.shape[0]
    vmem = pl.BlockSpec(memory_space=pltpu.VMEM)
    return pl.pallas_call(
        listen_backward_kernel,
        out_shape=jax.ShapeDtypeStruct((utts, time_len, 4 * units), BF16),
        in_specs=[pl.BlockSpec(memory_space=pltpu.SMEM)] + [vmem] * 4,
        out_specs=vmem,
        scratch_shapes=[
            pltpu.VMEM((utts, time_len, 4 * units), F32),
            pltpu.VMEM((utts, time_len, units), F32),
        ],
        compiler_params=pltpu.CompilerParams(vmem_limit_bytes=VMEM_BYTES),
    )(lengths, factors, grad_mine, grad_other, w_rec)


SEGMENT = 32
STREAMS = ((0, 3), (3, 5), (5, 6))


SP_CHUNKS = ((320, 352), (672, 352), (1024, 320), (0, 320))
LI_CHUNKS = ((0, 352), (352, 320))


def exchange_kernel(
    dims,
    lengths, factors, grad_mine, grad_other, w_in, w_rec, dp1, dp2, pack, acts_all, pairs_low, pairs_high, rows_all,
    frames_out, li_out, sp_out,
    grad_pre, grad_out, acts_buf, pairs_buf, rows_buf, dp_pair, got, got_t, prod, column,
    li_send, li_got, li_rows, li_acc, li_all, fr_send, fr_got, weave,
    pk_pair, pk_x, pk_xsum, pk_y, pk_ysum, pk_z,
    local_sem, chip_send, chip_recv, aa_send, aa_recv, li_aa_send, li_aa_recv,
    sp_send, sp_recv, li_ag_send, li_ag_recv, pk_send, pk_recv, far_grad,
):
    nz, ny, nx = dims
    chips = nz * ny * nx
    role = lax.axis_index("role")
    dp = lax.axis_index("dp")
    z, y, x = dp // (ny * nx), (dp // nx) % ny, dp % nx
    utts, time_len, width = grad_pre.shape
    units = w_rec.shape[0]
    cells = dp1.shape[1] // 4
    half_time = time_len // 2
    pads = dp1.shape[0]
    twin = (1 - role, dp)

    def slot_of(chip):
        return (((chip // nx) % ny) * nx + chip % nx) * nz + chip // (ny * nx)

    slot = slot_of(dp)
    lanes = pl.ds(pl.multiple_of(slot * 128, 128), 128)

    barrier = pltpu.get_barrier_semaphore()
    mesh = pl.DeviceIdType.MESH

    def greet(k, _):
        pl.semaphore_signal(barrier, inc=1, device_id=(role, (dp + k) % chips), device_id_type=mesh)
        return 0

    pl.semaphore_signal(barrier, inc=1, device_id=twin, device_id_type=mesh)
    lax.fori_loop(1, chips, greet, 0)
    load_acts = pltpu.make_async_copy(
        acts_all.at[:, pl.ds(pl.multiple_of(role * cells, 128), acts_buf.shape[1])],
        acts_buf, local_sem.at[0],
    )
    load_acts.start()
    load_rows = [pltpu.make_async_copy(rows_all, rows_buf.at[:, pl.ds(0, units)], local_sem.at[1])]
    rows_buf[:, units:] = jnp.ones((rows_buf.shape[0], rows_buf.shape[1] - units), BF16)
    start(load_rows)
    split = pairs_low.shape[0]
    load_pairs = [
        pltpu.make_async_copy(pairs_low, pairs_buf.at[pl.ds(0, split)], local_sem.at[4]),
        pltpu.make_async_copy(pairs_high, pairs_buf.at[pl.ds(split, pairs_high.shape[0])], local_sem.at[5]),
    ]
    start(load_pairs)
    dp_pair[role] = jnp.where(role == 0, dp1[...], dp2[...])
    dp_pair[2] = jnp.where(role == 0, dp2[...], dp1[...])
    grad_out[role] = grad_mine[...].astype(F32)
    pl.semaphore_wait(barrier, chips)
    last = chip_send.shape[0] - 1
    crossing = remote(grad_other, far_grad, chip_send.at[last], chip_recv.at[last], twin)
    crossing.start()

    to_twin = remote(dp_pair.at[2], dp_pair.at[role], chip_send.at[0], chip_recv.at[0], twin)
    to_twin.start()
    pack_twin = remote(pack, pk_pair, pk_send.at[0], pk_recv.at[0], twin)

    @pl.when(role == 0)
    def _():
        pack_twin.start()

    to_twin.wait()

    def block(k):
        chip = (dp + k) % chips
        cut = pl.ds(pl.multiple_of(slot_of(chip) * 128, 128), 128)
        return remote(
            dp_pair.at[pl.ds(0, 2), :, cut], got.at[dp],
            aa_send.at[k - 1], aa_recv.at[k - 1], (role, chip),
        )

    lax.fori_loop(1, chips, lambda k, _: (block(k).start(), 0)[1], 0)
    own_block = pltpu.make_async_copy(
        dp_pair.at[pl.ds(0, 2), :, lanes], got.at[dp], local_sem.at[2]
    )
    own_block.start()

    def rounded(total):
        value = total[:SMALL] + total[SMALL : 2 * SMALL]
        high = value.astype(BF16)
        low = (value - high.astype(F32)).astype(BF16)
        return jnp.concatenate([high, low, total[2 * SMALL :].astype(BF16)], 0)

    chip_at = lambda a, b, c: (role, (a * ny + b) * nx + c)
    x_other, y_other = (x + 1) % nx, (y + 1) % ny
    column_wide = nz * 128

    def pack_x(b):
        first = pl.multiple_of((b * nx + x_other) * column_wide, 128)
        return remote(
            pk_pair.at[:, pl.ds(first, column_wide)], pk_x.at[b],
            pk_send.at[1 + b], pk_recv.at[1 + b], chip_at(z, y, x_other),
        )

    pack_y = remote(
        pk_xsum.at[y_other], pk_y, pk_send.at[1 + ny], pk_recv.at[1 + ny], chip_at(z, y_other, x)
    )

    def pack_z(j):
        to = (z + j) % nz
        return remote(
            pk_ysum.at[:, pl.ds(pl.multiple_of(to * 128, 128), 128)], pk_z.at[z],
            pk_send.at[1 + ny + j], pk_recv.at[1 + ny + j], chip_at(to, y, x),
        )

    @pl.when(role == 0)
    def _():
        pack_twin.wait_send()

    @pl.when(role == 1)
    def _():
        pack_twin.wait_recv()

        def add(b, _):
            cut = pl.ds(pl.multiple_of(b * 128, 128), 128)
            total = pk_pair[:, cut].astype(F32) + pack[:, cut].astype(F32)
            pk_pair[:, cut] = rounded(total)
            return 0

        lax.fori_loop(0, pack.shape[1] // 128, add, 0)
        for b in range(ny):
            pack_x(b).start()

    def pack_after_x():
        for b in range(ny):
            pack_x(b).wait()
            first = pl.multiple_of((b * nx + x) * column_wide, 128)

            def add(c, _):
                here = pl.ds(pl.multiple_of(first + c * 128, 128), 128)
                cut = pl.ds(pl.multiple_of(c * 128, 128), 128)
                total = pk_pair[:, here].astype(F32) + pk_x[b, :, cut].astype(F32)
                pk_xsum[b, :, cut] = rounded(total)
                return 0

            lax.fori_loop(0, nz, add, 0)
        pack_y.start()

    def pack_after_y():
        pack_y.wait()

        def add(c, _):
            cut = pl.ds(pl.multiple_of(c * 128, 128), 128)
            total = pk_xsum[y, :, cut].astype(F32) + pk_y[:, cut].astype(F32)
            pk_ysum[:, cut] = rounded(total)
            return 0

        lax.fori_loop(0, nz, add, 0)
        for j in range(1, nz):
            pack_z(j).start()

    def pack_after_z():
        for j in range(1, nz):
            pack_z(j).wait()
        pk_z[z] = pk_ysum[:, pl.ds(pl.multiple_of(z * 128, 128), 128)]
        total = pk_z[0].astype(F32)
        for j in range(1, nz):
            total = total + pk_z[j].astype(F32)
        column[: total.shape[0], :] = rounded(total)

    def view_sp(which, k, first, count):
        rows = SP_CHUNKS[k]
        if which is not None:
            rows = (rows[0] + which * rows[1] // 2, rows[1] // 2)
        cut = pl.ds(pl.multiple_of(first * 128, 128), count * 128)
        return sp_out.at[role, pl.ds(*rows), cut]

    def view_li(which, k, first, count):
        rows = LI_CHUNKS[k]
        if which is not None:
            rows = (rows[0] + which * rows[1] // 2, rows[1] // 2)
        return li_all.at[pl.ds(first, count), pl.ds(*rows)]

    me = (role, z, y, x)
    sp = Gather(dims, me, view_sp, SP_CHUNKS, (sp_send, sp_recv))
    li = Gather(dims, me, view_li, LI_CHUNKS, (li_ag_send, li_ag_recv))

    def sp_last(k):
        ref = sp_out.at[role, pl.ds(*SP_CHUNKS[k])]
        return [remote(ref, ref, chip_send.at[2 + k], chip_recv.at[2 + k], twin)]

    def rows_of(j):
        return jnp.where(role == 1, SEGMENT * j, time_len - SEGMENT * (j + 1))

    def pack_columns(first_segment, last_segment):
        lane = lax.broadcasted_iota(jnp.int32, (SEGMENT, 128), 1)
        for j in range(first_segment, last_segment):
            rows = pl.ds(pl.multiple_of(rows_of(j), SEGMENT), SEGMENT)
            for b in range(width // 128):
                one = grad_pre[0, rows, b * 128 : (b + 1) * 128]
                two = grad_pre[1, rows, b * 128 : (b + 1) * 128]
                even = jnp.where(lane < 64, one, pltpu.roll(two, 64, 1))
                odd = jnp.where(lane < 64, pltpu.roll(one, 64, 1), two)
                li_send[2 * b, rows, :] = even.astype(BF16)
                li_send[2 * b + 1, rows, :] = odd.astype(BF16)

    def stream(n):
        first_segment, last_segment = STREAMS[n]
        count = SEGMENT * (last_segment - first_segment)
        begin = jnp.where(role == 1, SEGMENT * first_segment, time_len - SEGMENT * last_segment)
        rows = pl.ds(pl.multiple_of(begin, SEGMENT), count)

        def one(k):
            chip = (dp + k) % chips
            return remote(
                li_send.at[slot_of(chip), rows], li_got.at[dp, rows],
                li_aa_send.at[n, k - 1], li_aa_recv.at[n, k - 1], (role, chip),
            )

        return one

    def start_stream(n):
        pack_columns(*STREAMS[n])
        one = stream(n)
        lax.fori_loop(1, chips, lambda k, _: (one(k).start(), 0)[1], 0)

    def wait_stream(n):
        one = stream(n)
        lax.fori_loop(1, chips, lambda k, _: (one(k).wait(), 0)[1], 0)

    crossing.wait()
    grad_out[1 - role] = far_grad[...].astype(F32)
    zero = jnp.zeros((8, units), F32)
    carry = (zero, zero)

    def run(j, carry):
        return backward_steps(
            role, lengths, factors, grad_out, w_rec, grad_pre, SEGMENT * j, SEGMENT, carry
        )

    carry = run(0, carry)
    pl.when(role == 1)(pack_after_x)
    carry = run(1, carry)
    pl.when(role == 1)(pack_after_y)

    lax.fori_loop(1, chips, lambda k, _: (block(k).wait(), 0)[1], 0)
    own_block.wait()
    load_acts.wait()
    both = got[...].reshape(chips * 2 * pads, 128).astype(F32)
    rolled = pltpu.roll(both, chips * 2 * pads - 1, 0)
    got_t[0] = jnp.transpose(both).astype(BF16)
    got_t[1] = jnp.transpose(rolled).astype(BF16)
    groups = acts_buf.shape[1] // 256
    for g in range(groups):
        cut = slice(g * 256, (g + 1) * 256)
        if g == 0:
            left = got_t[0]
        elif g < groups - cells // 256:
            left = got_t[1 - role]
        else:
            left = got_t[1]
        prod[:, cut] = mm(left, acts_buf[:, cut])
    column[2 * SMALL :, :] = jnp.transpose(prod[...]).astype(BF16)
    column[: 2 * SMALL, :] = jnp.zeros((2 * SMALL, 128), BF16)

    def place(first, count):
        copy = pltpu.make_async_copy(
            column.at[pl.ds(first, count)], sp_out.at[role, pl.ds(first, count), lanes],
            local_sem.at[3],
        )
        copy.start()
        copy.wait()

    head = SP_CHUNKS[-1][1]
    place(head, column.shape[0] - head)
    for k in range(len(SP_CHUNKS) - 1):
        start(sp.first(k))

    carry = run(2, carry)
    pl.when(role == 1)(pack_after_z)
    place(0, head)
    start(sp.first(len(SP_CHUNKS) - 1))
    start_stream(0)
    far = jnp.where(role == 0, half_time, 0)
    near = half_time - far
    for u in range(utts):
        rows = pl.ds(pl.multiple_of(far, half_time), half_time)
        fr_send[u] = mm_nt(grad_pre[u, rows, :].astype(BF16), w_in[...]).astype(BF16)
    frames_copy = remote(fr_send, fr_got, chip_send.at[1], chip_recv.at[1], twin)
    frames_copy.start()
    wait(sp.first(0))
    start(sp.second(0))
    carry = run(3, carry)
    wait(sp.first(1))
    start(sp.second(1))
    wait(sp.second(0))
    start(sp.third(0))
    carry = run(4, carry)
    start_stream(1)
    wait(sp.first(2))
    start(sp.second(2))
    wait(sp.second(1))
    start(sp.third(1))
    carry = run(5, carry)
    start_stream(2)
    wait(sp.first(3))
    start(sp.second(3))
    wait(sp.second(2))
    start(sp.third(2))

    frames_copy.wait()
    feat = frames_out.shape[2]
    for u in range(utts):
        rows = pl.ds(pl.multiple_of(near, half_time), half_time)
        total = mm_nt(grad_pre[u, rows, :].astype(BF16), w_in[...]) + fr_got[u].astype(F32)
        for j in range(feat // 128):
            for half in range(2):
                cut = slice(half * feat + j * 128, half * feat + (j + 1) * 128)
                weave[pl.ds(half, half_time, stride=2), :] = total[:, cut]
            frames_out[u, :, j * 128 : (j + 1) * 128] = weave[...]

    li_got[dp] = li_send[slot]
    wait(load_rows)
    wait(load_pairs)
    for n in range(len(STREAMS)):
        wait_stream(n)

    def spread(c, _):
        value = li_got[c].astype(F32)
        for u, part in enumerate((value, pltpu.roll(value, 64, 1))):
            for p in range(time_len // PART):
                base = pl.multiple_of(((p * utts + u) * chips + slot_of(c)) * PART, PART)
                li_rows[pl.ds(base, PART), :] = part[p * PART : (p + 1) * PART].astype(BF16)
        return 0

    lax.fori_loop(0, chips, spread, 0)
    li_acc[...] = jnp.zeros_like(li_acc)
    deep = 4 * time_len
    features = pairs_buf.shape[1]

    def accumulate(c, _):
        rows = pl.ds(pl.multiple_of(c * deep, 256), deep)
        left = jnp.transpose(li_rows[rows, :])
        li_acc[:, :features] += mm(left, pairs_buf[rows, :])
        li_acc[:, features:] += mm(left, rows_buf[rows, :])
        return 0

    lax.fori_loop(0, chips * 2 * time_len // deep, accumulate, 0)
    flipped = jnp.transpose(li_acc[...])
    tall = flipped.shape[0] // 2
    lane = lax.broadcasted_iota(jnp.int32, (tall, 128), 1)
    packed = jnp.where(lane < 64, flipped[:tall], pltpu.roll(flipped[tall:], 64, 1))
    li_all[slot] = packed.astype(BF16)

    for k in range(len(LI_CHUNKS)):
        start(li.first(k))
    wait(sp.second(3))
    start(sp.third(3))
    wait(li.first(0))
    start(li.second(0))
    wait(sp.third(0))
    start(sp_last(0))
    wait(sp.third(1))
    start(sp_last(1))
    wait(li.first(1))
    start(li.second(1))
    wait(li.second(0))
    start(li.third(0))
    wait(sp.third(2))
    start(sp_last(2))
    wait(li.second(1))
    start(li.third(1))
    wait(sp.third(3))
    start(sp_last(3))
    wait(li.third(0))
    wait(li.third(1))

    def assemble(b, _):
        cut = pl.ds(pl.multiple_of(b * 128, 128), 128)
        even = li_all[2 * b].astype(F32)
        odd = li_all[2 * b + 1].astype(F32)
        li_out[:tall, cut] = jnp.where(lane < 64, even, pltpu.roll(odd, 64, 1)).astype(BF16)
        li_out[tall:, cut] = jnp.where(lane < 64, pltpu.roll(even, 64, 1), odd).astype(BF16)
        return 0

    lax.fori_loop(0, width // 128, assemble, 0)
    for k in range(len(SP_CHUNKS)):
        wait(sp_last(k))


def exchange(
    dims, lengths, factors, grad_mine, grad_other, w_in, w_rec, dp1, dp2, pack, acts_all,
    pairs_low, pairs_high, rows_all,
):
    utts, time_len, _ = factors.shape
    units = w_rec.shape[0]
    width = 4 * units
    pads, wide = dp1.shape
    cells = wide // 4
    chips = dims[0] * dims[1] * dims[2]
    span = acts_all.shape[1] - cells
    deep = sum(rows for _, rows in SP_CHUNKS)
    nz, ny, _ = dims
    packed = pack.shape[0]
    features = pairs_low.shape[1]
    total = features + units + 64
    feat = w_in.shape[0] // 2
    half_time = time_len // 2
    vmem = pl.BlockSpec(memory_space=pltpu.VMEM)
    anywhere = pl.BlockSpec(memory_space=pl.ANY)
    shape = jax.ShapeDtypeStruct
    dma = pltpu.SemaphoreType.DMA
    sp_sems = Gather.semaphores(dims, SP_CHUNKS)
    li_sems = Gather.semaphores(dims, LI_CHUNKS)
    return pl.pallas_call(
        functools.partial(exchange_kernel, dims),
        out_shape=(
            shape((utts, time_len, feat), F32),
            shape((total, width), BF16),
            shape((2, deep, wide), BF16),
        ),
        in_specs=[pl.BlockSpec(memory_space=pltpu.SMEM)] + [vmem] * 8 + [anywhere] * 4,
        out_specs=(vmem, vmem, anywhere),
        scratch_shapes=[
            pltpu.VMEM((utts, time_len, width), F32),
            pltpu.VMEM((utts, time_len, units), F32),
            pltpu.VMEM((acts_all.shape[0], span), BF16),
            pltpu.VMEM((chips * utts * time_len, features), BF16),
            pltpu.VMEM((chips * utts * time_len, units + 64), BF16),
            pltpu.VMEM((3, pads, wide), BF16),
            pltpu.VMEM((chips, 2, pads, 128), BF16),
            pltpu.VMEM((2, 128, chips * 2 * pads), BF16),
            pltpu.VMEM((128, span), F32),
            pltpu.VMEM((deep, 128), BF16),
            pltpu.VMEM((chips, time_len, 128), BF16),
            pltpu.VMEM((chips, time_len, 128), BF16),
            pltpu.VMEM((chips * 2 * time_len, 128), BF16),
            pltpu.VMEM((128, total), F32),
            pltpu.VMEM((chips, total // 2, 128), BF16),
            pltpu.VMEM((utts, half_time, 2 * feat), BF16),
            pltpu.VMEM((utts, half_time, 2 * feat), BF16),
            pltpu.VMEM((time_len, 128), F32),
            pltpu.VMEM((packed, wide), BF16),
            pltpu.VMEM((ny, packed, nz * 128), BF16),
            pltpu.VMEM((ny, packed, nz * 128), BF16),
            pltpu.VMEM((packed, nz * 128), BF16),
            pltpu.VMEM((packed, nz * 128), BF16),
            pltpu.VMEM((nz, packed, 128), BF16),
            dma((5 + 2 * 4,)),
            dma((3 + len(SP_CHUNKS),)),
            dma((3 + len(SP_CHUNKS),)),
            dma((chips - 1,)),
            dma((chips - 1,)),
            dma((len(STREAMS), chips - 1)),
            dma((len(STREAMS), chips - 1)),
            sp_sems,
            sp_sems,
            li_sems,
            li_sems,
            dma((1 + ny + nz,)),
            dma((1 + ny + nz,)),
            pltpu.VMEM(grad_other.shape, BF16),
        ],
        compiler_params=pltpu.CompilerParams(
            vmem_limit_bytes=VMEM_BYTES, collective_id=0, has_side_effects=True
        ),
    )(
        lengths, factors, grad_mine, grad_other, w_in, w_rec, dp1, dp2, pack,
        acts_all, pairs_low, pairs_high, rows_all,
    )


PIECE = 128
SLOTS = 3


def widen_kernel(jobs, sizes, sp, li, *refs):
    *outs, narrow, wide, few, last, in_sem, out_sem, few_sem = refs
    g_out, g_table, low_bias, up_bias, g_vec, g_obias, sum_bias = outs[-7:]

    def source(n):
        which, row, col, out, _, rows = jobs[n]
        ref = li if which == 2 else sp.at[which]
        width = outs[out].shape[-1]
        return pltpu.make_async_copy(
            ref.at[pl.ds(row, rows), pl.ds(col, width)],
            narrow.at[n % SLOTS, pl.ds(0, rows), pl.ds(0, width)],
            in_sem.at[n % SLOTS],
        )

    def target(n):
        _, _, _, out, row, rows = jobs[n]
        width = outs[out].shape[-1]
        return pltpu.make_async_copy(
            wide.at[n % SLOTS, pl.ds(0, rows), pl.ds(0, width)],
            outs[out].at[pl.ds(row, rows)],
            out_sem.at[n % SLOTS],
        )

    load_few = [
        pltpu.make_async_copy(sp.at[1, pl.ds(0, 2 * SMALL)], few, few_sem.at[0]),
        pltpu.make_async_copy(li.at[pl.ds(sizes[-1], 16)], last, few_sem.at[1]),
    ]
    for n in range(min(SLOTS, len(jobs))):
        source(n).start()
    start(load_few)
    for n in range(len(jobs)):
        source(n).wait()
        if n >= SLOTS:
            target(n - SLOTS).wait()
        rows, width = jobs[n][5], outs[jobs[n][3]].shape[-1]
        wide[n % SLOTS, :rows, :width] = narrow[n % SLOTS, :rows, :width].astype(F32)
        target(n).start()
        if n + SLOTS < len(jobs):
            source(n + SLOTS).start()
    wait(load_few)
    small = few[:SMALL].astype(F32) + few[SMALL:].astype(F32)
    cells, base, embed, att, vocab, _ = sizes
    g_out[...] = small[:vocab, :base]
    g_table[...] = small[:vocab, base : base + embed]
    base += embed
    for k in range(4):
        cut = slice(k * cells, (k + 1) * cells)
        low_bias[cut] = small[2 + k, base : base + cells]
        up_bias[cut] = small[6 + k, base : base + cells]
    g_vec[...] = small[0, base : base + att]
    g_obias[...] = small[1, base : base + vocab]
    sum_bias[...] = last[0:1, :].astype(F32)
    for n in range(max(0, len(jobs) - SLOTS), len(jobs)):
        target(n).wait()


def widen(sp, li, parts, sizes):
    jobs = []
    for out, (_, pieces) in enumerate(parts):
        done = 0
        for which, row, col, rows in pieces:
            for at in range(0, rows, PIECE):
                count = min(PIECE, rows - at)
                jobs.append((which, row + at, col, out, done, count))
                done += count
    cells, base, embed, att, vocab, _ = sizes
    wide = sp.shape[2]
    anywhere = pl.BlockSpec(memory_space=pl.ANY)
    vmem = pl.BlockSpec(memory_space=pltpu.VMEM)
    dma = pltpu.SemaphoreType.DMA
    few = ((vocab, base), (vocab, embed), (4 * cells,), (4 * cells,), (att,), (vocab,), (1, li.shape[1]))
    return pl.pallas_call(
        functools.partial(widen_kernel, jobs, sizes),
        out_shape=[jax.ShapeDtypeStruct(shape, F32) for shape, _ in parts]
        + [jax.ShapeDtypeStruct(shape, F32) for shape in few],
        in_specs=[anywhere] * 2,
        out_specs=[anywhere] * len(parts) + [vmem] * len(few),
        scratch_shapes=[
            pltpu.VMEM((SLOTS, PIECE, wide), BF16),
            pltpu.VMEM((SLOTS, PIECE, wide), F32),
            pltpu.VMEM((2 * SMALL, wide), BF16),
            pltpu.VMEM((16, li.shape[1]), BF16),
            dma((SLOTS,)),
            dma((SLOTS,)),
            dma((2,)),
        ],
        compiler_params=pltpu.CompilerParams(vmem_limit_bytes=VMEM_BYTES),
    )(sp, li)


def shards(
    frames,
    step_lengths,
    characters,
    char_lengths,
    listen_input,
    listen_hidden,
    listen_bias,
    lower_input,
    lower_hidden,
    lower_bias,
    upper_input,
    upper_hidden,
    upper_bias,
    key_proj,
    query_proj,
    score_vector,
    output_proj,
    output_bias,
    char_table,
):
    chips = lax.axis_size("dp")
    utts, frame_len, feat = frames.shape
    time_len = frame_len // 2
    swap = [(0, 1), (1, 0)]
    w_in, w_rec = listen_input[0], listen_hidden[0]
    units = w_rec.shape[0]
    cells = lower_hidden.shape[0]
    vocab, embed = char_table.shape
    fits = (
        chips % 4 == 0
        and 4 * cells == 128 * chips
        and 4 * units == 64 * chips
        and embed == 256
        and cells == 2 * units
        and time_len == SEGMENT * STREAMS[-1][1]
        and embed + 2 * units + cells + 2 * SMALL == sum(rows for _, rows in SP_CHUNKS)
        and embed + 2 * SMALL == SP_CHUNKS[-1][1]
        and time_len == 3 * PART
        and characters.shape[2] % SPELL_GROUPS == 0
        and 2 * feat + units + 64 == 2 * sum(rows for _, rows in LI_CHUNKS)
    )
    dims = (chips // 4, 2, 2) if fits else None
    pairs, rows, factors, mine, other, *low_pairs = listen_forward(
        dims, step_lengths, frames, w_in, w_rec, listen_bias
    )
    if not fits:
        other = lax.ppermute(other, "role", swap)
    vec = score_vector
    loss, prev_onehot, acts, key, *kept = speller_forward(
        dims, step_lengths, char_lengths, characters, pairs, rows, mine, other,
        lower_input, lower_hidden, lower_bias, upper_input, upper_hidden, upper_bias,
        key_proj, query_proj, vec, output_proj.T, output_bias, char_table,
    )
    if fits:
        *kept, high_pairs, rows_all = kept
    grad_mine, grad_other, dp1, dp2, pack = speller_backward(
        lower_input, lower_hidden, upper_input, upper_hidden, key_proj, query_proj, vec,
        prev_onehot, acts, key, *kept,
    )
    if fits:
        flat = lambda gathered: gathered.reshape(-1, gathered.shape[-1])
        acts_all = lax.all_gather(acts, ("dp", "role"), tiled=True)
        frame_grad, li, sp = exchange(
            dims, step_lengths, factors, grad_mine, grad_other, w_in, w_rec,
            dp1, dp2, pack, acts_all, flat(low_pairs[0]), flat(high_pairs), flat(rows_all),
        )
        width = 2 * feat
        att = key_proj.shape[1]
        first = 2 * SMALL
        low, high = first + embed, first + embed + 2 * units
        wide = 4 * cells
        deep = 2 * units * att // wide
        folded = lambda row: tuple((1, row, col, deep) for col in range(0, wide, att))
        *layers, sum_in, sum_rec, g_key, g_query, g_out, g_table, low_bias, up_bias, g_vec, g_obias, sum_bias = widen(
            sp,
            li,
            (
                ((high - first, wide), ((0, first, 0, high - first),)),
                ((cells, wide), ((0, high, 0, cells),)),
                ((cells, wide), ((1, low, 0, cells),)),
                ((cells, wide), ((1, low + cells, 0, cells),)),
                ((width, 4 * units), ((2, 0, 0, width),)),
                ((units, 4 * units), ((2, width, 0, units),)),
                ((2 * units, att), folded(first)),
                ((cells, att), folded(first + deep)),
            ),
            (cells, cells + 2 * units, embed, att, vocab, width + units),
        )
        lower, upper = layers[:2], layers[2:]
        g_out = g_out.T
    else:
        grad_other = lax.ppermute(grad_other, "role", swap)
        pack = lax.psum(pack.astype(F32), ("role", "dp"))
        small = pack[: 2 * SMALL]
        g_key, g_query = (
            unfold(part, cells) for part in jnp.split(pack[2 * SMALL :], 2, axis=0)
        )
        low_bias, up_bias, g_vec, g_out, g_obias, g_table = unpack(
            small, units, cells, key_proj.shape[1], vocab, embed
        )
        pre = listen_backward(step_lengths, factors, grad_mine, grad_other, w_rec)
        flat = pre.reshape(utts * time_len, 4 * units)
        sums = mm(jnp.concatenate([pairs.reshape(flat.shape[0], 2 * feat), rows], 1).T, flat)
        sums = lax.psum(sums, "dp")
        width = 2 * feat
        sum_in, sum_rec = sums[:width], sums[width : width + units]
        sum_bias = lax.psum(jnp.sum(flat.astype(F32), 0, keepdims=True), "dp")
        grad_pairs = mm(flat, w_in.T).reshape(utts, frame_len, feat)
        frame_grad = lax.psum_scatter(grad_pairs, "role", scatter_dimension=1, tiled=True)
        cuts = [embed, embed + 2 * units, embed + 2 * units + cells]
        emb, ctx, s1, s2 = jnp.split(acts, cuts, axis=1)
        local = (
            jnp.concatenate([mm(emb.T, dp1), mm(ctx[:-1].T, dp1[1:])], 0),
            mm(s1[:-1].T, dp1[1:]),
            mm(s1.T, dp2),
            mm(s2[:-1].T, dp2[1:]),
        )
        local = lax.psum(local, ("role", "dp"))
        lower, upper = local[:2], local[2:]
    return (
        loss, frame_grad, sum_in[None], sum_rec[None], sum_bias,
        *lower, low_bias, *upper, up_bias,
        g_key, g_query, g_vec, g_out, g_obias, g_table,
    )


def solution(mesh):
    whole = P()
    return jax.shard_map(
        shards,
        mesh=mesh,
        in_specs=(
            P("dp", None, None),
            P("dp"),
            P("dp", "role", None),
            P("dp", "role"),
            P("role", None, None),
            P("role", None, None),
            P("role", None),
        )
        + (whole,) * 12,
        out_specs=(
            P("dp", "role"),
            P("dp", "role", None),
            P("role", None, None),
            P("role", None, None),
            P("role", None),
        )
        + (whole,) * 12,
        check_vma=False,
    )
```

```python
import functools

import jax
import jax.numpy as jnp
from jax import lax
from jax.experimental import pallas as pl
from jax.experimental.pallas import tpu as pltpu
from jax.sharding import PartitionSpec as P

F32 = jnp.float32
BF16 = jnp.bfloat16
VMEM_BYTES = 60 * 1024 * 1024


def mm(left, right):
    return jnp.dot(left, right, preferred_element_type=F32)


def mm_nt(left, right):
    return lax.dot_general(left, right, (((1,), (1,)), ((), ())), preferred_element_type=F32)


def mm_tn(left, right):
    return lax.dot_general(left, right, (((0,), (0,)), ((), ())), preferred_element_type=F32)


def sigmoid(x):
    return 0.5 * jnp.tanh(0.5 * x) + 0.5


def cell_forward(preact, cell_prev):
    n = preact.shape[-1] // 4
    in_gate = sigmoid(preact[:, :n])
    forget = sigmoid(preact[:, n : 2 * n])
    candid = jnp.tanh(preact[:, 2 * n : 3 * n])
    out_gate = sigmoid(preact[:, 3 * n :])
    cell_new = forget * cell_prev + in_gate * candid
    tanh_cell = jnp.tanh(cell_new)
    hidden = out_gate * tanh_cell
    factors = (
        candid * in_gate * (1.0 - in_gate),
        cell_prev * forget * (1.0 - forget),
        in_gate * (1.0 - candid * candid),
        tanh_cell * out_gate * (1.0 - out_gate),
        out_gate * (1.0 - tanh_cell * tanh_cell),
        forget,
    )
    return cell_new, hidden, factors


def cell_backward(factors, grad_hidden, grad_cell):
    n = factors.shape[-1] // 6
    part = lambda k: factors[:, k * n : (k + 1) * n]
    total = grad_cell + grad_hidden * part(4)
    grad_preact = jnp.concatenate(
        [total * part(0), total * part(1), total * part(2), grad_hidden * part(3)], -1
    )
    return grad_preact, total * part(5)


def remote(src, dst, send, recv, device):
    return pltpu.make_async_remote_copy(
        src_ref=src, dst_ref=dst, send_sem=send, recv_sem=recv,
        device_id=device, device_id_type=pl.DeviceIdType.MESH,
    )


def start(copies):
    for copy in copies:
        copy.start()


def wait(copies):
    for copy in copies:
        copy.wait()


class Gather:
    def __init__(self, dims, me, view, chunks, sems):
        self.dims, self.view, self.chunks = dims, view, chunks
        self.role, self.z, self.y, self.x = me
        self.send, self.recv = sems

    def device(self, z, y, x):
        _, ny, nx = self.dims
        return (self.role, (z * ny + y) * nx + x)

    def copies(self, k, which, spans, others, base):
        out = []
        for device in others:
            for span in spans:
                ref = self.view(which, k, *span)
                out.append(
                    remote(ref, ref, self.send.at[k, base], self.recv.at[k, base], device)
                )
                base += 1
        return out

    def along_x(self):
        nx = self.dims[2]
        return [self.device(self.z, self.y, (self.x + j) % nx) for j in range(1, nx)]

    def along_y(self):
        ny = self.dims[1]
        return [self.device(self.z, (self.y + j) % ny, self.x) for j in range(1, ny)]

    def first(self, k):
        nz, ny, nx = self.dims
        slot = (self.y * nx + self.x) * nz + self.z
        others = [self.device((self.z + j) % nz, self.y, self.x) for j in range(1, nz)]
        return self.copies(k, None, [(slot, 1)], others, 0)

    def second(self, k):
        nz, ny, nx = self.dims
        column = ((self.y * nx + self.x) * nz, nz)
        base = nz - 1
        to_x = self.copies(k, 0, [column], self.along_x(), base)
        return to_x + self.copies(k, 1, [column], self.along_y(), base + nx - 1)

    def third(self, k):
        nz, ny, nx = self.dims
        base = nz - 1 + nx - 1 + ny - 1
        to_y = self.copies(k, 0, [(self.y * nx * nz, nx * nz)], self.along_y(), base)
        spans = [((b * nx + self.x) * nz, nz) for b in range(ny)]
        return to_y + self.copies(k, 1, spans, self.along_x(), base + ny - 1)

    @staticmethod
    def semaphores(dims, chunks):
        nz, ny, nx = dims
        count = nz - 1 + 2 * (nx - 1) + 2 * (ny - 1) + (nx - 1) * (ny - 1)
        return pltpu.SemaphoreType.DMA((len(chunks), count))


PART = 64
LISTEN_GROUPS = 6
LISTEN_CHUNKS = ((0, 0, 32), (0, 32, 32))
LISTEN_EVENTS = (
    ((), ((0, 0), (0, 1))),
    (((0, 0),), ((1, 0),)),
    (((1, 0), (0, 1)), ((2, 0), (1, 1))),
    (((2, 0),), ((3, 0),)),
    (((1, 1),), ((2, 1),)),
    (((2, 1),), ((3, 1),)),
    ((), ()),
)
SPELL_GROUPS = 18
SPELL_CHUNKS = ((0, 0, PART), (1, 0, PART))
SPELL_EVENTS = (
    ((), ((0, 0), (0, 1))),
    ((), ()),
    (((0, 0),), ((1, 0), (0, 2))),
    (((0, 1),), ((1, 1), (0, 3))),
    (((1, 0),), ((2, 0),)),
    (((1, 1), (0, 2)), ((2, 1), (1, 2), (0, 4))),
    (((2, 0),), ()),
    (((0, 3), (2, 1)), ((1, 3),)),
    (((1, 2),), ((2, 2),)),
    (((1, 3),), ((2, 3),)),
    (((0, 4),), ((1, 4),)),
    (((2, 2),), ()),
    ((), ()),
    (((2, 3),), ((3, 3),)),
    (((1, 4),), ((2, 4),)),
    ((), ()),
    ((), ()),
    (((2, 4),), ((3, 4),)),
    ((), ()),
)


class Gathers:
    def __init__(self, dims, role, dp, events, frames, chunks, states, sems):
        nz, ny, nx = dims
        me = (role, dp // (ny * nx), (dp // nx) % ny, dp % nx)
        self.twin = (1 - role, dp)
        self.role, self.frames, self.chunks, self.events = role, frames, chunks, events
        send, recv, self.last_send, self.last_recv = sems[:4]
        self.slot = (me[2] * nx + me[3]) * nz + me[1]

        def half(first, count, which):
            if which is not None:
                first, count = first + which * count // 2, count // 2
            return pl.ds(first, count)

        def view_frames(which, k, first, count):
            part, *rows = chunks[k]
            return frames.at[part, role, pl.ds(first, count), half(*rows, which)]

        self.two = Gather(dims, me, view_frames, chunks, (send, recv))
        self.lead = 0
        if states is not None:
            self.lead = states.shape[0]

            def view_states(which, k, first, count):
                rows = half(0, states.shape[3], which)
                return states.at[k, :, pl.ds(first, count), rows]

            self.one = Gather(dims, me, view_states, range(self.lead), sems[4:])
        g = self.two
        to_z = [g.device((g.z + j) % nz, g.y, g.x) for j in range(1, nz)]
        self.partners = to_z + g.along_x() + g.along_y() + [self.twin]

    def greet(self):
        barrier = pltpu.get_barrier_semaphore()
        for device in self.partners:
            pl.semaphore_signal(
                barrier, inc=1, device_id=device, device_id_type=pl.DeviceIdType.MESH
            )

    def phase(self, n, c):
        if n == 3:
            k = c - self.lead
            part, *rows = self.chunks[k]
            ref = self.frames.at[part, self.role, :, pl.ds(*rows)]
            return [remote(ref, ref, self.last_send.at[k], self.last_recv.at[k], self.twin)]
        gather, k = (self.one, c) if c < self.lead else (self.two, c - self.lead)
        return (gather.first, gather.second, gather.third)[n](k)

    def begin(self):
        pl.semaphore_wait(pltpu.get_barrier_semaphore(), len(self.partners))

    def look(self, group):
        ended, begun = self.events[group]
        for n, c in ended:
            wait(self.phase(n, c))
        for n, c in begun:
            start(self.phase(n, c))

    def finish(self):
        for k in range(len(self.chunks)):
            wait(self.phase(3, self.lead + k))

    @staticmethod
    def scratch(dims, chunks, states):
        dma = pltpu.SemaphoreType.DMA
        sems = [Gather.semaphores(dims, chunks)] * 2 + [dma((len(chunks),))] * 2
        if states:
            sems += [Gather.semaphores(dims, range(states))] * 2
        return sems


def stage(tiles):
    for k in range(2):
        for unit in range(2):
            pltpu.matmul_push_rhs(tiles(2 * unit + k), k, unit)


def multiply(totals, lefts):
    share = 4 // len(totals)
    for k in range(2):
        for unit in range(2):
            j = 2 * unit + k
            pltpu.matmul_acc_lhs(totals[j // share], lefts[j], load_staged_rhs=k)


SIDE = 256


def staged_product(left, tile, columns, flip=False):
    deep = left.shape[1] // SIDE

    def run(*totals):
        parts = []
        for n in range(0, columns, 2):
            units = range(min(2, columns - n))
            for k in range(deep):
                for unit in units:
                    pltpu.matmul_push_rhs(tile(k, n + unit), k % 2, unit, transpose=flip)
                    pltpu.matmul_acc_lhs(
                        totals[unit], left[:, k * SIDE : (k + 1) * SIDE], load_staged_rhs=k % 2
                    )
            parts += [pltpu.matmul_pop(totals[unit]) for unit in units]
        return jnp.concatenate(parts, 1) if len(parts) > 1 else parts[0]

    rows = left.shape[0]
    return pl.run_scoped(run, *[pltpu.ACC(mxu_id=unit)((rows, SIDE), F32) for unit in range(2)])


def tiles_of(ref):
    return lambda k, n: ref[k * SIDE : (k + 1) * SIDE, n * SIDE : (n + 1) * SIDE]


def staged_loop(first, last, step, carry, tiles, outputs):
    side = tiles(0).shape[0]

    def run(*totals):
        def product(left):
            tall = jnp.concatenate([left, jnp.zeros_like(left)], 0).astype(BF16)
            wide = tall.shape[1] // side
            multiply(totals, [tall[:, (j % wide) * side : (j % wide + 1) * side] for j in range(4)])
            stage(tiles)
            return [pltpu.matmul_pop(total)[: left.shape[0]] for total in totals]

        stage(tiles)
        end = lax.fori_loop(first, last, lambda s, c: step(product, s, c), carry)
        multiply(totals, [jnp.zeros((16, side), BF16)] * 4)
        for total in totals:
            pltpu.matmul_pop(total)
        return end

    units = [j * 2 // outputs for j in range(outputs)]
    return pl.run_scoped(run, *[pltpu.ACC(mxu_id=unit)((16, side), F32) for unit in units])


def listen_forward_kernel(
    dims, lengths, frames, w_in, w_rec, bias,
    pairs, rows_out, factors_out, mine_out, other_out, *rest
):
    role = lax.axis_index("role")
    if dims is not None:
        pairs_all, proj, emit, hprev, to_other, cross, *sems = rest
        gather = Gathers(
            dims, role, lax.axis_index("dp"), LISTEN_EVENTS, pairs_all, LISTEN_CHUNKS, None, sems
        )
        gather.greet()
    else:
        proj, emit, hprev = rest
    utts, time_len, width4 = proj.shape
    units = width4 // 4
    feat = frames.shape[-1]
    window = 2 * time_len - SIDE
    rows = lax.broadcasted_iota(jnp.int32, (time_len, 2 * SIDE), 0)
    cols = lax.broadcasted_iota(jnp.int32, (time_len, 2 * SIDE), 1)
    frame = jnp.where(cols < SIDE, cols, cols - SIDE + window)
    own = jnp.logical_or(cols < SIDE, frame >= SIDE)
    for half in range(2):
        pick = jnp.where(jnp.logical_and(own, frame == 2 * rows + half), 1.0, 0.0).astype(BF16)
        for u in range(utts):
            tile = lambda k, n: frames[
                u, k * window : k * window + SIDE, n * SIDE : (n + 1) * SIDE
            ]
            picked = staged_product(pick, tile, feat // SIDE)
            pairs[u, :, half * feat : (half + 1) * feat] = picked.astype(BF16)
    if dims is not None:
        place = pltpu.make_async_copy(
            pairs.at[role, pl.ds(0, PART)], pairs_all.at[0, role, gather.slot], cross.at[2]
        )
        place.start()
    bias_row = bias[...].astype(F32)
    for u in range(utts):
        proj[u] = staged_product(pairs[u], tiles_of(w_in), width4 // SIDE) + bias_row
    if dims is not None:
        place.wait()
        gather.begin()
    first = lax.broadcasted_iota(jnp.int32, (8, 1), 0) == 0
    row_lengths = jnp.where(first, lengths[0], lengths[1])

    tiles = lambda j: w_rec[:, j * units : (j + 1) * units]

    def step(product, s, carry):
        hidden, cell = carry
        t = jnp.where(role == 1, time_len - 1 - s, s)
        at = pl.ds(t, 1)
        pre_in = jnp.where(first, proj[0, at, :], proj[1, at, :])
        preact = pre_in + jnp.concatenate(product(hidden), 1)
        cell_new, hidden_new, factors = cell_forward(preact, cell)
        live = t < row_lengths
        hidden_next = jnp.where(live, hidden_new, hidden)
        cell_next = jnp.where(live, cell_new, cell)
        emitted = jnp.where(live, hidden_new, 0.0)
        for u in range(2):
            for k in range(6):
                factors_out[u, at, k * units : (k + 1) * units] = factors[k][u : u + 1]
            hprev[u, at, :] = hidden[u : u + 1]
            emit[u, at, :] = emitted[u : u + 1]
        return hidden_next, cell_next

    zero = jnp.zeros((8, units), F32)
    carry = (zero, zero)
    if dims is None:
        staged_loop(0, time_len, step, carry, tiles, 4)
    else:
        count = time_len // LISTEN_GROUPS
        for group in range(LISTEN_GROUPS):
            gather.look(group)
            carry = staged_loop(group * count, (group + 1) * count, step, carry, tiles, 4)
    mine_out[...] = emit[role].astype(BF16)
    if dims is None:
        other_out[...] = emit[1 - role].astype(BF16)
    else:
        to_other[...] = emit[1 - role].astype(BF16)
        crossing = remote(to_other, other_out, cross.at[0], cross.at[1], gather.twin)
        crossing.start()
        gather.look(LISTEN_GROUPS)
    for u in range(utts):
        own = slice(u * time_len, (u + 1) * time_len)
        rows_out[own, :] = hprev[u].astype(BF16)
    if dims is not None:
        crossing.wait()
        gather.finish()


def listen_forward(dims, lengths, frames, w_in, w_rec, bias):
    utts, time_len, width = frames.shape[0], frames.shape[1] // 2, 2 * frames.shape[2]
    units = w_rec.shape[0]
    vmem = pl.BlockSpec(memory_space=pltpu.VMEM)
    shape = jax.ShapeDtypeStruct
    outs = [
        shape((utts, time_len, width), BF16),
        shape((utts * time_len, units), BF16),
        shape((utts, time_len, 6 * units), F32),
        shape((time_len, units), BF16),
        shape((time_len, units), BF16),
    ]
    out_specs = [vmem] * 5
    scratch = [
        pltpu.VMEM((utts, time_len, 4 * units), F32),
        pltpu.VMEM((utts, time_len, units), F32),
        pltpu.VMEM((utts, time_len, units), F32),
    ]
    params = dict(vmem_limit_bytes=VMEM_BYTES)
    if dims is not None:
        chips = dims[0] * dims[1] * dims[2]
        outs.append(shape((1, 2, chips, PART, width), BF16))
        out_specs.append(pl.BlockSpec(memory_space=pl.ANY))
        scratch += [pltpu.VMEM((time_len, units), BF16), pltpu.SemaphoreType.DMA((3,))]
        scratch += Gathers.scratch(dims, LISTEN_CHUNKS, 0)
        params.update(collective_id=1, has_side_effects=True)
    return pl.pallas_call(
        functools.partial(listen_forward_kernel, dims),
        out_shape=outs,
        in_specs=[pl.BlockSpec(memory_space=pltpu.SMEM)] + [vmem] * 4,
        out_specs=out_specs,
        scratch_shapes=scratch,
        compiler_params=pltpu.CompilerParams(**params),
    )(lengths, frames, w_in, w_rec, bias)


def speller_forward_kernel(
    dims, lengths, text_lens, chars, pairs, states,
    mine, other,
    w_lin, w_lhid, b_low, w_uin, w_uhid, b_up, w_key, w_query, vec, w_out, b_out, table,
    loss, prev_onehot, acts, key, keys_proj, key_low, fact1, fact2, q_rows, w_cols, feat_rows, dw_cols,
    logit_grad_out, *rest
):
    role = lax.axis_index("role")
    gather = None
    if dims is not None:
        pairs_all, states_all, emb_proj, s1_rows, s2_rows, hot, stage, own_sem, *sems = rest
        gather = Gathers(
            dims, role, lax.axis_index("dp"), SPELL_EVENTS, pairs_all, SPELL_CHUNKS, states_all, sems
        )
        gather.greet()
        load = pltpu.make_async_copy(
            pairs.at[role, pl.ds(PART, stage.shape[0])], stage, own_sem.at[0]
        )
        load.start()
        parts, utts = states_all.shape[:2]
        place = [
            pltpu.make_async_copy(
                states.at[pl.ds((u * parts + part) * PART, PART)],
                states_all.at[part, u, gather.slot],
                own_sem.at[1 + u * parts + part],
            )
            for u in range(utts)
            for part in range(parts)
        ]
        start(place)
        staged = [
            pltpu.make_async_copy(
                stage.at[pl.ds(part * PART, PART)],
                pairs_all.at[part, role, gather.slot],
                own_sem.at[1 + len(place) + part],
            )
            for part in range(pairs_all.shape[0])
        ]
    else:
        emb_proj, s1_rows, s2_rows, hot = rest
    time_len, units = mine.shape
    steps = emb_proj.shape[0]
    cells = w_lhid.shape[0]
    embed = table.shape[1]
    length = lengths[role]
    text_len = text_lens[0, 0]

    key[:, :units] = jnp.where(role == 0, mine[...], other[...])
    key[:, units:] = jnp.where(role == 0, other[...], mine[...])
    keys_proj[...] = mm(key[...], w_key[...])
    if gather is not None:
        load.wait()
        start(staged)
    key_low[...] = mm(key[...], w_lin[embed:, :])
    ids = lax.broadcasted_iota(jnp.int32, (1, hot.shape[2]), 1)

    def mark(i, previous):
        here = chars[0, 0, i]
        hot[0, pl.ds(i, 1), :] = jnp.where(ids == previous, 1.0, 0.0)
        hot[1, pl.ds(i, 1), :] = jnp.where(ids == here, 1.0, 0.0)
        return here

    lax.fori_loop(0, steps, mark, 0)
    prev_onehot[...] = hot[0].astype(BF16)
    emb = mm(prev_onehot[...], table[...]).astype(BF16)
    emb_proj[...] = mm(emb, w_lin[:embed, :]) + b_low[...].astype(F32)[None]
    bias_up = b_up[...].astype(F32)[None]
    vec_row = vec[...].astype(F32)[None]
    frame_ok = lax.broadcasted_iota(jnp.int32, (time_len, 1), 0) < length
    lane = lax.broadcasted_iota(jnp.int32, w_cols.shape, 1)
    w_cols[...] = jnp.zeros_like(w_cols)
    if gather is not None:
        wait(place)
        wait(staged)
        gather.begin()

    def forward_step(i, carry):
        cell1, cell2, hid1, hid2, ctx_low = carry
        at = pl.ds(i, 1)
        pre1 = emb_proj[at, :] + hid1 + ctx_low
        cell1, s1, factors = cell_forward(pre1, cell1)
        for k in range(6):
            fact1[at, k * cells : (k + 1) * cells] = factors[k]
        s1_rows[at, :] = s1
        s1_low = s1.astype(BF16)
        pre2 = hid2 + bias_up + mm(s1_low, w_uin[...])
        hid1 = mm(s1_low, w_lhid[...])
        cell2, s2, factors = cell_forward(pre2, cell2)
        for k in range(6):
            fact2[at, k * cells : (k + 1) * cells] = factors[k]
        s2_rows[at, :] = s2
        s2_low = s2.astype(BF16)
        query = mm(s2_low, w_query[...])
        hid2 = mm(s2_low, w_uhid[...])
        q_rows[at, :] = query
        part = None
        for j in range(query.shape[1] // 128):
            cut = slice(j * 128, (j + 1) * 128)
            term = jnp.tanh(keys_proj[:, cut] + query[:, cut]) * vec_row[:, cut]
            part = term if part is None else part + term
        scores = jnp.sum(part, -1, keepdims=True)
        scores = jnp.where(frame_ok, scores, -1000000000.0)
        scores = scores - jnp.max(scores, 0, keepdims=True)
        expf = jnp.where(frame_ok, jnp.exp(scores), 0.0)
        rinv = 1.0 / jnp.sum(expf, 0, keepdims=True)
        w_cols[...] = jnp.where(lane == i, expf * rinv, w_cols[...])
        ctx_low = jnp.concatenate(
            [
                jnp.sum(expf * key_low[:, j * 128 : (j + 1) * 128], 0, keepdims=True)
                for j in range(key_low.shape[1] // 128)
            ],
            1,
        )
        return cell1, cell2, hid1, hid2, ctx_low * rinv

    zero = jnp.zeros((1, cells), F32)
    wide = jnp.zeros((1, 4 * cells), F32)
    carry = (zero, zero, wide, wide, wide)
    if gather is None:
        lax.fori_loop(0, steps, forward_step, carry)
    else:
        count = steps // SPELL_GROUPS
        for group in range(SPELL_GROUPS):
            gather.look(group)
            carry = lax.fori_loop(group * count, (group + 1) * count, forward_step, carry)
        gather.look(SPELL_GROUPS)

    w_low = jnp.transpose(w_cols[...])[:steps].astype(BF16)
    ctx = mm(w_low, key[...]).astype(BF16)
    s2_low = s2_rows[...].astype(BF16)
    logits = mm_nt(s2_low, w_out[:, :cells]) + mm_nt(ctx, w_out[:, cells:]) + b_out[...].astype(F32)[None]
    top = jnp.max(logits, -1, keepdims=True)
    log_total = top + jnp.log(jnp.sum(jnp.exp(logits - top), -1, keepdims=True))
    target = hot[1]
    cross = log_total - jnp.sum(logits * target, -1, keepdims=True)
    text = text_len.astype(F32)
    alive = lax.broadcasted_iota(jnp.int32, (steps, 1), 0) < text_len
    loss[...] = jnp.sum(jnp.where(alive, cross, 0.0), 0, keepdims=True) / text
    scale = jnp.where(alive, 1.0 / text, 0.0)
    logit_grad = (scale * (jnp.exp(logits - log_total) - target)).astype(BF16)
    logit_grad_out[...] = logit_grad
    feat_rows[...] = mm(logit_grad, w_out[...])
    dw_cols[...] = jnp.zeros_like(dw_cols)
    dw_cols[:, :steps] = mm_nt(key[...], feat_rows[:, cells:].astype(BF16))
    acts[steps:, :] = jnp.zeros((acts.shape[0] - steps, acts.shape[1]), BF16)
    acts[:steps, :embed] = emb
    acts[:steps, embed : embed + 2 * units] = ctx
    acts[:steps, embed + 2 * units : embed + 2 * units + cells] = s1_rows[...].astype(BF16)
    acts[:steps, embed + 2 * units + cells :] = s2_low
    if gather is not None:
        gather.finish()


def speller_forward(
    dims, lengths, text_lens, chars, pairs, states, mine, other,
    w_lin, w_lhid, b_low, w_uin, w_uhid, b_up, w_key, w_query, vec, w_out, b_out, table,
):
    time_len, units = mine.shape
    steps, vocab = chars.shape[2], table.shape[0]
    cells = w_lhid.shape[0]
    att = w_key.shape[1]
    embed = table.shape[1]
    pad_steps = -(-steps // 16) * 16
    vmem = pl.BlockSpec(memory_space=pltpu.VMEM)
    smem = pl.BlockSpec(memory_space=pltpu.SMEM)
    shape = jax.ShapeDtypeStruct
    outs = [
        shape((1, 1), F32),
        shape((steps, vocab), BF16),
        shape((pad_steps, embed + 2 * units + 2 * cells), BF16),
        shape((time_len, 2 * units), BF16),
        shape((time_len, att), F32),
        shape((time_len, 4 * cells), F32),
        shape((steps, 6 * cells), F32),
        shape((steps, 6 * cells), F32),
        shape((steps, att), F32),
        shape((time_len, -(-steps // 128) * 128), F32),
        shape((steps, w_out.shape[1]), F32),
        shape((time_len, -(-steps // 128) * 128), F32),
        shape((steps, vocab), BF16),
    ]
    out_specs = [vmem] * len(outs)
    scratch = [
        pltpu.VMEM((steps, 4 * cells), F32),
        pltpu.VMEM((steps, cells), F32),
        pltpu.VMEM((steps, cells), F32),
        pltpu.VMEM((2, steps, vocab), F32),
    ]
    params = dict(vmem_limit_bytes=VMEM_BYTES)
    if dims is not None:
        chips = dims[0] * dims[1] * dims[2]
        dma = pltpu.SemaphoreType.DMA
        utts, _, width = pairs.shape
        parts = time_len // PART
        high = parts - 1
        outs.append(shape((high, utts, chips, PART, width), BF16))
        outs.append(shape((parts, utts, chips, PART, units), BF16))
        out_specs += [pl.BlockSpec(memory_space=pl.ANY)] * 2
        scratch += [pltpu.VMEM((high * PART, width), BF16), dma((1 + high + utts * parts,))]
        scratch += Gathers.scratch(dims, SPELL_CHUNKS, parts)
        params.update(collective_id=2, has_side_effects=True)
    return pl.pallas_call(
        functools.partial(speller_forward_kernel, dims),
        out_shape=outs,
        in_specs=[smem] * 3 + [pl.BlockSpec(memory_space=pl.ANY)] + [vmem] * 15,
        out_specs=out_specs,
        scratch_shapes=scratch,
        compiler_params=pltpu.CompilerParams(**params),
    )(
        lengths, text_lens, chars, pairs, states, mine, other,
        w_lin, w_lhid, b_low, w_uin, w_uhid, b_up, w_key, w_query, vec, w_out, b_out, table,
    )


SMALL = 32


def shift_up(rows):
    count = rows.shape[0]
    rolled = pltpu.roll(rows, count - 1, 0)
    at = lax.broadcasted_iota(jnp.int32, rows.shape, 0)
    return jnp.where(at == count - 1, 0.0, rolled)


def speller_backward_kernel(
    w_lin, w_lhid, w_uin, w_uhid, w_key, w_query, vec, prev_onehot,
    acts, key, keys_proj, key_low, fact1, fact2, q_rows, w_cols, feat_rows, dw_cols, logit_grad,
    grad_mine, grad_other, dp1_out, dp2_out, pack,
    dp1_rows, dp2_rows, dq_rows, keys_acc, vec_acc, small, t_lhid, t_uin, t_uhid, t_query,
):
    role = lax.axis_index("role")
    time_len, att = keys_proj.shape
    steps, vocab = logit_grad.shape
    units = key.shape[1] // 2
    cells = w_lhid.shape[0]
    embed = acts.shape[1] - 2 * units - 2 * cells
    vec_row = vec[...].astype(F32)[None]
    zero = jnp.zeros((1, cells), F32)
    wide = jnp.zeros((1, 4 * cells), BF16)
    keys_acc[...] = jnp.zeros_like(keys_acc)
    vec_acc[...] = jnp.zeros_like(vec_acc)
    t_lhid[...] = w_lhid[...].T
    t_uin[...] = w_uin[...].T
    t_uhid[...] = w_uhid[...].T
    t_query[...] = w_query[...].T
    lane = lax.broadcasted_iota(jnp.int32, w_cols.shape, 1)

    def backward_step(s, carry):
        dp1, dp2, dcell1, dcell2 = carry
        i = steps - 1 - s
        at = pl.ds(i, 1)
        query = q_rows[at, :]
        dp1_row = dp1.astype(F32)
        here = lane == i
        part = jnp.where(here, dw_cols[...], 0.0)
        for j in range(key_low.shape[1] // 128):
            cut = slice(j * 128, (j + 1) * 128)
            part = part + dp1_row[:, cut] * key_low[:, cut]
        dweights = jnp.sum(part, -1, keepdims=True)
        weights = jnp.sum(jnp.where(here, w_cols[...], 0.0), -1, keepdims=True)
        back2 = mm(dp2, t_uhid[...])
        back1 = mm(dp1, t_lhid[...])
        shared = weights * dweights
        dscore = shared - weights * jnp.sum(shared, 0, keepdims=True)
        sums = []
        for j in range(query.shape[1] // 128):
            cut = slice(j * 128, (j + 1) * 128)
            energy = jnp.tanh(keys_proj[:, cut] + query[:, cut])
            moved = dscore * (1.0 - energy * energy)
            keys_acc[:, cut] += moved
            sums.append(jnp.sum(moved, 0, keepdims=True))
            vec_acc[:, cut] += jnp.sum((dscore * energy).reshape(time_len // 8, 8, 128), 0)
        dquery = (jnp.concatenate(sums, 1) * vec_row).astype(BF16)
        dq_rows[at, :] = dquery.astype(F32)
        ds2 = back2 + feat_rows[at, :cells] + mm(dquery, t_query[...])
        pre2, dcell2 = cell_backward(fact2[at, :], ds2, dcell2)
        dp2_rows[at, :] = pre2
        dp2 = pre2.astype(BF16)
        ds1 = back1 + mm(dp2, t_uin[...])
        pre1, dcell1 = cell_backward(fact1[at, :], ds1, dcell1)
        dp1_rows[at, :] = pre1
        return pre1.astype(BF16), dp2, dcell1, dcell2

    lax.fori_loop(0, steps, backward_step, (wide, wide, zero, zero))

    dp1 = dp1_rows[...].astype(BF16)
    dp2 = dp2_rows[...].astype(BF16)
    dq = dq_rows[...].astype(BF16)
    extra = jnp.zeros((dp1_out.shape[0] - steps, 4 * cells), BF16)
    dp1_out[steps:, :] = extra
    dp2_out[steps:, :] = extra
    dp1_out[:steps, :] = dp1
    dp2_out[:steps, :] = dp2
    next_dp1 = shift_up(dp1.astype(F32)).astype(BF16)
    ctx_grad = (feat_rows[:, cells:] + mm_nt(next_dp1, w_lin[embed:, :])).astype(BF16)
    keys_grad = (keys_acc[...] * vec_row).astype(BF16)
    w_low = w_cols[...].astype(BF16)[:, :steps]
    key_grad = mm_nt(keys_grad, w_key[...]) + mm(w_low, ctx_grad)
    key_grad = key_grad.astype(BF16)
    grad_mine[...] = jnp.where(role == 0, key_grad[:, :units], key_grad[:, units:])
    grad_other[...] = jnp.where(role == 0, key_grad[:, units:], key_grad[:, :units])
    ctx = acts[:steps, embed : embed + 2 * units]
    s2 = acts[:steps, embed + 2 * units + cells :]
    wide = pack.shape[1]
    deep = 2 * units * att // wide
    g_key = mm_tn(key[...], keys_grad)
    g_query = mm_tn(s2, dq)
    for k in range(wide // att):
        cut = slice(k * att, (k + 1) * att)
        first = 2 * SMALL
        pack[first : first + deep, cut] = g_key[k * deep : (k + 1) * deep].astype(BF16)
        first += deep
        pack[first : first + deep, cut] = g_query[k * deep : (k + 1) * deep].astype(BF16)
    emb_grad = mm_nt(dp1, w_lin[:embed, :])
    hot = prev_onehot[...]
    total = None
    for _ in range(3):
        low = emb_grad.astype(BF16)
        emb_grad = emb_grad - low.astype(F32)
        total = mm_tn(hot, low) if total is None else total + mm_tn(hot, low)
    small[...] = jnp.zeros_like(small)
    small[:vocab, :cells] = mm_tn(logit_grad[...], s2)
    small[:vocab, cells : cells + 2 * units] = mm_tn(logit_grad[...], ctx)
    base = cells + 2 * units
    small[:vocab, base : base + embed] = total
    base += embed
    small[0:1, base : base + att] = jnp.sum(vec_acc[...], 0, keepdims=True)
    small[1:2, base : base + vocab] = jnp.sum(logit_grad[...].astype(F32), 0, keepdims=True)
    low_bias = jnp.sum(dp1.astype(F32), 0, keepdims=True)
    up_bias = jnp.sum(dp2.astype(F32), 0, keepdims=True)
    for k in range(4):
        small[2 + k : 3 + k, base : base + cells] = low_bias[:, k * cells : (k + 1) * cells]
        small[6 + k : 7 + k, base : base + cells] = up_bias[:, k * cells : (k + 1) * cells]
    high = small[...].astype(BF16)
    pack[:SMALL, :] = high
    pack[SMALL : 2 * SMALL, :] = (small[...] - high.astype(F32)).astype(BF16)


def speller_backward(
    w_lin, w_lhid, w_uin, w_uhid, w_key, w_query, vec, prev_onehot,
    acts, key, keys_proj, key_low, fact1, fact2, q_rows, w_cols, feat_rows, dw_cols, logit_grad,
):
    time_len, att = keys_proj.shape
    steps, vocab = logit_grad.shape
    units = key.shape[1] // 2
    cells = w_lhid.shape[0]
    pad_steps = acts.shape[0]
    vmem = pl.BlockSpec(memory_space=pltpu.VMEM)
    shape = jax.ShapeDtypeStruct
    outs = [
        shape((time_len, units), BF16),
        shape((time_len, units), BF16),
        shape((pad_steps, 4 * cells), BF16),
        shape((pad_steps, 4 * cells), BF16),
        shape(((2 * units + cells) * att // (4 * cells) + 2 * SMALL, 4 * cells), BF16),
    ]
    out_specs = [vmem] * 5
    scratch = [
        pltpu.VMEM((steps, 4 * cells), F32),
        pltpu.VMEM((steps, 4 * cells), F32),
        pltpu.VMEM((steps, att), F32),
        pltpu.VMEM((time_len, att), F32),
        pltpu.VMEM((8, att), F32),
        pltpu.VMEM((SMALL, 4 * cells), F32),
        pltpu.VMEM((4 * cells, cells), BF16),
        pltpu.VMEM((4 * cells, cells), BF16),
        pltpu.VMEM((4 * cells, cells), BF16),
        pltpu.VMEM((att, cells), BF16),
    ]
    return pl.pallas_call(
        speller_backward_kernel,
        out_shape=outs,
        in_specs=[vmem] * 19,
        out_specs=out_specs,
        scratch_shapes=scratch,
        compiler_params=pltpu.CompilerParams(vmem_limit_bytes=VMEM_BYTES),
    )(
        w_lin, w_lhid, w_uin, w_uhid, w_key, w_query, vec, prev_onehot,
        acts, key, keys_proj, key_low, fact1, fact2, q_rows, w_cols, feat_rows, dw_cols, logit_grad,
    )


def unfold(folded, width):
    deep = folded.shape[0]
    return folded.reshape(deep, -1, width).swapaxes(0, 1).reshape(-1, width)


def unpack(small, units, cells, att, vocab, embed):
    small = small[:SMALL].astype(F32) + small[SMALL:].astype(F32)
    base = cells + 2 * units
    g_out = small[:vocab, :base].T
    g_table = small[:vocab, base : base + embed]
    base += embed
    low_bias = small[2:6, base : base + cells].reshape(-1)
    up_bias = small[6:10, base : base + cells].reshape(-1)
    g_vec = small[0, base : base + att]
    g_obias = small[1, base : base + vocab]
    return low_bias, up_bias, g_vec, g_out, g_obias, g_table


def backward_steps(role, lengths, factors, grad_out, w_back, grad_pre, first_step, count, carry):
    time_len = factors.shape[1]
    first = lax.broadcasted_iota(jnp.int32, (8, 1), 0) == 0
    row_lengths = jnp.where(first, lengths[0], lengths[1])

    units = w_back.shape[1]
    tiles = lambda j: w_back[j * units : (j + 1) * units, :]

    def step(product, s, carry):
        grad_hidden, grad_cell = carry
        t = jnp.where(role == 1, s, time_len - 1 - s)
        at = pl.ds(t, 1)
        live = t < row_lengths
        fact = jnp.where(first, factors[0, at, :], factors[1, at, :])
        arrived = jnp.where(first, grad_out[0, at, :], grad_out[1, at, :])
        fact = jnp.where(live, fact, 0.0)
        total = grad_hidden + jnp.where(live, arrived, 0.0)
        pre, cell_back = cell_backward(fact, total, grad_cell)
        for u in range(2):
            grad_pre[u, at, :] = pre[u : u + 1]
        back = sum(product(pre))
        return jnp.where(live, back, total), jnp.where(live, cell_back, grad_cell)

    return staged_loop(first_step, first_step + count, step, carry, tiles, 2)


def listen_backward_kernel(
    lengths, factors, grad_mine, grad_other, w_rec, pre_out, grad_pre, grad_out, w_back
):
    role = lax.axis_index("role")
    grad_out[role] = grad_mine[...].astype(F32)
    grad_out[1 - role] = grad_other[...].astype(F32)
    w_back[...] = w_rec[...].T
    zero = jnp.zeros((8, w_rec.shape[0]), F32)
    backward_steps(
        role, lengths, factors, grad_out, w_back, grad_pre, 0, factors.shape[1], (zero, zero)
    )
    pre_out[...] = grad_pre[...].astype(BF16)


def listen_backward(lengths, factors, grad_mine, grad_other, w_rec):
    utts, time_len, _ = factors.shape
    units = w_rec.shape[0]
    vmem = pl.BlockSpec(memory_space=pltpu.VMEM)
    return pl.pallas_call(
        listen_backward_kernel,
        out_shape=jax.ShapeDtypeStruct((utts, time_len, 4 * units), BF16),
        in_specs=[pl.BlockSpec(memory_space=pltpu.SMEM)] + [vmem] * 4,
        out_specs=vmem,
        scratch_shapes=[
            pltpu.VMEM((utts, time_len, 4 * units), F32),
            pltpu.VMEM((utts, time_len, units), F32),
            pltpu.VMEM((4 * units, units), BF16),
        ],
        compiler_params=pltpu.CompilerParams(vmem_limit_bytes=VMEM_BYTES),
    )(lengths, factors, grad_mine, grad_other, w_rec)


SEGMENT = 32
STREAMS = ((0, 3), (3, 5), (5, 6))


SP_CHUNKS = ((320, 352), (672, 352), (1024, 320), (0, 320))
LI_CHUNKS = ((0, 352), (352, 320))


def exchange_kernel(
    dims,
    lengths, factors, grad_mine, grad_other, w_in, w_rec, dp1, dp2, pack, acts_all, pairs_low, pairs_high, rows_all,
    frames_out, li_out, sp_out,
    grad_pre, grad_out, acts_buf, pairs_buf, rows_buf, dp_pair, got, got_t, prod, column,
    li_send, li_got, li_rows, li_acc, li_all, fr_send, fr_got, weave,
    pk_pair, pk_x, pk_xsum, pk_y, pk_ysum, pk_z,
    local_sem, chip_send, chip_recv, aa_send, aa_recv, li_aa_send, li_aa_recv,
    sp_send, sp_recv, li_ag_send, li_ag_recv, pk_send, pk_recv, far_grad, w_back,
):
    nz, ny, nx = dims
    chips = nz * ny * nx
    role = lax.axis_index("role")
    dp = lax.axis_index("dp")
    z, y, x = dp // (ny * nx), (dp // nx) % ny, dp % nx
    utts, time_len, width = grad_pre.shape
    units = w_rec.shape[0]
    cells = dp1.shape[1] // 4
    half_time = time_len // 2
    pads = dp1.shape[0]
    twin = (1 - role, dp)

    def slot_of(chip):
        return (((chip // nx) % ny) * nx + chip % nx) * nz + chip // (ny * nx)

    slot = slot_of(dp)
    lanes = pl.ds(pl.multiple_of(slot * 128, 128), 128)

    barrier = pltpu.get_barrier_semaphore()
    mesh = pl.DeviceIdType.MESH

    def greet(k, _):
        pl.semaphore_signal(barrier, inc=1, device_id=(role, (dp + k) % chips), device_id_type=mesh)
        return 0

    pl.semaphore_signal(barrier, inc=1, device_id=twin, device_id_type=mesh)
    lax.fori_loop(1, chips, greet, 0)
    load_acts = pltpu.make_async_copy(
        acts_all.at[:, pl.ds(pl.multiple_of(role * cells, 128), acts_buf.shape[1])],
        acts_buf, local_sem.at[0],
    )
    load_acts.start()
    load_rows = [pltpu.make_async_copy(rows_all, rows_buf.at[:, pl.ds(0, units)], local_sem.at[1])]
    rows_buf[:, units:] = jnp.ones((rows_buf.shape[0], rows_buf.shape[1] - units), BF16)
    start(load_rows)
    split = pairs_low.shape[0]
    load_pairs = [
        pltpu.make_async_copy(pairs_low, pairs_buf.at[pl.ds(0, split)], local_sem.at[4]),
        pltpu.make_async_copy(pairs_high, pairs_buf.at[pl.ds(split, pairs_high.shape[0])], local_sem.at[5]),
    ]
    start(load_pairs)
    dp_pair[role] = jnp.where(role == 0, dp1[...], dp2[...])
    dp_pair[2] = jnp.where(role == 0, dp2[...], dp1[...])
    grad_out[role] = grad_mine[...].astype(F32)
    w_back[...] = w_rec[...].T
    pl.semaphore_wait(barrier, chips)
    last = chip_send.shape[0] - 1
    crossing = remote(grad_other, far_grad, chip_send.at[last], chip_recv.at[last], twin)
    crossing.start()

    to_twin = remote(dp_pair.at[2], dp_pair.at[role], chip_send.at[0], chip_recv.at[0], twin)
    to_twin.start()
    pack_twin = remote(pack, pk_pair, pk_send.at[0], pk_recv.at[0], twin)

    @pl.when(role == 0)
    def _():
        pack_twin.start()

    to_twin.wait()

    def block(k):
        chip = (dp + k) % chips
        cut = pl.ds(pl.multiple_of(slot_of(chip) * 128, 128), 128)
        return remote(
            dp_pair.at[pl.ds(0, 2), :, cut], got.at[dp],
            aa_send.at[k - 1], aa_recv.at[k - 1], (role, chip),
        )

    lax.fori_loop(1, chips, lambda k, _: (block(k).start(), 0)[1], 0)
    own_block = pltpu.make_async_copy(
        dp_pair.at[pl.ds(0, 2), :, lanes], got.at[dp], local_sem.at[2]
    )
    own_block.start()

    def rounded(total):
        value = total[:SMALL] + total[SMALL : 2 * SMALL]
        high = value.astype(BF16)
        low = (value - high.astype(F32)).astype(BF16)
        return jnp.concatenate([high, low, total[2 * SMALL :].astype(BF16)], 0)

    chip_at = lambda a, b, c: (role, (a * ny + b) * nx + c)
    x_other, y_other = (x + 1) % nx, (y + 1) % ny
    column_wide = nz * 128

    def pack_x(b):
        first = pl.multiple_of((b * nx + x_other) * column_wide, 128)
        return remote(
            pk_pair.at[:, pl.ds(first, column_wide)], pk_x.at[b],
            pk_send.at[1 + b], pk_recv.at[1 + b], chip_at(z, y, x_other),
        )

    pack_y = remote(
        pk_xsum.at[y_other], pk_y, pk_send.at[1 + ny], pk_recv.at[1 + ny], chip_at(z, y_other, x)
    )

    def pack_z(j):
        to = (z + j) % nz
        return remote(
            pk_ysum.at[:, pl.ds(pl.multiple_of(to * 128, 128), 128)], pk_z.at[z],
            pk_send.at[1 + ny + j], pk_recv.at[1 + ny + j], chip_at(to, y, x),
        )

    @pl.when(role == 0)
    def _():
        pack_twin.wait_send()

    @pl.when(role == 1)
    def _():
        pack_twin.wait_recv()

        def add(b, _):
            cut = pl.ds(pl.multiple_of(b * 128, 128), 128)
            total = pk_pair[:, cut].astype(F32) + pack[:, cut].astype(F32)
            pk_pair[:, cut] = rounded(total)
            return 0

        lax.fori_loop(0, pack.shape[1] // 128, add, 0)
        for b in range(ny):
            pack_x(b).start()

    def pack_after_x():
        for b in range(ny):
            pack_x(b).wait()
            first = pl.multiple_of((b * nx + x) * column_wide, 128)

            def add(c, _):
                here = pl.ds(pl.multiple_of(first + c * 128, 128), 128)
                cut = pl.ds(pl.multiple_of(c * 128, 128), 128)
                total = pk_pair[:, here].astype(F32) + pk_x[b, :, cut].astype(F32)
                pk_xsum[b, :, cut] = rounded(total)
                return 0

            lax.fori_loop(0, nz, add, 0)
        pack_y.start()

    def pack_after_y():
        pack_y.wait()

        def add(c, _):
            cut = pl.ds(pl.multiple_of(c * 128, 128), 128)
            total = pk_xsum[y, :, cut].astype(F32) + pk_y[:, cut].astype(F32)
            pk_ysum[:, cut] = rounded(total)
            return 0

        lax.fori_loop(0, nz, add, 0)
        for j in range(1, nz):
            pack_z(j).start()

    def pack_after_z():
        for j in range(1, nz):
            pack_z(j).wait()
        pk_z[z] = pk_ysum[:, pl.ds(pl.multiple_of(z * 128, 128), 128)]
        total = pk_z[0].astype(F32)
        for j in range(1, nz):
            total = total + pk_z[j].astype(F32)
        column[: total.shape[0], :] = rounded(total)

    def view_sp(which, k, first, count):
        rows = SP_CHUNKS[k]
        if which is not None:
            rows = (rows[0] + which * rows[1] // 2, rows[1] // 2)
        cut = pl.ds(pl.multiple_of(first * 128, 128), count * 128)
        return sp_out.at[role, pl.ds(*rows), cut]

    def view_li(which, k, first, count):
        rows = LI_CHUNKS[k]
        if which is not None:
            rows = (rows[0] + which * rows[1] // 2, rows[1] // 2)
        return li_all.at[pl.ds(first, count), pl.ds(*rows)]

    me = (role, z, y, x)
    sp = Gather(dims, me, view_sp, SP_CHUNKS, (sp_send, sp_recv))
    li = Gather(dims, me, view_li, LI_CHUNKS, (li_ag_send, li_ag_recv))

    def sp_last(k):
        ref = sp_out.at[role, pl.ds(*SP_CHUNKS[k])]
        return [remote(ref, ref, chip_send.at[2 + k], chip_recv.at[2 + k], twin)]

    def rows_of(j):
        return jnp.where(role == 1, SEGMENT * j, time_len - SEGMENT * (j + 1))

    def pack_columns(first_segment, last_segment):
        lane = lax.broadcasted_iota(jnp.int32, (SEGMENT, 128), 1)
        for j in range(first_segment, last_segment):
            rows = pl.ds(pl.multiple_of(rows_of(j), SEGMENT), SEGMENT)
            for b in range(width // 128):
                one = grad_pre[0, rows, b * 128 : (b + 1) * 128]
                two = grad_pre[1, rows, b * 128 : (b + 1) * 128]
                even = jnp.where(lane < 64, one, pltpu.roll(two, 64, 1))
                odd = jnp.where(lane < 64, pltpu.roll(one, 64, 1), two)
                li_send[2 * b, rows, :] = even.astype(BF16)
                li_send[2 * b + 1, rows, :] = odd.astype(BF16)

    def stream(n):
        first_segment, last_segment = STREAMS[n]
        count = SEGMENT * (last_segment - first_segment)
        begin = jnp.where(role == 1, SEGMENT * first_segment, time_len - SEGMENT * last_segment)
        rows = pl.ds(pl.multiple_of(begin, SEGMENT), count)

        def one(k):
            chip = (dp + k) % chips
            return remote(
                li_send.at[slot_of(chip), rows], li_got.at[dp, rows],
                li_aa_send.at[n, k - 1], li_aa_recv.at[n, k - 1], (role, chip),
            )

        return one

    def start_stream(n):
        pack_columns(*STREAMS[n])
        one = stream(n)
        lax.fori_loop(1, chips, lambda k, _: (one(k).start(), 0)[1], 0)

    def wait_stream(n):
        one = stream(n)
        lax.fori_loop(1, chips, lambda k, _: (one(k).wait(), 0)[1], 0)

    crossing.wait()
    grad_out[1 - role] = far_grad[...].astype(F32)
    zero = jnp.zeros((8, units), F32)
    carry = (zero, zero)

    def back_to_frames(rows):
        tile = lambda k, n: w_in[n * SIDE : (n + 1) * SIDE, k * SIDE : (k + 1) * SIDE]
        return staged_product(rows.astype(BF16), tile, w_in.shape[0] // SIDE, flip=True)

    def run(j, carry):
        return backward_steps(
            role, lengths, factors, grad_out, w_back, grad_pre, SEGMENT * j, SEGMENT, carry
        )

    carry = run(0, carry)
    pl.when(role == 1)(pack_after_x)
    carry = run(1, carry)
    pl.when(role == 1)(pack_after_y)

    lax.fori_loop(1, chips, lambda k, _: (block(k).wait(), 0)[1], 0)
    own_block.wait()
    load_acts.wait()
    both = got[...].reshape(chips * 2 * pads, 128).astype(F32)
    rolled = pltpu.roll(both, chips * 2 * pads - 1, 0)
    got_t[0] = jnp.transpose(both).astype(BF16)
    got_t[1] = jnp.transpose(rolled).astype(BF16)
    groups = acts_buf.shape[1] // 256
    for g in range(groups):
        cut = slice(g * 256, (g + 1) * 256)
        if g == 0:
            left = got_t[0]
        elif g < groups - cells // 256:
            left = got_t[1 - role]
        else:
            left = got_t[1]
        prod[:, cut] = staged_product(left, lambda k, n: acts_buf[k * SIDE : (k + 1) * SIDE, cut], 1)
    column[2 * SMALL :, :] = jnp.transpose(prod[...]).astype(BF16)
    column[: 2 * SMALL, :] = jnp.zeros((2 * SMALL, 128), BF16)

    def place(first, count):
        copy = pltpu.make_async_copy(
            column.at[pl.ds(first, count)], sp_out.at[role, pl.ds(first, count), lanes],
            local_sem.at[3],
        )
        copy.start()
        copy.wait()

    head = SP_CHUNKS[-1][1]
    place(head, column.shape[0] - head)
    for k in range(len(SP_CHUNKS) - 1):
        start(sp.first(k))

    carry = run(2, carry)
    pl.when(role == 1)(pack_after_z)
    place(0, head)
    start(sp.first(len(SP_CHUNKS) - 1))
    start_stream(0)
    far = jnp.where(role == 0, half_time, 0)
    near = half_time - far
    for u in range(utts):
        rows = pl.ds(pl.multiple_of(far, half_time), half_time)
        fr_send[u] = back_to_frames(grad_pre[u, rows, :]).astype(BF16)
    frames_copy = remote(fr_send, fr_got, chip_send.at[1], chip_recv.at[1], twin)
    frames_copy.start()
    wait(sp.first(0))
    start(sp.second(0))
    carry = run(3, carry)
    wait(sp.first(1))
    start(sp.second(1))
    wait(sp.second(0))
    start(sp.third(0))
    carry = run(4, carry)
    start_stream(1)
    wait(sp.first(2))
    start(sp.second(2))
    wait(sp.second(1))
    start(sp.third(1))
    carry = run(5, carry)
    start_stream(2)
    wait(sp.first(3))
    start(sp.second(3))
    wait(sp.second(2))
    start(sp.third(2))

    frames_copy.wait()
    feat = frames_out.shape[2]
    for u in range(utts):
        rows = pl.ds(pl.multiple_of(near, half_time), half_time)
        total = back_to_frames(grad_pre[u, rows, :]) + fr_got[u].astype(F32)
        for j in range(feat // 128):
            for half in range(2):
                cut = slice(half * feat + j * 128, half * feat + (j + 1) * 128)
                weave[pl.ds(half, half_time, stride=2), :] = total[:, cut]
            frames_out[u, :, j * 128 : (j + 1) * 128] = weave[...]

    li_got[dp] = li_send[slot]
    wait(load_rows)
    wait(load_pairs)
    for n in range(len(STREAMS)):
        wait_stream(n)

    def spread(c, _):
        value = li_got[c].astype(F32)
        for u, part in enumerate((value, pltpu.roll(value, 64, 1))):
            for p in range(time_len // PART):
                base = pl.multiple_of(((p * utts + u) * chips + slot_of(c)) * PART, PART)
                li_rows[pl.ds(base, PART), :] = part[p * PART : (p + 1) * PART].astype(BF16)
        return 0

    lax.fori_loop(0, chips, spread, 0)
    li_acc[...] = jnp.zeros_like(li_acc)
    deep = 4 * time_len
    features = pairs_buf.shape[1]

    def accumulate(c, _):
        rows = pl.ds(pl.multiple_of(c * deep, 256), deep)
        left = jnp.transpose(li_rows[rows, :])
        for source, base in ((pairs_buf, 0), (rows_buf, features)):
            piece = lambda k, n: source[
                pl.ds(pl.multiple_of(c * deep + k * SIDE, SIDE), SIDE), n * SIDE : (n + 1) * SIDE
            ]
            wide = source.shape[1]
            li_acc[:, base : base + wide] += staged_product(left, piece, wide // SIDE)
        return 0

    lax.fori_loop(0, chips * 2 * time_len // deep, accumulate, 0)
    flipped = jnp.transpose(li_acc[:, : features + units + 64])
    tall = flipped.shape[0] // 2
    lane = lax.broadcasted_iota(jnp.int32, (tall, 128), 1)
    packed = jnp.where(lane < 64, flipped[:tall], pltpu.roll(flipped[tall:], 64, 1))
    li_all[slot] = packed.astype(BF16)

    for k in range(len(LI_CHUNKS)):
        start(li.first(k))
    wait(sp.second(3))
    start(sp.third(3))
    wait(li.first(0))
    start(li.second(0))
    wait(sp.third(0))
    start(sp_last(0))
    wait(sp.third(1))
    start(sp_last(1))
    wait(li.first(1))
    start(li.second(1))
    wait(li.second(0))
    start(li.third(0))
    wait(sp.third(2))
    start(sp_last(2))
    wait(li.second(1))
    start(li.third(1))
    wait(sp.third(3))
    start(sp_last(3))
    wait(li.third(0))
    wait(li.third(1))

    def assemble(b, _):
        cut = pl.ds(pl.multiple_of(b * 128, 128), 128)
        even = li_all[2 * b].astype(F32)
        odd = li_all[2 * b + 1].astype(F32)
        li_out[:tall, cut] = jnp.where(lane < 64, even, pltpu.roll(odd, 64, 1)).astype(BF16)
        li_out[tall:, cut] = jnp.where(lane < 64, pltpu.roll(even, 64, 1), odd).astype(BF16)
        return 0

    lax.fori_loop(0, width // 128, assemble, 0)
    for k in range(len(SP_CHUNKS)):
        wait(sp_last(k))


def exchange(
    dims, lengths, factors, grad_mine, grad_other, w_in, w_rec, dp1, dp2, pack, acts_all,
    pairs_low, pairs_high, rows_all,
):
    utts, time_len, _ = factors.shape
    units = w_rec.shape[0]
    width = 4 * units
    pads, wide = dp1.shape
    cells = wide // 4
    chips = dims[0] * dims[1] * dims[2]
    span = acts_all.shape[1] - cells
    deep = sum(rows for _, rows in SP_CHUNKS)
    nz, ny, _ = dims
    packed = pack.shape[0]
    features = pairs_low.shape[1]
    total = features + units + 64
    feat = w_in.shape[0] // 2
    half_time = time_len // 2
    vmem = pl.BlockSpec(memory_space=pltpu.VMEM)
    anywhere = pl.BlockSpec(memory_space=pl.ANY)
    shape = jax.ShapeDtypeStruct
    dma = pltpu.SemaphoreType.DMA
    sp_sems = Gather.semaphores(dims, SP_CHUNKS)
    li_sems = Gather.semaphores(dims, LI_CHUNKS)
    return pl.pallas_call(
        functools.partial(exchange_kernel, dims),
        out_shape=(
            shape((utts, time_len, feat), F32),
            shape((total, width), BF16),
            shape((2, deep, wide), BF16),
        ),
        in_specs=[pl.BlockSpec(memory_space=pltpu.SMEM)] + [vmem] * 8 + [anywhere] * 4,
        out_specs=(vmem, vmem, anywhere),
        scratch_shapes=[
            pltpu.VMEM((utts, time_len, width), F32),
            pltpu.VMEM((utts, time_len, units), F32),
            pltpu.VMEM((acts_all.shape[0], span), BF16),
            pltpu.VMEM((chips * utts * time_len, features), BF16),
            pltpu.VMEM((chips * utts * time_len, 2 * SIDE), BF16),
            pltpu.VMEM((3, pads, wide), BF16),
            pltpu.VMEM((chips, 2, pads, 128), BF16),
            pltpu.VMEM((2, 128, chips * 2 * pads), BF16),
            pltpu.VMEM((128, span), F32),
            pltpu.VMEM((deep, 128), BF16),
            pltpu.VMEM((chips, time_len, 128), BF16),
            pltpu.VMEM((chips, time_len, 128), BF16),
            pltpu.VMEM((chips * 2 * time_len, 128), BF16),
            pltpu.VMEM((128, features + 2 * SIDE), F32),
            pltpu.VMEM((chips, total // 2, 128), BF16),
            pltpu.VMEM((utts, half_time, 2 * feat), BF16),
            pltpu.VMEM((utts, half_time, 2 * feat), BF16),
            pltpu.VMEM((time_len, 128), F32),
            pltpu.VMEM((packed, wide), BF16),
            pltpu.VMEM((ny, packed, nz * 128), BF16),
            pltpu.VMEM((ny, packed, nz * 128), BF16),
            pltpu.VMEM((packed, nz * 128), BF16),
            pltpu.VMEM((packed, nz * 128), BF16),
            pltpu.VMEM((nz, packed, 128), BF16),
            dma((5 + 2 * 4,)),
            dma((3 + len(SP_CHUNKS),)),
            dma((3 + len(SP_CHUNKS),)),
            dma((chips - 1,)),
            dma((chips - 1,)),
            dma((len(STREAMS), chips - 1)),
            dma((len(STREAMS), chips - 1)),
            sp_sems,
            sp_sems,
            li_sems,
            li_sems,
            dma((1 + ny + nz,)),
            dma((1 + ny + nz,)),
            pltpu.VMEM(grad_other.shape, BF16),
            pltpu.VMEM((width, units), BF16),
        ],
        compiler_params=pltpu.CompilerParams(
            vmem_limit_bytes=VMEM_BYTES, collective_id=0, has_side_effects=True
        ),
    )(
        lengths, factors, grad_mine, grad_other, w_in, w_rec, dp1, dp2, pack,
        acts_all, pairs_low, pairs_high, rows_all,
    )


PIECE = 128
SLOTS = 3


def widen_kernel(jobs, sizes, sp, li, *refs):
    *outs, narrow, wide, few, last, in_sem, out_sem, few_sem = refs
    g_out, g_table, low_bias, up_bias, g_vec, g_obias, sum_bias = outs[-7:]

    def source(n):
        which, row, col, out, _, rows = jobs[n]
        ref = li if which == 2 else sp.at[which]
        width = outs[out].shape[-1]
        return pltpu.make_async_copy(
            ref.at[pl.ds(row, rows), pl.ds(col, width)],
            narrow.at[n % SLOTS, pl.ds(0, rows), pl.ds(0, width)],
            in_sem.at[n % SLOTS],
        )

    def target(n):
        _, _, _, out, row, rows = jobs[n]
        width = outs[out].shape[-1]
        return pltpu.make_async_copy(
            wide.at[n % SLOTS, pl.ds(0, rows), pl.ds(0, width)],
            outs[out].at[pl.ds(row, rows)],
            out_sem.at[n % SLOTS],
        )

    load_few = [
        pltpu.make_async_copy(sp.at[1, pl.ds(0, 2 * SMALL)], few, few_sem.at[0]),
        pltpu.make_async_copy(li.at[pl.ds(sizes[-1], 16)], last, few_sem.at[1]),
    ]
    for n in range(min(SLOTS, len(jobs))):
        source(n).start()
    start(load_few)
    for n in range(len(jobs)):
        source(n).wait()
        if n >= SLOTS:
            target(n - SLOTS).wait()
        rows, width = jobs[n][5], outs[jobs[n][3]].shape[-1]
        wide[n % SLOTS, :rows, :width] = narrow[n % SLOTS, :rows, :width].astype(F32)
        target(n).start()
        if n + SLOTS < len(jobs):
            source(n + SLOTS).start()
    wait(load_few)
    small = few[:SMALL].astype(F32) + few[SMALL:].astype(F32)
    cells, base, embed, att, vocab, _ = sizes
    g_out[...] = small[:vocab, :base]
    g_table[...] = small[:vocab, base : base + embed]
    base += embed
    for k in range(4):
        cut = slice(k * cells, (k + 1) * cells)
        low_bias[cut] = small[2 + k, base : base + cells]
        up_bias[cut] = small[6 + k, base : base + cells]
    g_vec[...] = small[0, base : base + att]
    g_obias[...] = small[1, base : base + vocab]
    sum_bias[...] = last[0:1, :].astype(F32)
    for n in range(max(0, len(jobs) - SLOTS), len(jobs)):
        target(n).wait()


def widen(sp, li, parts, sizes):
    jobs = []
    for out, (_, pieces) in enumerate(parts):
        done = 0
        for which, row, col, rows in pieces:
            for at in range(0, rows, PIECE):
                count = min(PIECE, rows - at)
                jobs.append((which, row + at, col, out, done, count))
                done += count
    cells, base, embed, att, vocab, _ = sizes
    wide = sp.shape[2]
    anywhere = pl.BlockSpec(memory_space=pl.ANY)
    vmem = pl.BlockSpec(memory_space=pltpu.VMEM)
    dma = pltpu.SemaphoreType.DMA
    few = ((vocab, base), (vocab, embed), (4 * cells,), (4 * cells,), (att,), (vocab,), (1, li.shape[1]))
    return pl.pallas_call(
        functools.partial(widen_kernel, jobs, sizes),
        out_shape=[jax.ShapeDtypeStruct(shape, F32) for shape, _ in parts]
        + [jax.ShapeDtypeStruct(shape, F32) for shape in few],
        in_specs=[anywhere] * 2,
        out_specs=[anywhere] * len(parts) + [vmem] * len(few),
        scratch_shapes=[
            pltpu.VMEM((SLOTS, PIECE, wide), BF16),
            pltpu.VMEM((SLOTS, PIECE, wide), F32),
            pltpu.VMEM((2 * SMALL, wide), BF16),
            pltpu.VMEM((16, li.shape[1]), BF16),
            dma((SLOTS,)),
            dma((SLOTS,)),
            dma((2,)),
        ],
        compiler_params=pltpu.CompilerParams(vmem_limit_bytes=VMEM_BYTES),
    )(sp, li)


def shards(
    frames,
    step_lengths,
    characters,
    char_lengths,
    listen_input,
    listen_hidden,
    listen_bias,
    lower_input,
    lower_hidden,
    lower_bias,
    upper_input,
    upper_hidden,
    upper_bias,
    key_proj,
    query_proj,
    score_vector,
    output_proj,
    output_bias,
    char_table,
):
    chips = lax.axis_size("dp")
    utts, frame_len, feat = frames.shape
    time_len = frame_len // 2
    swap = [(0, 1), (1, 0)]
    w_in, w_rec = listen_input[0], listen_hidden[0]
    units = w_rec.shape[0]
    cells = lower_hidden.shape[0]
    vocab, embed = char_table.shape
    fits = (
        chips % 4 == 0
        and 4 * cells == 128 * chips
        and 4 * units == 64 * chips
        and embed == 256
        and cells == 2 * units
        and time_len == SEGMENT * STREAMS[-1][1]
        and embed + 2 * units + cells + 2 * SMALL == sum(rows for _, rows in SP_CHUNKS)
        and embed + 2 * SMALL == SP_CHUNKS[-1][1]
        and time_len == 3 * PART
        and characters.shape[2] % SPELL_GROUPS == 0
        and 2 * feat + units + 64 == 2 * sum(rows for _, rows in LI_CHUNKS)
    )
    dims = (chips // 4, 2, 2) if fits else None
    pairs, rows, factors, mine, other, *low_pairs = listen_forward(
        dims, step_lengths, frames, w_in, w_rec, listen_bias
    )
    if not fits:
        other = lax.ppermute(other, "role", swap)
    vec = score_vector
    loss, prev_onehot, acts, key, *kept = speller_forward(
        dims, step_lengths, char_lengths, characters, pairs, rows, mine, other,
        lower_input, lower_hidden, lower_bias, upper_input, upper_hidden, upper_bias,
        key_proj, query_proj, vec, output_proj.T, output_bias, char_table,
    )
    if fits:
        *kept, high_pairs, rows_all = kept
    grad_mine, grad_other, dp1, dp2, pack = speller_backward(
        lower_input, lower_hidden, upper_input, upper_hidden, key_proj, query_proj, vec,
        prev_onehot, acts, key, *kept,
    )
    if fits:
        flat = lambda gathered: gathered.reshape(-1, gathered.shape[-1])
        acts_all = lax.all_gather(acts, ("dp", "role"), tiled=True)
        frame_grad, li, sp = exchange(
            dims, step_lengths, factors, grad_mine, grad_other, w_in, w_rec,
            dp1, dp2, pack, acts_all, flat(low_pairs[0]), flat(high_pairs), flat(rows_all),
        )
        width = 2 * feat
        att = key_proj.shape[1]
        first = 2 * SMALL
        low, high = first + embed, first + embed + 2 * units
        wide = 4 * cells
        deep = 2 * units * att // wide
        folded = lambda row: tuple((1, row, col, deep) for col in range(0, wide, att))
        *layers, sum_in, sum_rec, g_key, g_query, g_out, g_table, low_bias, up_bias, g_vec, g_obias, sum_bias = widen(
            sp,
            li,
            (
                ((high - first, wide), ((0, first, 0, high - first),)),
                ((cells, wide), ((0, high, 0, cells),)),
                ((cells, wide), ((1, low, 0, cells),)),
                ((cells, wide), ((1, low + cells, 0, cells),)),
                ((width, 4 * units), ((2, 0, 0, width),)),
                ((units, 4 * units), ((2, width, 0, units),)),
                ((2 * units, att), folded(first)),
                ((cells, att), folded(first + deep)),
            ),
            (cells, cells + 2 * units, embed, att, vocab, width + units),
        )
        lower, upper = layers[:2], layers[2:]
        g_out = g_out.T
    else:
        grad_other = lax.ppermute(grad_other, "role", swap)
        pack = lax.psum(pack.astype(F32), ("role", "dp"))
        small = pack[: 2 * SMALL]
        g_key, g_query = (
            unfold(part, cells) for part in jnp.split(pack[2 * SMALL :], 2, axis=0)
        )
        low_bias, up_bias, g_vec, g_out, g_obias, g_table = unpack(
            small, units, cells, key_proj.shape[1], vocab, embed
        )
        pre = listen_backward(step_lengths, factors, grad_mine, grad_other, w_rec)
        flat = pre.reshape(utts * time_len, 4 * units)
        sums = mm(jnp.concatenate([pairs.reshape(flat.shape[0], 2 * feat), rows], 1).T, flat)
        sums = lax.psum(sums, "dp")
        width = 2 * feat
        sum_in, sum_rec = sums[:width], sums[width : width + units]
        sum_bias = lax.psum(jnp.sum(flat.astype(F32), 0, keepdims=True), "dp")
        grad_pairs = mm(flat, w_in.T).reshape(utts, frame_len, feat)
        frame_grad = lax.psum_scatter(grad_pairs, "role", scatter_dimension=1, tiled=True)
        cuts = [embed, embed + 2 * units, embed + 2 * units + cells]
        emb, ctx, s1, s2 = jnp.split(acts, cuts, axis=1)
        local = (
            jnp.concatenate([mm(emb.T, dp1), mm(ctx[:-1].T, dp1[1:])], 0),
            mm(s1[:-1].T, dp1[1:]),
            mm(s1.T, dp2),
            mm(s2[:-1].T, dp2[1:]),
        )
        local = lax.psum(local, ("role", "dp"))
        lower, upper = local[:2], local[2:]
    return (
        loss, frame_grad, sum_in[None], sum_rec[None], sum_bias,
        *lower, low_bias, *upper, up_bias,
        g_key, g_query, g_vec, g_out, g_obias, g_table,
    )


def solution(mesh):
    whole = P()
    return jax.shard_map(
        shards,
        mesh=mesh,
        in_specs=(
            P("dp", None, None),
            P("dp"),
            P("dp", "role", None),
            P("dp", "role"),
            P("role", None, None),
            P("role", None, None),
            P("role", None),
        )
        + (whole,) * 12,
        out_specs=(
            P("dp", "role"),
            P("dp", "role", None),
            P("role", None, None),
            P("role", None, None),
            P("role", None),
        )
        + (whole,) * 12,
        check_vma=False,
    )
```

```python
import functools

import jax
import jax.numpy as jnp
from jax import lax
from jax.experimental import pallas as pl
from jax.experimental.pallas import tpu as pltpu
from jax.sharding import PartitionSpec as P

F32 = jnp.float32
BF16 = jnp.bfloat16
VMEM_BYTES = 60 * 1024 * 1024


def mm(left, right):
    return jnp.dot(left, right, preferred_element_type=F32)


def mm_nt(left, right):
    return lax.dot_general(left, right, (((1,), (1,)), ((), ())), preferred_element_type=F32)


def mm_tn(left, right):
    return lax.dot_general(left, right, (((0,), (0,)), ((), ())), preferred_element_type=F32)


def sigmoid(x):
    return 0.5 * jnp.tanh(0.5 * x) + 0.5


def cell_forward(preact, cell_prev):
    n = preact.shape[-1] // 4
    in_gate = sigmoid(preact[:, :n])
    forget = sigmoid(preact[:, n : 2 * n])
    candid = jnp.tanh(preact[:, 2 * n : 3 * n])
    out_gate = sigmoid(preact[:, 3 * n :])
    cell_new = forget * cell_prev + in_gate * candid
    tanh_cell = jnp.tanh(cell_new)
    hidden = out_gate * tanh_cell
    factors = (
        candid * in_gate * (1.0 - in_gate),
        cell_prev * forget * (1.0 - forget),
        in_gate * (1.0 - candid * candid),
        tanh_cell * out_gate * (1.0 - out_gate),
        out_gate * (1.0 - tanh_cell * tanh_cell),
        forget,
    )
    return cell_new, hidden, factors


def cell_backward(factors, grad_hidden, grad_cell):
    n = factors.shape[-1] // 6
    part = lambda k: factors[:, k * n : (k + 1) * n]
    total = grad_cell + grad_hidden * part(4)
    grad_preact = jnp.concatenate(
        [total * part(0), total * part(1), total * part(2), grad_hidden * part(3)], -1
    )
    return grad_preact, total * part(5)


def remote(src, dst, send, recv, device):
    return pltpu.make_async_remote_copy(
        src_ref=src, dst_ref=dst, send_sem=send, recv_sem=recv,
        device_id=device, device_id_type=pl.DeviceIdType.MESH,
    )


def start(copies):
    for copy in copies:
        copy.start()


def wait(copies):
    for copy in copies:
        copy.wait()


class Gather:
    def __init__(self, dims, me, view, chunks, sems):
        self.dims, self.view, self.chunks = dims, view, chunks
        self.role, self.z, self.y, self.x = me
        self.send, self.recv = sems

    def device(self, z, y, x):
        _, ny, nx = self.dims
        return (self.role, (z * ny + y) * nx + x)

    def copies(self, k, which, spans, others, base):
        out = []
        for device in others:
            for span in spans:
                ref = self.view(which, k, *span)
                out.append(
                    remote(ref, ref, self.send.at[k, base], self.recv.at[k, base], device)
                )
                base += 1
        return out

    def along_x(self):
        nx = self.dims[2]
        return [self.device(self.z, self.y, (self.x + j) % nx) for j in range(1, nx)]

    def along_y(self):
        ny = self.dims[1]
        return [self.device(self.z, (self.y + j) % ny, self.x) for j in range(1, ny)]

    def first(self, k):
        nz, ny, nx = self.dims
        slot = (self.y * nx + self.x) * nz + self.z
        others = [self.device((self.z + j) % nz, self.y, self.x) for j in range(1, nz)]
        return self.copies(k, None, [(slot, 1)], others, 0)

    def second(self, k):
        nz, ny, nx = self.dims
        column = ((self.y * nx + self.x) * nz, nz)
        base = nz - 1
        to_x = self.copies(k, 0, [column], self.along_x(), base)
        return to_x + self.copies(k, 1, [column], self.along_y(), base + nx - 1)

    def third(self, k):
        nz, ny, nx = self.dims
        base = nz - 1 + nx - 1 + ny - 1
        to_y = self.copies(k, 0, [(self.y * nx * nz, nx * nz)], self.along_y(), base)
        spans = [((b * nx + self.x) * nz, nz) for b in range(ny)]
        return to_y + self.copies(k, 1, spans, self.along_x(), base + ny - 1)

    @staticmethod
    def semaphores(dims, chunks):
        nz, ny, nx = dims
        count = nz - 1 + 2 * (nx - 1) + 2 * (ny - 1) + (nx - 1) * (ny - 1)
        return pltpu.SemaphoreType.DMA((len(chunks), count))


PART = 64
LISTEN_GROUPS = 16
LISTEN_CHUNKS = ((0, 0, 32), (0, 32, 32))
LISTEN_EVENTS = (
    ((), ((0, 0), (0, 1))),
    ((), ()),
    ((), ()),
    ((), ()),
    (((0, 0),), ((1, 0),)),
    ((), ()),
    ((), ()),
    (((1, 0), (0, 1)), ((2, 0), (1, 1))),
    ((), ()),
    ((), ()),
    ((), ()),
    (((2, 0),), ((3, 0),)),
    ((), ()),
    (((1, 1),), ((2, 1),)),
    ((), ()),
    ((), ()),
    (((2, 1),), ((3, 1),)),
)
SPELL_GROUPS = 18
SPELL_CHUNKS = ((0, 0, PART), (1, 0, PART))
SPELL_EVENTS = (
    ((), ((0, 0), (0, 1))),
    ((), ()),
    (((0, 0),), ((1, 0), (0, 2))),
    (((0, 1),), ((1, 1), (0, 3))),
    (((1, 0),), ((2, 0),)),
    (((1, 1), (0, 2)), ((2, 1), (1, 2), (0, 4))),
    (((2, 0),), ()),
    (((0, 3), (2, 1)), ((1, 3),)),
    (((1, 2),), ((2, 2),)),
    (((1, 3),), ((2, 3),)),
    (((0, 4),), ((1, 4),)),
    (((2, 2),), ()),
    ((), ()),
    (((2, 3),), ((3, 3),)),
    (((1, 4),), ((2, 4),)),
    ((), ()),
    ((), ()),
    (((2, 4),), ((3, 4),)),
    ((), ()),
)


class Gathers:
    def __init__(self, dims, role, dp, events, frames, chunks, states, sems):
        nz, ny, nx = dims
        me = (role, dp // (ny * nx), (dp // nx) % ny, dp % nx)
        self.twin = (1 - role, dp)
        self.role, self.frames, self.chunks, self.events = role, frames, chunks, events
        send, recv, self.last_send, self.last_recv = sems[:4]
        self.slot = (me[2] * nx + me[3]) * nz + me[1]

        def half(first, count, which):
            if which is not None:
                first, count = first + which * count // 2, count // 2
            return pl.ds(first, count)

        def view_frames(which, k, first, count):
            part, *rows = chunks[k]
            return frames.at[part, role, pl.ds(first, count), half(*rows, which)]

        self.two = Gather(dims, me, view_frames, chunks, (send, recv))
        self.lead = 0
        if states is not None:
            self.lead = states.shape[0]

            def view_states(which, k, first, count):
                rows = half(0, states.shape[3], which)
                return states.at[k, :, pl.ds(first, count), rows]

            self.one = Gather(dims, me, view_states, range(self.lead), sems[4:])
        g = self.two
        to_z = [g.device((g.z + j) % nz, g.y, g.x) for j in range(1, nz)]
        self.partners = to_z + g.along_x() + g.along_y() + [self.twin]

    def greet(self):
        barrier = pltpu.get_barrier_semaphore()
        for device in self.partners:
            pl.semaphore_signal(
                barrier, inc=1, device_id=device, device_id_type=pl.DeviceIdType.MESH
            )

    def phase(self, n, c):
        if n == 3:
            k = c - self.lead
            part, *rows = self.chunks[k]
            ref = self.frames.at[part, self.role, :, pl.ds(*rows)]
            return [remote(ref, ref, self.last_send.at[k], self.last_recv.at[k], self.twin)]
        gather, k = (self.one, c) if c < self.lead else (self.two, c - self.lead)
        return (gather.first, gather.second, gather.third)[n](k)

    def begin(self):
        pl.semaphore_wait(pltpu.get_barrier_semaphore(), len(self.partners))

    def look(self, group):
        ended, begun = self.events[group]
        for n, c in ended:
            wait(self.phase(n, c))
        for n, c in begun:
            start(self.phase(n, c))

    def finish(self):
        for k in range(len(self.chunks)):
            wait(self.phase(3, self.lead + k))

    @staticmethod
    def scratch(dims, chunks, states):
        dma = pltpu.SemaphoreType.DMA
        sems = [Gather.semaphores(dims, chunks)] * 2 + [dma((len(chunks),))] * 2
        if states:
            sems += [Gather.semaphores(dims, range(states))] * 2
        return sems


def stage(tiles):
    for k in range(2):
        for unit in range(2):
            pltpu.matmul_push_rhs(tiles(2 * unit + k), k, unit)


def multiply(totals, lefts):
    share = 4 // len(totals)
    for k in range(2):
        for unit in range(2):
            j = 2 * unit + k
            pltpu.matmul_acc_lhs(totals[j // share], lefts[j], load_staged_rhs=k)


SIDE = 256


def staged_product(left, tile, columns, flip=False):
    deep = left.shape[1] // SIDE

    def run(*totals):
        parts = []
        for n in range(0, columns, 2):
            units = range(min(2, columns - n))
            for k in range(deep):
                for unit in units:
                    pltpu.matmul_push_rhs(tile(k, n + unit), k % 2, unit, transpose=flip)
                    pltpu.matmul_acc_lhs(
                        totals[unit], left[:, k * SIDE : (k + 1) * SIDE], load_staged_rhs=k % 2
                    )
            parts += [pltpu.matmul_pop(totals[unit]) for unit in units]
        return jnp.concatenate(parts, 1) if len(parts) > 1 else parts[0]

    rows = left.shape[0]
    return pl.run_scoped(run, *[pltpu.ACC(mxu_id=unit)((rows, SIDE), F32) for unit in range(2)])


def tiles_of(ref):
    return lambda k, n: ref[k * SIDE : (k + 1) * SIDE, n * SIDE : (n + 1) * SIDE]


def staged_loop(first, last, step, carry, tiles, outputs):
    side = tiles(0).shape[0]

    def run(*totals):
        def product(left):
            tall = jnp.concatenate([left, jnp.zeros_like(left)], 0).astype(BF16)
            wide = tall.shape[1] // side
            multiply(totals, [tall[:, (j % wide) * side : (j % wide + 1) * side] for j in range(4)])
            stage(tiles)
            return [pltpu.matmul_pop(total)[: left.shape[0]] for total in totals]

        stage(tiles)
        end = lax.fori_loop(first, last, lambda s, c: step(product, s, c), carry)
        multiply(totals, [jnp.zeros((16, side), BF16)] * 4)
        for total in totals:
            pltpu.matmul_pop(total)
        return end

    units = [j * 2 // outputs for j in range(outputs)]
    return pl.run_scoped(run, *[pltpu.ACC(mxu_id=unit)((16, side), F32) for unit in units])


def listen_forward_kernel(
    dims, lengths, frames, w_in, w_rec, bias,
    pairs, rows_out, factors_out, mine_out, other_out, *rest
):
    role = lax.axis_index("role")
    if dims is not None:
        pairs_all, proj, emit, hprev, to_other, cross, *sems = rest
        gather = Gathers(
            dims, role, lax.axis_index("dp"), LISTEN_EVENTS, pairs_all, LISTEN_CHUNKS, None, sems
        )
        gather.greet()
    else:
        proj, emit, hprev = rest
    utts, time_len, width4 = proj.shape
    units = width4 // 4
    feat = frames.shape[-1]
    window = 2 * time_len - SIDE
    rows = lax.broadcasted_iota(jnp.int32, (time_len, 2 * SIDE), 0)
    cols = lax.broadcasted_iota(jnp.int32, (time_len, 2 * SIDE), 1)
    frame = jnp.where(cols < SIDE, cols, cols - SIDE + window)
    own = jnp.logical_or(cols < SIDE, frame >= SIDE)
    for half in range(2):
        pick = jnp.where(jnp.logical_and(own, frame == 2 * rows + half), 1.0, 0.0).astype(BF16)
        for u in range(utts):
            tile = lambda k, n: frames[
                u, k * window : k * window + SIDE, n * SIDE : (n + 1) * SIDE
            ]
            picked = staged_product(pick, tile, feat // SIDE)
            pairs[u, :, half * feat : (half + 1) * feat] = picked.astype(BF16)
    if dims is not None:
        place = pltpu.make_async_copy(
            pairs.at[role, pl.ds(0, PART)], pairs_all.at[0, role, gather.slot], cross.at[2]
        )
        place.start()
    bias_row = bias[...].astype(F32)
    for u in range(utts):
        proj[u] = staged_product(pairs[u], tiles_of(w_in), width4 // SIDE) + bias_row
    if dims is not None:
        place.wait()
        gather.begin()
    first = lax.broadcasted_iota(jnp.int32, (8, 1), 0) == 0
    row_lengths = jnp.where(first, lengths[0], lengths[1])

    tiles = lambda j: w_rec[:, j * units : (j + 1) * units]

    def step(product, s, carry):
        hidden, cell = carry
        t = jnp.where(role == 1, time_len - 1 - s, s)
        at = pl.ds(t, 1)
        pre_in = jnp.where(first, proj[0, at, :], proj[1, at, :])
        preact = pre_in + jnp.concatenate(product(hidden), 1)
        cell_new, hidden_new, factors = cell_forward(preact, cell)
        live = t < row_lengths
        hidden_next = jnp.where(live, hidden_new, hidden)
        cell_next = jnp.where(live, cell_new, cell)
        emitted = jnp.where(live, hidden_new, 0.0)
        for u in range(2):
            for k in range(6):
                factors_out[u, at, k * units : (k + 1) * units] = factors[k][u : u + 1]
            hprev[u, at, :] = hidden[u : u + 1]
            emit[u, at, :] = emitted[u : u + 1]
        return hidden_next, cell_next

    zero = jnp.zeros((8, units), F32)
    carry = (zero, zero)
    if dims is None:
        staged_loop(0, time_len, step, carry, tiles, 4)
    else:
        count = time_len // LISTEN_GROUPS
        for group in range(LISTEN_GROUPS):
            gather.look(group)
            carry = staged_loop(group * count, (group + 1) * count, step, carry, tiles, 4)
    mine_out[...] = emit[role].astype(BF16)
    if dims is None:
        other_out[...] = emit[1 - role].astype(BF16)
    else:
        to_other[...] = emit[1 - role].astype(BF16)
        crossing = remote(to_other, other_out, cross.at[0], cross.at[1], gather.twin)
        crossing.start()
        gather.look(LISTEN_GROUPS)
    for u in range(utts):
        own = slice(u * time_len, (u + 1) * time_len)
        rows_out[own, :] = hprev[u].astype(BF16)
    if dims is not None:
        crossing.wait()
        gather.finish()


def listen_forward(dims, lengths, frames, w_in, w_rec, bias):
    utts, time_len, width = frames.shape[0], frames.shape[1] // 2, 2 * frames.shape[2]
    units = w_rec.shape[0]
    vmem = pl.BlockSpec(memory_space=pltpu.VMEM)
    shape = jax.ShapeDtypeStruct
    outs = [
        shape((utts, time_len, width), BF16),
        shape((utts * time_len, units), BF16),
        shape((utts, time_len, 6 * units), F32),
        shape((time_len, units), BF16),
        shape((time_len, units), BF16),
    ]
    out_specs = [vmem] * 5
    scratch = [
        pltpu.VMEM((utts, time_len, 4 * units), F32),
        pltpu.VMEM((utts, time_len, units), F32),
        pltpu.VMEM((utts, time_len, units), F32),
    ]
    params = dict(vmem_limit_bytes=VMEM_BYTES)
    if dims is not None:
        chips = dims[0] * dims[1] * dims[2]
        outs.append(shape((1, 2, chips, PART, width), BF16))
        out_specs.append(pl.BlockSpec(memory_space=pl.ANY))
        scratch += [pltpu.VMEM((time_len, units), BF16), pltpu.SemaphoreType.DMA((3,))]
        scratch += Gathers.scratch(dims, LISTEN_CHUNKS, 0)
        params.update(collective_id=1, has_side_effects=True)
    return pl.pallas_call(
        functools.partial(listen_forward_kernel, dims),
        out_shape=outs,
        in_specs=[pl.BlockSpec(memory_space=pltpu.SMEM)] + [vmem] * 4,
        out_specs=out_specs,
        scratch_shapes=scratch,
        compiler_params=pltpu.CompilerParams(**params),
    )(lengths, frames, w_in, w_rec, bias)


def speller_forward_kernel(
    dims, lengths, text_lens, chars, pairs, states,
    mine, other,
    w_lin, w_lhid, b_low, w_uin, w_uhid, b_up, w_key, w_query, vec, w_out, b_out, table,
    loss, prev_onehot, acts, key, keys_proj, key_low, fact1, fact2, q_rows, w_cols, feat_rows, dw_cols,
    logit_grad_out, *rest
):
    role = lax.axis_index("role")
    gather = None
    if dims is not None:
        pairs_all, states_all, emb_proj, s1_rows, s2_rows, hot, stage, own_sem, *sems = rest
        gather = Gathers(
            dims, role, lax.axis_index("dp"), SPELL_EVENTS, pairs_all, SPELL_CHUNKS, states_all, sems
        )
        gather.greet()
        load = pltpu.make_async_copy(
            pairs.at[role, pl.ds(PART, stage.shape[0])], stage, own_sem.at[0]
        )
        load.start()
        parts, utts = states_all.shape[:2]
        place = [
            pltpu.make_async_copy(
                states.at[pl.ds((u * parts + part) * PART, PART)],
                states_all.at[part, u, gather.slot],
                own_sem.at[1 + u * parts + part],
            )
            for u in range(utts)
            for part in range(parts)
        ]
        start(place)
        staged = [
            pltpu.make_async_copy(
                stage.at[pl.ds(part * PART, PART)],
                pairs_all.at[part, role, gather.slot],
                own_sem.at[1 + len(place) + part],
            )
            for part in range(pairs_all.shape[0])
        ]
    else:
        emb_proj, s1_rows, s2_rows, hot = rest
    time_len, units = mine.shape
    steps = emb_proj.shape[0]
    cells = w_lhid.shape[0]
    embed = table.shape[1]
    length = lengths[role]
    text_len = text_lens[0, 0]

    key[:, :units] = jnp.where(role == 0, mine[...], other[...])
    key[:, units:] = jnp.where(role == 0, other[...], mine[...])
    keys_proj[...] = mm(key[...], w_key[...])
    if gather is not None:
        load.wait()
        start(staged)
    key_low[...] = mm(key[...], w_lin[embed:, :])
    ids = lax.broadcasted_iota(jnp.int32, (1, hot.shape[2]), 1)

    def mark(i, previous):
        here = chars[0, 0, i]
        hot[0, pl.ds(i, 1), :] = jnp.where(ids == previous, 1.0, 0.0)
        hot[1, pl.ds(i, 1), :] = jnp.where(ids == here, 1.0, 0.0)
        return here

    lax.fori_loop(0, steps, mark, 0)
    prev_onehot[...] = hot[0].astype(BF16)
    emb = mm(prev_onehot[...], table[...]).astype(BF16)
    emb_proj[...] = mm(emb, w_lin[:embed, :]) + b_low[...].astype(F32)[None]
    bias_up = b_up[...].astype(F32)[None]
    vec_row = vec[...].astype(F32)[None]
    frame_ok = lax.broadcasted_iota(jnp.int32, (time_len, 1), 0) < length
    lane = lax.broadcasted_iota(jnp.int32, w_cols.shape, 1)
    w_cols[...] = jnp.zeros_like(w_cols)
    if gather is not None:
        wait(place)
        wait(staged)
        gather.begin()

    def forward_step(i, carry):
        cell1, cell2, hid1, hid2, ctx_low = carry
        at = pl.ds(i, 1)
        pre1 = emb_proj[at, :] + hid1 + ctx_low
        cell1, s1, factors = cell_forward(pre1, cell1)
        for k in range(6):
            fact1[at, k * cells : (k + 1) * cells] = factors[k]
        s1_rows[at, :] = s1
        s1_low = s1.astype(BF16)
        pre2 = hid2 + bias_up + mm(s1_low, w_uin[...])
        hid1 = mm(s1_low, w_lhid[...])
        cell2, s2, factors = cell_forward(pre2, cell2)
        for k in range(6):
            fact2[at, k * cells : (k + 1) * cells] = factors[k]
        s2_rows[at, :] = s2
        s2_low = s2.astype(BF16)
        query = mm(s2_low, w_query[...])
        hid2 = mm(s2_low, w_uhid[...])
        q_rows[at, :] = query
        part = None
        for j in range(query.shape[1] // 128):
            cut = slice(j * 128, (j + 1) * 128)
            term = jnp.tanh(keys_proj[:, cut] + query[:, cut]) * vec_row[:, cut]
            part = term if part is None else part + term
        scores = jnp.sum(part, -1, keepdims=True)
        scores = jnp.where(frame_ok, scores, -1000000000.0)
        scores = scores - jnp.max(scores, 0, keepdims=True)
        expf = jnp.where(frame_ok, jnp.exp(scores), 0.0)
        rinv = 1.0 / jnp.sum(expf, 0, keepdims=True)
        w_cols[...] = jnp.where(lane == i, expf * rinv, w_cols[...])
        ctx_low = jnp.concatenate(
            [
                jnp.sum(expf * key_low[:, j * 128 : (j + 1) * 128], 0, keepdims=True)
                for j in range(key_low.shape[1] // 128)
            ],
            1,
        )
        return cell1, cell2, hid1, hid2, ctx_low * rinv

    zero = jnp.zeros((1, cells), F32)
    wide = jnp.zeros((1, 4 * cells), F32)
    carry = (zero, zero, wide, wide, wide)
    if gather is None:
        lax.fori_loop(0, steps, forward_step, carry)
    else:
        count = steps // SPELL_GROUPS
        for group in range(SPELL_GROUPS):
            gather.look(group)
            carry = lax.fori_loop(group * count, (group + 1) * count, forward_step, carry)
        gather.look(SPELL_GROUPS)

    w_low = jnp.transpose(w_cols[...])[:steps].astype(BF16)
    ctx = mm(w_low, key[...]).astype(BF16)
    s2_low = s2_rows[...].astype(BF16)
    logits = mm_nt(s2_low, w_out[:, :cells]) + mm_nt(ctx, w_out[:, cells:]) + b_out[...].astype(F32)[None]
    top = jnp.max(logits, -1, keepdims=True)
    log_total = top + jnp.log(jnp.sum(jnp.exp(logits - top), -1, keepdims=True))
    target = hot[1]
    cross = log_total - jnp.sum(logits * target, -1, keepdims=True)
    text = text_len.astype(F32)
    alive = lax.broadcasted_iota(jnp.int32, (steps, 1), 0) < text_len
    loss[...] = jnp.sum(jnp.where(alive, cross, 0.0), 0, keepdims=True) / text
    scale = jnp.where(alive, 1.0 / text, 0.0)
    logit_grad = (scale * (jnp.exp(logits - log_total) - target)).astype(BF16)
    logit_grad_out[...] = logit_grad
    feat_rows[...] = mm(logit_grad, w_out[...])
    dw_cols[...] = jnp.zeros_like(dw_cols)
    dw_cols[:, :steps] = mm_nt(key[...], feat_rows[:, cells:].astype(BF16))
    acts[steps:, :] = jnp.zeros((acts.shape[0] - steps, acts.shape[1]), BF16)
    acts[:steps, :embed] = emb
    acts[:steps, embed : embed + 2 * units] = ctx
    acts[:steps, embed + 2 * units : embed + 2 * units + cells] = s1_rows[...].astype(BF16)
    acts[:steps, embed + 2 * units + cells :] = s2_low
    if gather is not None:
        gather.finish()


def speller_forward(
    dims, lengths, text_lens, chars, pairs, states, mine, other,
    w_lin, w_lhid, b_low, w_uin, w_uhid, b_up, w_key, w_query, vec, w_out, b_out, table,
):
    time_len, units = mine.shape
    steps, vocab = chars.shape[2], table.shape[0]
    cells = w_lhid.shape[0]
    att = w_key.shape[1]
    embed = table.shape[1]
    pad_steps = -(-steps // 16) * 16
    vmem = pl.BlockSpec(memory_space=pltpu.VMEM)
    smem = pl.BlockSpec(memory_space=pltpu.SMEM)
    shape = jax.ShapeDtypeStruct
    outs = [
        shape((1, 1), F32),
        shape((steps, vocab), BF16),
        shape((pad_steps, embed + 2 * units + 2 * cells), BF16),
        shape((time_len, 2 * units), BF16),
        shape((time_len, att), F32),
        shape((time_len, 4 * cells), F32),
        shape((steps, 6 * cells), F32),
        shape((steps, 6 * cells), F32),
        shape((steps, att), F32),
        shape((time_len, -(-steps // 128) * 128), F32),
        shape((steps, w_out.shape[1]), F32),
        shape((time_len, -(-steps // 128) * 128), F32),
        shape((steps, vocab), BF16),
    ]
    out_specs = [vmem] * len(outs)
    scratch = [
        pltpu.VMEM((steps, 4 * cells), F32),
        pltpu.VMEM((steps, cells), F32),
        pltpu.VMEM((steps, cells), F32),
        pltpu.VMEM((2, steps, vocab), F32),
    ]
    params = dict(vmem_limit_bytes=VMEM_BYTES)
    if dims is not None:
        chips = dims[0] * dims[1] * dims[2]
        dma = pltpu.SemaphoreType.DMA
        utts, _, width = pairs.shape
        parts = time_len // PART
        high = parts - 1
        outs.append(shape((high, utts, chips, PART, width), BF16))
        outs.append(shape((parts, utts, chips, PART, units), BF16))
        out_specs += [pl.BlockSpec(memory_space=pl.ANY)] * 2
        scratch += [pltpu.VMEM((high * PART, width), BF16), dma((1 + high + utts * parts,))]
        scratch += Gathers.scratch(dims, SPELL_CHUNKS, parts)
        params.update(collective_id=2, has_side_effects=True)
    return pl.pallas_call(
        functools.partial(speller_forward_kernel, dims),
        out_shape=outs,
        in_specs=[smem] * 3 + [pl.BlockSpec(memory_space=pl.ANY)] + [vmem] * 15,
        out_specs=out_specs,
        scratch_shapes=scratch,
        compiler_params=pltpu.CompilerParams(**params),
    )(
        lengths, text_lens, chars, pairs, states, mine, other,
        w_lin, w_lhid, b_low, w_uin, w_uhid, b_up, w_key, w_query, vec, w_out, b_out, table,
    )


SMALL = 32


def shift_up(rows):
    count = rows.shape[0]
    rolled = pltpu.roll(rows, count - 1, 0)
    at = lax.broadcasted_iota(jnp.int32, rows.shape, 0)
    return jnp.where(at == count - 1, 0.0, rolled)


def speller_backward_kernel(
    w_lin, w_lhid, w_uin, w_uhid, w_key, w_query, vec, prev_onehot,
    acts, key, keys_proj, key_low, fact1, fact2, q_rows, w_cols, feat_rows, dw_cols, logit_grad,
    grad_mine, grad_other, dp1_out, dp2_out, pack,
    dp1_rows, dp2_rows, dq_rows, keys_acc, vec_acc, small, t_lhid, t_uin, t_uhid, t_query,
):
    role = lax.axis_index("role")
    time_len, att = keys_proj.shape
    steps, vocab = logit_grad.shape
    units = key.shape[1] // 2
    cells = w_lhid.shape[0]
    embed = acts.shape[1] - 2 * units - 2 * cells
    vec_row = vec[...].astype(F32)[None]
    zero = jnp.zeros((1, cells), F32)
    wide = jnp.zeros((1, 4 * cells), BF16)
    keys_acc[...] = jnp.zeros_like(keys_acc)
    vec_acc[...] = jnp.zeros_like(vec_acc)
    t_lhid[...] = w_lhid[...].T
    t_uin[...] = w_uin[...].T
    t_uhid[...] = w_uhid[...].T
    t_query[...] = w_query[...].T
    lane = lax.broadcasted_iota(jnp.int32, w_cols.shape, 1)

    def backward_step(s, carry):
        dp1, dp2, dcell1, dcell2 = carry
        i = steps - 1 - s
        at = pl.ds(i, 1)
        query = q_rows[at, :]
        dp1_row = dp1.astype(F32)
        here = lane == i
        part = jnp.where(here, dw_cols[...], 0.0)
        for j in range(key_low.shape[1] // 128):
            cut = slice(j * 128, (j + 1) * 128)
            part = part + dp1_row[:, cut] * key_low[:, cut]
        dweights = jnp.sum(part, -1, keepdims=True)
        weights = jnp.sum(jnp.where(here, w_cols[...], 0.0), -1, keepdims=True)
        back2 = mm(dp2, t_uhid[...])
        back1 = mm(dp1, t_lhid[...])
        shared = weights * dweights
        dscore = shared - weights * jnp.sum(shared, 0, keepdims=True)
        sums = []
        for j in range(query.shape[1] // 128):
            cut = slice(j * 128, (j + 1) * 128)
            energy = jnp.tanh(keys_proj[:, cut] + query[:, cut])
            moved = dscore * (1.0 - energy * energy)
            keys_acc[:, cut] += moved
            sums.append(jnp.sum(moved, 0, keepdims=True))
            vec_acc[:, cut] += jnp.sum((dscore * energy).reshape(time_len // 8, 8, 128), 0)
        dquery = (jnp.concatenate(sums, 1) * vec_row).astype(BF16)
        dq_rows[at, :] = dquery.astype(F32)
        ds2 = back2 + feat_rows[at, :cells] + mm(dquery, t_query[...])
        pre2, dcell2 = cell_backward(fact2[at, :], ds2, dcell2)
        dp2_rows[at, :] = pre2
        dp2 = pre2.astype(BF16)
        ds1 = back1 + mm(dp2, t_uin[...])
        pre1, dcell1 = cell_backward(fact1[at, :], ds1, dcell1)
        dp1_rows[at, :] = pre1
        return pre1.astype(BF16), dp2, dcell1, dcell2

    lax.fori_loop(0, steps, backward_step, (wide, wide, zero, zero))

    dp1 = dp1_rows[...].astype(BF16)
    dp2 = dp2_rows[...].astype(BF16)
    dq = dq_rows[...].astype(BF16)
    extra = jnp.zeros((dp1_out.shape[0] - steps, 4 * cells), BF16)
    dp1_out[steps:, :] = extra
    dp2_out[steps:, :] = extra
    dp1_out[:steps, :] = dp1
    dp2_out[:steps, :] = dp2
    next_dp1 = shift_up(dp1.astype(F32)).astype(BF16)
    ctx_grad = (feat_rows[:, cells:] + mm_nt(next_dp1, w_lin[embed:, :])).astype(BF16)
    keys_grad = (keys_acc[...] * vec_row).astype(BF16)
    w_low = w_cols[...].astype(BF16)[:, :steps]
    key_grad = mm_nt(keys_grad, w_key[...]) + mm(w_low, ctx_grad)
    key_grad = key_grad.astype(BF16)
    grad_mine[...] = jnp.where(role == 0, key_grad[:, :units], key_grad[:, units:])
    grad_other[...] = jnp.where(role == 0, key_grad[:, units:], key_grad[:, :units])
    ctx = acts[:steps, embed : embed + 2 * units]
    s2 = acts[:steps, embed + 2 * units + cells :]
    wide = pack.shape[1]
    deep = 2 * units * att // wide
    g_key = mm_tn(key[...], keys_grad)
    g_query = mm_tn(s2, dq)
    for k in range(wide // att):
        cut = slice(k * att, (k + 1) * att)
        first = 2 * SMALL
        pack[first : first + deep, cut] = g_key[k * deep : (k + 1) * deep].astype(BF16)
        first += deep
        pack[first : first + deep, cut] = g_query[k * deep : (k + 1) * deep].astype(BF16)
    emb_grad = mm_nt(dp1, w_lin[:embed, :])
    hot = prev_onehot[...]
    total = None
    for _ in range(3):
        low = emb_grad.astype(BF16)
        emb_grad = emb_grad - low.astype(F32)
        total = mm_tn(hot, low) if total is None else total + mm_tn(hot, low)
    small[...] = jnp.zeros_like(small)
    small[:vocab, :cells] = mm_tn(logit_grad[...], s2)
    small[:vocab, cells : cells + 2 * units] = mm_tn(logit_grad[...], ctx)
    base = cells + 2 * units
    small[:vocab, base : base + embed] = total
    base += embed
    small[0:1, base : base + att] = jnp.sum(vec_acc[...], 0, keepdims=True)
    small[1:2, base : base + vocab] = jnp.sum(logit_grad[...].astype(F32), 0, keepdims=True)
    low_bias = jnp.sum(dp1.astype(F32), 0, keepdims=True)
    up_bias = jnp.sum(dp2.astype(F32), 0, keepdims=True)
    for k in range(4):
        small[2 + k : 3 + k, base : base + cells] = low_bias[:, k * cells : (k + 1) * cells]
        small[6 + k : 7 + k, base : base + cells] = up_bias[:, k * cells : (k + 1) * cells]
    high = small[...].astype(BF16)
    pack[:SMALL, :] = high
    pack[SMALL : 2 * SMALL, :] = (small[...] - high.astype(F32)).astype(BF16)


def speller_backward(
    w_lin, w_lhid, w_uin, w_uhid, w_key, w_query, vec, prev_onehot,
    acts, key, keys_proj, key_low, fact1, fact2, q_rows, w_cols, feat_rows, dw_cols, logit_grad,
):
    time_len, att = keys_proj.shape
    steps, vocab = logit_grad.shape
    units = key.shape[1] // 2
    cells = w_lhid.shape[0]
    pad_steps = acts.shape[0]
    vmem = pl.BlockSpec(memory_space=pltpu.VMEM)
    shape = jax.ShapeDtypeStruct
    outs = [
        shape((time_len, units), BF16),
        shape((time_len, units), BF16),
        shape((pad_steps, 4 * cells), BF16),
        shape((pad_steps, 4 * cells), BF16),
        shape(((2 * units + cells) * att // (4 * cells) + 2 * SMALL, 4 * cells), BF16),
    ]
    out_specs = [vmem] * 5
    scratch = [
        pltpu.VMEM((steps, 4 * cells), F32),
        pltpu.VMEM((steps, 4 * cells), F32),
        pltpu.VMEM((steps, att), F32),
        pltpu.VMEM((time_len, att), F32),
        pltpu.VMEM((8, att), F32),
        pltpu.VMEM((SMALL, 4 * cells), F32),
        pltpu.VMEM((4 * cells, cells), BF16),
        pltpu.VMEM((4 * cells, cells), BF16),
        pltpu.VMEM((4 * cells, cells), BF16),
        pltpu.VMEM((att, cells), BF16),
    ]
    return pl.pallas_call(
        speller_backward_kernel,
        out_shape=outs,
        in_specs=[vmem] * 19,
        out_specs=out_specs,
        scratch_shapes=scratch,
        compiler_params=pltpu.CompilerParams(vmem_limit_bytes=VMEM_BYTES),
    )(
        w_lin, w_lhid, w_uin, w_uhid, w_key, w_query, vec, prev_onehot,
        acts, key, keys_proj, key_low, fact1, fact2, q_rows, w_cols, feat_rows, dw_cols, logit_grad,
    )


def unfold(folded, width):
    deep = folded.shape[0]
    return folded.reshape(deep, -1, width).swapaxes(0, 1).reshape(-1, width)


def unpack(small, units, cells, att, vocab, embed):
    small = small[:SMALL].astype(F32) + small[SMALL:].astype(F32)
    base = cells + 2 * units
    g_out = small[:vocab, :base].T
    g_table = small[:vocab, base : base + embed]
    base += embed
    low_bias = small[2:6, base : base + cells].reshape(-1)
    up_bias = small[6:10, base : base + cells].reshape(-1)
    g_vec = small[0, base : base + att]
    g_obias = small[1, base : base + vocab]
    return low_bias, up_bias, g_vec, g_out, g_obias, g_table


def backward_steps(role, lengths, factors, grad_out, w_back, grad_pre, first_step, count, carry):
    time_len = factors.shape[1]
    first = lax.broadcasted_iota(jnp.int32, (8, 1), 0) == 0
    row_lengths = jnp.where(first, lengths[0], lengths[1])

    units = w_back.shape[1]
    tiles = lambda j: w_back[j * units : (j + 1) * units, :]

    def step(product, s, carry):
        grad_hidden, grad_cell = carry
        t = jnp.where(role == 1, s, time_len - 1 - s)
        at = pl.ds(t, 1)
        live = t < row_lengths
        fact = jnp.where(first, factors[0, at, :], factors[1, at, :])
        arrived = jnp.where(first, grad_out[0, at, :], grad_out[1, at, :])
        fact = jnp.where(live, fact, 0.0)
        total = grad_hidden + jnp.where(live, arrived, 0.0)
        pre, cell_back = cell_backward(fact, total, grad_cell)
        for u in range(2):
            grad_pre[u, at, :] = pre[u : u + 1]
        back = sum(product(pre))
        return jnp.where(live, back, total), jnp.where(live, cell_back, grad_cell)

    return staged_loop(first_step, first_step + count, step, carry, tiles, 2)


def listen_backward_kernel(
    lengths, factors, grad_mine, grad_other, w_rec, pre_out, grad_pre, grad_out, w_back
):
    role = lax.axis_index("role")
    grad_out[role] = grad_mine[...].astype(F32)
    grad_out[1 - role] = grad_other[...].astype(F32)
    w_back[...] = w_rec[...].T
    zero = jnp.zeros((8, w_rec.shape[0]), F32)
    backward_steps(
        role, lengths, factors, grad_out, w_back, grad_pre, 0, factors.shape[1], (zero, zero)
    )
    pre_out[...] = grad_pre[...].astype(BF16)


def listen_backward(lengths, factors, grad_mine, grad_other, w_rec):
    utts, time_len, _ = factors.shape
    units = w_rec.shape[0]
    vmem = pl.BlockSpec(memory_space=pltpu.VMEM)
    return pl.pallas_call(
        listen_backward_kernel,
        out_shape=jax.ShapeDtypeStruct((utts, time_len, 4 * units), BF16),
        in_specs=[pl.BlockSpec(memory_space=pltpu.SMEM)] + [vmem] * 4,
        out_specs=vmem,
        scratch_shapes=[
            pltpu.VMEM((utts, time_len, 4 * units), F32),
            pltpu.VMEM((utts, time_len, units), F32),
            pltpu.VMEM((4 * units, units), BF16),
        ],
        compiler_params=pltpu.CompilerParams(vmem_limit_bytes=VMEM_BYTES),
    )(lengths, factors, grad_mine, grad_other, w_rec)


SEGMENT = 32
STREAMS = ((0, 3), (3, 5), (5, 6))


SP_CHUNKS = ((320, 352), (672, 352), (1024, 320), (0, 320))
LI_CHUNKS = ((0, 96), (96, 160), (256, 192), (448, 224))
HEAD = 320
EXCHANGE_PROGRAM = (
    (),
    (),
    (),
    (),
    (),
    (),
    ('pack_x',),
    (),
    ('columns', ('s', 'sp', 0, 0), ('s', 'sp', 0, 1), 'pack_y',),
    (),
    (),
    (),
    ('stream0', 'far', ('w', 'sp', 0, 0), ('s', 'sp', 1, 0), ('s', 'sp', 0, 2),),
    (),
    (),
    (),
    (('w', 'sp', 1, 0), ('s', 'sp', 2, 0), ('w', 'sp', 0, 1), ('s', 'sp', 1, 1),),
    ('pack_z', ('s', 'sp', 0, 3),),
    (),
    (),
    ('stream1', ('w', 'sp', 2, 0), ('s', 'sp', 3, 0),),
    (),
    (('w', 'sp', 1, 1), ('s', 'sp', 2, 1),),
    (('w', 'sp', 0, 2), ('s', 'sp', 1, 2),),
    ('stream2', 'near',),
    (('w', 'sp', 0, 3), ('s', 'sp', 1, 3), ('w', 'sp', 2, 1), ('s', 'sp', 3, 1), ('w', 'sp', 1, 2), ('s', 'sp', 2, 2), ('w', 'sp', 1, 3), ('s', 'sp', 2, 3), 'li_columns', ('s', 'li', 0, 0), ('s', 'li', 0, 1), ('w', 'sp', 2, 2), ('s', 'sp', 3, 2), ('w', 'li', 0, 0), ('s', 'li', 1, 0), ('s', 'li', 0, 2), ('w', 'li', 0, 1), ('s', 'li', 1, 1), ('s', 'li', 0, 3), ('w', 'sp', 2, 3), ('s', 'sp', 3, 3), ('w', 'li', 1, 0), ('s', 'li', 2, 0), ('w', 'li', 1, 1), ('s', 'li', 2, 1), ('w', 'li', 0, 2), ('s', 'li', 1, 2), ('w', 'li', 0, 3), ('s', 'li', 1, 3), ('w', 'li', 1, 2), ('s', 'li', 2, 2), ('w', 'li', 1, 3), ('s', 'li', 2, 3),),
)


def exchange_kernel(
    dims,
    lengths, factors, grad_mine, grad_other, w_in, w_rec, dp1, dp2, pack, acts_all, pairs_low, pairs_high, rows_all,
    frames_out, li_out, sp_out,
    grad_pre, grad_out, acts_buf, pairs_buf, rows_buf, dp_pair, got, got_t, prod, column,
    li_send, li_got, li_rows, li_acc, li_all, fr_send, fr_got, weave,
    pk_pair, pk_x, pk_xsum, pk_y, pk_ysum, pk_z,
    local_sem, chip_send, chip_recv, aa_send, aa_recv, li_aa_send, li_aa_recv,
    sp_send, sp_recv, li_ag_send, li_ag_recv, pk_send, pk_recv, far_grad, w_back,
):
    nz, ny, nx = dims
    chips = nz * ny * nx
    role = lax.axis_index("role")
    dp = lax.axis_index("dp")
    z, y, x = dp // (ny * nx), (dp // nx) % ny, dp % nx
    utts, time_len, width = grad_pre.shape
    units = w_rec.shape[0]
    cells = dp1.shape[1] // 4
    half_time = time_len // 2
    pads = dp1.shape[0]
    twin = (1 - role, dp)

    def slot_of(chip):
        return (((chip // nx) % ny) * nx + chip % nx) * nz + chip // (ny * nx)

    slot = slot_of(dp)
    lanes = pl.ds(pl.multiple_of(slot * 128, 128), 128)

    barrier = pltpu.get_barrier_semaphore()
    mesh = pl.DeviceIdType.MESH

    def greet(k, _):
        pl.semaphore_signal(barrier, inc=1, device_id=(role, (dp + k) % chips), device_id_type=mesh)
        return 0

    pl.semaphore_signal(barrier, inc=1, device_id=twin, device_id_type=mesh)
    lax.fori_loop(1, chips, greet, 0)
    load_acts = pltpu.make_async_copy(
        acts_all.at[:, pl.ds(pl.multiple_of(role * cells, 128), acts_buf.shape[1])],
        acts_buf, local_sem.at[0],
    )
    load_acts.start()
    load_rows = [pltpu.make_async_copy(rows_all, rows_buf.at[:, pl.ds(0, units)], local_sem.at[1])]
    rows_buf[:, units:] = jnp.ones((rows_buf.shape[0], rows_buf.shape[1] - units), BF16)
    start(load_rows)
    split = pairs_low.shape[0]
    load_pairs = [
        pltpu.make_async_copy(pairs_low, pairs_buf.at[pl.ds(0, split)], local_sem.at[4]),
        pltpu.make_async_copy(pairs_high, pairs_buf.at[pl.ds(split, pairs_high.shape[0])], local_sem.at[5]),
    ]
    start(load_pairs)
    dp_pair[role] = jnp.where(role == 0, dp1[...], dp2[...])
    dp_pair[2] = jnp.where(role == 0, dp2[...], dp1[...])
    grad_out[role] = grad_mine[...].astype(F32)
    w_back[...] = w_rec[...].T
    pl.semaphore_wait(barrier, chips)
    last = chip_send.shape[0] - 1
    crossing = remote(grad_other, far_grad, chip_send.at[last], chip_recv.at[last], twin)
    crossing.start()

    to_twin = remote(dp_pair.at[2], dp_pair.at[role], chip_send.at[0], chip_recv.at[0], twin)
    to_twin.start()
    pack_twin = remote(pack, pk_pair, pk_send.at[0], pk_recv.at[0], twin)

    @pl.when(role == 0)
    def _():
        pack_twin.start()

    to_twin.wait()

    def block(k):
        chip = (dp + k) % chips
        cut = pl.ds(pl.multiple_of(slot_of(chip) * 128, 128), 128)
        return remote(
            dp_pair.at[pl.ds(0, 2), :, cut], got.at[dp],
            aa_send.at[k - 1], aa_recv.at[k - 1], (role, chip),
        )

    lax.fori_loop(1, chips, lambda k, _: (block(k).start(), 0)[1], 0)
    own_block = pltpu.make_async_copy(
        dp_pair.at[pl.ds(0, 2), :, lanes], got.at[dp], local_sem.at[2]
    )
    own_block.start()

    def rounded(total):
        value = total[:SMALL] + total[SMALL : 2 * SMALL]
        high = value.astype(BF16)
        low = (value - high.astype(F32)).astype(BF16)
        return jnp.concatenate([high, low, total[2 * SMALL :].astype(BF16)], 0)

    chip_at = lambda a, b, c: (role, (a * ny + b) * nx + c)
    x_other, y_other = (x + 1) % nx, (y + 1) % ny
    column_wide = nz * 128

    def pack_x(b):
        first = pl.multiple_of((b * nx + x_other) * column_wide, 128)
        return remote(
            pk_pair.at[:, pl.ds(first, column_wide)], pk_x.at[b],
            pk_send.at[1 + b], pk_recv.at[1 + b], chip_at(z, y, x_other),
        )

    pack_y = remote(
        pk_xsum.at[y_other], pk_y, pk_send.at[1 + ny], pk_recv.at[1 + ny], chip_at(z, y_other, x)
    )

    def pack_z(j):
        to = (z + j) % nz
        return remote(
            pk_ysum.at[:, pl.ds(pl.multiple_of(to * 128, 128), 128)], pk_z.at[z],
            pk_send.at[1 + ny + j], pk_recv.at[1 + ny + j], chip_at(to, y, x),
        )

    @pl.when(role == 0)
    def _():
        pack_twin.wait_send()

    @pl.when(role == 1)
    def _():
        pack_twin.wait_recv()

        def add(b, _):
            cut = pl.ds(pl.multiple_of(b * 128, 128), 128)
            total = pk_pair[:, cut].astype(F32) + pack[:, cut].astype(F32)
            pk_pair[:, cut] = rounded(total)
            return 0

        lax.fori_loop(0, pack.shape[1] // 128, add, 0)
        for b in range(ny):
            pack_x(b).start()

    def pack_after_x():
        for b in range(ny):
            pack_x(b).wait()
            first = pl.multiple_of((b * nx + x) * column_wide, 128)

            def add(c, _):
                here = pl.ds(pl.multiple_of(first + c * 128, 128), 128)
                cut = pl.ds(pl.multiple_of(c * 128, 128), 128)
                total = pk_pair[:, here].astype(F32) + pk_x[b, :, cut].astype(F32)
                pk_xsum[b, :, cut] = rounded(total)
                return 0

            lax.fori_loop(0, nz, add, 0)
        pack_y.start()

    def pack_after_y():
        pack_y.wait()

        def add(c, _):
            cut = pl.ds(pl.multiple_of(c * 128, 128), 128)
            total = pk_xsum[y, :, cut].astype(F32) + pk_y[:, cut].astype(F32)
            pk_ysum[:, cut] = rounded(total)
            return 0

        lax.fori_loop(0, nz, add, 0)
        for j in range(1, nz):
            pack_z(j).start()

    def pack_after_z():
        for j in range(1, nz):
            pack_z(j).wait()
        pk_z[z] = pk_ysum[:, pl.ds(pl.multiple_of(z * 128, 128), 128)]
        total = pk_z[0].astype(F32)
        for j in range(1, nz):
            total = total + pk_z[j].astype(F32)
        column[: total.shape[0], :] = rounded(total)

    def view_sp(which, k, first, count):
        rows = SP_CHUNKS[k]
        if which is not None:
            rows = (rows[0] + which * rows[1] // 2, rows[1] // 2)
        cut = pl.ds(pl.multiple_of(first * 128, 128), count * 128)
        return sp_out.at[role, pl.ds(*rows), cut]

    def view_li(which, k, first, count):
        rows = LI_CHUNKS[k]
        if which is not None:
            rows = (rows[0] + which * rows[1] // 2, rows[1] // 2)
        return li_all.at[pl.ds(first, count), pl.ds(*rows)]

    me = (role, z, y, x)
    sp = Gather(dims, me, view_sp, SP_CHUNKS, (sp_send, sp_recv))
    li = Gather(dims, me, view_li, LI_CHUNKS, (li_ag_send, li_ag_recv))

    def sp_last(k):
        ref = sp_out.at[role, pl.ds(*SP_CHUNKS[k])]
        return [remote(ref, ref, chip_send.at[2 + k], chip_recv.at[2 + k], twin)]

    def rows_of(j):
        return jnp.where(role == 1, SEGMENT * j, time_len - SEGMENT * (j + 1))

    def pack_columns(first_segment, last_segment):
        lane = lax.broadcasted_iota(jnp.int32, (SEGMENT, 128), 1)
        for j in range(first_segment, last_segment):
            rows = pl.ds(pl.multiple_of(rows_of(j), SEGMENT), SEGMENT)
            for b in range(width // 128):
                one = grad_pre[0, rows, b * 128 : (b + 1) * 128]
                two = grad_pre[1, rows, b * 128 : (b + 1) * 128]
                even = jnp.where(lane < 64, one, pltpu.roll(two, 64, 1))
                odd = jnp.where(lane < 64, pltpu.roll(one, 64, 1), two)
                li_send[2 * b, rows, :] = even.astype(BF16)
                li_send[2 * b + 1, rows, :] = odd.astype(BF16)

    def stream(n):
        first_segment, last_segment = STREAMS[n]
        count = SEGMENT * (last_segment - first_segment)
        begin = jnp.where(role == 1, SEGMENT * first_segment, time_len - SEGMENT * last_segment)
        rows = pl.ds(pl.multiple_of(begin, SEGMENT), count)

        def one(k):
            chip = (dp + k) % chips
            return remote(
                li_send.at[slot_of(chip), rows], li_got.at[dp, rows],
                li_aa_send.at[n, k - 1], li_aa_recv.at[n, k - 1], (role, chip),
            )

        return one

    def start_stream(n):
        pack_columns(*STREAMS[n])
        one = stream(n)
        lax.fori_loop(1, chips, lambda k, _: (one(k).start(), 0)[1], 0)

    def wait_stream(n):
        one = stream(n)
        lax.fori_loop(1, chips, lambda k, _: (one(k).wait(), 0)[1], 0)

    crossing.wait()
    grad_out[1 - role] = far_grad[...].astype(F32)
    zero = jnp.zeros((8, units), F32)
    carry = (zero, zero)

    def back_to_frames(rows):
        tile = lambda k, n: w_in[n * SIDE : (n + 1) * SIDE, k * SIDE : (k + 1) * SIDE]
        return staged_product(rows.astype(BF16), tile, w_in.shape[0] // SIDE, flip=True)

    def run(j, count, carry):
        return backward_steps(
            role, lengths, factors, grad_out, w_back, grad_pre, count * j, count, carry
        )

    def place(first, count):
        copy = pltpu.make_async_copy(
            column.at[pl.ds(first, count)], sp_out.at[role, pl.ds(first, count), lanes],
            local_sem.at[3],
        )
        copy.start()
        copy.wait()

    def columns():
        lax.fori_loop(1, chips, lambda k, _: (block(k).wait(), 0)[1], 0)
        own_block.wait()
        load_acts.wait()
        both = got[...].reshape(chips * 2 * pads, 128).astype(F32)
        rolled = pltpu.roll(both, chips * 2 * pads - 1, 0)
        got_t[0] = jnp.transpose(both).astype(BF16)
        got_t[1] = jnp.transpose(rolled).astype(BF16)
        groups = acts_buf.shape[1] // 256
        for g in range(groups):
            cut = slice(g * 256, (g + 1) * 256)
            if g == 0:
                left = got_t[0]
            elif g < groups - cells // 256:
                left = got_t[1 - role]
            else:
                left = got_t[1]
            prod[:, cut] = staged_product(left, lambda k, n: acts_buf[k * SIDE : (k + 1) * SIDE, cut], 1)
        column[2 * SMALL :, :] = jnp.transpose(prod[...]).astype(BF16)
        column[: 2 * SMALL, :] = jnp.zeros((2 * SMALL, 128), BF16)

        place(HEAD, column.shape[0] - HEAD)

    far = jnp.where(role == 0, half_time, 0)
    near = half_time - far
    frames_copy = remote(fr_send, fr_got, chip_send.at[1], chip_recv.at[1], twin)

    def far_frames():
        for u in range(utts):
            rows = pl.ds(pl.multiple_of(far, half_time), half_time)
            fr_send[u] = back_to_frames(grad_pre[u, rows, :]).astype(BF16)
        frames_copy.start()

    def near_frames():
        frames_copy.wait()
        feat = frames_out.shape[2]
        for u in range(utts):
            rows = pl.ds(pl.multiple_of(near, half_time), half_time)
            total = back_to_frames(grad_pre[u, rows, :]) + fr_got[u].astype(F32)
            for j in range(feat // 128):
                for half in range(2):
                    cut = slice(half * feat + j * 128, half * feat + (j + 1) * 128)
                    weave[pl.ds(half, half_time, stride=2), :] = total[:, cut]
                frames_out[u, :, j * 128 : (j + 1) * 128] = weave[...]

    def listener_columns():
        li_got[dp] = li_send[slot]
        wait(load_rows)
        wait(load_pairs)
        for n in range(len(STREAMS)):
            wait_stream(n)

        def spread(c, _):
            value = li_got[c].astype(F32)
            for u, part in enumerate((value, pltpu.roll(value, 64, 1))):
                for p in range(time_len // PART):
                    base = pl.multiple_of(((p * utts + u) * chips + slot_of(c)) * PART, PART)
                    li_rows[pl.ds(base, PART), :] = part[p * PART : (p + 1) * PART].astype(BF16)
            return 0

        lax.fori_loop(0, chips, spread, 0)
        li_acc[...] = jnp.zeros_like(li_acc)
        deep = 4 * time_len
        features = pairs_buf.shape[1]

        def accumulate(c, _):
            rows = pl.ds(pl.multiple_of(c * deep, 256), deep)
            left = jnp.transpose(li_rows[rows, :])
            for source, base in ((pairs_buf, 0), (rows_buf, features)):
                piece = lambda k, n: source[
                    pl.ds(pl.multiple_of(c * deep + k * SIDE, SIDE), SIDE), n * SIDE : (n + 1) * SIDE
                ]
                wide = source.shape[1]
                li_acc[:, base : base + wide] += staged_product(left, piece, wide // SIDE)
            return 0

        lax.fori_loop(0, chips * 2 * time_len // deep, accumulate, 0)
        flipped = jnp.transpose(li_acc[:, : features + units + 64])
        tall = flipped.shape[0] // 2
        lane = lax.broadcasted_iota(jnp.int32, (tall, 128), 1)
        packed = jnp.where(lane < 64, flipped[:tall], pltpu.roll(flipped[tall:], 64, 1))
        li_all[slot] = packed.astype(BF16)

    def finish_pack():
        pl.when(role == 1)(pack_after_z)
        place(0, HEAD)

    work = {
        "pack_x": lambda: pl.when(role == 1)(pack_after_x),
        "pack_y": lambda: pl.when(role == 1)(pack_after_y),
        "pack_z": finish_pack,
        "columns": columns,
        "far": far_frames,
        "near": near_frames,
        "li_columns": listener_columns,
    }
    work.update({"stream%d" % n: functools.partial(start_stream, n) for n in range(len(STREAMS))})
    phases = {
        "sp": (sp.first, sp.second, sp.third, sp_last),
        "li": (li.first, li.second, li.third),
    }

    def perform(items):
        for item in items:
            if item in work:
                work[item]()
            else:
                verb, gather, phase, k = item
                (start if verb == "s" else wait)(phases[gather][phase](k))

    groups = len(EXCHANGE_PROGRAM) - 2
    count = time_len // groups
    for group in range(groups):
        perform(EXCHANGE_PROGRAM[group])
        carry = run(group, count, carry)
    perform(EXCHANGE_PROGRAM[groups])
    perform(EXCHANGE_PROGRAM[groups + 1])
    for k in range(len(LI_CHUNKS)):
        wait(li.third(k))
    tall = li_all.shape[1]
    lane = lax.broadcasted_iota(jnp.int32, (tall, 128), 1)

    def assemble(b, _):
        cut = pl.ds(pl.multiple_of(b * 128, 128), 128)
        even = li_all[2 * b].astype(F32)
        odd = li_all[2 * b + 1].astype(F32)
        li_out[:tall, cut] = jnp.where(lane < 64, even, pltpu.roll(odd, 64, 1)).astype(BF16)
        li_out[tall:, cut] = jnp.where(lane < 64, pltpu.roll(even, 64, 1), odd).astype(BF16)
        return 0

    lax.fori_loop(0, width // 128, assemble, 0)
    for k in range(len(SP_CHUNKS)):
        wait(sp_last(k))


def exchange(
    dims, lengths, factors, grad_mine, grad_other, w_in, w_rec, dp1, dp2, pack, acts_all,
    pairs_low, pairs_high, rows_all,
):
    utts, time_len, _ = factors.shape
    units = w_rec.shape[0]
    width = 4 * units
    pads, wide = dp1.shape
    cells = wide // 4
    chips = dims[0] * dims[1] * dims[2]
    span = acts_all.shape[1] - cells
    deep = sum(rows for _, rows in SP_CHUNKS)
    nz, ny, _ = dims
    packed = pack.shape[0]
    features = pairs_low.shape[1]
    total = features + units + 64
    feat = w_in.shape[0] // 2
    half_time = time_len // 2
    vmem = pl.BlockSpec(memory_space=pltpu.VMEM)
    anywhere = pl.BlockSpec(memory_space=pl.ANY)
    shape = jax.ShapeDtypeStruct
    dma = pltpu.SemaphoreType.DMA
    sp_sems = Gather.semaphores(dims, SP_CHUNKS)
    li_sems = Gather.semaphores(dims, LI_CHUNKS)
    return pl.pallas_call(
        functools.partial(exchange_kernel, dims),
        out_shape=(
            shape((utts, time_len, feat), F32),
            shape((total, width), BF16),
            shape((2, deep, wide), BF16),
        ),
        in_specs=[pl.BlockSpec(memory_space=pltpu.SMEM)] + [vmem] * 8 + [anywhere] * 4,
        out_specs=(vmem, vmem, anywhere),
        scratch_shapes=[
            pltpu.VMEM((utts, time_len, width), F32),
            pltpu.VMEM((utts, time_len, units), F32),
            pltpu.VMEM((acts_all.shape[0], span), BF16),
            pltpu.VMEM((chips * utts * time_len, features), BF16),
            pltpu.VMEM((chips * utts * time_len, 2 * SIDE), BF16),
            pltpu.VMEM((3, pads, wide), BF16),
            pltpu.VMEM((chips, 2, pads, 128), BF16),
            pltpu.VMEM((2, 128, chips * 2 * pads), BF16),
            pltpu.VMEM((128, span), F32),
            pltpu.VMEM((deep, 128), BF16),
            pltpu.VMEM((chips, time_len, 128), BF16),
            pltpu.VMEM((chips, time_len, 128), BF16),
            pltpu.VMEM((chips * 2 * time_len, 128), BF16),
            pltpu.VMEM((128, features + 2 * SIDE), F32),
            pltpu.VMEM((chips, total // 2, 128), BF16),
            pltpu.VMEM((utts, half_time, 2 * feat), BF16),
            pltpu.VMEM((utts, half_time, 2 * feat), BF16),
            pltpu.VMEM((time_len, 128), F32),
            pltpu.VMEM((packed, wide), BF16),
            pltpu.VMEM((ny, packed, nz * 128), BF16),
            pltpu.VMEM((ny, packed, nz * 128), BF16),
            pltpu.VMEM((packed, nz * 128), BF16),
            pltpu.VMEM((packed, nz * 128), BF16),
            pltpu.VMEM((nz, packed, 128), BF16),
            dma((5 + 2 * 4,)),
            dma((3 + len(SP_CHUNKS),)),
            dma((3 + len(SP_CHUNKS),)),
            dma((chips - 1,)),
            dma((chips - 1,)),
            dma((len(STREAMS), chips - 1)),
            dma((len(STREAMS), chips - 1)),
            sp_sems,
            sp_sems,
            li_sems,
            li_sems,
            dma((1 + ny + nz,)),
            dma((1 + ny + nz,)),
            pltpu.VMEM(grad_other.shape, BF16),
            pltpu.VMEM((width, units), BF16),
        ],
        compiler_params=pltpu.CompilerParams(
            vmem_limit_bytes=VMEM_BYTES, collective_id=0, has_side_effects=True
        ),
    )(
        lengths, factors, grad_mine, grad_other, w_in, w_rec, dp1, dp2, pack,
        acts_all, pairs_low, pairs_high, rows_all,
    )


PIECE = 128
SLOTS = 3


def widen_kernel(jobs, sizes, sp, li, *refs):
    *outs, narrow, wide, few, last, in_sem, out_sem, few_sem = refs
    g_out, g_table, low_bias, up_bias, g_vec, g_obias, sum_bias = outs[-7:]

    def source(n):
        which, row, col, out, _, rows = jobs[n]
        ref = li if which == 2 else sp.at[which]
        width = outs[out].shape[-1]
        return pltpu.make_async_copy(
            ref.at[pl.ds(row, rows), pl.ds(col, width)],
            narrow.at[n % SLOTS, pl.ds(0, rows), pl.ds(0, width)],
            in_sem.at[n % SLOTS],
        )

    def target(n):
        _, _, _, out, row, rows = jobs[n]
        width = outs[out].shape[-1]
        return pltpu.make_async_copy(
            wide.at[n % SLOTS, pl.ds(0, rows), pl.ds(0, width)],
            outs[out].at[pl.ds(row, rows)],
            out_sem.at[n % SLOTS],
        )

    load_few = [
        pltpu.make_async_copy(sp.at[1, pl.ds(0, 2 * SMALL)], few, few_sem.at[0]),
        pltpu.make_async_copy(li.at[pl.ds(sizes[-1], 16)], last, few_sem.at[1]),
    ]
    for n in range(min(SLOTS, len(jobs))):
        source(n).start()
    start(load_few)
    for n in range(len(jobs)):
        source(n).wait()
        if n >= SLOTS:
            target(n - SLOTS).wait()
        rows, width = jobs[n][5], outs[jobs[n][3]].shape[-1]
        wide[n % SLOTS, :rows, :width] = narrow[n % SLOTS, :rows, :width].astype(F32)
        target(n).start()
        if n + SLOTS < len(jobs):
            source(n + SLOTS).start()
    wait(load_few)
    small = few[:SMALL].astype(F32) + few[SMALL:].astype(F32)
    cells, base, embed, att, vocab, _ = sizes
    g_out[...] = small[:vocab, :base]
    g_table[...] = small[:vocab, base : base + embed]
    base += embed
    for k in range(4):
        cut = slice(k * cells, (k + 1) * cells)
        low_bias[cut] = small[2 + k, base : base + cells]
        up_bias[cut] = small[6 + k, base : base + cells]
    g_vec[...] = small[0, base : base + att]
    g_obias[...] = small[1, base : base + vocab]
    sum_bias[...] = last[0:1, :].astype(F32)
    for n in range(max(0, len(jobs) - SLOTS), len(jobs)):
        target(n).wait()


def widen(sp, li, parts, sizes):
    jobs = []
    for out, (_, pieces) in enumerate(parts):
        done = 0
        for which, row, col, rows in pieces:
            for at in range(0, rows, PIECE):
                count = min(PIECE, rows - at)
                jobs.append((which, row + at, col, out, done, count))
                done += count
    cells, base, embed, att, vocab, _ = sizes
    wide = sp.shape[2]
    anywhere = pl.BlockSpec(memory_space=pl.ANY)
    vmem = pl.BlockSpec(memory_space=pltpu.VMEM)
    dma = pltpu.SemaphoreType.DMA
    few = ((vocab, base), (vocab, embed), (4 * cells,), (4 * cells,), (att,), (vocab,), (1, li.shape[1]))
    return pl.pallas_call(
        functools.partial(widen_kernel, jobs, sizes),
        out_shape=[jax.ShapeDtypeStruct(shape, F32) for shape, _ in parts]
        + [jax.ShapeDtypeStruct(shape, F32) for shape in few],
        in_specs=[anywhere] * 2,
        out_specs=[anywhere] * len(parts) + [vmem] * len(few),
        scratch_shapes=[
            pltpu.VMEM((SLOTS, PIECE, wide), BF16),
            pltpu.VMEM((SLOTS, PIECE, wide), F32),
            pltpu.VMEM((2 * SMALL, wide), BF16),
            pltpu.VMEM((16, li.shape[1]), BF16),
            dma((SLOTS,)),
            dma((SLOTS,)),
            dma((2,)),
        ],
        compiler_params=pltpu.CompilerParams(vmem_limit_bytes=VMEM_BYTES),
    )(sp, li)


def shards(
    frames,
    step_lengths,
    characters,
    char_lengths,
    listen_input,
    listen_hidden,
    listen_bias,
    lower_input,
    lower_hidden,
    lower_bias,
    upper_input,
    upper_hidden,
    upper_bias,
    key_proj,
    query_proj,
    score_vector,
    output_proj,
    output_bias,
    char_table,
):
    chips = lax.axis_size("dp")
    utts, frame_len, feat = frames.shape
    time_len = frame_len // 2
    swap = [(0, 1), (1, 0)]
    w_in, w_rec = listen_input[0], listen_hidden[0]
    units = w_rec.shape[0]
    cells = lower_hidden.shape[0]
    vocab, embed = char_table.shape
    fits = (
        chips % 4 == 0
        and 4 * cells == 128 * chips
        and 4 * units == 64 * chips
        and embed == 256
        and cells == 2 * units
        and time_len == SEGMENT * STREAMS[-1][1]
        and embed + 2 * units + cells + 2 * SMALL == sum(rows for _, rows in SP_CHUNKS)
        and embed + 2 * SMALL == HEAD
        and time_len == 3 * PART
        and characters.shape[2] % SPELL_GROUPS == 0
        and 2 * feat + units + 64 == 2 * sum(rows for _, rows in LI_CHUNKS)
    )
    dims = (chips // 4, 2, 2) if fits else None
    pairs, rows, factors, mine, other, *low_pairs = listen_forward(
        dims, step_lengths, frames, w_in, w_rec, listen_bias
    )
    if not fits:
        other = lax.ppermute(other, "role", swap)
    vec = score_vector
    loss, prev_onehot, acts, key, *kept = speller_forward(
        dims, step_lengths, char_lengths, characters, pairs, rows, mine, other,
        lower_input, lower_hidden, lower_bias, upper_input, upper_hidden, upper_bias,
        key_proj, query_proj, vec, output_proj.T, output_bias, char_table,
    )
    if fits:
        *kept, high_pairs, rows_all = kept
    grad_mine, grad_other, dp1, dp2, pack = speller_backward(
        lower_input, lower_hidden, upper_input, upper_hidden, key_proj, query_proj, vec,
        prev_onehot, acts, key, *kept,
    )
    if fits:
        flat = lambda gathered: gathered.reshape(-1, gathered.shape[-1])
        acts_all = lax.all_gather(acts, ("dp", "role"), tiled=True)
        frame_grad, li, sp = exchange(
            dims, step_lengths, factors, grad_mine, grad_other, w_in, w_rec,
            dp1, dp2, pack, acts_all, flat(low_pairs[0]), flat(high_pairs), flat(rows_all),
        )
        width = 2 * feat
        att = key_proj.shape[1]
        first = 2 * SMALL
        low, high = first + embed, first + embed + 2 * units
        wide = 4 * cells
        deep = 2 * units * att // wide
        folded = lambda row: tuple((1, row, col, deep) for col in range(0, wide, att))
        *layers, sum_in, sum_rec, g_key, g_query, g_out, g_table, low_bias, up_bias, g_vec, g_obias, sum_bias = widen(
            sp,
            li,
            (
                ((high - first, wide), ((0, first, 0, high - first),)),
                ((cells, wide), ((0, high, 0, cells),)),
                ((cells, wide), ((1, low, 0, cells),)),
                ((cells, wide), ((1, low + cells, 0, cells),)),
                ((width, 4 * units), ((2, 0, 0, width),)),
                ((units, 4 * units), ((2, width, 0, units),)),
                ((2 * units, att), folded(first)),
                ((cells, att), folded(first + deep)),
            ),
            (cells, cells + 2 * units, embed, att, vocab, width + units),
        )
        lower, upper = layers[:2], layers[2:]
        g_out = g_out.T
    else:
        grad_other = lax.ppermute(grad_other, "role", swap)
        pack = lax.psum(pack.astype(F32), ("role", "dp"))
        small = pack[: 2 * SMALL]
        g_key, g_query = (
            unfold(part, cells) for part in jnp.split(pack[2 * SMALL :], 2, axis=0)
        )
        low_bias, up_bias, g_vec, g_out, g_obias, g_table = unpack(
            small, units, cells, key_proj.shape[1], vocab, embed
        )
        pre = listen_backward(step_lengths, factors, grad_mine, grad_other, w_rec)
        flat = pre.reshape(utts * time_len, 4 * units)
        sums = mm(jnp.concatenate([pairs.reshape(flat.shape[0], 2 * feat), rows], 1).T, flat)
        sums = lax.psum(sums, "dp")
        width = 2 * feat
        sum_in, sum_rec = sums[:width], sums[width : width + units]
        sum_bias = lax.psum(jnp.sum(flat.astype(F32), 0, keepdims=True), "dp")
        grad_pairs = mm(flat, w_in.T).reshape(utts, frame_len, feat)
        frame_grad = lax.psum_scatter(grad_pairs, "role", scatter_dimension=1, tiled=True)
        cuts = [embed, embed + 2 * units, embed + 2 * units + cells]
        emb, ctx, s1, s2 = jnp.split(acts, cuts, axis=1)
        local = (
            jnp.concatenate([mm(emb.T, dp1), mm(ctx[:-1].T, dp1[1:])], 0),
            mm(s1[:-1].T, dp1[1:]),
            mm(s1.T, dp2),
            mm(s2[:-1].T, dp2[1:]),
        )
        local = lax.psum(local, ("role", "dp"))
        lower, upper = local[:2], local[2:]
    return (
        loss, frame_grad, sum_in[None], sum_rec[None], sum_bias,
        *lower, low_bias, *upper, up_bias,
        g_key, g_query, g_vec, g_out, g_obias, g_table,
    )


def solution(mesh):
    whole = P()
    return jax.shard_map(
        shards,
        mesh=mesh,
        in_specs=(
            P("dp", None, None),
            P("dp"),
            P("dp", "role", None),
            P("dp", "role"),
            P("role", None, None),
            P("role", None, None),
            P("role", None),
        )
        + (whole,) * 12,
        out_specs=(
            P("dp", "role"),
            P("dp", "role", None),
            P("role", None, None),
            P("role", None, None),
            P("role", None),
        )
        + (whole,) * 12,
        check_vma=False,
    )
```

```python
import functools

import jax
import jax.numpy as jnp
from jax import lax
from jax.experimental import pallas as pl
from jax.experimental.pallas import tpu as pltpu
from jax.sharding import PartitionSpec as P

F32 = jnp.float32
BF16 = jnp.bfloat16
VMEM_BYTES = 60 * 1024 * 1024


def mm(left, right):
    return jnp.dot(left, right, preferred_element_type=F32)


def mm_nt(left, right):
    return lax.dot_general(left, right, (((1,), (1,)), ((), ())), preferred_element_type=F32)


def mm_tn(left, right):
    return lax.dot_general(left, right, (((0,), (0,)), ((), ())), preferred_element_type=F32)


def sigmoid(x):
    return 0.5 * jnp.tanh(0.5 * x) + 0.5


def cell_forward(preact, cell_prev):
    n = preact.shape[-1] // 4
    in_gate = sigmoid(preact[:, :n])
    forget = sigmoid(preact[:, n : 2 * n])
    candid = jnp.tanh(preact[:, 2 * n : 3 * n])
    out_gate = sigmoid(preact[:, 3 * n :])
    cell_new = forget * cell_prev + in_gate * candid
    tanh_cell = jnp.tanh(cell_new)
    hidden = out_gate * tanh_cell
    factors = (
        candid * in_gate * (1.0 - in_gate),
        cell_prev * forget * (1.0 - forget),
        in_gate * (1.0 - candid * candid),
        tanh_cell * out_gate * (1.0 - out_gate),
        out_gate * (1.0 - tanh_cell * tanh_cell),
        forget,
    )
    return cell_new, hidden, factors


def cell_backward(factors, grad_hidden, grad_cell):
    n = factors.shape[-1] // 6
    part = lambda k: factors[:, k * n : (k + 1) * n]
    total = grad_cell + grad_hidden * part(4)
    grad_preact = jnp.concatenate(
        [total * part(0), total * part(1), total * part(2), grad_hidden * part(3)], -1
    )
    return grad_preact, total * part(5)


def remote(src, dst, send, recv, device):
    return pltpu.make_async_remote_copy(
        src_ref=src, dst_ref=dst, send_sem=send, recv_sem=recv,
        device_id=device, device_id_type=pl.DeviceIdType.MESH,
    )


def start(copies):
    for copy in copies:
        copy.start()


def wait(copies):
    for copy in copies:
        copy.wait()


class Gather:
    def __init__(self, dims, me, view, chunks, sems):
        self.dims, self.view, self.chunks = dims, view, chunks
        self.role, self.z, self.y, self.x = me
        self.send, self.recv = sems

    def device(self, z, y, x):
        _, ny, nx = self.dims
        return (self.role, (z * ny + y) * nx + x)

    def copies(self, k, which, spans, others, base):
        out = []
        for device in others:
            for span in spans:
                ref = self.view(which, k, *span)
                out.append(
                    remote(ref, ref, self.send.at[k, base], self.recv.at[k, base], device)
                )
                base += 1
        return out

    def along_x(self):
        nx = self.dims[2]
        return [self.device(self.z, self.y, (self.x + j) % nx) for j in range(1, nx)]

    def along_y(self):
        ny = self.dims[1]
        return [self.device(self.z, (self.y + j) % ny, self.x) for j in range(1, ny)]

    def first(self, k):
        nz, ny, nx = self.dims
        slot = (self.y * nx + self.x) * nz + self.z
        others = [self.device((self.z + j) % nz, self.y, self.x) for j in range(1, nz)]
        return self.copies(k, None, [(slot, 1)], others, 0)

    def second(self, k):
        nz, ny, nx = self.dims
        column = ((self.y * nx + self.x) * nz, nz)
        base = nz - 1
        to_x = self.copies(k, 0, [column], self.along_x(), base)
        return to_x + self.copies(k, 1, [column], self.along_y(), base + nx - 1)

    def third(self, k):
        nz, ny, nx = self.dims
        base = nz - 1 + nx - 1 + ny - 1
        to_y = self.copies(k, 0, [(self.y * nx * nz, nx * nz)], self.along_y(), base)
        spans = [((b * nx + self.x) * nz, nz) for b in range(ny)]
        return to_y + self.copies(k, 1, spans, self.along_x(), base + ny - 1)

    @staticmethod
    def semaphores(dims, chunks):
        nz, ny, nx = dims
        count = nz - 1 + 2 * (nx - 1) + 2 * (ny - 1) + (nx - 1) * (ny - 1)
        return pltpu.SemaphoreType.DMA((len(chunks), count))


PART = 64
LISTEN_GROUPS = 16
LISTEN_CHUNKS = ((0, 0, 32), (0, 32, 32))
LISTEN_EVENTS = (
    ((), ((0, 0), (0, 1))),
    ((), ()),
    ((), ()),
    ((), ()),
    (((0, 0),), ((1, 0),)),
    ((), ()),
    ((), ()),
    (((1, 0), (0, 1)), ((2, 0), (1, 1))),
    ((), ()),
    ((), ()),
    ((), ()),
    (((2, 0),), ((3, 0),)),
    ((), ()),
    (((1, 1),), ((2, 1),)),
    ((), ()),
    ((), ()),
    (((2, 1),), ((3, 1),)),
)
SPELL_GROUPS = 18
SPELL_CHUNKS = ((0, 0, PART), (1, 0, PART))
SPELL_EVENTS = (
    ((), ((0, 0), (0, 1))),
    ((), ()),
    (((0, 0),), ((1, 0), (0, 2))),
    (((0, 1),), ((1, 1), (0, 3))),
    (((1, 0),), ((2, 0),)),
    (((1, 1), (0, 2)), ((2, 1), (1, 2), (0, 4))),
    (((2, 0),), ()),
    (((0, 3), (2, 1)), ((1, 3),)),
    (((1, 2),), ((2, 2),)),
    (((1, 3),), ((2, 3),)),
    (((0, 4),), ((1, 4),)),
    (((2, 2),), ()),
    ((), ()),
    (((2, 3),), ((3, 3),)),
    (((1, 4),), ((2, 4),)),
    ((), ()),
    ((), ()),
    (((2, 4),), ((3, 4),)),
    ((), ()),
)


class Gathers:
    def __init__(self, dims, role, dp, events, frames, chunks, states, sems):
        nz, ny, nx = dims
        me = (role, dp // (ny * nx), (dp // nx) % ny, dp % nx)
        self.twin = (1 - role, dp)
        self.role, self.frames, self.chunks, self.events = role, frames, chunks, events
        send, recv, self.last_send, self.last_recv = sems[:4]
        self.slot = (me[2] * nx + me[3]) * nz + me[1]

        def half(first, count, which):
            if which is not None:
                first, count = first + which * count // 2, count // 2
            return pl.ds(first, count)

        def view_frames(which, k, first, count):
            part, *rows = chunks[k]
            return frames.at[part, role, pl.ds(first, count), half(*rows, which)]

        self.two = Gather(dims, me, view_frames, chunks, (send, recv))
        self.lead = 0
        if states is not None:
            self.lead = states.shape[0]

            def view_states(which, k, first, count):
                rows = half(0, states.shape[3], which)
                return states.at[k, :, pl.ds(first, count), rows]

            self.one = Gather(dims, me, view_states, range(self.lead), sems[4:])
        g = self.two
        to_z = [g.device((g.z + j) % nz, g.y, g.x) for j in range(1, nz)]
        self.partners = to_z + g.along_x() + g.along_y() + [self.twin]

    def greet(self):
        barrier = pltpu.get_barrier_semaphore()
        for device in self.partners:
            pl.semaphore_signal(
                barrier, inc=1, device_id=device, device_id_type=pl.DeviceIdType.MESH
            )

    def phase(self, n, c):
        if n == 3:
            k = c - self.lead
            part, *rows = self.chunks[k]
            ref = self.frames.at[part, self.role, :, pl.ds(*rows)]
            return [remote(ref, ref, self.last_send.at[k], self.last_recv.at[k], self.twin)]
        gather, k = (self.one, c) if c < self.lead else (self.two, c - self.lead)
        return (gather.first, gather.second, gather.third)[n](k)

    def begin(self):
        pl.semaphore_wait(pltpu.get_barrier_semaphore(), len(self.partners))

    def look(self, group):
        ended, begun = self.events[group]
        for n, c in ended:
            wait(self.phase(n, c))
        for n, c in begun:
            start(self.phase(n, c))

    def finish(self):
        for k in range(len(self.chunks)):
            wait(self.phase(3, self.lead + k))

    @staticmethod
    def scratch(dims, chunks, states):
        dma = pltpu.SemaphoreType.DMA
        sems = [Gather.semaphores(dims, chunks)] * 2 + [dma((len(chunks),))] * 2
        if states:
            sems += [Gather.semaphores(dims, range(states))] * 2
        return sems


def stage(tiles):
    for k in range(2):
        for unit in range(2):
            pltpu.matmul_push_rhs(tiles(2 * unit + k), k, unit)


def multiply(totals, lefts):
    share = 4 // len(totals)
    for k in range(2):
        for unit in range(2):
            j = 2 * unit + k
            pltpu.matmul_acc_lhs(totals[j // share], lefts[j], load_staged_rhs=k)


SIDE = 256


def staged_product(left, tile, columns, flip=False):
    deep = left.shape[1] // SIDE

    def run(*totals):
        parts = []
        for n in range(0, columns, 2):
            units = range(min(2, columns - n))
            for k in range(deep):
                for unit in units:
                    pltpu.matmul_push_rhs(tile(k, n + unit), k % 2, unit, transpose=flip)
                    pltpu.matmul_acc_lhs(
                        totals[unit], left[:, k * SIDE : (k + 1) * SIDE], load_staged_rhs=k % 2
                    )
            parts += [pltpu.matmul_pop(totals[unit]) for unit in units]
        return jnp.concatenate(parts, 1) if len(parts) > 1 else parts[0]

    rows = left.shape[0]
    return pl.run_scoped(run, *[pltpu.ACC(mxu_id=unit)((rows, SIDE), F32) for unit in range(2)])


def tiles_of(ref):
    return lambda k, n: ref[k * SIDE : (k + 1) * SIDE, n * SIDE : (n + 1) * SIDE]


def staged_loop(first, last, step, carry, tiles, outputs):
    side = tiles(0).shape[0]

    def run(*totals):
        def product(left):
            tall = jnp.concatenate([left, jnp.zeros_like(left)], 0).astype(BF16)
            wide = tall.shape[1] // side
            multiply(totals, [tall[:, (j % wide) * side : (j % wide + 1) * side] for j in range(4)])
            stage(tiles)
            return [pltpu.matmul_pop(total)[: left.shape[0]] for total in totals]

        stage(tiles)
        end = lax.fori_loop(first, last, lambda s, c: step(product, s, c), carry)
        multiply(totals, [jnp.zeros((16, side), BF16)] * 4)
        for total in totals:
            pltpu.matmul_pop(total)
        return end

    units = [j * 2 // outputs for j in range(outputs)]
    return pl.run_scoped(run, *[pltpu.ACC(mxu_id=unit)((16, side), F32) for unit in units])


def listen_forward_kernel(
    dims, lengths, frames, w_in, w_rec, bias,
    pairs, rows_out, factors_out, mine_out, other_out, *rest
):
    role = lax.axis_index("role")
    if dims is not None:
        pairs_all, proj, emit, hprev, to_other, cross, *sems = rest
        gather = Gathers(
            dims, role, lax.axis_index("dp"), LISTEN_EVENTS, pairs_all, LISTEN_CHUNKS, None, sems
        )
        gather.greet()
    else:
        proj, emit, hprev = rest
    utts, time_len, width4 = proj.shape
    units = width4 // 4
    feat = frames.shape[-1]
    window = 2 * time_len - SIDE
    rows = lax.broadcasted_iota(jnp.int32, (time_len, 2 * SIDE), 0)
    cols = lax.broadcasted_iota(jnp.int32, (time_len, 2 * SIDE), 1)
    frame = jnp.where(cols < SIDE, cols, cols - SIDE + window)
    own = jnp.logical_or(cols < SIDE, frame >= SIDE)
    for half in range(2):
        pick = jnp.where(jnp.logical_and(own, frame == 2 * rows + half), 1.0, 0.0).astype(BF16)
        for u in range(utts):
            tile = lambda k, n: frames[
                u, k * window : k * window + SIDE, n * SIDE : (n + 1) * SIDE
            ]
            picked = staged_product(pick, tile, feat // SIDE)
            pairs[u, :, half * feat : (half + 1) * feat] = picked.astype(BF16)
    if dims is not None:
        place = pltpu.make_async_copy(
            pairs.at[role, pl.ds(0, PART)], pairs_all.at[0, role, gather.slot], cross.at[2]
        )
        place.start()
    bias_row = bias[...].astype(F32)
    for u in range(utts):
        proj[u] = staged_product(pairs[u], tiles_of(w_in), width4 // SIDE) + bias_row
    if dims is not None:
        place.wait()
        gather.begin()
    first = lax.broadcasted_iota(jnp.int32, (8, 1), 0) == 0
    row_lengths = jnp.where(first, lengths[0], lengths[1])

    tiles = lambda j: w_rec[:, j * units : (j + 1) * units]

    def step(product, s, carry):
        hidden, cell = carry
        t = jnp.where(role == 1, time_len - 1 - s, s)
        at = pl.ds(t, 1)
        pre_in = jnp.where(first, proj[0, at, :], proj[1, at, :])
        preact = pre_in + jnp.concatenate(product(hidden), 1)
        cell_new, hidden_new, factors = cell_forward(preact, cell)
        live = t < row_lengths
        hidden_next = jnp.where(live, hidden_new, hidden)
        cell_next = jnp.where(live, cell_new, cell)
        emitted = jnp.where(live, hidden_new, 0.0)
        for u in range(2):
            for k in range(6):
                factors_out[u, at, k * units : (k + 1) * units] = factors[k][u : u + 1]
            hprev[u, at, :] = hidden[u : u + 1]
            emit[u, at, :] = emitted[u : u + 1]
        return hidden_next, cell_next

    zero = jnp.zeros((8, units), F32)
    carry = (zero, zero)
    if dims is None:
        staged_loop(0, time_len, step, carry, tiles, 4)
    else:
        count = time_len // LISTEN_GROUPS
        for group in range(LISTEN_GROUPS):
            gather.look(group)
            carry = staged_loop(group * count, (group + 1) * count, step, carry, tiles, 4)
    mine_out[...] = emit[role].astype(BF16)
    if dims is None:
        other_out[...] = emit[1 - role].astype(BF16)
    else:
        to_other[...] = emit[1 - role].astype(BF16)
        crossing = remote(to_other, other_out, cross.at[0], cross.at[1], gather.twin)
        crossing.start()
        gather.look(LISTEN_GROUPS)
    for u in range(utts):
        own = slice(u * time_len, (u + 1) * time_len)
        rows_out[own, :] = hprev[u].astype(BF16)
    if dims is not None:
        crossing.wait()
        gather.finish()


def listen_forward(dims, lengths, frames, w_in, w_rec, bias):
    utts, time_len, width = frames.shape[0], frames.shape[1] // 2, 2 * frames.shape[2]
    units = w_rec.shape[0]
    vmem = pl.BlockSpec(memory_space=pltpu.VMEM)
    shape = jax.ShapeDtypeStruct
    outs = [
        shape((utts, time_len, width), BF16),
        shape((utts * time_len, units), BF16),
        shape((utts, time_len, 6 * units), F32),
        shape((time_len, units), BF16),
        shape((time_len, units), BF16),
    ]
    out_specs = [vmem] * 5
    scratch = [
        pltpu.VMEM((utts, time_len, 4 * units), F32),
        pltpu.VMEM((utts, time_len, units), F32),
        pltpu.VMEM((utts, time_len, units), F32),
    ]
    params = dict(vmem_limit_bytes=VMEM_BYTES)
    if dims is not None:
        chips = dims[0] * dims[1] * dims[2]
        outs.append(shape((1, 2, chips, PART, width), BF16))
        out_specs.append(pl.BlockSpec(memory_space=pl.ANY))
        scratch += [pltpu.VMEM((time_len, units), BF16), pltpu.SemaphoreType.DMA((3,))]
        scratch += Gathers.scratch(dims, LISTEN_CHUNKS, 0)
        params.update(collective_id=1, has_side_effects=True)
    return pl.pallas_call(
        functools.partial(listen_forward_kernel, dims),
        out_shape=outs,
        in_specs=[pl.BlockSpec(memory_space=pltpu.SMEM)] + [vmem] * 4,
        out_specs=out_specs,
        scratch_shapes=scratch,
        compiler_params=pltpu.CompilerParams(**params),
    )(lengths, frames, w_in, w_rec, bias)


def speller_forward_kernel(
    dims, lengths, text_lens, chars, pairs, states,
    mine, other,
    w_lin, w_lhid, b_low, w_uin, w_uhid, b_up, w_key, w_query, vec, w_out, b_out, table,
    loss, prev_onehot, acts, key, keys_proj, key_low, fact1, fact2, q_rows, w_cols, feat_rows, dw_cols,
    logit_grad_out, *rest
):
    role = lax.axis_index("role")
    gather = None
    if dims is not None:
        pairs_all, states_all, emb_proj, s1_rows, s2_rows, hot, stage, own_sem, *sems = rest
        gather = Gathers(
            dims, role, lax.axis_index("dp"), SPELL_EVENTS, pairs_all, SPELL_CHUNKS, states_all, sems
        )
        gather.greet()
        load = pltpu.make_async_copy(
            pairs.at[role, pl.ds(PART, stage.shape[0])], stage, own_sem.at[0]
        )
        load.start()
        parts, utts = states_all.shape[:2]
        place = [
            pltpu.make_async_copy(
                states.at[pl.ds((u * parts + part) * PART, PART)],
                states_all.at[part, u, gather.slot],
                own_sem.at[1 + u * parts + part],
            )
            for u in range(utts)
            for part in range(parts)
        ]
        start(place)
        staged = [
            pltpu.make_async_copy(
                stage.at[pl.ds(part * PART, PART)],
                pairs_all.at[part, role, gather.slot],
                own_sem.at[1 + len(place) + part],
            )
            for part in range(pairs_all.shape[0])
        ]
    else:
        emb_proj, s1_rows, s2_rows, hot = rest
    time_len, units = mine.shape
    steps = emb_proj.shape[0]
    cells = w_lhid.shape[0]
    embed = table.shape[1]
    length = lengths[role]
    text_len = text_lens[0, 0]

    key[:, :units] = jnp.where(role == 0, mine[...], other[...])
    key[:, units:] = jnp.where(role == 0, other[...], mine[...])
    keys_proj[...] = mm(key[...], w_key[...])
    if gather is not None:
        load.wait()
        start(staged)
    key_low[...] = mm(key[...], w_lin[embed:, :])
    ids = lax.broadcasted_iota(jnp.int32, (1, hot.shape[2]), 1)

    def mark(i, previous):
        here = chars[0, 0, i]
        hot[0, pl.ds(i, 1), :] = jnp.where(ids == previous, 1.0, 0.0)
        hot[1, pl.ds(i, 1), :] = jnp.where(ids == here, 1.0, 0.0)
        return here

    lax.fori_loop(0, steps, mark, 0)
    prev_onehot[...] = hot[0].astype(BF16)
    emb = mm(prev_onehot[...], table[...]).astype(BF16)
    emb_proj[...] = mm(emb, w_lin[:embed, :]) + b_low[...].astype(F32)[None]
    bias_up = b_up[...].astype(F32)[None]
    vec_row = vec[...].astype(F32)[None]
    frame_ok = lax.broadcasted_iota(jnp.int32, (time_len, 1), 0) < length
    lane = lax.broadcasted_iota(jnp.int32, w_cols.shape, 1)
    w_cols[...] = jnp.zeros_like(w_cols)
    if gather is not None:
        wait(place)
        wait(staged)
        gather.begin()

    def forward_step(i, carry):
        cell1, cell2, hid1, hid2, ctx_low = carry
        at = pl.ds(i, 1)
        pre1 = emb_proj[at, :] + hid1 + ctx_low
        cell1, s1, factors = cell_forward(pre1, cell1)
        for k in range(6):
            fact1[at, k * cells : (k + 1) * cells] = factors[k]
        s1_rows[at, :] = s1
        s1_low = s1.astype(BF16)
        pre2 = hid2 + bias_up + mm(s1_low, w_uin[...])
        hid1 = mm(s1_low, w_lhid[...])
        cell2, s2, factors = cell_forward(pre2, cell2)
        for k in range(6):
            fact2[at, k * cells : (k + 1) * cells] = factors[k]
        s2_rows[at, :] = s2
        s2_low = s2.astype(BF16)
        query = mm(s2_low, w_query[...])
        hid2 = mm(s2_low, w_uhid[...])
        q_rows[at, :] = query
        part = None
        for j in range(query.shape[1] // 128):
            cut = slice(j * 128, (j + 1) * 128)
            term = jnp.tanh(keys_proj[:, cut] + query[:, cut]) * vec_row[:, cut]
            part = term if part is None else part + term
        scores = jnp.sum(part, -1, keepdims=True)
        scores = jnp.where(frame_ok, scores, -1000000000.0)
        scores = scores - jnp.max(scores, 0, keepdims=True)
        expf = jnp.where(frame_ok, jnp.exp(scores), 0.0)
        rinv = 1.0 / jnp.sum(expf, 0, keepdims=True)
        w_cols[...] = jnp.where(lane == i, expf * rinv, w_cols[...])
        ctx_low = jnp.concatenate(
            [
                jnp.sum(expf * key_low[:, j * 128 : (j + 1) * 128], 0, keepdims=True)
                for j in range(key_low.shape[1] // 128)
            ],
            1,
        )
        return cell1, cell2, hid1, hid2, ctx_low * rinv

    zero = jnp.zeros((1, cells), F32)
    wide = jnp.zeros((1, 4 * cells), F32)
    carry = (zero, zero, wide, wide, wide)
    if gather is None:
        lax.fori_loop(0, steps, forward_step, carry)
    else:
        count = steps // SPELL_GROUPS
        for group in range(SPELL_GROUPS):
            gather.look(group)
            carry = lax.fori_loop(group * count, (group + 1) * count, forward_step, carry)
        gather.look(SPELL_GROUPS)

    w_low = jnp.transpose(w_cols[...])[:steps].astype(BF16)
    ctx = mm(w_low, key[...]).astype(BF16)
    s2_low = s2_rows[...].astype(BF16)
    logits = mm_nt(s2_low, w_out[:, :cells]) + mm_nt(ctx, w_out[:, cells:]) + b_out[...].astype(F32)[None]
    top = jnp.max(logits, -1, keepdims=True)
    log_total = top + jnp.log(jnp.sum(jnp.exp(logits - top), -1, keepdims=True))
    target = hot[1]
    cross = log_total - jnp.sum(logits * target, -1, keepdims=True)
    text = text_len.astype(F32)
    alive = lax.broadcasted_iota(jnp.int32, (steps, 1), 0) < text_len
    loss[...] = jnp.sum(jnp.where(alive, cross, 0.0), 0, keepdims=True) / text
    scale = jnp.where(alive, 1.0 / text, 0.0)
    logit_grad = (scale * (jnp.exp(logits - log_total) - target)).astype(BF16)
    logit_grad_out[...] = logit_grad
    feat_rows[...] = mm(logit_grad, w_out[...])
    dw_cols[...] = jnp.zeros_like(dw_cols)
    dw_cols[:, :steps] = mm_nt(key[...], feat_rows[:, cells:].astype(BF16))
    acts[steps:, :] = jnp.zeros((acts.shape[0] - steps, acts.shape[1]), BF16)
    acts[:steps, :embed] = emb
    acts[:steps, embed : embed + 2 * units] = ctx
    acts[:steps, embed + 2 * units : embed + 2 * units + cells] = s1_rows[...].astype(BF16)
    acts[:steps, embed + 2 * units + cells :] = s2_low
    if gather is not None:
        gather.finish()


def speller_forward(
    dims, lengths, text_lens, chars, pairs, states, mine, other,
    w_lin, w_lhid, b_low, w_uin, w_uhid, b_up, w_key, w_query, vec, w_out, b_out, table,
):
    time_len, units = mine.shape
    steps, vocab = chars.shape[2], table.shape[0]
    cells = w_lhid.shape[0]
    att = w_key.shape[1]
    embed = table.shape[1]
    pad_steps = -(-steps // 16) * 16
    vmem = pl.BlockSpec(memory_space=pltpu.VMEM)
    smem = pl.BlockSpec(memory_space=pltpu.SMEM)
    shape = jax.ShapeDtypeStruct
    outs = [
        shape((1, 1), F32),
        shape((steps, vocab), BF16),
        shape((pad_steps, embed + 2 * units + 2 * cells), BF16),
        shape((time_len, 2 * units), BF16),
        shape((time_len, att), F32),
        shape((time_len, 4 * cells), F32),
        shape((steps, 6 * cells), F32),
        shape((steps, 6 * cells), F32),
        shape((steps, att), F32),
        shape((time_len, -(-steps // 128) * 128), F32),
        shape((steps, w_out.shape[1]), F32),
        shape((time_len, -(-steps // 128) * 128), F32),
        shape((steps, vocab), BF16),
    ]
    out_specs = [vmem] * len(outs)
    scratch = [
        pltpu.VMEM((steps, 4 * cells), F32),
        pltpu.VMEM((steps, cells), F32),
        pltpu.VMEM((steps, cells), F32),
        pltpu.VMEM((2, steps, vocab), F32),
    ]
    params = dict(vmem_limit_bytes=VMEM_BYTES)
    if dims is not None:
        chips = dims[0] * dims[1] * dims[2]
        dma = pltpu.SemaphoreType.DMA
        utts, _, width = pairs.shape
        parts = time_len // PART
        high = parts - 1
        outs.append(shape((high, utts, chips, PART, width), BF16))
        outs.append(shape((parts, utts, chips, PART, units), BF16))
        out_specs += [pl.BlockSpec(memory_space=pl.ANY)] * 2
        scratch += [pltpu.VMEM((high * PART, width), BF16), dma((1 + high + utts * parts,))]
        scratch += Gathers.scratch(dims, SPELL_CHUNKS, parts)
        params.update(collective_id=2, has_side_effects=True)
    return pl.pallas_call(
        functools.partial(speller_forward_kernel, dims),
        out_shape=outs,
        in_specs=[smem] * 3 + [pl.BlockSpec(memory_space=pl.ANY)] + [vmem] * 15,
        out_specs=out_specs,
        scratch_shapes=scratch,
        compiler_params=pltpu.CompilerParams(**params),
    )(
        lengths, text_lens, chars, pairs, states, mine, other,
        w_lin, w_lhid, b_low, w_uin, w_uhid, b_up, w_key, w_query, vec, w_out, b_out, table,
    )


SMALL = 32


def shift_up(rows):
    count = rows.shape[0]
    rolled = pltpu.roll(rows, count - 1, 0)
    at = lax.broadcasted_iota(jnp.int32, rows.shape, 0)
    return jnp.where(at == count - 1, 0.0, rolled)


def speller_backward_kernel(
    w_lin, w_lhid, w_uin, w_uhid, w_key, w_query, vec, prev_onehot,
    acts, key, keys_proj, key_low, fact1, fact2, q_rows, w_cols, feat_rows, dw_cols, logit_grad,
    grad_mine, grad_other, dp1_out, dp2_out, pack,
    dp1_rows, dp2_rows, dq_rows, keys_acc, vec_acc, small, t_lhid, t_uin, t_uhid, t_query,
):
    role = lax.axis_index("role")
    time_len, att = keys_proj.shape
    steps, vocab = logit_grad.shape
    units = key.shape[1] // 2
    cells = w_lhid.shape[0]
    embed = acts.shape[1] - 2 * units - 2 * cells
    vec_row = vec[...].astype(F32)[None]
    zero = jnp.zeros((1, cells), F32)
    wide = jnp.zeros((1, 4 * cells), BF16)
    keys_acc[...] = jnp.zeros_like(keys_acc)
    vec_acc[...] = jnp.zeros_like(vec_acc)
    t_lhid[...] = w_lhid[...].T
    t_uin[...] = w_uin[...].T
    t_uhid[...] = w_uhid[...].T
    t_query[...] = w_query[...].T
    lane = lax.broadcasted_iota(jnp.int32, w_cols.shape, 1)

    def backward_step(s, carry):
        dp1, dp2, dcell1, dcell2 = carry
        i = steps - 1 - s
        at = pl.ds(i, 1)
        query = q_rows[at, :]
        dp1_row = dp1.astype(F32)
        here = lane == i
        part = jnp.where(here, dw_cols[...], 0.0)
        for j in range(key_low.shape[1] // 128):
            cut = slice(j * 128, (j + 1) * 128)
            part = part + dp1_row[:, cut] * key_low[:, cut]
        dweights = jnp.sum(part, -1, keepdims=True)
        weights = jnp.sum(jnp.where(here, w_cols[...], 0.0), -1, keepdims=True)
        back2 = mm(dp2, t_uhid[...])
        back1 = mm(dp1, t_lhid[...])
        shared = weights * dweights
        dscore = shared - weights * jnp.sum(shared, 0, keepdims=True)
        sums = []
        for j in range(query.shape[1] // 128):
            cut = slice(j * 128, (j + 1) * 128)
            energy = jnp.tanh(keys_proj[:, cut] + query[:, cut])
            moved = dscore * (1.0 - energy * energy)
            keys_acc[:, cut] += moved
            sums.append(jnp.sum(moved, 0, keepdims=True))
            vec_acc[:, cut] += jnp.sum((dscore * energy).reshape(time_len // 8, 8, 128), 0)
        dquery = (jnp.concatenate(sums, 1) * vec_row).astype(BF16)
        dq_rows[at, :] = dquery.astype(F32)
        ds2 = back2 + feat_rows[at, :cells] + mm(dquery, t_query[...])
        pre2, dcell2 = cell_backward(fact2[at, :], ds2, dcell2)
        dp2_rows[at, :] = pre2
        dp2 = pre2.astype(BF16)
        ds1 = back1 + mm(dp2, t_uin[...])
        pre1, dcell1 = cell_backward(fact1[at, :], ds1, dcell1)
        dp1_rows[at, :] = pre1
        return pre1.astype(BF16), dp2, dcell1, dcell2

    lax.fori_loop(0, steps, backward_step, (wide, wide, zero, zero))

    dp1 = dp1_rows[...].astype(BF16)
    dp2 = dp2_rows[...].astype(BF16)
    dq = dq_rows[...].astype(BF16)
    extra = jnp.zeros((dp1_out.shape[0] - steps, 4 * cells), BF16)
    dp1_out[steps:, :] = extra
    dp2_out[steps:, :] = extra
    dp1_out[:steps, :] = dp1
    dp2_out[:steps, :] = dp2
    next_dp1 = shift_up(dp1.astype(F32)).astype(BF16)
    ctx_grad = (feat_rows[:, cells:] + mm_nt(next_dp1, w_lin[embed:, :])).astype(BF16)
    keys_grad = (keys_acc[...] * vec_row).astype(BF16)
    w_low = w_cols[...].astype(BF16)[:, :steps]
    key_grad = mm_nt(keys_grad, w_key[...]) + mm(w_low, ctx_grad)
    key_grad = key_grad.astype(BF16)
    grad_mine[...] = jnp.where(role == 0, key_grad[:, :units], key_grad[:, units:])
    grad_other[...] = jnp.where(role == 0, key_grad[:, units:], key_grad[:, :units])
    ctx = acts[:steps, embed : embed + 2 * units]
    s2 = acts[:steps, embed + 2 * units + cells :]
    wide = pack.shape[1]
    deep = 2 * units * att // wide
    g_key = mm_tn(key[...], keys_grad)
    g_query = mm_tn(s2, dq)
    for k in range(wide // att):
        cut = slice(k * att, (k + 1) * att)
        first = 2 * SMALL
        pack[first : first + deep, cut] = g_key[k * deep : (k + 1) * deep].astype(BF16)
        first += deep
        pack[first : first + deep, cut] = g_query[k * deep : (k + 1) * deep].astype(BF16)
    emb_grad = mm_nt(dp1, w_lin[:embed, :])
    hot = prev_onehot[...]
    total = None
    for _ in range(3):
        low = emb_grad.astype(BF16)
        emb_grad = emb_grad - low.astype(F32)
        total = mm_tn(hot, low) if total is None else total + mm_tn(hot, low)
    small[...] = jnp.zeros_like(small)
    small[:vocab, :cells] = mm_tn(logit_grad[...], s2)
    small[:vocab, cells : cells + 2 * units] = mm_tn(logit_grad[...], ctx)
    base = cells + 2 * units
    small[:vocab, base : base + embed] = total
    base += embed
    small[0:1, base : base + att] = jnp.sum(vec_acc[...], 0, keepdims=True)
    small[1:2, base : base + vocab] = jnp.sum(logit_grad[...].astype(F32), 0, keepdims=True)
    low_bias = jnp.sum(dp1.astype(F32), 0, keepdims=True)
    up_bias = jnp.sum(dp2.astype(F32), 0, keepdims=True)
    for k in range(4):
        small[2 + k : 3 + k, base : base + cells] = low_bias[:, k * cells : (k + 1) * cells]
        small[6 + k : 7 + k, base : base + cells] = up_bias[:, k * cells : (k + 1) * cells]
    high = small[...].astype(BF16)
    pack[:SMALL, :] = high
    pack[SMALL : 2 * SMALL, :] = (small[...] - high.astype(F32)).astype(BF16)


def speller_backward(
    w_lin, w_lhid, w_uin, w_uhid, w_key, w_query, vec, prev_onehot,
    acts, key, keys_proj, key_low, fact1, fact2, q_rows, w_cols, feat_rows, dw_cols, logit_grad,
):
    time_len, att = keys_proj.shape
    steps, vocab = logit_grad.shape
    units = key.shape[1] // 2
    cells = w_lhid.shape[0]
    pad_steps = acts.shape[0]
    vmem = pl.BlockSpec(memory_space=pltpu.VMEM)
    shape = jax.ShapeDtypeStruct
    outs = [
        shape((time_len, units), BF16),
        shape((time_len, units), BF16),
        shape((pad_steps, 4 * cells), BF16),
        shape((pad_steps, 4 * cells), BF16),
        shape(((2 * units + cells) * att // (4 * cells) + 2 * SMALL, 4 * cells), BF16),
    ]
    out_specs = [vmem] * 5
    scratch = [
        pltpu.VMEM((steps, 4 * cells), F32),
        pltpu.VMEM((steps, 4 * cells), F32),
        pltpu.VMEM((steps, att), F32),
        pltpu.VMEM((time_len, att), F32),
        pltpu.VMEM((8, att), F32),
        pltpu.VMEM((SMALL, 4 * cells), F32),
        pltpu.VMEM((4 * cells, cells), BF16),
        pltpu.VMEM((4 * cells, cells), BF16),
        pltpu.VMEM((4 * cells, cells), BF16),
        pltpu.VMEM((att, cells), BF16),
    ]
    return pl.pallas_call(
        speller_backward_kernel,
        out_shape=outs,
        in_specs=[vmem] * 19,
        out_specs=out_specs,
        scratch_shapes=scratch,
        compiler_params=pltpu.CompilerParams(vmem_limit_bytes=VMEM_BYTES),
    )(
        w_lin, w_lhid, w_uin, w_uhid, w_key, w_query, vec, prev_onehot,
        acts, key, keys_proj, key_low, fact1, fact2, q_rows, w_cols, feat_rows, dw_cols, logit_grad,
    )


def unfold(folded, width):
    deep = folded.shape[0]
    return folded.reshape(deep, -1, width).swapaxes(0, 1).reshape(-1, width)


def unpack(small, units, cells, att, vocab, embed):
    small = small[:SMALL].astype(F32) + small[SMALL:].astype(F32)
    base = cells + 2 * units
    g_out = small[:vocab, :base].T
    g_table = small[:vocab, base : base + embed]
    base += embed
    low_bias = small[2:6, base : base + cells].reshape(-1)
    up_bias = small[6:10, base : base + cells].reshape(-1)
    g_vec = small[0, base : base + att]
    g_obias = small[1, base : base + vocab]
    return low_bias, up_bias, g_vec, g_out, g_obias, g_table


def backward_steps(role, lengths, factors, grad_out, w_back, grad_pre, first_step, count, carry):
    time_len = factors.shape[1]
    first = lax.broadcasted_iota(jnp.int32, (8, 1), 0) == 0
    row_lengths = jnp.where(first, lengths[0], lengths[1])

    units = w_back.shape[1]
    tiles = lambda j: w_back[j * units : (j + 1) * units, :]

    def step(product, s, carry):
        grad_hidden, grad_cell = carry
        t = jnp.where(role == 1, s, time_len - 1 - s)
        at = pl.ds(t, 1)
        live = t < row_lengths
        fact = jnp.where(first, factors[0, at, :], factors[1, at, :])
        arrived = jnp.where(first, grad_out[0, at, :], grad_out[1, at, :])
        fact = jnp.where(live, fact, 0.0)
        total = grad_hidden + jnp.where(live, arrived, 0.0)
        pre, cell_back = cell_backward(fact, total, grad_cell)
        for u in range(2):
            grad_pre[u, at, :] = pre[u : u + 1]
        back = sum(product(pre))
        return jnp.where(live, back, total), jnp.where(live, cell_back, grad_cell)

    return staged_loop(first_step, first_step + count, step, carry, tiles, 2)


def listen_backward_kernel(
    lengths, factors, grad_mine, grad_other, w_rec, pre_out, grad_pre, grad_out, w_back
):
    role = lax.axis_index("role")
    grad_out[role] = grad_mine[...].astype(F32)
    grad_out[1 - role] = grad_other[...].astype(F32)
    w_back[...] = w_rec[...].T
    zero = jnp.zeros((8, w_rec.shape[0]), F32)
    backward_steps(
        role, lengths, factors, grad_out, w_back, grad_pre, 0, factors.shape[1], (zero, zero)
    )
    pre_out[...] = grad_pre[...].astype(BF16)


def listen_backward(lengths, factors, grad_mine, grad_other, w_rec):
    utts, time_len, _ = factors.shape
    units = w_rec.shape[0]
    vmem = pl.BlockSpec(memory_space=pltpu.VMEM)
    return pl.pallas_call(
        listen_backward_kernel,
        out_shape=jax.ShapeDtypeStruct((utts, time_len, 4 * units), BF16),
        in_specs=[pl.BlockSpec(memory_space=pltpu.SMEM)] + [vmem] * 4,
        out_specs=vmem,
        scratch_shapes=[
            pltpu.VMEM((utts, time_len, 4 * units), F32),
            pltpu.VMEM((utts, time_len, units), F32),
            pltpu.VMEM((4 * units, units), BF16),
        ],
        compiler_params=pltpu.CompilerParams(vmem_limit_bytes=VMEM_BYTES),
    )(lengths, factors, grad_mine, grad_other, w_rec)


SEGMENT = 32
STREAMS = ((0, 3), (3, 5), (5, 6))


SP_CHUNKS = ((320, 352), (672, 352), (1024, 320), (0, 320))
LI_CHUNKS = ((0, 96), (96, 160), (256, 192), (448, 224))
HEAD = 320
EXCHANGE_PROGRAM = (
    (),
    (),
    (),
    (),
    (),
    (),
    ('pack_x',),
    (),
    ('columns', ('s', 'sp', 0, 0), ('s', 'sp', 0, 1), 'pack_y',),
    (),
    (),
    (),
    ('stream0', 'far', ('w', 'sp', 0, 0), ('s', 'sp', 1, 0), ('s', 'sp', 0, 2),),
    (),
    (),
    (),
    (('w', 'sp', 1, 0), ('s', 'sp', 2, 0), ('w', 'sp', 0, 1), ('s', 'sp', 1, 1),),
    ('pack_z', ('s', 'sp', 0, 3),),
    (),
    (),
    ('stream1', ('w', 'sp', 2, 0), ('s', 'sp', 3, 0),),
    (),
    (('w', 'sp', 1, 1), ('s', 'sp', 2, 1),),
    (('w', 'sp', 0, 2), ('s', 'sp', 1, 2),),
    ('stream2', 'near',),
    (('w', 'sp', 0, 3), ('s', 'sp', 1, 3), ('w', 'sp', 2, 1), ('s', 'sp', 3, 1), ('w', 'sp', 1, 2), ('s', 'sp', 2, 2), ('w', 'sp', 1, 3), ('s', 'sp', 2, 3), 'li_columns', ('s', 'li', 0, 0), ('s', 'li', 0, 1), ('w', 'sp', 2, 2), ('s', 'sp', 3, 2), ('w', 'li', 0, 0), ('s', 'li', 1, 0), ('s', 'li', 0, 2), ('w', 'li', 0, 1), ('s', 'li', 1, 1), ('s', 'li', 0, 3), ('w', 'sp', 2, 3), ('s', 'sp', 3, 3), ('w', 'li', 1, 0), ('s', 'li', 2, 0), ('w', 'li', 1, 1), ('s', 'li', 2, 1), ('w', 'li', 0, 2), ('s', 'li', 1, 2), ('w', 'li', 0, 3), ('s', 'li', 1, 3), ('w', 'li', 1, 2), ('s', 'li', 2, 2), ('w', 'li', 1, 3), ('s', 'li', 2, 3),),
)


def exchange_kernel(
    dims,
    lengths, factors, grad_mine, grad_other, w_in, w_rec, dp1, dp2, pack, acts_all, pairs_low, pairs_high, rows_all,
    frames_out, li_out, sp_out,
    grad_pre, grad_out, acts_buf, pairs_buf, rows_buf, dp_pair, got, got_t, prod, column,
    li_send, li_got, li_rows, li_acc, li_all, fr_send, fr_got, weave,
    pk_pair, pk_x, pk_xsum, pk_y, pk_ysum, pk_z,
    local_sem, chip_send, chip_recv, aa_send, aa_recv, li_aa_send, li_aa_recv,
    sp_send, sp_recv, li_ag_send, li_ag_recv, pk_send, pk_recv, far_grad, w_back,
):
    nz, ny, nx = dims
    chips = nz * ny * nx
    role = lax.axis_index("role")
    dp = lax.axis_index("dp")
    z, y, x = dp // (ny * nx), (dp // nx) % ny, dp % nx
    utts, time_len, width = grad_pre.shape
    units = w_rec.shape[0]
    cells = dp1.shape[1] // 4
    half_time = time_len // 2
    pads = dp1.shape[0]
    twin = (1 - role, dp)

    def slot_of(chip):
        return (((chip // nx) % ny) * nx + chip % nx) * nz + chip // (ny * nx)

    slot = slot_of(dp)
    lanes = pl.ds(pl.multiple_of(slot * 128, 128), 128)

    barrier = pltpu.get_barrier_semaphore()
    mesh = pl.DeviceIdType.MESH

    def greet(k, _):
        pl.semaphore_signal(barrier, inc=1, device_id=(role, (dp + k) % chips), device_id_type=mesh)
        return 0

    pl.semaphore_signal(barrier, inc=1, device_id=twin, device_id_type=mesh)
    lax.fori_loop(1, chips, greet, 0)
    load_acts = pltpu.make_async_copy(
        acts_all.at[:, pl.ds(pl.multiple_of(role * cells, 128), acts_buf.shape[1])],
        acts_buf, local_sem.at[0],
    )
    load_acts.start()
    load_rows = [pltpu.make_async_copy(rows_all, rows_buf.at[:, pl.ds(0, units)], local_sem.at[1])]
    rows_buf[:, units:] = jnp.ones((rows_buf.shape[0], rows_buf.shape[1] - units), BF16)
    start(load_rows)
    split = pairs_low.shape[0]
    load_pairs = [
        pltpu.make_async_copy(pairs_low, pairs_buf.at[pl.ds(0, split)], local_sem.at[4]),
        pltpu.make_async_copy(pairs_high, pairs_buf.at[pl.ds(split, pairs_high.shape[0])], local_sem.at[5]),
    ]
    start(load_pairs)
    dp_pair[role] = jnp.where(role == 0, dp1[...], dp2[...])
    dp_pair[2] = jnp.where(role == 0, dp2[...], dp1[...])
    grad_out[role] = grad_mine[...].astype(F32)
    w_back[...] = w_rec[...].T
    pl.semaphore_wait(barrier, chips)
    last = chip_send.shape[0] - 1
    crossing = remote(grad_other, far_grad, chip_send.at[last], chip_recv.at[last], twin)
    crossing.start()

    to_twin = remote(dp_pair.at[2], dp_pair.at[role], chip_send.at[0], chip_recv.at[0], twin)
    to_twin.start()
    pack_twin = remote(pack, pk_pair, pk_send.at[0], pk_recv.at[0], twin)

    @pl.when(role == 0)
    def _():
        pack_twin.start()

    to_twin.wait()

    def block(k):
        chip = (dp + k) % chips
        cut = pl.ds(pl.multiple_of(slot_of(chip) * 128, 128), 128)
        return remote(
            dp_pair.at[pl.ds(0, 2), :, cut], got.at[dp],
            aa_send.at[k - 1], aa_recv.at[k - 1], (role, chip),
        )

    lax.fori_loop(1, chips, lambda k, _: (block(k).start(), 0)[1], 0)
    own_block = pltpu.make_async_copy(
        dp_pair.at[pl.ds(0, 2), :, lanes], got.at[dp], local_sem.at[2]
    )
    own_block.start()

    def rounded(total):
        value = total[:SMALL] + total[SMALL : 2 * SMALL]
        high = value.astype(BF16)
        low = (value - high.astype(F32)).astype(BF16)
        return jnp.concatenate([high, low, total[2 * SMALL :].astype(BF16)], 0)

    chip_at = lambda a, b, c: (role, (a * ny + b) * nx + c)
    x_other, y_other = (x + 1) % nx, (y + 1) % ny
    column_wide = nz * 128

    def pack_x(b):
        first = pl.multiple_of((b * nx + x_other) * column_wide, 128)
        return remote(
            pk_pair.at[:, pl.ds(first, column_wide)], pk_x.at[b],
            pk_send.at[1 + b], pk_recv.at[1 + b], chip_at(z, y, x_other),
        )

    pack_y = remote(
        pk_xsum.at[y_other], pk_y, pk_send.at[1 + ny], pk_recv.at[1 + ny], chip_at(z, y_other, x)
    )

    def pack_z(j):
        to = (z + j) % nz
        return remote(
            pk_ysum.at[:, pl.ds(pl.multiple_of(to * 128, 128), 128)], pk_z.at[z],
            pk_send.at[1 + ny + j], pk_recv.at[1 + ny + j], chip_at(to, y, x),
        )

    @pl.when(role == 0)
    def _():
        pack_twin.wait_send()

    @pl.when(role == 1)
    def _():
        pack_twin.wait_recv()

        def add(b, _):
            cut = pl.ds(pl.multiple_of(b * 128, 128), 128)
            total = pk_pair[:, cut].astype(F32) + pack[:, cut].astype(F32)
            pk_pair[:, cut] = rounded(total)
            return 0

        lax.fori_loop(0, pack.shape[1] // 128, add, 0)
        for b in range(ny):
            pack_x(b).start()

    def pack_after_x():
        for b in range(ny):
            pack_x(b).wait()
            first = pl.multiple_of((b * nx + x) * column_wide, 128)

            def add(c, _):
                here = pl.ds(pl.multiple_of(first + c * 128, 128), 128)
                cut = pl.ds(pl.multiple_of(c * 128, 128), 128)
                total = pk_pair[:, here].astype(F32) + pk_x[b, :, cut].astype(F32)
                pk_xsum[b, :, cut] = rounded(total)
                return 0

            lax.fori_loop(0, nz, add, 0)
        pack_y.start()

    def pack_after_y():
        pack_y.wait()

        def add(c, _):
            cut = pl.ds(pl.multiple_of(c * 128, 128), 128)
            total = pk_xsum[y, :, cut].astype(F32) + pk_y[:, cut].astype(F32)
            pk_ysum[:, cut] = rounded(total)
            return 0

        lax.fori_loop(0, nz, add, 0)
        for j in range(1, nz):
            pack_z(j).start()

    def pack_after_z():
        for j in range(1, nz):
            pack_z(j).wait()
        pk_z[z] = pk_ysum[:, pl.ds(pl.multiple_of(z * 128, 128), 128)]
        total = pk_z[0].astype(F32)
        for j in range(1, nz):
            total = total + pk_z[j].astype(F32)
        column[: total.shape[0], :] = rounded(total)

    def view_sp(which, k, first, count):
        rows = SP_CHUNKS[k]
        if which is not None:
            rows = (rows[0] + which * rows[1] // 2, rows[1] // 2)
        cut = pl.ds(pl.multiple_of(first * 128, 128), count * 128)
        return sp_out.at[role, pl.ds(*rows), cut]

    def view_li(which, k, first, count):
        rows = LI_CHUNKS[k]
        if which is not None:
            rows = (rows[0] + which * rows[1] // 2, rows[1] // 2)
        return li_all.at[pl.ds(first, count), pl.ds(*rows)]

    me = (role, z, y, x)
    sp = Gather(dims, me, view_sp, SP_CHUNKS, (sp_send, sp_recv))
    li = Gather(dims, me, view_li, LI_CHUNKS, (li_ag_send, li_ag_recv))

    def sp_last(k):
        ref = sp_out.at[role, pl.ds(*SP_CHUNKS[k])]
        return [remote(ref, ref, chip_send.at[2 + k], chip_recv.at[2 + k], twin)]

    def rows_of(j):
        return jnp.where(role == 1, SEGMENT * j, time_len - SEGMENT * (j + 1))

    def pack_columns(first_segment, last_segment):
        lane = lax.broadcasted_iota(jnp.int32, (SEGMENT, 128), 1)
        for j in range(first_segment, last_segment):
            rows = pl.ds(pl.multiple_of(rows_of(j), SEGMENT), SEGMENT)
            for b in range(width // 128):
                one = grad_pre[0, rows, b * 128 : (b + 1) * 128]
                two = grad_pre[1, rows, b * 128 : (b + 1) * 128]
                even = jnp.where(lane < 64, one, pltpu.roll(two, 64, 1))
                odd = jnp.where(lane < 64, pltpu.roll(one, 64, 1), two)
                li_send[2 * b, rows, :] = even.astype(BF16)
                li_send[2 * b + 1, rows, :] = odd.astype(BF16)

    def stream(n):
        first_segment, last_segment = STREAMS[n]
        count = SEGMENT * (last_segment - first_segment)
        begin = jnp.where(role == 1, SEGMENT * first_segment, time_len - SEGMENT * last_segment)
        rows = pl.ds(pl.multiple_of(begin, SEGMENT), count)

        def one(k):
            chip = (dp + k) % chips
            return remote(
                li_send.at[slot_of(chip), rows], li_got.at[dp, rows],
                li_aa_send.at[n, k - 1], li_aa_recv.at[n, k - 1], (role, chip),
            )

        return one

    def start_stream(n):
        pack_columns(*STREAMS[n])
        one = stream(n)
        lax.fori_loop(1, chips, lambda k, _: (one(k).start(), 0)[1], 0)

    def wait_stream(n):
        one = stream(n)
        lax.fori_loop(1, chips, lambda k, _: (one(k).wait(), 0)[1], 0)

    crossing.wait()
    grad_out[1 - role] = far_grad[...].astype(F32)
    zero = jnp.zeros((8, units), F32)
    carry = (zero, zero)

    def back_to_frames(rows):
        tile = lambda k, n: w_in[n * SIDE : (n + 1) * SIDE, k * SIDE : (k + 1) * SIDE]
        return staged_product(rows.astype(BF16), tile, w_in.shape[0] // SIDE, flip=True)

    def run(j, count, carry):
        return backward_steps(
            role, lengths, factors, grad_out, w_back, grad_pre, count * j, count, carry
        )

    def place(first, count):
        copy = pltpu.make_async_copy(
            column.at[pl.ds(first, count)], sp_out.at[role, pl.ds(first, count), lanes],
            local_sem.at[3],
        )
        copy.start()
        copy.wait()

    def columns():
        lax.fori_loop(1, chips, lambda k, _: (block(k).wait(), 0)[1], 0)
        own_block.wait()
        load_acts.wait()
        both = got[...].reshape(chips * 2 * pads, 128).astype(F32)
        rolled = pltpu.roll(both, chips * 2 * pads - 1, 0)
        got_t[0] = jnp.transpose(both).astype(BF16)
        got_t[1] = jnp.transpose(rolled).astype(BF16)
        groups = acts_buf.shape[1] // 256
        for g in range(groups):
            cut = slice(g * 256, (g + 1) * 256)
            if g == 0:
                left = got_t[0]
            elif g < groups - cells // 256:
                left = got_t[1 - role]
            else:
                left = got_t[1]
            prod[:, cut] = staged_product(left, lambda k, n: acts_buf[k * SIDE : (k + 1) * SIDE, cut], 1)
        column[2 * SMALL :, :] = jnp.transpose(prod[...]).astype(BF16)
        column[: 2 * SMALL, :] = jnp.zeros((2 * SMALL, 128), BF16)

        place(HEAD, column.shape[0] - HEAD)

    far = jnp.where(role == 0, half_time, 0)
    near = half_time - far
    frames_copy = remote(fr_send, fr_got, chip_send.at[1], chip_recv.at[1], twin)

    def far_frames():
        for u in range(utts):
            rows = pl.ds(pl.multiple_of(far, half_time), half_time)
            fr_send[u] = back_to_frames(grad_pre[u, rows, :]).astype(BF16)
        frames_copy.start()

    def near_frames():
        frames_copy.wait()
        feat = frames_out.shape[2]
        for u in range(utts):
            rows = pl.ds(pl.multiple_of(near, half_time), half_time)
            total = back_to_frames(grad_pre[u, rows, :]) + fr_got[u].astype(F32)
            for j in range(feat // 128):
                for half in range(2):
                    cut = slice(half * feat + j * 128, half * feat + (j + 1) * 128)
                    weave[pl.ds(half, half_time, stride=2), :] = total[:, cut]
                frames_out[u, :, j * 128 : (j + 1) * 128] = weave[...]

    def listener_columns():
        li_got[dp] = li_send[slot]
        wait(load_rows)
        wait(load_pairs)
        for n in range(len(STREAMS)):
            wait_stream(n)

        def spread(c, _):
            value = li_got[c].astype(F32)
            for u, part in enumerate((value, pltpu.roll(value, 64, 1))):
                for p in range(time_len // PART):
                    base = pl.multiple_of(((p * utts + u) * chips + slot_of(c)) * PART, PART)
                    li_rows[pl.ds(base, PART), :] = part[p * PART : (p + 1) * PART].astype(BF16)
            return 0

        lax.fori_loop(0, chips, spread, 0)
        li_acc[...] = jnp.zeros_like(li_acc)
        deep = 4 * time_len
        features = pairs_buf.shape[1]

        def accumulate(c, _):
            rows = pl.ds(pl.multiple_of(c * deep, 256), deep)
            left = jnp.transpose(li_rows[rows, :])
            for source, base in ((pairs_buf, 0), (rows_buf, features)):
                piece = lambda k, n: source[
                    pl.ds(pl.multiple_of(c * deep + k * SIDE, SIDE), SIDE), n * SIDE : (n + 1) * SIDE
                ]
                wide = source.shape[1]
                li_acc[:, base : base + wide] += staged_product(left, piece, wide // SIDE)
            return 0

        lax.fori_loop(0, chips * 2 * time_len // deep, accumulate, 0)
        flipped = jnp.transpose(li_acc[:, : features + units + 64])
        tall = flipped.shape[0] // 2
        lane = lax.broadcasted_iota(jnp.int32, (tall, 128), 1)
        packed = jnp.where(lane < 64, flipped[:tall], pltpu.roll(flipped[tall:], 64, 1))
        li_all[slot] = packed.astype(BF16)

    def finish_pack():
        pl.when(role == 1)(pack_after_z)
        place(0, HEAD)

    work = {
        "pack_x": lambda: pl.when(role == 1)(pack_after_x),
        "pack_y": lambda: pl.when(role == 1)(pack_after_y),
        "pack_z": finish_pack,
        "columns": columns,
        "far": far_frames,
        "near": near_frames,
        "li_columns": listener_columns,
    }
    work.update({"stream%d" % n: functools.partial(start_stream, n) for n in range(len(STREAMS))})
    phases = {
        "sp": (sp.first, sp.second, sp.third, sp_last),
        "li": (li.first, li.second, li.third),
    }

    def perform(items):
        for item in items:
            if item in work:
                work[item]()
            else:
                verb, gather, phase, k = item
                (start if verb == "s" else wait)(phases[gather][phase](k))

    groups = len(EXCHANGE_PROGRAM) - 2
    count = time_len // groups
    for group in range(groups):
        perform(EXCHANGE_PROGRAM[group])
        carry = run(group, count, carry)
    perform(EXCHANGE_PROGRAM[groups])
    perform(EXCHANGE_PROGRAM[groups + 1])
    for k in range(len(LI_CHUNKS)):
        wait(li.third(k))
    tall = li_all.shape[1]
    lane = lax.broadcasted_iota(jnp.int32, (tall, 128), 1)

    def assemble(b, _):
        cut = pl.ds(pl.multiple_of(b * 128, 128), 128)
        even = li_all[2 * b].astype(F32)
        odd = li_all[2 * b + 1].astype(F32)
        li_out[:tall, cut] = jnp.where(lane < 64, even, pltpu.roll(odd, 64, 1)).astype(BF16)
        li_out[tall:, cut] = jnp.where(lane < 64, pltpu.roll(even, 64, 1), odd).astype(BF16)
        return 0

    lax.fori_loop(0, width // 128, assemble, 0)
    for k in range(len(SP_CHUNKS)):
        wait(sp_last(k))


def exchange(
    dims, lengths, factors, grad_mine, grad_other, w_in, w_rec, dp1, dp2, pack, acts_all,
    pairs_low, pairs_high, rows_all,
):
    utts, time_len, _ = factors.shape
    units = w_rec.shape[0]
    width = 4 * units
    pads, wide = dp1.shape
    cells = wide // 4
    chips = dims[0] * dims[1] * dims[2]
    span = acts_all.shape[1] - cells
    deep = sum(rows for _, rows in SP_CHUNKS)
    nz, ny, _ = dims
    packed = pack.shape[0]
    features = pairs_low.shape[1]
    total = features + units + 64
    feat = w_in.shape[0] // 2
    half_time = time_len // 2
    vmem = pl.BlockSpec(memory_space=pltpu.VMEM)
    anywhere = pl.BlockSpec(memory_space=pl.ANY)
    shape = jax.ShapeDtypeStruct
    dma = pltpu.SemaphoreType.DMA
    sp_sems = Gather.semaphores(dims, SP_CHUNKS)
    li_sems = Gather.semaphores(dims, LI_CHUNKS)
    return pl.pallas_call(
        functools.partial(exchange_kernel, dims),
        out_shape=(
            shape((utts, time_len, feat), F32),
            shape((total, width), BF16),
            shape((2, deep, wide), BF16),
        ),
        in_specs=[pl.BlockSpec(memory_space=pltpu.SMEM)] + [vmem] * 8 + [anywhere] * 4,
        out_specs=(vmem, vmem, anywhere),
        scratch_shapes=[
            pltpu.VMEM((utts, time_len, width), F32),
            pltpu.VMEM((utts, time_len, units), F32),
            pltpu.VMEM((acts_all.shape[0], span), BF16),
            pltpu.VMEM((chips * utts * time_len, features), BF16),
            pltpu.VMEM((chips * utts * time_len, 2 * SIDE), BF16),
            pltpu.VMEM((3, pads, wide), BF16),
            pltpu.VMEM((chips, 2, pads, 128), BF16),
            pltpu.VMEM((2, 128, chips * 2 * pads), BF16),
            pltpu.VMEM((128, span), F32),
            pltpu.VMEM((deep, 128), BF16),
            pltpu.VMEM((chips, time_len, 128), BF16),
            pltpu.VMEM((chips, time_len, 128), BF16),
            pltpu.VMEM((chips * 2 * time_len, 128), BF16),
            pltpu.VMEM((128, features + 2 * SIDE), F32),
            pltpu.VMEM((chips, total // 2, 128), BF16),
            pltpu.VMEM((utts, half_time, 2 * feat), BF16),
            pltpu.VMEM((utts, half_time, 2 * feat), BF16),
            pltpu.VMEM((time_len, 128), F32),
            pltpu.VMEM((packed, wide), BF16),
            pltpu.VMEM((ny, packed, nz * 128), BF16),
            pltpu.VMEM((ny, packed, nz * 128), BF16),
            pltpu.VMEM((packed, nz * 128), BF16),
            pltpu.VMEM((packed, nz * 128), BF16),
            pltpu.VMEM((nz, packed, 128), BF16),
            dma((5 + 2 * 4,)),
            dma((3 + len(SP_CHUNKS),)),
            dma((3 + len(SP_CHUNKS),)),
            dma((chips - 1,)),
            dma((chips - 1,)),
            dma((len(STREAMS), chips - 1)),
            dma((len(STREAMS), chips - 1)),
            sp_sems,
            sp_sems,
            li_sems,
            li_sems,
            dma((1 + ny + nz,)),
            dma((1 + ny + nz,)),
            pltpu.VMEM(grad_other.shape, BF16),
            pltpu.VMEM((width, units), BF16),
        ],
        compiler_params=pltpu.CompilerParams(
            vmem_limit_bytes=VMEM_BYTES, collective_id=0, has_side_effects=True
        ),
    )(
        lengths, factors, grad_mine, grad_other, w_in, w_rec, dp1, dp2, pack,
        acts_all, pairs_low, pairs_high, rows_all,
    )


PIECE = 128
SLOTS = 6


def widen_kernel(jobs, sizes, sp, li, *refs):
    *outs, narrow, wide, few, last, in_sem, out_sem, few_sem = refs
    g_out, g_table, low_bias, up_bias, g_vec, g_obias, sum_bias = outs[-7:]

    def source(n):
        which, row, col, out, _, rows = jobs[n]
        ref = li if which == 2 else sp.at[which]
        width = outs[out].shape[-1]
        return pltpu.make_async_copy(
            ref.at[pl.ds(row, rows), pl.ds(col, width)],
            narrow.at[n % SLOTS, pl.ds(0, rows), pl.ds(0, width)],
            in_sem.at[n % SLOTS],
        )

    def target(n):
        _, _, _, out, row, rows = jobs[n]
        width = outs[out].shape[-1]
        return pltpu.make_async_copy(
            wide.at[n % SLOTS, pl.ds(0, rows), pl.ds(0, width)],
            outs[out].at[pl.ds(row, rows)],
            out_sem.at[n % SLOTS],
        )

    load_few = [
        pltpu.make_async_copy(sp.at[1, pl.ds(0, 2 * SMALL)], few, few_sem.at[0]),
        pltpu.make_async_copy(li.at[pl.ds(sizes[-1], 16)], last, few_sem.at[1]),
    ]
    for n in range(min(SLOTS, len(jobs))):
        source(n).start()
    start(load_few)
    for n in range(len(jobs)):
        source(n).wait()
        if n >= SLOTS:
            target(n - SLOTS).wait()
        rows, width = jobs[n][5], outs[jobs[n][3]].shape[-1]
        wide[n % SLOTS, :rows, :width] = narrow[n % SLOTS, :rows, :width].astype(F32)
        target(n).start()
        if n + SLOTS < len(jobs):
            source(n + SLOTS).start()
    wait(load_few)
    small = few[:SMALL].astype(F32) + few[SMALL:].astype(F32)
    cells, base, embed, att, vocab, _ = sizes
    g_out[...] = small[:vocab, :base]
    g_table[...] = small[:vocab, base : base + embed]
    base += embed
    for k in range(4):
        cut = slice(k * cells, (k + 1) * cells)
        low_bias[cut] = small[2 + k, base : base + cells]
        up_bias[cut] = small[6 + k, base : base + cells]
    g_vec[...] = small[0, base : base + att]
    g_obias[...] = small[1, base : base + vocab]
    sum_bias[...] = last[0:1, :].astype(F32)
    for n in range(max(0, len(jobs) - SLOTS), len(jobs)):
        target(n).wait()


def widen(sp, li, parts, sizes):
    jobs = []
    for out, (_, pieces) in enumerate(parts):
        done = 0
        for which, row, col, rows in pieces:
            for at in range(0, rows, PIECE):
                count = min(PIECE, rows - at)
                jobs.append((which, row + at, col, out, done, count))
                done += count
    cells, base, embed, att, vocab, _ = sizes
    wide = sp.shape[2]
    anywhere = pl.BlockSpec(memory_space=pl.ANY)
    vmem = pl.BlockSpec(memory_space=pltpu.VMEM)
    dma = pltpu.SemaphoreType.DMA
    few = ((vocab, base), (vocab, embed), (4 * cells,), (4 * cells,), (att,), (vocab,), (1, li.shape[1]))
    return pl.pallas_call(
        functools.partial(widen_kernel, jobs, sizes),
        out_shape=[jax.ShapeDtypeStruct(shape, F32) for shape, _ in parts]
        + [jax.ShapeDtypeStruct(shape, F32) for shape in few],
        in_specs=[anywhere] * 2,
        out_specs=[anywhere] * len(parts) + [vmem] * len(few),
        scratch_shapes=[
            pltpu.VMEM((SLOTS, PIECE, wide), BF16),
            pltpu.VMEM((SLOTS, PIECE, wide), F32),
            pltpu.VMEM((2 * SMALL, wide), BF16),
            pltpu.VMEM((16, li.shape[1]), BF16),
            dma((SLOTS,)),
            dma((SLOTS,)),
            dma((2,)),
        ],
        compiler_params=pltpu.CompilerParams(vmem_limit_bytes=VMEM_BYTES),
    )(sp, li)


def shards(
    frames,
    step_lengths,
    characters,
    char_lengths,
    listen_input,
    listen_hidden,
    listen_bias,
    lower_input,
    lower_hidden,
    lower_bias,
    upper_input,
    upper_hidden,
    upper_bias,
    key_proj,
    query_proj,
    score_vector,
    output_proj,
    output_bias,
    char_table,
):
    chips = lax.axis_size("dp")
    utts, frame_len, feat = frames.shape
    time_len = frame_len // 2
    swap = [(0, 1), (1, 0)]
    w_in, w_rec = listen_input[0], listen_hidden[0]
    units = w_rec.shape[0]
    cells = lower_hidden.shape[0]
    vocab, embed = char_table.shape
    fits = (
        chips % 4 == 0
        and 4 * cells == 128 * chips
        and 4 * units == 64 * chips
        and embed == 256
        and cells == 2 * units
        and time_len == SEGMENT * STREAMS[-1][1]
        and embed + 2 * units + cells + 2 * SMALL == sum(rows for _, rows in SP_CHUNKS)
        and embed + 2 * SMALL == HEAD
        and time_len == 3 * PART
        and characters.shape[2] % SPELL_GROUPS == 0
        and 2 * feat + units + 64 == 2 * sum(rows for _, rows in LI_CHUNKS)
    )
    dims = (chips // 4, 2, 2) if fits else None
    pairs, rows, factors, mine, other, *low_pairs = listen_forward(
        dims, step_lengths, frames, w_in, w_rec, listen_bias
    )
    if not fits:
        other = lax.ppermute(other, "role", swap)
    vec = score_vector
    loss, prev_onehot, acts, key, *kept = speller_forward(
        dims, step_lengths, char_lengths, characters, pairs, rows, mine, other,
        lower_input, lower_hidden, lower_bias, upper_input, upper_hidden, upper_bias,
        key_proj, query_proj, vec, output_proj.T, output_bias, char_table,
    )
    if fits:
        *kept, high_pairs, rows_all = kept
    grad_mine, grad_other, dp1, dp2, pack = speller_backward(
        lower_input, lower_hidden, upper_input, upper_hidden, key_proj, query_proj, vec,
        prev_onehot, acts, key, *kept,
    )
    if fits:
        flat = lambda gathered: gathered.reshape(-1, gathered.shape[-1])
        acts_all = lax.all_gather(acts, ("dp", "role"), tiled=True)
        frame_grad, li, sp = exchange(
            dims, step_lengths, factors, grad_mine, grad_other, w_in, w_rec,
            dp1, dp2, pack, acts_all, flat(low_pairs[0]), flat(high_pairs), flat(rows_all),
        )
        width = 2 * feat
        att = key_proj.shape[1]
        first = 2 * SMALL
        low, high = first + embed, first + embed + 2 * units
        wide = 4 * cells
        deep = 2 * units * att // wide
        folded = lambda row: tuple((1, row, col, deep) for col in range(0, wide, att))
        *layers, sum_in, sum_rec, g_key, g_query, g_out, g_table, low_bias, up_bias, g_vec, g_obias, sum_bias = widen(
            sp,
            li,
            (
                ((high - first, wide), ((0, first, 0, high - first),)),
                ((cells, wide), ((0, high, 0, cells),)),
                ((cells, wide), ((1, low, 0, cells),)),
                ((cells, wide), ((1, low + cells, 0, cells),)),
                ((width, 4 * units), ((2, 0, 0, width),)),
                ((units, 4 * units), ((2, width, 0, units),)),
                ((2 * units, att), folded(first)),
                ((cells, att), folded(first + deep)),
            ),
            (cells, cells + 2 * units, embed, att, vocab, width + units),
        )
        lower, upper = layers[:2], layers[2:]
        g_out = g_out.T
    else:
        grad_other = lax.ppermute(grad_other, "role", swap)
        pack = lax.psum(pack.astype(F32), ("role", "dp"))
        small = pack[: 2 * SMALL]
        g_key, g_query = (
            unfold(part, cells) for part in jnp.split(pack[2 * SMALL :], 2, axis=0)
        )
        low_bias, up_bias, g_vec, g_out, g_obias, g_table = unpack(
            small, units, cells, key_proj.shape[1], vocab, embed
        )
        pre = listen_backward(step_lengths, factors, grad_mine, grad_other, w_rec)
        flat = pre.reshape(utts * time_len, 4 * units)
        sums = mm(jnp.concatenate([pairs.reshape(flat.shape[0], 2 * feat), rows], 1).T, flat)
        sums = lax.psum(sums, "dp")
        width = 2 * feat
        sum_in, sum_rec = sums[:width], sums[width : width + units]
        sum_bias = lax.psum(jnp.sum(flat.astype(F32), 0, keepdims=True), "dp")
        grad_pairs = mm(flat, w_in.T).reshape(utts, frame_len, feat)
        frame_grad = lax.psum_scatter(grad_pairs, "role", scatter_dimension=1, tiled=True)
        cuts = [embed, embed + 2 * units, embed + 2 * units + cells]
        emb, ctx, s1, s2 = jnp.split(acts, cuts, axis=1)
        local = (
            jnp.concatenate([mm(emb.T, dp1), mm(ctx[:-1].T, dp1[1:])], 0),
            mm(s1[:-1].T, dp1[1:]),
            mm(s1.T, dp2),
            mm(s2[:-1].T, dp2[1:]),
        )
        local = lax.psum(local, ("role", "dp"))
        lower, upper = local[:2], local[2:]
    return (
        loss, frame_grad, sum_in[None], sum_rec[None], sum_bias,
        *lower, low_bias, *upper, up_bias,
        g_key, g_query, g_vec, g_out, g_obias, g_table,
    )


def solution(mesh):
    whole = P()
    return jax.shard_map(
        shards,
        mesh=mesh,
        in_specs=(
            P("dp", None, None),
            P("dp"),
            P("dp", "role", None),
            P("dp", "role"),
            P("role", None, None),
            P("role", None, None),
            P("role", None),
        )
        + (whole,) * 12,
        out_specs=(
            P("dp", "role"),
            P("dp", "role", None),
            P("role", None, None),
            P("role", None, None),
            P("role", None),
        )
        + (whole,) * 12,
        check_vma=False,
    )
```
